32 devices in a mesh: groups: 2 (over y), seq: 4 (over z), tp: 4 (over x, core).
Axes of the slice: x: 2, y: 2, z: 4, core: 2. Of those that a mesh axis runs over, the one named last changes fastest.
Arguments:
- hidden: bfloat16 [8, 192, 8192], P(('groups', 'seq')), parts along dimension 0, may hold values from -6 to 6
- queries: bfloat16 [8, 192, 4096], P(('groups', 'seq'), None, 'tp'), parts along dimension 0, may hold values from -6 to 6
- w_key: bfloat16 [8192, 512], P('seq', 'tp'), may hold values from -0.0625 to 0.0625
- w_value: bfloat16 [8192, 512], P('seq', 'tp'), may hold values from -0.0625 to 0.0625
- store_keys: bfloat16 [64, 128, 512], P(('groups', 'seq'), None, 'tp'), parts along dimension 0, may hold values from -160 to 160
- store_values: bfloat16 [64, 128, 512], P(('groups', 'seq'), None, 'tp'), parts along dimension 0, may hold values from -6 to 6
- request_docs: int32 [8, 16], P('groups'), parts along dimension 0, may hold values from 0 to 31, as said below
- doc_lengths: int32 [64], P('groups'), parts along dimension 0, may hold values from 48 to 128, as said below
- recompute_rows: int32 [8, 16, 12], P(('groups', 'seq')), parts along dimension 0, may hold values from 0 to 127, as said below
Outputs:
- mixed: bfloat16 [8, 192, 4096], P(('groups', 'seq'), None, 'tp'), parts along dimension 0
- returned: bfloat16 [8, 4, 4, 12, 2, 512], P(('groups', 'seq'), None, None, None, None, 'tp'), parts along dimension 0
The draws below stay inside these ranges and needn't reach their ends.
There are 2 independent parts, one for each index of `groups`. The reference program is written for one: setup_inputs(seed, part) draws one part's arguments, and reference() takes and returns one part's arrays. A program takes and returns all parts, laid end to end along the dimension named above; an argument that names none is the same for every part. Nothing has to cross between parts.
Inputs may be any that keep to these rules, and one draw needn't show every extreme that they name: `request_docs`: the 16 documents of a request are distinct; no owner holds more than 4 of them, and some owner holds exactly 4 in every request. `doc_lengths`: some document has exactly 128 tokens. `recompute_rows`: the 12 positions of one document in one request are distinct and below that document's length.
All inputs are finite; a program needn't handle non-finite values.
Results may differ from the reference program's by a relative error of at most 0.0052.
Values may be sent and summed in bfloat16 or wider, within the bound.
No kernel may reach another device: no remote copies, remote signals or barrier semaphores. Data moves between devices by JAX's collectives and lax.ppermute only.
A program may use at most 64 MiB of HBM per device.

```python
import math
import jax
import jax.numpy as jnp
from jax import lax

D = 8192
HEAD = 128
NDOC = 16
DOC_LEN = 128
R_DOC = 12
QW = 4096
KVW = 512
CAP = 4
SLOTS = 8
STORE = 32
REQUESTS = 4
NROWS = 192
CTX = 2048
N_SEQ = 4


def common_docs(key):
    key = jax.random.fold_in(key, 101)
    order_keys = jax.random.split(key, REQUESTS + 1)

    def one_request(order_key):
        return jax.random.permutation(order_key, N_SEQ * CAP)[:NDOC]
    tickets = jax.vmap(one_request)(order_keys[:REQUESTS])
    halves = jax.random.randint(order_keys[REQUESTS], (REQUESTS, NDOC), 0, 2)
    owner_ids = tickets // CAP
    places = tickets % CAP
    return (owner_ids * SLOTS + 2 * places + halves).astype(jnp.int32)


def common_lengths(key):
    key = jax.random.fold_in(key, 202)
    first_key, second_key = jax.random.split(key)
    lengths = jax.random.randint(first_key, (STORE,), 4 * R_DOC, DOC_LEN + 1)
    longest = jax.random.randint(second_key, (), 0, STORE)
    return lengths.at[longest].set(DOC_LEN).astype(jnp.int32)


def draw_request_docs(key, part):
    return common_docs(key)


def draw_doc_lengths(key, part):
    return common_lengths(key)


def draw_recompute_rows(key, part):
    doc_ids = common_docs(key)
    lengths = common_lengths(key)
    key = jax.random.fold_in(key, 7)
    doc_size = lengths[doc_ids]
    places = jnp.arange(DOC_LEN, dtype=jnp.int32)[None, None, :]
    tickets = jax.random.randint(key, (REQUESTS, NDOC, DOC_LEN), 0, 1 << 20) * DOC_LEN + places
    ranked = jnp.where(places < doc_size[:, :, None], tickets, (1 << 30) + places)
    chosen = jnp.argsort(ranked, axis=-1)[:, :, :R_DOC]
    return chosen.astype(jnp.int32)


def draw_store_keys(key, part):
    key = jax.random.fold_in(key, 11)
    first_key = jax.random.fold_in(key, 0)
    shape = (STORE, DOC_LEN, KVW)
    return jnp.clip(jax.random.normal(first_key, shape), -5.0, 5.0).astype(jnp.bfloat16)


def block_levels(rng, dims, cuts, least, high):
    loudness = 1.0
    for dim, parts in cuts:
        heights = jax.random.uniform(jax.random.fold_in(jax.random.fold_in(rng, 6), dim), (parts,), jnp.float32, least / len(cuts), high / len(cuts))
        loudness = loudness * jnp.repeat(jnp.exp(heights), dims[dim] // parts).reshape((-1,) + (1,) * (len(dims) - 1 - dim))
    return loudness


def normal_values(stream_key, extent, spread, reach, pieces=(), held_as=jnp.bfloat16):
    entries = jax.random.normal(stream_key, extent, jnp.float32) * spread
    if len(pieces) > 0:
        entries = block_levels(stream_key, extent, pieces, -0.22, 0.18) * entries
    return jnp.clip(entries, min=-reach, max=reach).astype(held_as)


def setup_inputs(seed: int = 0, part: int = 0) -> dict:
    key_list = jax.random.split(jax.random.key(seed), 10)
    part_keys = jax.random.split(jax.random.fold_in(key_list[9], part), 10)
    return {
        "hidden": normal_values(part_keys[0], (REQUESTS, NROWS, D), 1.0, 6.0, ((0, 4),)),
        "queries": normal_values(part_keys[1], (REQUESTS, NROWS, QW), 1.0, 6.0, ((0, 4), (2, 4))),
        "w_key": normal_values(key_list[2], (D, KVW), D ** -0.5, 0.0625, ((0, 4), (1, 4))),
        "w_value": normal_values(key_list[3], (D, KVW), D ** -0.5, 0.0625, ((0, 4), (1, 4))),
        "store_keys": draw_store_keys(jax.random.fold_in(jax.random.fold_in(key_list[9], part), 71), part),
        "store_values": normal_values(part_keys[5], (STORE, DOC_LEN, KVW), 1.0, 6.0, ((0, 4), (2, 4))),
        "request_docs": draw_request_docs(jax.random.fold_in(jax.random.fold_in(key_list[9], part), 71), part),
        "doc_lengths": draw_doc_lengths(jax.random.fold_in(jax.random.fold_in(key_list[9], part), 71), part),
        "recompute_rows": draw_recompute_rows(jax.random.fold_in(jax.random.fold_in(key_list[9], part), 71), part),
    }


def owner_ranks(owners):
    same_owner = owners[:, :, None] == owners[:, None, :]
    earlier = jnp.arange(NDOC)[None, :] < jnp.arange(NDOC)[:, None]
    return lax.optimization_barrier(jnp.sum((same_owner & earlier[None]).astype(jnp.int32), axis=2)).astype(jnp.int32)

def reference(hidden, queries, w_key, w_value, store_keys, store_values, request_docs, doc_lengths, recompute_rows):
    kv_width = w_key.shape[1]
    kv_heads = kv_width // HEAD
    q_heads = queries.shape[2] // HEAD
    group_size = q_heads // kv_heads
    score_scale = 1.0 / math.sqrt(HEAD)
    positions = jnp.arange(DOC_LEN, dtype=jnp.int32)
    doc_column = jnp.arange(NDOC, dtype=jnp.int32)[:, None]

    def serve_one(inputs):
        row_states, row_queries, doc_ids, row_ids = inputs
        fresh_k = jnp.dot(row_states, w_key, preferred_element_type=jnp.float32).astype(jnp.bfloat16)
        fresh_v = jnp.dot(row_states, w_value, preferred_element_type=jnp.float32).astype(jnp.bfloat16)
        context_k = store_keys[doc_ids].at[doc_column, row_ids].set(fresh_k.reshape(NDOC, R_DOC, kv_width))
        context_v = store_values[doc_ids].at[doc_column, row_ids].set(fresh_v.reshape(NDOC, R_DOC, kv_width))
        in_length = positions[None, :] < doc_lengths[doc_ids][:, None]
        key_place = (doc_column * DOC_LEN + positions[None, :]).reshape(CTX)
        query_place = (doc_column * DOC_LEN + row_ids).reshape(NROWS)
        allowed = in_length.reshape(CTX)[None, :] & (key_place[None, :] <= query_place[:, None])
        q_float = row_queries.astype(jnp.float32).reshape(NROWS, kv_heads, group_size, HEAD)
        k_float = context_k.astype(jnp.float32).reshape(CTX, kv_heads, HEAD)
        v_float = context_v.astype(jnp.float32).reshape(CTX, kv_heads, HEAD)
        scores = jnp.einsum('qhgd,khd->hgqk', q_float, k_float) * score_scale
        scores = jnp.where(allowed[None, None], scores, -jnp.inf)
        row_max = lax.optimization_barrier(jnp.max(scores, axis=-1, keepdims=True))
        powers = jnp.exp(scores - row_max)
        row_sum = lax.optimization_barrier(jnp.sum(powers, axis=-1, keepdims=True))
        probs = (powers / row_sum).astype(jnp.bfloat16)
        outputs = jnp.einsum('hgqk,khd->qhgd', probs.astype(jnp.float32), v_float)
        mixed = outputs.reshape(NROWS, q_heads * HEAD).astype(jnp.bfloat16)
        fresh_kv = jnp.stack([fresh_k, fresh_v], axis=1).reshape(NDOC, R_DOC, 2, kv_width)
        return (mixed, fresh_kv)
    mixed, fresh_kv = lax.map(serve_one, (hidden, queries, request_docs, recompute_rows))
    owners = (request_docs // SLOTS).astype(jnp.int32)
    ranks = owner_ranks(owners)
    requester = jnp.broadcast_to(jnp.arange(REQUESTS, dtype=jnp.int32)[:, None], (REQUESTS, NDOC))
    returned = jnp.zeros((N_SEQ, REQUESTS, CAP, R_DOC, 2, kv_width), jnp.bfloat16)
    returned = returned.at[owners, requester, ranks].set(fresh_kv)
    return (mixed, returned)
```

```python
import functools
import math

import jax
import jax.numpy as jnp
from jax import lax
from jax.experimental import pallas as pl
from jax.experimental.pallas import tpu as pltpu
from jax.sharding import PartitionSpec as P

ANY = pl.BlockSpec(memory_space=pl.ANY)
SMEM = pl.BlockSpec(memory_space=pltpu.SMEM)
VMEM = pl.BlockSpec(memory_space=pltpu.VMEM)
MASKED = -1e30


def cut_kernel(hidden, w_key, w_value, w_out, h_out, sems):
    group = lax.axis_index("groups")
    me = lax.axis_index("seq")
    core = lax.rem(lax.axis_index("tp"), 2)
    depth = w_key.shape[0]
    half = w_out.shape[1]
    rows = h_out.shape[1]
    copies = []
    for i, weight in enumerate((w_key, w_value)):
        source = weight.at[pl.ds(pl.multiple_of(group * half, half), half)]
        copies.append(pltpu.make_async_copy(source, w_out.at[i], sems.at[i]))
    first = me + 1 - 2 * lax.rem(me, 2)
    second = lax.rem(first + 2, 4)
    for i, block in enumerate((first, second)):
        source = hidden.at[
            0,
            pl.ds(pl.multiple_of(core * rows, rows), rows),
            pl.ds(pl.multiple_of(block * depth, depth), depth),
        ]
        copies.append(pltpu.make_async_copy(source, h_out.at[i], sems.at[2 + i]))
    for copy in copies:
        copy.start()
    for copy in copies:
        copy.wait()


def cut(hidden, w_key, w_value):
    depth = w_key.shape[0]
    return pl.pallas_call(
        cut_kernel,
        out_shape=(
            jax.ShapeDtypeStruct((2, depth // 2, w_key.shape[1]), jnp.bfloat16),
            jax.ShapeDtypeStruct((2, hidden.shape[1] // 2, depth), jnp.bfloat16),
        ),
        in_specs=[ANY] * 3,
        out_specs=(ANY, ANY),
        scratch_shapes=[pltpu.SemaphoreType.DMA((4,))],
        name="cut",
    )(hidden, w_key, w_value)


def docs_kernel(by_owner, request_docs, store_keys, store_values, *rest):
    outs, (picks, sems) = rest[:-2], rest[-2:]
    me = lax.axis_index("seq")
    requests, doc_count = request_docs.shape
    slots = store_keys.shape[0]
    capacity = slots // 2

    def one_request(r, carry):
        for c in range(capacity):
            picks[r, c] = 0

        def one_doc(j, count):
            doc = request_docs[r, j]
            mine = lax.div(doc, slots) == me

            @pl.when(mine)
            def _():
                picks[r, jnp.minimum(count, capacity - 1)] = lax.rem(doc, slots)

            return count + mine.astype(jnp.int32)

        lax.fori_loop(0, doc_count, one_doc, jnp.int32(0), unroll=True)
        return carry

    lax.fori_loop(0, requests, one_request, 0)

    def send(r, out, sem):
        for c in range(capacity):
            slot = picks[r, c]
            pltpu.make_async_copy(store_keys.at[slot], out.at[c, 0], sem).start()
            pltpu.make_async_copy(store_values.at[slot], out.at[c, 1], sem).start()

    if by_owner:
        out = outs[0]

        def one_send(r, carry):
            send(r, out.at[r], sems.at[0])
            return carry

        lax.fori_loop(0, requests, one_send, 0)
    else:
        for i, out in enumerate(outs):
            send(lax.bitwise_xor(me, i + 1), out, sems.at[i])
    for i, out in enumerate(outs):
        pltpu.make_async_copy(out, out, sems.at[i]).wait()


def cut_docs(request_docs, store_keys, store_values, by_owner):
    requests = request_docs.shape[0]
    capacity = store_keys.shape[0] // 2
    one = (capacity, 2) + store_keys.shape[1:]
    if by_owner:
        shapes = (jax.ShapeDtypeStruct((requests,) + one, jnp.bfloat16),)
    else:
        shapes = (jax.ShapeDtypeStruct(one, jnp.bfloat16),) * (requests - 1)
    return pl.pallas_call(
        functools.partial(docs_kernel, by_owner),
        out_shape=shapes,
        in_specs=[SMEM, ANY, ANY],
        out_specs=(ANY,) * len(shapes),
        scratch_shapes=[
            pltpu.SMEM((requests, capacity), jnp.int32),
            pltpu.SemaphoreType.DMA((len(shapes),)),
        ],
        name="cut_docs",
    )(request_docs, store_keys, store_values)


def project_kernel(hidden, w_key, w_value, w_mine, w_other, h_mine, h_other, own, part, w, h, sems):
    group = lax.axis_index("groups")
    me = lax.axis_index("seq")
    core = lax.rem(lax.axis_index("tp"), 2)
    depth, width = w_key.shape
    half = depth // 2
    rows = hidden.shape[1]
    far = lax.rem(me + 2, 4)
    copies = []

    def copy(source, target):
        copies.append(pltpu.make_async_copy(source, target, sems.at[len(copies)]))

    for i, weight in enumerate((w_key, w_value)):
        columns = pl.ds(i * width, width)
        copy(weight, w.at[pl.ds(0, depth), columns])
        for held, place in ((w_mine, group), (w_other, 1 - group)):
            copy(held.at[i], w.at[pl.ds(pl.multiple_of(depth + place * half, half), half), columns])
    for i, block in enumerate((me, far)):
        columns = pl.ds(i * depth, depth)
        copy(
            hidden.at[0, :, pl.ds(pl.multiple_of(block * depth, depth), depth)],
            h.at[pl.ds(0, rows), columns],
        )
        for held, place in ((h_mine, core), (h_other, 1 - core)):
            start = rows + place * (rows // 2)
            copy(held.at[i], h.at[pl.ds(pl.multiple_of(start, rows // 2), rows // 2), columns])
    for one in copies:
        one.start()
    for one in copies:
        one.wait()
    total = jnp.dot(h[...], w[...], preferred_element_type=jnp.float32)
    own[...] = total[:rows]
    part[...] = total[rows:].astype(part.dtype)


def project(hidden, w_key, w_value, w_mine, w_other, h_mine, h_other):
    depth, width = w_key.shape
    rows = hidden.shape[1]
    return pl.pallas_call(
        project_kernel,
        out_shape=(
            jax.ShapeDtypeStruct((rows, 2 * width), jnp.float32),
            jax.ShapeDtypeStruct((rows, 2 * width), jnp.bfloat16),
        ),
        in_specs=[ANY] * 7,
        out_specs=(VMEM, VMEM),
        scratch_shapes=[
            pltpu.VMEM((2 * depth, 2 * width), jnp.bfloat16),
            pltpu.VMEM((2 * rows, 2 * depth), jnp.bfloat16),
            pltpu.SemaphoreType.DMA((12,)),
        ],
        compiler_params=pltpu.CompilerParams(vmem_limit_bytes=32 * 1024 * 1024),
        name="project",
    )(hidden, w_key, w_value, w_mine, w_other, h_mine, h_other)


def attend_kernel(
    by_owner, request_docs, queries, fresh, key_bias, row_place, key_place, *rest
):
    sources, (mixed, context_k, context_v, counts, sems) = rest[:-5], rest[-5:]
    me = lax.axis_index("seq")
    doc_count = request_docs.shape[1]
    head_dim = context_k.shape[1]
    doc_len = context_k.shape[0] // doc_count
    row_count = queries.shape[1]
    per_doc = row_count // doc_count
    heads = queries.shape[2] // head_dim
    owners = request_docs.shape[0]
    slots = sources[0].shape[0] if not by_owner else 2 * sources[0].shape[1]

    for o in range(owners):
        counts[o] = 0

    def one_doc(j, carry):
        doc = request_docs[me, j]
        owner = lax.div(doc, slots)
        rank = counts[owner]
        counts[owner] = rank + 1
        place = pl.ds(pl.multiple_of(j * doc_len, doc_len), doc_len)

        def fetch(key_source, value_source):
            pltpu.make_async_copy(key_source, context_k.at[place], sems.at[0]).start()
            pltpu.make_async_copy(value_source, context_v.at[place], sems.at[1]).start()

        if by_owner:
            fetch(sources[0].at[owner, rank, 0], sources[0].at[owner, rank, 1])
        else:
            away = lax.bitwise_xor(me, owner)

            @pl.when(away == 0)
            def _():
                slot = lax.rem(doc, slots)
                fetch(sources[0].at[slot], sources[1].at[slot])

            for k in range(1, owners):

                @pl.when(away == k)
                def _():
                    fetch(sources[1 + k].at[rank, 0], sources[1 + k].at[rank, 1])

        return carry

    lax.fori_loop(0, doc_count, one_doc, 0)
    pltpu.make_async_copy(context_k, context_k, sems.at[0]).wait()
    pltpu.make_async_copy(context_v, context_v, sems.at[1]).wait()

    scale = math.log2(math.e) / math.sqrt(head_dim)
    fresh_k = fresh[:, :head_dim]
    fresh_v = fresh[:, head_dim:]
    step = 4 if doc_count % 4 == 0 else 1
    block_rows = step * per_doc
    block_keys = step * doc_len
    slot_place = lax.broadcasted_iota(jnp.int32, (1, block_keys), 1)
    contract_last = (((1,), (1,)), ((), ()))
    for b in range(doc_count // step):
        rows = slice(b * block_rows, (b + 1) * block_rows)
        q = jnp.concatenate(
            [queries[0, rows, h * head_dim : (h + 1) * head_dim] for h in range(heads)], axis=0
        )
        own_place = row_place[rows, :]

        def masked(keys, bias):
            scores = lax.dot_general(q, keys, contract_last, preferred_element_type=jnp.float32)
            scores = (scores * scale).reshape(heads, block_rows, keys.shape[0])
            return (scores + bias[None]).reshape(heads * block_rows, keys.shape[0])

        chunks, values = [], []
        for c in range(b + 1):
            keys = slice(c * block_keys, (c + 1) * block_keys)
            bias = jnp.broadcast_to(key_bias[:, keys], (block_rows, block_keys))
            if c == b:
                bias = jnp.where(slot_place + c * block_keys <= own_place, bias, MASKED)
            chunks.append(masked(context_k[keys, :], bias))
            values.append(context_v[keys, :])
        bias = jnp.where(key_place[...] <= own_place, 0.0, MASKED)
        chunks.append(masked(fresh_k, bias))
        values.append(fresh_v)
        row_max = functools.reduce(
            jnp.maximum, [jnp.max(one, axis=1, keepdims=True) for one in chunks]
        )
        total = jnp.zeros((heads * block_rows, head_dim), jnp.float32)
        row_sum = jnp.zeros((heads * block_rows, 1), jnp.float32)
        for one, value in zip(chunks, values):
            powers = jnp.exp2(one - row_max)
            row_sum += jnp.sum(powers, axis=1, keepdims=True)
            total += jnp.dot(
                powers.astype(jnp.bfloat16), value, preferred_element_type=jnp.float32
            )
        result = (total / row_sum).astype(mixed.dtype)
        for h in range(heads):
            mixed[0, rows, h * head_dim : (h + 1) * head_dim] = result[
                h * block_rows : (h + 1) * block_rows
            ]


def attend(request_docs, queries, fresh, key_bias, row_place, key_place, sources, by_owner):
    head_dim = fresh.shape[1] // 2
    context = key_bias.shape[1]
    return pl.pallas_call(
        functools.partial(attend_kernel, by_owner),
        out_shape=jax.ShapeDtypeStruct(queries.shape, jnp.bfloat16),
        in_specs=[SMEM] + [VMEM] * 5 + [ANY] * len(sources),
        out_specs=VMEM,
        scratch_shapes=[
            pltpu.VMEM((context, head_dim), jnp.bfloat16),
            pltpu.VMEM((context, head_dim), jnp.bfloat16),
            pltpu.SMEM((request_docs.shape[0],), jnp.int32),
            pltpu.SemaphoreType.DMA((2,)),
        ],
        compiler_params=pltpu.CompilerParams(vmem_limit_bytes=32 * 1024 * 1024),
        name="attend",
    )(request_docs, queries, fresh, key_bias, row_place, key_place, *sources)


def shards(
    pairs,
    hidden,
    queries,
    w_key,
    w_value,
    store_keys,
    store_values,
    request_docs,
    doc_lengths,
    recompute_rows,
):
    my_index = lax.axis_index("seq")
    seq_count = lax.axis_size("seq")
    slot_count, doc_len, head_dim = store_keys.shape
    capacity = slot_count // 2
    doc_count = request_docs.shape[1]
    row_ids = recompute_rows[0]
    per_doc = row_ids.shape[1]
    row_count = doc_count * per_doc

    if pairs:
        def swap(array, axis, apart):
            count = lax.axis_size(axis)
            return lax.ppermute(array, axis, [(i, i ^ apart) for i in range(count)])

        w_send, h_send = cut(hidden, w_key, w_value)
        w_mine = swap(w_send, "seq", 2)
        h_mine = swap(h_send, "seq", 1)
        docs = cut_docs(request_docs, store_keys, store_values, False)
        docs = [swap(doc, "seq", k + 1) for k, doc in enumerate(docs)]
        w_other = swap(w_mine, "groups", 1)
        h_other = swap(h_mine, "tp", 1)
        own, part = project(hidden, w_key, w_value, w_mine, w_other, h_mine, h_other)
        fresh = (own + swap(part, "seq", 1).astype(jnp.float32)).astype(jnp.bfloat16)
        sources = (store_keys, store_values, *docs)
    else:
        (docs,) = cut_docs(request_docs, store_keys, store_values, True)
        sources = (lax.all_to_all(docs, "seq", split_axis=0, concat_axis=0, tiled=True),)
        weights = lax.all_gather(
            jnp.concatenate([w_key, w_value], axis=1), "seq", axis=0, tiled=True
        )
        fresh = jnp.dot(hidden[0], weights, preferred_element_type=jnp.float32)
        fresh = fresh.astype(jnp.bfloat16)

    my_docs = lax.dynamic_index_in_dim(request_docs, my_index, 0, keepdims=False)
    owners = my_docs // slot_count
    earlier = jnp.arange(doc_count)[None, :] < jnp.arange(doc_count)[:, None]
    ranks = jnp.sum(((owners[:, None] == owners[None, :]) & earlier).astype(jnp.int32), axis=1)
    positions = jnp.arange(doc_len, dtype=jnp.int32)
    held = positions[None, :] < doc_lengths[my_docs][:, None]
    held &= jnp.all(positions[None, None, :] != row_ids[:, :, None], axis=1)
    key_bias = jnp.where(held, 0.0, MASKED).astype(jnp.float32).reshape(1, doc_count * doc_len)
    place = jnp.arange(doc_count, dtype=jnp.int32)[:, None] * doc_len + row_ids
    mixed = attend(
        request_docs,
        queries,
        fresh,
        key_bias,
        place.reshape(row_count, 1),
        place.reshape(1, row_count),
        sources,
        not pairs,
    )

    slot_of_row = jnp.repeat(owners * capacity + ranks, per_doc) * per_doc + jnp.tile(
        jnp.arange(per_doc), doc_count
    )
    slots = jnp.arange(seq_count * capacity * per_doc)
    pick = (slots[:, None] == slot_of_row[None, :]).astype(jnp.bfloat16)
    outgoing = jnp.dot(pick, fresh, preferred_element_type=jnp.float32).astype(jnp.bfloat16)
    outgoing = outgoing.reshape(seq_count, capacity, per_doc, 2 * head_dim)
    returned = lax.all_to_all(outgoing, "seq", split_axis=0, concat_axis=0, tiled=True)
    returned = returned.reshape(seq_count, capacity, per_doc, 2, head_dim)
    return (mixed, returned[None])


def solution(mesh):
    pairs = mesh.shape["seq"] == 4 and mesh.shape["groups"] == 2 and mesh.shape["tp"] % 2 == 0
    return jax.shard_map(
        functools.partial(shards, pairs),
        mesh=mesh,
        in_specs=(
            P(("groups", "seq"), None, None),
            P(("groups", "seq"), None, "tp"),
            P("seq", "tp"),
            P("seq", "tp"),
            P(("groups", "seq"), None, "tp"),
            P(("groups", "seq"), None, "tp"),
            P("groups", None),
            P("groups"),
            P(("groups", "seq"), None, None),
        ),
        out_specs=(
            P(("groups", "seq"), None, "tp"),
            P(("groups", "seq"), None, None, None, None, "tp"),
        ),
        check_vma=False,
    )
```

```python
import functools
import math

import jax
import jax.numpy as jnp
from jax import lax
from jax.experimental import pallas as pl
from jax.experimental.pallas import tpu as pltpu
from jax.sharding import PartitionSpec as P

ANY = pl.BlockSpec(memory_space=pl.ANY)
SMEM = pl.BlockSpec(memory_space=pltpu.SMEM)
VMEM = pl.BlockSpec(memory_space=pltpu.VMEM)
MASKED = -1e30


def cut_kernel(hidden, w_key, w_value, w_out, h_out, sems):
    group = lax.axis_index("groups")
    me = lax.axis_index("seq")
    core = lax.rem(lax.axis_index("tp"), 2)
    depth = w_key.shape[0]
    half = w_out.shape[1]
    rows = h_out.shape[1]
    copies = []
    for i, weight in enumerate((w_key, w_value)):
        source = weight.at[pl.ds(pl.multiple_of(group * half, half), half)]
        copies.append(pltpu.make_async_copy(source, w_out.at[i], sems.at[i]))
    first = me + 1 - 2 * lax.rem(me, 2)
    second = lax.rem(first + 2, 4)
    for i, block in enumerate((first, second)):
        source = hidden.at[
            0,
            pl.ds(pl.multiple_of(core * rows, rows), rows),
            pl.ds(pl.multiple_of(block * depth, depth), depth),
        ]
        copies.append(pltpu.make_async_copy(source, h_out.at[i], sems.at[2 + i]))
    for copy in copies:
        copy.start()
    for copy in copies:
        copy.wait()


def cut(hidden, w_key, w_value):
    depth = w_key.shape[0]
    return pl.pallas_call(
        cut_kernel,
        out_shape=(
            jax.ShapeDtypeStruct((2, depth // 2, w_key.shape[1]), jnp.bfloat16),
            jax.ShapeDtypeStruct((2, hidden.shape[1] // 2, depth), jnp.bfloat16),
        ),
        in_specs=[ANY] * 3,
        out_specs=(VMEM, VMEM),
        scratch_shapes=[pltpu.SemaphoreType.DMA((4,))],
        name="cut",
    )(hidden, w_key, w_value)


def docs_kernel(by_owner, request_docs, store_keys, store_values, *rest):
    outs, (picks, sems) = rest[:-2], rest[-2:]
    me = lax.axis_index("seq")
    requests, doc_count = request_docs.shape
    slots = store_keys.shape[0]
    capacity = slots // 2

    def one_request(r, carry):
        for c in range(capacity):
            picks[r, c] = 0

        def one_doc(j, count):
            doc = request_docs[r, j]
            mine = lax.div(doc, slots) == me

            @pl.when(mine)
            def _():
                picks[r, jnp.minimum(count, capacity - 1)] = lax.rem(doc, slots)

            return count + mine.astype(jnp.int32)

        lax.fori_loop(0, doc_count, one_doc, jnp.int32(0), unroll=True)
        return carry

    lax.fori_loop(0, requests, one_request, 0)

    def send(r, out, sem):
        for c in range(capacity):
            slot = picks[r, c]
            pltpu.make_async_copy(store_keys.at[slot], out.at[c, 0], sem).start()
            pltpu.make_async_copy(store_values.at[slot], out.at[c, 1], sem).start()

    if by_owner:
        out = outs[0]

        def one_send(r, carry):
            send(r, out.at[r], sems.at[0])
            return carry

        lax.fori_loop(0, requests, one_send, 0)
    else:
        for i, out in enumerate(outs):
            send(lax.bitwise_xor(me, i + 1), out, sems.at[i])
    for i, out in enumerate(outs):
        pltpu.make_async_copy(out, out, sems.at[i]).wait()


def cut_docs(request_docs, store_keys, store_values, by_owner):
    requests = request_docs.shape[0]
    capacity = store_keys.shape[0] // 2
    one = (capacity, 2) + store_keys.shape[1:]
    if by_owner:
        shapes = (jax.ShapeDtypeStruct((requests,) + one, jnp.bfloat16),)
    else:
        shapes = (jax.ShapeDtypeStruct(one, jnp.bfloat16),) * (requests - 1)
    return pl.pallas_call(
        functools.partial(docs_kernel, by_owner),
        out_shape=shapes,
        in_specs=[SMEM, ANY, ANY],
        out_specs=(VMEM,) * len(shapes),
        scratch_shapes=[
            pltpu.SMEM((requests, capacity), jnp.int32),
            pltpu.SemaphoreType.DMA((len(shapes),)),
        ],
        name="cut_docs",
    )(request_docs, store_keys, store_values)


def project_kernel(hidden, w_key, w_value, w_mine, w_other, h_mine, h_other, own, part, w, h, sems):
    group = lax.axis_index("groups")
    me = lax.axis_index("seq")
    core = lax.rem(lax.axis_index("tp"), 2)
    depth, width = w_key.shape
    half = depth // 2
    rows = hidden.shape[1]
    far = lax.rem(me + 2, 4)
    copies = []

    def copy(source, target):
        copies.append(pltpu.make_async_copy(source, target, sems.at[len(copies)]))

    for i, weight in enumerate((w_key, w_value)):
        columns = pl.ds(i * width, width)
        copy(weight, w.at[pl.ds(0, depth), columns])
        for held, place in ((w_mine, group), (w_other, 1 - group)):
            copy(held.at[i], w.at[pl.ds(pl.multiple_of(depth + place * half, half), half), columns])
    for i, block in enumerate((me, far)):
        columns = pl.ds(i * depth, depth)
        copy(
            hidden.at[0, :, pl.ds(pl.multiple_of(block * depth, depth), depth)],
            h.at[pl.ds(0, rows), columns],
        )
        for held, place in ((h_mine, core), (h_other, 1 - core)):
            start = rows + place * (rows // 2)
            copy(held.at[i], h.at[pl.ds(pl.multiple_of(start, rows // 2), rows // 2), columns])
    for one in copies:
        one.start()
    for one in copies:
        one.wait()
    total = jnp.dot(h[...], w[...], preferred_element_type=jnp.float32)
    own[...] = total[:rows]
    part[...] = total[rows:].astype(part.dtype)


def project(hidden, w_key, w_value, w_mine, w_other, h_mine, h_other):
    depth, width = w_key.shape
    rows = hidden.shape[1]
    return pl.pallas_call(
        project_kernel,
        out_shape=(
            jax.ShapeDtypeStruct((rows, 2 * width), jnp.float32),
            jax.ShapeDtypeStruct((rows, 2 * width), jnp.bfloat16),
        ),
        in_specs=[ANY] * 7,
        out_specs=(VMEM, VMEM),
        scratch_shapes=[
            pltpu.VMEM((2 * depth, 2 * width), jnp.bfloat16),
            pltpu.VMEM((2 * rows, 2 * depth), jnp.bfloat16),
            pltpu.SemaphoreType.DMA((12,)),
        ],
        compiler_params=pltpu.CompilerParams(vmem_limit_bytes=32 * 1024 * 1024),
        name="project",
    )(hidden, w_key, w_value, w_mine, w_other, h_mine, h_other)


def attend_kernel(
    by_owner, request_docs, queries, fresh, key_bias, row_place, key_place, *rest
):
    sources, (mixed, context_k, context_v, counts, sems) = rest[:-5], rest[-5:]
    me = lax.axis_index("seq")
    doc_count = request_docs.shape[1]
    head_dim = context_k.shape[1]
    doc_len = context_k.shape[0] // doc_count
    row_count = queries.shape[1]
    per_doc = row_count // doc_count
    heads = queries.shape[2] // head_dim
    owners = request_docs.shape[0]
    slots = sources[0].shape[0] if not by_owner else 2 * sources[0].shape[1]

    for o in range(owners):
        counts[o] = 0

    def one_doc(j, carry):
        doc = request_docs[me, j]
        owner = lax.div(doc, slots)
        rank = counts[owner]
        counts[owner] = rank + 1
        place = pl.ds(pl.multiple_of(j * doc_len, doc_len), doc_len)

        def fetch(key_source, value_source):
            pltpu.make_async_copy(key_source, context_k.at[place], sems.at[0]).start()
            pltpu.make_async_copy(value_source, context_v.at[place], sems.at[1]).start()

        if by_owner:
            fetch(sources[0].at[owner, rank, 0], sources[0].at[owner, rank, 1])
        else:
            away = lax.bitwise_xor(me, owner)

            @pl.when(away == 0)
            def _():
                slot = lax.rem(doc, slots)
                fetch(sources[0].at[slot], sources[1].at[slot])

            for k in range(1, owners):

                @pl.when(away == k)
                def _():
                    fetch(sources[1 + k].at[rank, 0], sources[1 + k].at[rank, 1])

        return carry

    lax.fori_loop(0, doc_count, one_doc, 0)
    pltpu.make_async_copy(context_k, context_k, sems.at[0]).wait()
    pltpu.make_async_copy(context_v, context_v, sems.at[1]).wait()

    scale = math.log2(math.e) / math.sqrt(head_dim)
    fresh_k = fresh[:, :head_dim]
    fresh_v = fresh[:, head_dim:]
    step = 4 if doc_count % 4 == 0 else 1
    block_rows = step * per_doc
    block_keys = step * doc_len
    slot_place = lax.broadcasted_iota(jnp.int32, (1, block_keys), 1)
    contract_last = (((1,), (1,)), ((), ()))
    for b in range(doc_count // step):
        rows = slice(b * block_rows, (b + 1) * block_rows)
        q = jnp.concatenate(
            [queries[0, rows, h * head_dim : (h + 1) * head_dim] for h in range(heads)], axis=0
        )
        own_place = row_place[rows, :]

        def masked(keys, bias):
            scores = lax.dot_general(q, keys, contract_last, preferred_element_type=jnp.float32)
            scores = (scores * scale).reshape(heads, block_rows, keys.shape[0])
            return (scores + bias[None]).reshape(heads * block_rows, keys.shape[0])

        chunks, values = [], []
        for c in range(b + 1):
            keys = slice(c * block_keys, (c + 1) * block_keys)
            bias = jnp.broadcast_to(key_bias[:, keys], (block_rows, block_keys))
            if c == b:
                bias = jnp.where(slot_place + c * block_keys <= own_place, bias, MASKED)
            chunks.append(masked(context_k[keys, :], bias))
            values.append(context_v[keys, :])
        bias = jnp.where(key_place[...] <= own_place, 0.0, MASKED)
        chunks.append(masked(fresh_k, bias))
        values.append(fresh_v)
        row_max = functools.reduce(
            jnp.maximum, [jnp.max(one, axis=1, keepdims=True) for one in chunks]
        )
        total = jnp.zeros((heads * block_rows, head_dim), jnp.float32)
        row_sum = jnp.zeros((heads * block_rows, 1), jnp.float32)
        for one, value in zip(chunks, values):
            powers = jnp.exp2(one - row_max)
            row_sum += jnp.sum(powers, axis=1, keepdims=True)
            total += jnp.dot(
                powers.astype(jnp.bfloat16), value, preferred_element_type=jnp.float32
            )
        result = (total / row_sum).astype(mixed.dtype)
        for h in range(heads):
            mixed[0, rows, h * head_dim : (h + 1) * head_dim] = result[
                h * block_rows : (h + 1) * block_rows
            ]


def attend(request_docs, queries, fresh, key_bias, row_place, key_place, sources, by_owner):
    head_dim = fresh.shape[1] // 2
    context = key_bias.shape[1]
    return pl.pallas_call(
        functools.partial(attend_kernel, by_owner),
        out_shape=jax.ShapeDtypeStruct(queries.shape, jnp.bfloat16),
        in_specs=[SMEM] + [VMEM] * 5 + [ANY] * len(sources),
        out_specs=VMEM,
        scratch_shapes=[
            pltpu.VMEM((context, head_dim), jnp.bfloat16),
            pltpu.VMEM((context, head_dim), jnp.bfloat16),
            pltpu.SMEM((request_docs.shape[0],), jnp.int32),
            pltpu.SemaphoreType.DMA((2,)),
        ],
        compiler_params=pltpu.CompilerParams(vmem_limit_bytes=32 * 1024 * 1024),
        name="attend",
    )(request_docs, queries, fresh, key_bias, row_place, key_place, *sources)


def shards(
    pairs,
    hidden,
    queries,
    w_key,
    w_value,
    store_keys,
    store_values,
    request_docs,
    doc_lengths,
    recompute_rows,
):
    my_index = lax.axis_index("seq")
    seq_count = lax.axis_size("seq")
    slot_count, doc_len, head_dim = store_keys.shape
    capacity = slot_count // 2
    doc_count = request_docs.shape[1]
    row_ids = recompute_rows[0]
    per_doc = row_ids.shape[1]
    row_count = doc_count * per_doc

    if pairs:
        def swap(array, axis, apart):
            count = lax.axis_size(axis)
            return lax.ppermute(array, axis, [(i, i ^ apart) for i in range(count)])

        w_send, h_send = cut(hidden, w_key, w_value)
        w_mine = swap(w_send, "seq", 2)
        h_mine = swap(h_send, "seq", 1)
        docs = cut_docs(request_docs, store_keys, store_values, False)
        docs = [swap(doc, "seq", k + 1) for k, doc in enumerate(docs)]
        w_other = swap(w_mine, "groups", 1)
        h_other = swap(h_mine, "tp", 1)
        own, part = project(hidden, w_key, w_value, w_mine, w_other, h_mine, h_other)
        fresh = (own + swap(part, "seq", 1).astype(jnp.float32)).astype(jnp.bfloat16)
        sources = (store_keys, store_values, *docs)
    else:
        (docs,) = cut_docs(request_docs, store_keys, store_values, True)
        sources = (lax.all_to_all(docs, "seq", split_axis=0, concat_axis=0, tiled=True),)
        weights = lax.all_gather(
            jnp.concatenate([w_key, w_value], axis=1), "seq", axis=0, tiled=True
        )
        fresh = jnp.dot(hidden[0], weights, preferred_element_type=jnp.float32)
        fresh = fresh.astype(jnp.bfloat16)

    my_docs = lax.dynamic_index_in_dim(request_docs, my_index, 0, keepdims=False)
    owners = my_docs // slot_count
    earlier = jnp.arange(doc_count)[None, :] < jnp.arange(doc_count)[:, None]
    ranks = jnp.sum(((owners[:, None] == owners[None, :]) & earlier).astype(jnp.int32), axis=1)
    positions = jnp.arange(doc_len, dtype=jnp.int32)
    held = positions[None, :] < doc_lengths[my_docs][:, None]
    held &= jnp.all(positions[None, None, :] != row_ids[:, :, None], axis=1)
    key_bias = jnp.where(held, 0.0, MASKED).astype(jnp.float32).reshape(1, doc_count * doc_len)
    place = jnp.arange(doc_count, dtype=jnp.int32)[:, None] * doc_len + row_ids
    mixed = attend(
        request_docs,
        queries,
        fresh,
        key_bias,
        place.reshape(row_count, 1),
        place.reshape(1, row_count),
        sources,
        not pairs,
    )

    slot_of_row = jnp.repeat(owners * capacity + ranks, per_doc) * per_doc + jnp.tile(
        jnp.arange(per_doc), doc_count
    )
    slots = jnp.arange(seq_count * capacity * per_doc)
    pick = (slots[:, None] == slot_of_row[None, :]).astype(jnp.bfloat16)
    outgoing = jnp.dot(pick, fresh, preferred_element_type=jnp.float32).astype(jnp.bfloat16)
    outgoing = outgoing.reshape(seq_count, capacity, per_doc, 2 * head_dim)
    returned = lax.all_to_all(outgoing, "seq", split_axis=0, concat_axis=0, tiled=True)
    returned = returned.reshape(seq_count, capacity, per_doc, 2, head_dim)
    return (mixed, returned[None])


def solution(mesh):
    pairs = mesh.shape["seq"] == 4 and mesh.shape["groups"] == 2 and mesh.shape["tp"] % 2 == 0
    return jax.shard_map(
        functools.partial(shards, pairs),
        mesh=mesh,
        in_specs=(
            P(("groups", "seq"), None, None),
            P(("groups", "seq"), None, "tp"),
            P("seq", "tp"),
            P("seq", "tp"),
            P(("groups", "seq"), None, "tp"),
            P(("groups", "seq"), None, "tp"),
            P("groups", None),
            P("groups"),
            P(("groups", "seq"), None, None),
        ),
        out_specs=(
            P(("groups", "seq"), None, "tp"),
            P(("groups", "seq"), None, None, None, None, "tp"),
        ),
        check_vma=False,
    )
```

```python
import functools
import math

import jax
import jax.numpy as jnp
from jax import lax
from jax.experimental import pallas as pl
from jax.experimental.pallas import tpu as pltpu
from jax.sharding import PartitionSpec as P

ANY = pl.BlockSpec(memory_space=pl.ANY)
SMEM = pl.BlockSpec(memory_space=pltpu.SMEM)
VMEM = pl.BlockSpec(memory_space=pltpu.VMEM)
MASKED = -1e30


def cut_kernel(hidden, h_out, staged, sems):
    me = lax.axis_index("seq")
    core = lax.rem(lax.axis_index("tp"), 2)
    rows, depth = h_out.shape[1:]
    first = me + 1 - 2 * lax.rem(me, 2)
    second = lax.rem(first + 2, 4)
    fetches, stores = [], []
    for i, block in enumerate((first, second)):
        source = hidden.at[
            0,
            pl.ds(pl.multiple_of(core * rows, rows), rows),
            pl.ds(pl.multiple_of(block * depth, depth), depth),
        ]
        fetches.append(pltpu.make_async_copy(source, staged.at[i], sems.at[i]))
        stores.append(pltpu.make_async_copy(staged.at[i], h_out.at[i], sems.at[2 + i]))
    for fetch in fetches:
        fetch.start()
    for fetch, store in zip(fetches, stores):
        fetch.wait()
        store.start()
    for store in stores:
        store.wait()


def cut(hidden, depth):
    shape = (2, hidden.shape[1] // 2, depth)
    return pl.pallas_call(
        cut_kernel,
        out_shape=jax.ShapeDtypeStruct(shape, jnp.bfloat16),
        in_specs=[ANY],
        out_specs=ANY,
        scratch_shapes=[pltpu.VMEM(shape, jnp.bfloat16), pltpu.SemaphoreType.DMA((4,))],
        name="cut",
    )(hidden)


def gate_kernel(*refs):
    pass


def gate(arrays, first):
    return pl.pallas_call(
        gate_kernel,
        out_shape=tuple(jax.ShapeDtypeStruct(one.shape, one.dtype) for one in arrays),
        in_specs=[ANY] * (len(arrays) + len(first)),
        out_specs=(ANY,) * len(arrays),
        input_output_aliases={i: i for i in range(len(arrays))},
        name="gate",
    )(*arrays, *first)


def docs_kernel(by_owner, request_docs, store_keys, store_values, *rest):
    outs, (picks, sems) = rest[:-2], rest[-2:]
    me = lax.axis_index("seq")
    requests, doc_count = request_docs.shape
    slots = store_keys.shape[0]
    capacity = slots // 2

    def one_request(r, carry):
        for c in range(capacity):
            picks[r, c] = 0

        def one_doc(j, count):
            doc = request_docs[r, j]
            mine = lax.div(doc, slots) == me

            @pl.when(mine)
            def _():
                picks[r, jnp.minimum(count, capacity - 1)] = lax.rem(doc, slots)

            return count + mine.astype(jnp.int32)

        lax.fori_loop(0, doc_count, one_doc, jnp.int32(0), unroll=True)
        return carry

    lax.fori_loop(0, requests, one_request, 0)

    def send(r, out, sem):
        for c in range(capacity):
            slot = picks[r, c]
            pltpu.make_async_copy(store_keys.at[slot], out.at[c, 0], sem).start()
            pltpu.make_async_copy(store_values.at[slot], out.at[c, 1], sem).start()

    if by_owner:
        out = outs[0]

        def one_send(r, carry):
            send(r, out.at[r], sems.at[0])
            return carry

        lax.fori_loop(0, requests, one_send, 0)
    else:
        for i, out in enumerate(outs):
            send(lax.bitwise_xor(me, i + 1), out, sems.at[i])
    for i, out in enumerate(outs):
        pltpu.make_async_copy(out, out, sems.at[i]).wait()


def cut_docs(request_docs, store_keys, store_values, by_owner):
    requests = request_docs.shape[0]
    capacity = store_keys.shape[0] // 2
    one = (capacity, 2) + store_keys.shape[1:]
    if by_owner:
        shapes = (jax.ShapeDtypeStruct((requests,) + one, jnp.bfloat16),)
    else:
        shapes = (jax.ShapeDtypeStruct(one, jnp.bfloat16),) * (requests - 1)
    return pl.pallas_call(
        functools.partial(docs_kernel, by_owner),
        out_shape=shapes,
        in_specs=[SMEM, ANY, ANY],
        out_specs=(VMEM,) * len(shapes),
        scratch_shapes=[
            pltpu.SMEM((requests, capacity), jnp.int32),
            pltpu.SemaphoreType.DMA((len(shapes),)),
        ],
        name="cut_docs",
    )(request_docs, store_keys, store_values)


def project_kernel(
    hidden, w_key, w_value, k_far, v_far, k_swapped, v_swapped, h_mine, h_other, own, part, w, h, sems
):
    group = lax.axis_index("groups")
    me = lax.axis_index("seq")
    core = lax.rem(lax.axis_index("tp"), 2)
    depth, width = w_key.shape
    rows = hidden.shape[1]
    far = lax.rem(me + 2, 4)
    near = pl.ds(0, depth)
    rest = pl.ds(depth, depth)
    keys = pl.ds(0, width)
    values = pl.ds(width, width)
    copies = [
        pltpu.make_async_copy(w_key, w.at[near, keys], sems.at[0]),
        pltpu.make_async_copy(w_value, w.at[near, values], sems.at[1]),
    ]
    for i, block in enumerate((me, far)):
        columns = pl.ds(i * depth, depth)
        source = hidden.at[0, :, pl.ds(pl.multiple_of(block * depth, depth), depth)]
        copies.append(
            pltpu.make_async_copy(source, h.at[pl.ds(0, rows), columns], sems.at[2 + 3 * i])
        )
        for k, (held, place) in enumerate(((h_mine, core), (h_other, 1 - core))):
            start = pl.multiple_of(rows + place * (rows // 2), rows // 2)
            target = h.at[pl.ds(start, rows // 2), columns]
            copies.append(pltpu.make_async_copy(held.at[i], target, sems.at[3 + 3 * i + k]))
    for one in copies:
        one.start()

    @pl.when(group == 0)
    def _():
        pltpu.make_async_copy(k_far, w.at[rest, keys], sems.at[8]).start()
        pltpu.make_async_copy(v_swapped, w.at[rest, values], sems.at[9]).start()

    @pl.when(group != 0)
    def _():
        pltpu.make_async_copy(k_swapped, w.at[rest, keys], sems.at[8]).start()
        pltpu.make_async_copy(v_far, w.at[rest, values], sems.at[9]).start()

    for one in copies:
        one.wait()
    pltpu.make_async_copy(k_far, w.at[rest, keys], sems.at[8]).wait()
    pltpu.make_async_copy(v_far, w.at[rest, values], sems.at[9]).wait()
    total = jnp.dot(h[...], w[...], preferred_element_type=jnp.float32)
    own[...] = total[:rows]
    part[...] = total[rows:].astype(part.dtype)


def project(hidden, w_key, w_value, *arrived):
    depth, width = w_key.shape
    rows = hidden.shape[1]
    return pl.pallas_call(
        project_kernel,
        out_shape=(
            jax.ShapeDtypeStruct((rows, 2 * width), jnp.float32),
            jax.ShapeDtypeStruct((rows, 2 * width), jnp.bfloat16),
        ),
        in_specs=[ANY] * (3 + len(arrived)),
        out_specs=(VMEM, VMEM),
        scratch_shapes=[
            pltpu.VMEM((2 * depth, 2 * width), jnp.bfloat16),
            pltpu.VMEM((2 * rows, 2 * depth), jnp.bfloat16),
            pltpu.SemaphoreType.DMA((10,)),
        ],
        compiler_params=pltpu.CompilerParams(vmem_limit_bytes=32 * 1024 * 1024),
        name="project",
    )(hidden, w_key, w_value, *arrived)


def attend_kernel(
    by_owner, request_docs, queries, fresh, key_bias, row_place, key_place, *rest
):
    sources, (mixed, context_k, context_v, counts, sems) = rest[:-5], rest[-5:]
    me = lax.axis_index("seq")
    doc_count = request_docs.shape[1]
    head_dim = context_k.shape[1]
    doc_len = context_k.shape[0] // doc_count
    row_count = queries.shape[1]
    per_doc = row_count // doc_count
    heads = queries.shape[2] // head_dim
    owners = request_docs.shape[0]
    slots = sources[0].shape[0] if not by_owner else 2 * sources[0].shape[1]

    for o in range(owners):
        counts[o] = 0

    def one_doc(j, carry):
        doc = request_docs[me, j]
        owner = lax.div(doc, slots)
        rank = counts[owner]
        counts[owner] = rank + 1
        place = pl.ds(pl.multiple_of(j * doc_len, doc_len), doc_len)

        def fetch(key_source, value_source):
            pltpu.make_async_copy(key_source, context_k.at[place], sems.at[0]).start()
            pltpu.make_async_copy(value_source, context_v.at[place], sems.at[1]).start()

        if by_owner:
            fetch(sources[0].at[owner, rank, 0], sources[0].at[owner, rank, 1])
        else:
            away = lax.bitwise_xor(me, owner)

            @pl.when(away == 0)
            def _():
                slot = lax.rem(doc, slots)
                fetch(sources[0].at[slot], sources[1].at[slot])

            for k in range(1, owners):

                @pl.when(away == k)
                def _():
                    fetch(sources[1 + k].at[rank, 0], sources[1 + k].at[rank, 1])

        return carry

    lax.fori_loop(0, doc_count, one_doc, 0)
    pltpu.make_async_copy(context_k, context_k, sems.at[0]).wait()
    pltpu.make_async_copy(context_v, context_v, sems.at[1]).wait()

    scale = math.log2(math.e) / math.sqrt(head_dim)
    fresh_k = fresh[:, :head_dim]
    fresh_v = fresh[:, head_dim:]
    step = 4 if doc_count % 4 == 0 else 1
    block_rows = step * per_doc
    block_keys = step * doc_len
    slot_place = lax.broadcasted_iota(jnp.int32, (1, block_keys), 1)
    contract_last = (((1,), (1,)), ((), ()))
    for b in range(doc_count // step):
        rows = slice(b * block_rows, (b + 1) * block_rows)
        q = jnp.concatenate(
            [queries[0, rows, h * head_dim : (h + 1) * head_dim] for h in range(heads)], axis=0
        )
        own_place = row_place[rows, :]

        def masked(keys, bias):
            scores = lax.dot_general(q, keys, contract_last, preferred_element_type=jnp.float32)
            scores = (scores * scale).reshape(heads, block_rows, keys.shape[0])
            return (scores + bias[None]).reshape(heads * block_rows, keys.shape[0])

        chunks, values = [], []
        for c in range(b + 1):
            keys = slice(c * block_keys, (c + 1) * block_keys)
            bias = jnp.broadcast_to(key_bias[:, keys], (block_rows, block_keys))
            if c == b:
                bias = jnp.where(slot_place + c * block_keys <= own_place, bias, MASKED)
            chunks.append(masked(context_k[keys, :], bias))
            values.append(context_v[keys, :])
        bias = jnp.where(key_place[...] <= own_place, 0.0, MASKED)
        chunks.append(masked(fresh_k, bias))
        values.append(fresh_v)
        row_max = functools.reduce(
            jnp.maximum, [jnp.max(one, axis=1, keepdims=True) for one in chunks]
        )
        total = jnp.zeros((heads * block_rows, head_dim), jnp.float32)
        row_sum = jnp.zeros((heads * block_rows, 1), jnp.float32)
        for one, value in zip(chunks, values):
            powers = jnp.exp2(one - row_max)
            row_sum += jnp.sum(powers, axis=1, keepdims=True)
            total += jnp.dot(
                powers.astype(jnp.bfloat16), value, preferred_element_type=jnp.float32
            )
        result = (total / row_sum).astype(mixed.dtype)
        for h in range(heads):
            mixed[0, rows, h * head_dim : (h + 1) * head_dim] = result[
                h * block_rows : (h + 1) * block_rows
            ]


def attend(request_docs, queries, fresh, key_bias, row_place, key_place, sources, by_owner):
    head_dim = fresh.shape[1] // 2
    context = key_bias.shape[1]
    return pl.pallas_call(
        functools.partial(attend_kernel, by_owner),
        out_shape=jax.ShapeDtypeStruct(queries.shape, jnp.bfloat16),
        in_specs=[SMEM] + [VMEM] * 5 + [ANY] * len(sources),
        out_specs=VMEM,
        scratch_shapes=[
            pltpu.VMEM((context, head_dim), jnp.bfloat16),
            pltpu.VMEM((context, head_dim), jnp.bfloat16),
            pltpu.SMEM((request_docs.shape[0],), jnp.int32),
            pltpu.SemaphoreType.DMA((2,)),
        ],
        compiler_params=pltpu.CompilerParams(vmem_limit_bytes=32 * 1024 * 1024),
        name="attend",
    )(request_docs, queries, fresh, key_bias, row_place, key_place, *sources)


def shards(
    pairs,
    hidden,
    queries,
    w_key,
    w_value,
    store_keys,
    store_values,
    request_docs,
    doc_lengths,
    recompute_rows,
):
    my_index = lax.axis_index("seq")
    seq_count = lax.axis_size("seq")
    slot_count, doc_len, head_dim = store_keys.shape
    capacity = slot_count // 2
    doc_count = request_docs.shape[1]
    row_ids = recompute_rows[0]
    per_doc = row_ids.shape[1]
    row_count = doc_count * per_doc

    if pairs:
        def swap(array, axis, apart):
            count = lax.axis_size(axis)
            return lax.ppermute(array, axis, [(i, i ^ apart) for i in range(count)])

        both = ("groups", "seq")
        k_far = lax.ppermute(w_key, both, [(s, s ^ 2) for s in range(4)])
        v_far = lax.ppermute(w_value, both, [(4 + s, 4 + (s ^ 2)) for s in range(4)])
        h_mine = swap(cut(hidden, w_key.shape[0]), "seq", 1)
        k_swapped = lax.ppermute(k_far, "groups", [(0, 1)])
        v_swapped = lax.ppermute(v_far, "groups", [(1, 0)])
        docs = cut_docs(request_docs, store_keys, store_values, False)
        docs = gate(docs, (k_far, v_far))
        docs = [swap(doc, "seq", k + 1) for k, doc in enumerate(docs)]
        h_other = swap(h_mine, "tp", 1)
        own, part = project(
            hidden, w_key, w_value, k_far, v_far, k_swapped, v_swapped, h_mine, h_other
        )
        fresh = (own + swap(part, "seq", 1).astype(jnp.float32)).astype(jnp.bfloat16)
        sources = (store_keys, store_values, *docs)
    else:
        (docs,) = cut_docs(request_docs, store_keys, store_values, True)
        sources = (lax.all_to_all(docs, "seq", split_axis=0, concat_axis=0, tiled=True),)
        weights = lax.all_gather(
            jnp.concatenate([w_key, w_value], axis=1), "seq", axis=0, tiled=True
        )
        fresh = jnp.dot(hidden[0], weights, preferred_element_type=jnp.float32)
        fresh = fresh.astype(jnp.bfloat16)

    my_docs = lax.dynamic_index_in_dim(request_docs, my_index, 0, keepdims=False)
    owners = my_docs // slot_count
    earlier = jnp.arange(doc_count)[None, :] < jnp.arange(doc_count)[:, None]
    ranks = jnp.sum(((owners[:, None] == owners[None, :]) & earlier).astype(jnp.int32), axis=1)
    positions = jnp.arange(doc_len, dtype=jnp.int32)
    held = positions[None, :] < doc_lengths[my_docs][:, None]
    held &= jnp.all(positions[None, None, :] != row_ids[:, :, None], axis=1)
    key_bias = jnp.where(held, 0.0, MASKED).astype(jnp.float32).reshape(1, doc_count * doc_len)
    place = jnp.arange(doc_count, dtype=jnp.int32)[:, None] * doc_len + row_ids
    mixed = attend(
        request_docs,
        queries,
        fresh,
        key_bias,
        place.reshape(row_count, 1),
        place.reshape(1, row_count),
        sources,
        not pairs,
    )

    slot_of_row = jnp.repeat(owners * capacity + ranks, per_doc) * per_doc + jnp.tile(
        jnp.arange(per_doc), doc_count
    )
    slots = jnp.arange(seq_count * capacity * per_doc)
    pick = (slots[:, None] == slot_of_row[None, :]).astype(jnp.bfloat16)
    outgoing = jnp.dot(pick, fresh, preferred_element_type=jnp.float32).astype(jnp.bfloat16)
    outgoing = outgoing.reshape(seq_count, capacity, per_doc, 2 * head_dim)
    returned = lax.all_to_all(outgoing, "seq", split_axis=0, concat_axis=0, tiled=True)
    returned = returned.reshape(seq_count, capacity, per_doc, 2, head_dim)
    return (mixed, returned[None])


def solution(mesh):
    pairs = mesh.shape["seq"] == 4 and mesh.shape["groups"] == 2 and mesh.shape["tp"] % 2 == 0
    return jax.shard_map(
        functools.partial(shards, pairs),
        mesh=mesh,
        in_specs=(
            P(("groups", "seq"), None, None),
            P(("groups", "seq"), None, "tp"),
            P("seq", "tp"),
            P("seq", "tp"),
            P(("groups", "seq"), None, "tp"),
            P(("groups", "seq"), None, "tp"),
            P("groups", None),
            P("groups"),
            P(("groups", "seq"), None, None),
        ),
        out_specs=(
            P(("groups", "seq"), None, "tp"),
            P(("groups", "seq"), None, None, None, None, "tp"),
        ),
        check_vma=False,
    )
```

```python
import functools
import math

import jax
import jax.numpy as jnp
from jax import lax
from jax.experimental import pallas as pl
from jax.experimental.pallas import tpu as pltpu
from jax.sharding import PartitionSpec as P

ANY = pl.BlockSpec(memory_space=pl.ANY)
SMEM = pl.BlockSpec(memory_space=pltpu.SMEM)
VMEM = pl.BlockSpec(memory_space=pltpu.VMEM)
MASKED = -1e30


def cut_kernel(hidden, h_out, staged, sems):
    me = lax.axis_index("seq")
    core = lax.rem(lax.axis_index("tp"), 2)
    rows, depth = h_out.shape[1:]
    first = me + 1 - 2 * lax.rem(me, 2)
    second = lax.rem(first + 2, 4)
    fetches, stores = [], []
    for i, block in enumerate((first, second)):
        source = hidden.at[
            0,
            pl.ds(pl.multiple_of(core * rows, rows), rows),
            pl.ds(pl.multiple_of(block * depth, depth), depth),
        ]
        fetches.append(pltpu.make_async_copy(source, staged.at[i], sems.at[i]))
        stores.append(pltpu.make_async_copy(staged.at[i], h_out.at[i], sems.at[2 + i]))
    for fetch in fetches:
        fetch.start()
    for fetch, store in zip(fetches, stores):
        fetch.wait()
        store.start()
    for store in stores:
        store.wait()


def cut(hidden, depth):
    shape = (2, hidden.shape[1] // 2, depth)
    return pl.pallas_call(
        cut_kernel,
        out_shape=jax.ShapeDtypeStruct(shape, jnp.bfloat16),
        in_specs=[ANY],
        out_specs=ANY,
        scratch_shapes=[pltpu.VMEM(shape, jnp.bfloat16), pltpu.SemaphoreType.DMA((4,))],
        name="cut",
    )(hidden)


def gate_kernel(*refs):
    pass


def gate(arrays):
    return pl.pallas_call(
        gate_kernel,
        out_shape=tuple(jax.ShapeDtypeStruct(one.shape, one.dtype) for one in arrays),
        in_specs=[ANY] * len(arrays),
        out_specs=(ANY,) * len(arrays),
        input_output_aliases={i: i for i in range(len(arrays))},
        name="gate",
    )(*arrays)


def docs_kernel(by_owner, request_docs, store_keys, store_values, *rest):
    outs, (picks, sems) = rest[:-2], rest[-2:]
    me = lax.axis_index("seq")
    requests, doc_count = request_docs.shape
    slots = store_keys.shape[0]
    capacity = slots // 2

    def one_request(r, carry):
        for c in range(capacity):
            picks[r, c] = 0

        def one_doc(j, count):
            doc = request_docs[r, j]
            mine = lax.div(doc, slots) == me

            @pl.when(mine)
            def _():
                picks[r, jnp.minimum(count, capacity - 1)] = lax.rem(doc, slots)

            return count + mine.astype(jnp.int32)

        lax.fori_loop(0, doc_count, one_doc, jnp.int32(0), unroll=True)
        return carry

    lax.fori_loop(0, requests, one_request, 0)

    def send(r, out, sem):
        for c in range(capacity):
            slot = picks[r, c]
            pltpu.make_async_copy(store_keys.at[slot], out.at[c, 0], sem).start()
            pltpu.make_async_copy(store_values.at[slot], out.at[c, 1], sem).start()

    if by_owner:
        out = outs[0]

        def one_send(r, carry):
            send(r, out.at[r], sems.at[0])
            return carry

        lax.fori_loop(0, requests, one_send, 0)
    else:
        for i, out in enumerate(outs):
            send(lax.bitwise_xor(me, i + 1), out, sems.at[i])
    for i, out in enumerate(outs):
        pltpu.make_async_copy(out, out, sems.at[i]).wait()


def cut_docs(request_docs, store_keys, store_values, by_owner):
    requests = request_docs.shape[0]
    capacity = store_keys.shape[0] // 2
    one = (capacity, 2) + store_keys.shape[1:]
    if by_owner:
        shapes = (jax.ShapeDtypeStruct((requests,) + one, jnp.bfloat16),)
    else:
        shapes = (jax.ShapeDtypeStruct(one, jnp.bfloat16),) * (requests - 1)
    return pl.pallas_call(
        functools.partial(docs_kernel, by_owner),
        out_shape=shapes,
        in_specs=[SMEM, ANY, ANY],
        out_specs=(VMEM,) * len(shapes),
        scratch_shapes=[
            pltpu.SMEM((requests, capacity), jnp.int32),
            pltpu.SemaphoreType.DMA((len(shapes),)),
        ],
        name="cut_docs",
    )(request_docs, store_keys, store_values)


def project_kernel(
    hidden, w_key, w_value, k_far, v_far, k_swapped, v_swapped, h_mine, h_other, own, part, w, h, sems
):
    group = lax.axis_index("groups")
    me = lax.axis_index("seq")
    core = lax.rem(lax.axis_index("tp"), 2)
    depth, width = w_key.shape
    rows = hidden.shape[1]
    far = lax.rem(me + 2, 4)
    near = pl.ds(0, depth)
    rest = pl.ds(depth, depth)
    keys = pl.ds(0, width)
    values = pl.ds(width, width)
    copies = [
        pltpu.make_async_copy(w_key, w.at[near, keys], sems.at[0]),
        pltpu.make_async_copy(w_value, w.at[near, values], sems.at[1]),
    ]
    for i, block in enumerate((me, far)):
        columns = pl.ds(i * depth, depth)
        source = hidden.at[0, :, pl.ds(pl.multiple_of(block * depth, depth), depth)]
        copies.append(
            pltpu.make_async_copy(source, h.at[pl.ds(0, rows), columns], sems.at[2 + 3 * i])
        )
        for k, (held, place) in enumerate(((h_mine, core), (h_other, 1 - core))):
            start = pl.multiple_of(rows + place * (rows // 2), rows // 2)
            target = h.at[pl.ds(start, rows // 2), columns]
            copies.append(pltpu.make_async_copy(held.at[i], target, sems.at[3 + 3 * i + k]))
    for one in copies:
        one.start()

    @pl.when(group == 0)
    def _():
        pltpu.make_async_copy(k_far, w.at[rest, keys], sems.at[8]).start()
        pltpu.make_async_copy(v_swapped, w.at[rest, values], sems.at[9]).start()

    @pl.when(group != 0)
    def _():
        pltpu.make_async_copy(k_swapped, w.at[rest, keys], sems.at[8]).start()
        pltpu.make_async_copy(v_far, w.at[rest, values], sems.at[9]).start()

    for one in copies:
        one.wait()
    pltpu.make_async_copy(k_far, w.at[rest, keys], sems.at[8]).wait()
    pltpu.make_async_copy(v_far, w.at[rest, values], sems.at[9]).wait()
    total = jnp.dot(h[...], w[...], preferred_element_type=jnp.float32)
    own[...] = total[:rows]
    part[...] = total[rows:].astype(part.dtype)


def project(hidden, w_key, w_value, *arrived):
    depth, width = w_key.shape
    rows = hidden.shape[1]
    return pl.pallas_call(
        project_kernel,
        out_shape=(
            jax.ShapeDtypeStruct((rows, 2 * width), jnp.float32),
            jax.ShapeDtypeStruct((rows, 2 * width), jnp.bfloat16),
        ),
        in_specs=[ANY] * (3 + len(arrived)),
        out_specs=(VMEM, VMEM),
        scratch_shapes=[
            pltpu.VMEM((2 * depth, 2 * width), jnp.bfloat16),
            pltpu.VMEM((2 * rows, 2 * depth), jnp.bfloat16),
            pltpu.SemaphoreType.DMA((10,)),
        ],
        compiler_params=pltpu.CompilerParams(vmem_limit_bytes=32 * 1024 * 1024),
        cost_estimate=pl.CostEstimate(flops=1, bytes_accessed=1, transcendentals=0),
        name="project",
    )(hidden, w_key, w_value, *arrived)


def attend_kernel(
    by_owner, request_docs, queries, fresh, key_bias, row_place, key_place, *rest
):
    sources, (mixed, context_k, context_v, counts, sems) = rest[:-5], rest[-5:]
    me = lax.axis_index("seq")
    doc_count = request_docs.shape[1]
    head_dim = context_k.shape[1]
    doc_len = context_k.shape[0] // doc_count
    row_count = queries.shape[1]
    per_doc = row_count // doc_count
    heads = queries.shape[2] // head_dim
    owners = request_docs.shape[0]
    slots = sources[0].shape[0] if not by_owner else 2 * sources[0].shape[1]

    for o in range(owners):
        counts[o] = 0

    def one_doc(j, carry):
        doc = request_docs[me, j]
        owner = lax.div(doc, slots)
        rank = counts[owner]
        counts[owner] = rank + 1
        place = pl.ds(pl.multiple_of(j * doc_len, doc_len), doc_len)

        def fetch(key_source, value_source):
            pltpu.make_async_copy(key_source, context_k.at[place], sems.at[0]).start()
            pltpu.make_async_copy(value_source, context_v.at[place], sems.at[1]).start()

        if by_owner:
            fetch(sources[0].at[owner, rank, 0], sources[0].at[owner, rank, 1])
        else:
            away = lax.bitwise_xor(me, owner)

            @pl.when(away == 0)
            def _():
                slot = lax.rem(doc, slots)
                fetch(sources[0].at[slot], sources[1].at[slot])

            for k in range(1, owners):

                @pl.when(away == k)
                def _():
                    fetch(sources[1 + k].at[rank, 0], sources[1 + k].at[rank, 1])

        return carry

    lax.fori_loop(0, doc_count, one_doc, 0)
    pltpu.make_async_copy(context_k, context_k, sems.at[0]).wait()
    pltpu.make_async_copy(context_v, context_v, sems.at[1]).wait()

    scale = math.log2(math.e) / math.sqrt(head_dim)
    fresh_k = fresh[:, :head_dim]
    fresh_v = fresh[:, head_dim:]
    step = 4 if doc_count % 4 == 0 else 1
    block_rows = step * per_doc
    block_keys = step * doc_len
    slot_place = lax.broadcasted_iota(jnp.int32, (1, block_keys), 1)
    contract_last = (((1,), (1,)), ((), ()))
    for b in range(doc_count // step):
        rows = slice(b * block_rows, (b + 1) * block_rows)
        q = jnp.concatenate(
            [queries[0, rows, h * head_dim : (h + 1) * head_dim] for h in range(heads)], axis=0
        )
        own_place = row_place[rows, :]

        def masked(keys, bias):
            scores = lax.dot_general(q, keys, contract_last, preferred_element_type=jnp.float32)
            scores = (scores * scale).reshape(heads, block_rows, keys.shape[0])
            return (scores + bias[None]).reshape(heads * block_rows, keys.shape[0])

        chunks, values = [], []
        for c in range(b + 1):
            keys = slice(c * block_keys, (c + 1) * block_keys)
            bias = jnp.broadcast_to(key_bias[:, keys], (block_rows, block_keys))
            if c == b:
                bias = jnp.where(slot_place + c * block_keys <= own_place, bias, MASKED)
            chunks.append(masked(context_k[keys, :], bias))
            values.append(context_v[keys, :])
        bias = jnp.where(key_place[...] <= own_place, 0.0, MASKED)
        chunks.append(masked(fresh_k, bias))
        values.append(fresh_v)
        row_max = functools.reduce(
            jnp.maximum, [jnp.max(one, axis=1, keepdims=True) for one in chunks]
        )
        total = jnp.zeros((heads * block_rows, head_dim), jnp.float32)
        row_sum = jnp.zeros((heads * block_rows, 1), jnp.float32)
        for one, value in zip(chunks, values):
            powers = jnp.exp2(one - row_max)
            row_sum += jnp.sum(powers, axis=1, keepdims=True)
            total += jnp.dot(
                powers.astype(jnp.bfloat16), value, preferred_element_type=jnp.float32
            )
        result = (total / row_sum).astype(mixed.dtype)
        for h in range(heads):
            mixed[0, rows, h * head_dim : (h + 1) * head_dim] = result[
                h * block_rows : (h + 1) * block_rows
            ]


def attend(request_docs, queries, fresh, key_bias, row_place, key_place, sources, by_owner):
    head_dim = fresh.shape[1] // 2
    context = key_bias.shape[1]
    return pl.pallas_call(
        functools.partial(attend_kernel, by_owner),
        out_shape=jax.ShapeDtypeStruct(queries.shape, jnp.bfloat16),
        in_specs=[SMEM] + [VMEM] * 5 + [ANY] * len(sources),
        out_specs=VMEM,
        scratch_shapes=[
            pltpu.VMEM((context, head_dim), jnp.bfloat16),
            pltpu.VMEM((context, head_dim), jnp.bfloat16),
            pltpu.SMEM((request_docs.shape[0],), jnp.int32),
            pltpu.SemaphoreType.DMA((2,)),
        ],
        compiler_params=pltpu.CompilerParams(vmem_limit_bytes=32 * 1024 * 1024),
        name="attend",
    )(request_docs, queries, fresh, key_bias, row_place, key_place, *sources)


def shards(
    pairs,
    hidden,
    queries,
    w_key,
    w_value,
    store_keys,
    store_values,
    request_docs,
    doc_lengths,
    recompute_rows,
):
    my_index = lax.axis_index("seq")
    seq_count = lax.axis_size("seq")
    slot_count, doc_len, head_dim = store_keys.shape
    capacity = slot_count // 2
    doc_count = request_docs.shape[1]
    row_ids = recompute_rows[0]
    per_doc = row_ids.shape[1]
    row_count = doc_count * per_doc

    if pairs:
        def swap(array, axis, apart):
            count = lax.axis_size(axis)
            return lax.ppermute(array, axis, [(i, i ^ apart) for i in range(count)])

        both = ("groups", "seq")
        k_far = lax.ppermute(w_key, both, [(s, s ^ 2) for s in range(4)])
        v_far = lax.ppermute(w_value, both, [(4 + s, 4 + (s ^ 2)) for s in range(4)])
        h_mine = swap(cut(hidden, w_key.shape[0]), "seq", 1)
        (docs,) = cut_docs(request_docs, store_keys, store_values, True)
        docs, k_far, v_far = gate((docs, k_far, v_far))
        k_swapped = lax.ppermute(k_far, "groups", [(0, 1)])
        v_swapped = lax.ppermute(v_far, "groups", [(1, 0)])
        docs = lax.all_to_all(docs, "seq", split_axis=0, concat_axis=0, tiled=True)
        h_other = swap(h_mine, "tp", 1)
        own, part = project(
            hidden, w_key, w_value, k_far, v_far, k_swapped, v_swapped, h_mine, h_other
        )
        fresh = (own + swap(part, "seq", 1).astype(jnp.float32)).astype(jnp.bfloat16)
        sources = (docs,)
    else:
        (docs,) = cut_docs(request_docs, store_keys, store_values, True)
        sources = (lax.all_to_all(docs, "seq", split_axis=0, concat_axis=0, tiled=True),)
        weights = lax.all_gather(
            jnp.concatenate([w_key, w_value], axis=1), "seq", axis=0, tiled=True
        )
        fresh = jnp.dot(hidden[0], weights, preferred_element_type=jnp.float32)
        fresh = fresh.astype(jnp.bfloat16)

    my_docs = lax.dynamic_index_in_dim(request_docs, my_index, 0, keepdims=False)
    owners = my_docs // slot_count
    earlier = jnp.arange(doc_count)[None, :] < jnp.arange(doc_count)[:, None]
    ranks = jnp.sum(((owners[:, None] == owners[None, :]) & earlier).astype(jnp.int32), axis=1)
    positions = jnp.arange(doc_len, dtype=jnp.int32)
    held = positions[None, :] < doc_lengths[my_docs][:, None]
    held &= jnp.all(positions[None, None, :] != row_ids[:, :, None], axis=1)
    key_bias = jnp.where(held, 0.0, MASKED).astype(jnp.float32).reshape(1, doc_count * doc_len)
    place = jnp.arange(doc_count, dtype=jnp.int32)[:, None] * doc_len + row_ids
    mixed = attend(
        request_docs,
        queries,
        fresh,
        key_bias,
        place.reshape(row_count, 1),
        place.reshape(1, row_count),
        sources,
        True,
    )

    slot_of_row = jnp.repeat(owners * capacity + ranks, per_doc) * per_doc + jnp.tile(
        jnp.arange(per_doc), doc_count
    )
    slots = jnp.arange(seq_count * capacity * per_doc)
    pick = (slots[:, None] == slot_of_row[None, :]).astype(jnp.bfloat16)
    outgoing = jnp.dot(pick, fresh, preferred_element_type=jnp.float32).astype(jnp.bfloat16)
    outgoing = outgoing.reshape(seq_count, capacity, per_doc, 2 * head_dim)
    returned = lax.all_to_all(outgoing, "seq", split_axis=0, concat_axis=0, tiled=True)
    returned = returned.reshape(seq_count, capacity, per_doc, 2, head_dim)
    return (mixed, returned[None])


def solution(mesh):
    pairs = mesh.shape["seq"] == 4 and mesh.shape["groups"] == 2 and mesh.shape["tp"] % 2 == 0
    return jax.shard_map(
        functools.partial(shards, pairs),
        mesh=mesh,
        in_specs=(
            P(("groups", "seq"), None, None),
            P(("groups", "seq"), None, "tp"),
            P("seq", "tp"),
            P("seq", "tp"),
            P(("groups", "seq"), None, "tp"),
            P(("groups", "seq"), None, "tp"),
            P("groups", None),
            P("groups"),
            P(("groups", "seq"), None, None),
        ),
        out_specs=(
            P(("groups", "seq"), None, "tp"),
            P(("groups", "seq"), None, None, None, None, "tp"),
        ),
        check_vma=False,
    )
```

```python
import functools
import math

import jax
import jax.numpy as jnp
from jax import lax
from jax.experimental import pallas as pl
from jax.experimental.pallas import tpu as pltpu
from jax.sharding import PartitionSpec as P

ANY = pl.BlockSpec(memory_space=pl.ANY)
SMEM = pl.BlockSpec(memory_space=pltpu.SMEM)
VMEM = pl.BlockSpec(memory_space=pltpu.VMEM)
MASKED = -1e30


def pick_kernel(w_key, w_value, w_out, sem):
    group = lax.axis_index("groups")

    @pl.when(group == 0)
    def _():
        pltpu.make_async_copy(w_key, w_out, sem).start()

    @pl.when(group != 0)
    def _():
        pltpu.make_async_copy(w_value, w_out, sem).start()

    pltpu.make_async_copy(w_key, w_out, sem).wait()


def pick_weights(w_key, w_value):
    return pl.pallas_call(
        pick_kernel,
        out_shape=jax.ShapeDtypeStruct(w_key.shape, jnp.bfloat16),
        in_specs=[ANY, ANY],
        out_specs=VMEM,
        scratch_shapes=[pltpu.SemaphoreType.DMA],
        name="pick_weights",
    )(w_key, w_value)


def cut_kernel(hidden, h_out, staged, sems):
    me = lax.axis_index("seq")
    core = lax.rem(lax.axis_index("tp"), 2)
    rows, depth = h_out.shape[1:]
    first = me + 1 - 2 * lax.rem(me, 2)
    second = lax.rem(first + 2, 4)
    fetches, stores = [], []
    for i, block in enumerate((first, second)):
        source = hidden.at[
            0,
            pl.ds(pl.multiple_of(core * rows, rows), rows),
            pl.ds(pl.multiple_of(block * depth, depth), depth),
        ]
        fetches.append(pltpu.make_async_copy(source, staged.at[i], sems.at[i]))
        stores.append(pltpu.make_async_copy(staged.at[i], h_out.at[i], sems.at[2 + i]))
    for fetch in fetches:
        fetch.start()
    for fetch, store in zip(fetches, stores):
        fetch.wait()
        store.start()
    for store in stores:
        store.wait()


def cut(hidden, depth):
    shape = (2, hidden.shape[1] // 2, depth)
    return pl.pallas_call(
        cut_kernel,
        out_shape=jax.ShapeDtypeStruct(shape, jnp.bfloat16),
        in_specs=[ANY],
        out_specs=ANY,
        scratch_shapes=[pltpu.VMEM(shape, jnp.bfloat16), pltpu.SemaphoreType.DMA((4,))],
        name="cut",
    )(hidden)


def gate_kernel(*refs):
    pass


def gate(arrays):
    return pl.pallas_call(
        gate_kernel,
        out_shape=tuple(jax.ShapeDtypeStruct(one.shape, one.dtype) for one in arrays),
        in_specs=[ANY] * len(arrays),
        out_specs=(ANY,) * len(arrays),
        input_output_aliases={i: i for i in range(len(arrays))},
        name="gate",
    )(*arrays)


def docs_kernel(by_owner, request_docs, store_keys, store_values, *rest):
    outs, (picks, sems) = rest[:-2], rest[-2:]
    me = lax.axis_index("seq")
    requests, doc_count = request_docs.shape
    slots = store_keys.shape[0]
    capacity = slots // 2

    def one_request(r, carry):
        for c in range(capacity):
            picks[r, c] = 0

        def one_doc(j, count):
            doc = request_docs[r, j]
            mine = lax.div(doc, slots) == me

            @pl.when(mine)
            def _():
                picks[r, jnp.minimum(count, capacity - 1)] = lax.rem(doc, slots)

            return count + mine.astype(jnp.int32)

        lax.fori_loop(0, doc_count, one_doc, jnp.int32(0), unroll=True)
        return carry

    lax.fori_loop(0, requests, one_request, 0)

    def send(r, out, sem):
        for c in range(capacity):
            slot = picks[r, c]
            pltpu.make_async_copy(store_keys.at[slot], out.at[c, 0], sem).start()
            pltpu.make_async_copy(store_values.at[slot], out.at[c, 1], sem).start()

    if by_owner:
        out = outs[0]

        def one_send(r, carry):
            send(r, out.at[r], sems.at[0])
            return carry

        lax.fori_loop(0, requests, one_send, 0)
    else:
        for i, out in enumerate(outs):
            send(lax.bitwise_xor(me, i + 1), out, sems.at[i])
    for i, out in enumerate(outs):
        pltpu.make_async_copy(out, out, sems.at[i]).wait()


def cut_docs(request_docs, store_keys, store_values, by_owner):
    requests = request_docs.shape[0]
    capacity = store_keys.shape[0] // 2
    one = (capacity, 2) + store_keys.shape[1:]
    if by_owner:
        shapes = (jax.ShapeDtypeStruct((requests,) + one, jnp.bfloat16),)
    else:
        shapes = (jax.ShapeDtypeStruct(one, jnp.bfloat16),) * (requests - 1)
    return pl.pallas_call(
        functools.partial(docs_kernel, by_owner),
        out_shape=shapes,
        in_specs=[SMEM, ANY, ANY],
        out_specs=(VMEM,) * len(shapes),
        scratch_shapes=[
            pltpu.SMEM((requests, capacity), jnp.int32),
            pltpu.SemaphoreType.DMA((len(shapes),)),
        ],
        name="cut_docs",
    )(request_docs, store_keys, store_values)


def project_kernel(
    hidden, w_key, w_value, w_far, w_swapped, h_mine, h_other, own, part, w, h, sems
):
    group = lax.axis_index("groups")
    me = lax.axis_index("seq")
    core = lax.rem(lax.axis_index("tp"), 2)
    depth, width = w_key.shape
    rows = hidden.shape[1]
    far = lax.rem(me + 2, 4)
    near = pl.ds(0, depth)
    rest = pl.ds(depth, depth)
    keys = pl.ds(0, width)
    values = pl.ds(width, width)
    copies = [
        pltpu.make_async_copy(w_key, w.at[near, keys], sems.at[0]),
        pltpu.make_async_copy(w_value, w.at[near, values], sems.at[1]),
    ]
    for i, block in enumerate((me, far)):
        columns = pl.ds(i * depth, depth)
        source = hidden.at[0, :, pl.ds(pl.multiple_of(block * depth, depth), depth)]
        copies.append(
            pltpu.make_async_copy(source, h.at[pl.ds(0, rows), columns], sems.at[2 + 3 * i])
        )
        for k, (held, place) in enumerate(((h_mine, core), (h_other, 1 - core))):
            start = pl.multiple_of(rows + place * (rows // 2), rows // 2)
            target = h.at[pl.ds(start, rows // 2), columns]
            copies.append(pltpu.make_async_copy(held.at[i], target, sems.at[3 + 3 * i + k]))
    for one in copies:
        one.start()

    first = pl.multiple_of(group * width, width)
    second = pl.multiple_of((1 - group) * width, width)
    for i, (held, column) in enumerate(((w_far, first), (w_swapped, second))):
        copies.append(
            pltpu.make_async_copy(held, w.at[rest, pl.ds(column, width)], sems.at[8 + i])
        )
        copies[-1].start()
    for one in copies:
        one.wait()
    total = jnp.dot(h[...], w[...], preferred_element_type=jnp.float32)
    own[...] = total[:rows]
    part[...] = total[rows:].astype(part.dtype)


def project(hidden, w_key, w_value, *arrived):
    depth, width = w_key.shape
    rows = hidden.shape[1]
    return pl.pallas_call(
        project_kernel,
        out_shape=(
            jax.ShapeDtypeStruct((rows, 2 * width), jnp.float32),
            jax.ShapeDtypeStruct((rows, 2 * width), jnp.bfloat16),
        ),
        in_specs=[ANY] * (3 + len(arrived)),
        out_specs=(VMEM, VMEM),
        scratch_shapes=[
            pltpu.VMEM((2 * depth, 2 * width), jnp.bfloat16),
            pltpu.VMEM((2 * rows, 2 * depth), jnp.bfloat16),
            pltpu.SemaphoreType.DMA((10,)),
        ],
        compiler_params=pltpu.CompilerParams(vmem_limit_bytes=32 * 1024 * 1024),
        cost_estimate=pl.CostEstimate(flops=1, bytes_accessed=1, transcendentals=0),
        name="project",
    )(hidden, w_key, w_value, *arrived)


def assemble_kernel(
    by_owner, request_docs, held, spare, *rest
):
    sources, (keys, values, counts, sems) = rest[:-4], rest[-4:]
    me = lax.axis_index("seq")
    doc_count = request_docs.shape[1]
    head_dim = keys.shape[1] // 2
    doc_len = keys.shape[0] // doc_count
    owners = request_docs.shape[0]
    slots = sources[0].shape[0] if not by_owner else 2 * sources[0].shape[1]
    left = pl.ds(0, head_dim)

    for o in range(owners):
        counts[o] = 0

    def one_doc(j, carry):
        doc = request_docs[me, j]
        owner = lax.div(doc, slots)
        rank = counts[owner]
        counts[owner] = rank + 1
        place = pl.ds(pl.multiple_of(j * doc_len, doc_len), doc_len)

        def fetch(key_source, value_source):
            pltpu.make_async_copy(key_source, keys.at[place, left], sems.at[0]).start()
            pltpu.make_async_copy(value_source, values.at[place, left], sems.at[1]).start()

        if by_owner:
            fetch(sources[0].at[owner, rank, 0], sources[0].at[owner, rank, 1])
        else:
            away = lax.bitwise_xor(me, owner)

            @pl.when(away == 0)
            def _():
                slot = lax.rem(doc, slots)
                fetch(sources[0].at[slot], sources[1].at[slot])

            for k in range(1, owners):

                @pl.when(away == k)
                def _():
                    fetch(sources[1 + k].at[rank, 0], sources[1 + k].at[rank, 1])

        return carry

    lax.fori_loop(0, doc_count, one_doc, 0)
    pltpu.make_async_copy(keys.at[:, left], keys.at[:, left], sems.at[0]).wait()
    pltpu.make_async_copy(values.at[:, left], values.at[:, left], sems.at[1]).wait()
    spares = jnp.dot(spare[...], keys[:, :head_dim], preferred_element_type=jnp.float32)
    spares = spares.astype(jnp.bfloat16)
    for j in range(doc_count):
        place = slice(j * doc_len, (j + 1) * doc_len)
        used = held[place, :]
        key = jnp.where(used > 0, keys[place, :head_dim], spares[j : j + 1, :])
        keys[place, :head_dim] = key
        keys[place, head_dim:] = key
        values[place, :head_dim] = values[place, :head_dim] * used
        values[place, head_dim:] = used


def assemble(request_docs, held, spare, sources, by_owner):
    context, head_dim = held.shape
    wide = jax.ShapeDtypeStruct((context, 2 * head_dim), jnp.bfloat16)
    return pl.pallas_call(
        functools.partial(assemble_kernel, by_owner),
        out_shape=(wide, wide),
        in_specs=[SMEM, VMEM, VMEM] + [ANY] * len(sources),
        out_specs=(VMEM, VMEM),
        scratch_shapes=[
            pltpu.SMEM((request_docs.shape[0],), jnp.int32),
            pltpu.SemaphoreType.DMA((2,)),
        ],
        compiler_params=pltpu.CompilerParams(vmem_limit_bytes=32 * 1024 * 1024),
        cost_estimate=pl.CostEstimate(flops=0, bytes_accessed=16 * 1024 * 1024, transcendentals=0),
        name="assemble",
    )(request_docs, held, spare, *sources)


def attend_kernel(queries, fresh, keys, values, key_bias, row_place, key_place, mixed):
    row_count = queries.shape[1]
    head_dim = fresh.shape[1] // 2
    heads = queries.shape[2] // head_dim
    step = 4
    blocks = key_bias.shape[1] // (step * 128)
    block_rows = row_count // blocks
    block_keys = key_bias.shape[1] // blocks
    scale = math.log2(math.e) / math.sqrt(head_dim)
    fresh_k = jnp.concatenate([fresh[:, :head_dim]] * 2, axis=1)
    fresh_v = jnp.concatenate([fresh[:, head_dim:], jnp.ones_like(fresh[:, head_dim:])], axis=1)
    slot_place = lax.broadcasted_iota(jnp.int32, (1, block_keys), 1)
    contract_last = (((1,), (1,)), ((), ()))
    for b in range(blocks):
        rows = slice(b * block_rows, (b + 1) * block_rows)
        q = jnp.concatenate(
            [queries[0, rows, h * head_dim : (h + 1) * head_dim] for h in range(heads)], axis=0
        )
        q = q.astype(jnp.float32) * scale
        high = q.astype(jnp.bfloat16)
        low = (q - high.astype(jnp.float32)).astype(jnp.bfloat16)
        q = jnp.concatenate([high, low], axis=1)
        own_place = row_place[rows, :]

        def scores(some_keys):
            return lax.dot_general(
                q, some_keys, contract_last, preferred_element_type=jnp.float32
            )

        def masked(some_keys, allowed):
            shape = (heads, block_rows, some_keys.shape[0])
            kept = jnp.where(allowed[None], scores(some_keys).reshape(shape), MASKED)
            return kept.reshape(heads * block_rows, some_keys.shape[0])

        chunks, sides = [], []
        for c in range(b):
            part = slice(c * block_keys, (c + 1) * block_keys)
            chunks.append(scores(keys[part, :]))
            sides.append(values[part, :])
        part = slice(b * block_keys, (b + 1) * block_keys)
        allowed = (slot_place + b * block_keys <= own_place) & (key_bias[:, part] == 0)
        chunks.append(masked(keys[part, :], allowed))
        sides.append(values[part, :])
        chunks.append(masked(fresh_k, key_place[...] <= own_place))
        sides.append(fresh_v)
        row_max = functools.reduce(
            jnp.maximum, [jnp.max(one, axis=1, keepdims=True) for one in chunks]
        )
        total = jnp.zeros((heads * block_rows, 2 * head_dim), jnp.float32)
        for one, side in zip(chunks, sides):
            powers = jnp.exp2(one - row_max).astype(jnp.bfloat16)
            total += jnp.dot(powers, side, preferred_element_type=jnp.float32)
        result = (total[:, :head_dim] / total[:, head_dim:]).astype(mixed.dtype)
        for h in range(heads):
            mixed[0, rows, h * head_dim : (h + 1) * head_dim] = result[
                h * block_rows : (h + 1) * block_rows
            ]


def attend(queries, fresh, keys, values, key_bias, row_place, key_place):
    return pl.pallas_call(
        attend_kernel,
        out_shape=jax.ShapeDtypeStruct(queries.shape, jnp.bfloat16),
        in_specs=[VMEM] * 7,
        out_specs=VMEM,
        compiler_params=pltpu.CompilerParams(vmem_limit_bytes=32 * 1024 * 1024),
        cost_estimate=pl.CostEstimate(flops=1, bytes_accessed=1, transcendentals=0),
        name="attend",
    )(queries, fresh, keys, values, key_bias, row_place, key_place)


def shards(
    pairs,
    hidden,
    queries,
    w_key,
    w_value,
    store_keys,
    store_values,
    request_docs,
    doc_lengths,
    recompute_rows,
):
    my_index = lax.axis_index("seq")
    seq_count = lax.axis_size("seq")
    slot_count, doc_len, head_dim = store_keys.shape
    capacity = slot_count // 2
    doc_count = request_docs.shape[1]
    row_ids = recompute_rows[0]
    per_doc = row_ids.shape[1]
    row_count = doc_count * per_doc

    if pairs:
        def swap(array, axis, apart):
            count = lax.axis_size(axis)
            return lax.ppermute(array, axis, [(i, i ^ apart) for i in range(count)])

        w_far = swap(pick_weights(w_key, w_value), "seq", 2)
        h_mine = swap(cut(hidden, w_key.shape[0]), "seq", 1)
        docs = cut_docs(request_docs, store_keys, store_values, False)
        *docs, w_far = gate((*docs, w_far))
        w_swapped = swap(w_far, "groups", 1)
        docs = [swap(doc, "seq", k + 1) for k, doc in enumerate(docs)]
        h_other = swap(h_mine, "tp", 1)
        own, part = project(hidden, w_key, w_value, w_far, w_swapped, h_mine, h_other)
        fresh = (own + swap(part, "seq", 1).astype(jnp.float32)).astype(jnp.bfloat16)
        sources = (store_keys, store_values, *docs)
    else:
        (docs,) = cut_docs(request_docs, store_keys, store_values, True)
        sources = (lax.all_to_all(docs, "seq", split_axis=0, concat_axis=0, tiled=True),)
        weights = lax.all_gather(
            jnp.concatenate([w_key, w_value], axis=1), "seq", axis=0, tiled=True
        )
        fresh = jnp.dot(hidden[0], weights, preferred_element_type=jnp.float32)
        fresh = fresh.astype(jnp.bfloat16)

    my_docs = lax.dynamic_index_in_dim(request_docs, my_index, 0, keepdims=False)
    owners = my_docs // slot_count
    earlier = jnp.arange(doc_count)[None, :] < jnp.arange(doc_count)[:, None]
    ranks = jnp.sum(((owners[:, None] == owners[None, :]) & earlier).astype(jnp.int32), axis=1)
    positions = jnp.arange(doc_len, dtype=jnp.int32)
    held = positions[None, :] < doc_lengths[my_docs][:, None]
    held &= jnp.all(positions[None, None, :] != row_ids[:, :, None], axis=1)
    key_bias = jnp.where(held, 0.0, MASKED).astype(jnp.float32).reshape(1, doc_count * doc_len)
    place = jnp.arange(doc_count, dtype=jnp.int32)[:, None] * doc_len + row_ids
    context = doc_count * doc_len
    used = held.astype(jnp.bfloat16).reshape(context, 1)
    first_used = jnp.argmax(held, axis=1) + jnp.arange(doc_count) * doc_len
    spare = (jnp.arange(context)[None, :] == first_used[:, None]).astype(jnp.bfloat16)
    keys, values = assemble(
        request_docs, jnp.broadcast_to(used, (context, head_dim)), spare, sources, not pairs
    )
    mixed = attend(
        queries,
        fresh,
        keys,
        values,
        key_bias,
        place.reshape(row_count, 1),
        place.reshape(1, row_count),
    )

    slot_of_row = jnp.repeat(owners * capacity + ranks, per_doc) * per_doc + jnp.tile(
        jnp.arange(per_doc), doc_count
    )
    slots = jnp.arange(seq_count * capacity * per_doc)
    pick = (slots[:, None] == slot_of_row[None, :]).astype(jnp.bfloat16)
    outgoing = jnp.dot(pick, fresh, preferred_element_type=jnp.float32).astype(jnp.bfloat16)
    outgoing = outgoing.reshape(seq_count, capacity, per_doc, 2 * head_dim)
    returned = lax.all_to_all(outgoing, "seq", split_axis=0, concat_axis=0, tiled=True)
    returned = returned.reshape(seq_count, capacity, per_doc, 2, head_dim)
    return (mixed, returned[None])


def solution(mesh):
    pairs = mesh.shape["seq"] == 4 and mesh.shape["groups"] == 2 and mesh.shape["tp"] % 2 == 0
    return jax.shard_map(
        functools.partial(shards, pairs),
        mesh=mesh,
        in_specs=(
            P(("groups", "seq"), None, None),
            P(("groups", "seq"), None, "tp"),
            P("seq", "tp"),
            P("seq", "tp"),
            P(("groups", "seq"), None, "tp"),
            P(("groups", "seq"), None, "tp"),
            P("groups", None),
            P("groups"),
            P(("groups", "seq"), None, None),
        ),
        out_specs=(
            P(("groups", "seq"), None, "tp"),
            P(("groups", "seq"), None, None, None, None, "tp"),
        ),
        check_vma=False,
    )
```

```python
import functools
import math

import jax
import jax.numpy as jnp
from jax import lax
from jax.experimental import pallas as pl
from jax.experimental.pallas import tpu as pltpu
from jax.sharding import PartitionSpec as P

ANY = pl.BlockSpec(memory_space=pl.ANY)
HBM = pl.BlockSpec(memory_space=pltpu.HBM)
SMEM = pl.BlockSpec(memory_space=pltpu.SMEM)
VMEM = pl.BlockSpec(memory_space=pltpu.VMEM)
MASKED = -1e30


def pick_kernel(w_key, w_value, w_out, staged, sems):
    group = lax.axis_index("groups")
    pieces = staged.shape[0]
    rows = staged.shape[1]

    def fetch(i, weight):
        source = weight.at[pl.ds(i * rows, rows)]
        return pltpu.make_async_copy(source, staged.at[i], sems.at[0, i])

    for chosen, weight in ((0, w_key), (1, w_value)):

        @pl.when(group == chosen)
        def _():
            for i in range(pieces):
                fetch(i, weight).start()

    stores = []
    for i in range(pieces):
        fetch(i, w_key).wait()
        target = w_out.at[pl.ds(i * rows, rows)]
        stores.append(pltpu.make_async_copy(staged.at[i], target, sems.at[1, i]))
        stores[-1].start()
    for store in stores:
        store.wait()


def pick_weights(w_key, w_value):
    pieces = 4
    return pl.pallas_call(
        pick_kernel,
        out_shape=jax.ShapeDtypeStruct(w_key.shape, jnp.bfloat16),
        in_specs=[HBM, HBM],
        out_specs=HBM,
        scratch_shapes=[
            pltpu.VMEM((pieces, w_key.shape[0] // pieces, w_key.shape[1]), jnp.bfloat16),
            pltpu.SemaphoreType.DMA((2, pieces)),
        ],
        name="pick_weights",
    )(w_key, w_value)


def gate_kernel(*refs):
    pass


def gate(arrays):
    return pl.pallas_call(
        gate_kernel,
        out_shape=tuple(jax.ShapeDtypeStruct(one.shape, one.dtype) for one in arrays),
        in_specs=[ANY] * len(arrays),
        out_specs=(ANY,) * len(arrays),
        input_output_aliases={i: i for i in range(len(arrays))},
        compiler_params=pltpu.CompilerParams(vmem_limit_bytes=1 * 1024 * 1024),
        name="gate",
    )(*arrays)


def cut_kernel(by_owner, request_docs, store_keys, store_values, *rest):
    if by_owner:
        out, picks, sems = rest
        outs = (out,)
    else:
        hidden, h_out, *outs, picks, sems = rest
    me = lax.axis_index("seq")
    requests, doc_count = request_docs.shape
    slots = store_keys.shape[0]
    capacity = slots // 2
    h_copies = []
    if not by_owner:
        core = lax.rem(lax.axis_index("tp"), 2)
        rows, depth = h_out.shape[1:]
        first = me + 1 - 2 * lax.rem(me, 2)
        second = lax.rem(first + 2, 4)
        for i, block in enumerate((first, second)):
            source = hidden.at[
                0,
                pl.ds(pl.multiple_of(core * rows, rows), rows),
                pl.ds(pl.multiple_of(block * depth, depth), depth),
            ]
            h_copies.append(pltpu.make_async_copy(source, h_out.at[i], sems.at[len(outs) + i]))
            h_copies[-1].start()

    def one_request(r, carry):
        for c in range(capacity):
            picks[r, c] = 0

        def one_doc(j, count):
            doc = request_docs[r, j]
            mine = lax.div(doc, slots) == me

            @pl.when(mine)
            def _():
                picks[r, jnp.minimum(count, capacity - 1)] = lax.rem(doc, slots)

            return count + mine.astype(jnp.int32)

        lax.fori_loop(0, doc_count, one_doc, jnp.int32(0), unroll=True)
        return carry

    lax.fori_loop(0, requests, one_request, 0)

    def send(r, out, sem):
        for c in range(capacity):
            slot = picks[r, c]
            pltpu.make_async_copy(store_keys.at[slot], out.at[c, 0], sem).start()
            pltpu.make_async_copy(store_values.at[slot], out.at[c, 1], sem).start()

    if by_owner:

        def one_send(r, carry):
            send(r, outs[0].at[r], sems.at[0])
            return carry

        lax.fori_loop(0, requests, one_send, 0)
    else:
        for i, out in enumerate(outs):
            send(lax.bitwise_xor(me, i + 1), out, sems.at[i])
    for copy in h_copies:
        copy.wait()
    for i, out in enumerate(outs):
        pltpu.make_async_copy(out, out, sems.at[i]).wait()


def cut(request_docs, store_keys, store_values, hidden, depth):
    requests = request_docs.shape[0]
    capacity = store_keys.shape[0] // 2
    one = (capacity, 2) + store_keys.shape[1:]
    if hidden is None:
        shapes = ((requests,) + one,)
        inputs = (store_keys, store_values)
    else:
        shapes = ((2, hidden.shape[1] // 2, depth),) + (one,) * (requests - 1)
        inputs = (store_keys, store_values, hidden)
    return pl.pallas_call(
        functools.partial(cut_kernel, hidden is None),
        out_shape=tuple(jax.ShapeDtypeStruct(one, jnp.bfloat16) for one in shapes),
        in_specs=[SMEM] + [HBM] * len(inputs),
        out_specs=(VMEM,) * len(shapes),
        scratch_shapes=[
            pltpu.SMEM((requests, capacity), jnp.int32),
            pltpu.SemaphoreType.DMA((len(shapes) + 1,)),
        ],
        name="cut",
    )(request_docs, *inputs)


def project_kernel(
    hidden, w_key, w_value, w_far, w_swapped, h_mine, h_other, own, part, w, h, sems
):
    group = lax.axis_index("groups")
    me = lax.axis_index("seq")
    core = lax.rem(lax.axis_index("tp"), 2)
    depth, width = w_key.shape
    rows = hidden.shape[1]
    far = lax.rem(me + 2, 4)
    near = pl.ds(0, depth)
    rest = pl.ds(depth, depth)
    keys = pl.ds(0, width)
    values = pl.ds(width, width)
    copies = [
        pltpu.make_async_copy(w_key, w.at[near, keys], sems.at[0]),
        pltpu.make_async_copy(w_value, w.at[near, values], sems.at[1]),
    ]
    for i, block in enumerate((me, far)):
        columns = pl.ds(i * depth, depth)
        source = hidden.at[0, :, pl.ds(pl.multiple_of(block * depth, depth), depth)]
        copies.append(
            pltpu.make_async_copy(source, h.at[pl.ds(0, rows), columns], sems.at[2 + 3 * i])
        )
        for k, (held, place) in enumerate(((h_mine, core), (h_other, 1 - core))):
            start = pl.multiple_of(rows + place * (rows // 2), rows // 2)
            target = h.at[pl.ds(start, rows // 2), columns]
            copies.append(pltpu.make_async_copy(held.at[i], target, sems.at[3 + 3 * i + k]))
    for one in copies:
        one.start()

    first = pl.multiple_of(group * width, width)
    second = pl.multiple_of((1 - group) * width, width)
    for i, (held, column) in enumerate(((w_far, first), (w_swapped, second))):
        copies.append(
            pltpu.make_async_copy(held, w.at[rest, pl.ds(column, width)], sems.at[8 + i])
        )
        copies[-1].start()
    for one in copies:
        one.wait()
    total = jnp.dot(h[...], w[...], preferred_element_type=jnp.float32)
    own[...] = total[:rows]
    part[...] = total[rows:].astype(part.dtype)


def project(hidden, w_key, w_value, *arrived):
    depth, width = w_key.shape
    rows = hidden.shape[1]
    return pl.pallas_call(
        project_kernel,
        out_shape=(
            jax.ShapeDtypeStruct((rows, 2 * width), jnp.float32),
            jax.ShapeDtypeStruct((rows, 2 * width), jnp.bfloat16),
        ),
        in_specs=[HBM] * (3 + len(arrived)),
        out_specs=(VMEM, VMEM),
        scratch_shapes=[
            pltpu.VMEM((2 * depth, 2 * width), jnp.bfloat16),
            pltpu.VMEM((2 * rows, 2 * depth), jnp.bfloat16),
            pltpu.SemaphoreType.DMA((10,)),
        ],
        compiler_params=pltpu.CompilerParams(vmem_limit_bytes=32 * 1024 * 1024),
        cost_estimate=pl.CostEstimate(flops=1, bytes_accessed=1, transcendentals=0),
        name="project",
    )(hidden, w_key, w_value, *arrived)


def assemble_kernel(
    by_owner, request_docs, held, spare, *rest
):
    sources, (keys, values, counts, sems) = rest[:-4], rest[-4:]
    me = lax.axis_index("seq")
    doc_count = request_docs.shape[1]
    head_dim = keys.shape[1] // 2
    doc_len = keys.shape[0] // doc_count
    owners = request_docs.shape[0]
    slots = sources[0].shape[0] if not by_owner else 2 * sources[0].shape[1]
    left = pl.ds(0, head_dim)

    for o in range(owners):
        counts[o] = 0

    def one_doc(j, carry):
        doc = request_docs[me, j]
        owner = lax.div(doc, slots)
        rank = counts[owner]
        counts[owner] = rank + 1
        place = pl.ds(pl.multiple_of(j * doc_len, doc_len), doc_len)

        def fetch(key_source, value_source):
            pltpu.make_async_copy(key_source, keys.at[place, left], sems.at[0]).start()
            pltpu.make_async_copy(value_source, values.at[place, left], sems.at[1]).start()

        if by_owner:
            fetch(sources[0].at[owner, rank, 0], sources[0].at[owner, rank, 1])
        else:
            away = lax.bitwise_xor(me, owner)

            @pl.when(away == 0)
            def _():
                slot = lax.rem(doc, slots)
                fetch(sources[0].at[slot], sources[1].at[slot])

            for k in range(1, owners):

                @pl.when(away == k)
                def _():
                    fetch(sources[1 + k].at[rank, 0], sources[1 + k].at[rank, 1])

        return carry

    lax.fori_loop(0, doc_count, one_doc, 0)
    pltpu.make_async_copy(keys.at[:, left], keys.at[:, left], sems.at[0]).wait()
    pltpu.make_async_copy(values.at[:, left], values.at[:, left], sems.at[1]).wait()
    spares = jnp.dot(spare[...], keys[:, :head_dim], preferred_element_type=jnp.float32)
    spares = spares.astype(jnp.bfloat16)
    for j in range(doc_count):
        place = slice(j * doc_len, (j + 1) * doc_len)
        used = held[place, :]
        key = jnp.where(used > 0, keys[place, :head_dim], spares[j : j + 1, :])
        keys[place, :head_dim] = key
        keys[place, head_dim:] = key
        values[place, :head_dim] = values[place, :head_dim] * used
        values[place, head_dim:] = used


def assemble(request_docs, held, spare, sources, by_owner):
    context, head_dim = held.shape
    wide = jax.ShapeDtypeStruct((context, 2 * head_dim), jnp.bfloat16)
    return pl.pallas_call(
        functools.partial(assemble_kernel, by_owner),
        out_shape=(wide, wide),
        in_specs=[SMEM, VMEM, VMEM] + [HBM] * len(sources),
        out_specs=(VMEM, VMEM),
        scratch_shapes=[
            pltpu.SMEM((request_docs.shape[0],), jnp.int32),
            pltpu.SemaphoreType.DMA((2,)),
        ],
        compiler_params=pltpu.CompilerParams(vmem_limit_bytes=32 * 1024 * 1024),
        cost_estimate=pl.CostEstimate(flops=0, bytes_accessed=16 * 1024 * 1024, transcendentals=0),
        name="assemble",
    )(request_docs, held, spare, *sources)


def finish_kernel(own, arrived, slot_row, fresh, outgoing):
    total = (own[...] + arrived[...].astype(jnp.float32)).astype(jnp.bfloat16)
    fresh[...] = total
    rows = lax.broadcasted_iota(jnp.int32, (1, total.shape[0]), 1)
    pick = (rows == slot_row[...]).astype(jnp.bfloat16)
    outgoing[...] = jnp.dot(pick, total, preferred_element_type=jnp.float32).astype(jnp.bfloat16)


def finish(own, arrived, slot_row):
    shapes = (own.shape, (slot_row.shape[0], own.shape[1]))
    return pl.pallas_call(
        finish_kernel,
        out_shape=tuple(jax.ShapeDtypeStruct(one, jnp.bfloat16) for one in shapes),
        in_specs=[VMEM] * 3,
        out_specs=(VMEM, VMEM),
        compiler_params=pltpu.CompilerParams(vmem_limit_bytes=16 * 1024 * 1024),
        name="finish",
    )(own, arrived, slot_row)


def attend_kernel(queries, fresh, keys, values, key_bias, row_place, key_place, mixed):
    row_count = queries.shape[1]
    head_dim = fresh.shape[1] // 2
    heads = queries.shape[2] // head_dim
    step = 4
    blocks = key_bias.shape[1] // (step * 128)
    block_rows = row_count // blocks
    block_keys = key_bias.shape[1] // blocks
    scale = math.log2(math.e) / math.sqrt(head_dim)
    fresh_k = jnp.concatenate([fresh[:, :head_dim]] * 2, axis=1)
    fresh_v = jnp.concatenate([fresh[:, head_dim:], jnp.ones_like(fresh[:, head_dim:])], axis=1)
    slot_place = lax.broadcasted_iota(jnp.int32, (1, block_keys), 1)
    contract_last = (((1,), (1,)), ((), ()))
    for b in range(blocks):
        rows = slice(b * block_rows, (b + 1) * block_rows)
        q = jnp.concatenate(
            [queries[0, rows, h * head_dim : (h + 1) * head_dim] for h in range(heads)], axis=0
        )
        q = q.astype(jnp.float32) * scale
        high = q.astype(jnp.bfloat16)
        low = (q - high.astype(jnp.float32)).astype(jnp.bfloat16)
        q = jnp.concatenate([high, low], axis=1)
        own_place = row_place[rows, :]

        def scores(some_keys):
            return lax.dot_general(
                q, some_keys, contract_last, preferred_element_type=jnp.float32
            )

        def masked(some_keys, allowed):
            shape = (heads, block_rows, some_keys.shape[0])
            kept = jnp.where(allowed[None], scores(some_keys).reshape(shape), MASKED)
            return kept.reshape(heads * block_rows, some_keys.shape[0])

        chunks, sides = [], []
        for c in range(b):
            part = slice(c * block_keys, (c + 1) * block_keys)
            chunks.append(scores(keys[part, :]))
            sides.append(values[part, :])
        part = slice(b * block_keys, (b + 1) * block_keys)
        allowed = (slot_place + b * block_keys <= own_place) & (key_bias[:, part] == 0)
        chunks.append(masked(keys[part, :], allowed))
        sides.append(values[part, :])
        chunks.append(masked(fresh_k, key_place[...] <= own_place))
        sides.append(fresh_v)
        row_max = functools.reduce(
            jnp.maximum, [jnp.max(one, axis=1, keepdims=True) for one in chunks]
        )
        total = jnp.zeros((heads * block_rows, 2 * head_dim), jnp.float32)
        for one, side in zip(chunks, sides):
            powers = jnp.exp2(one - row_max).astype(jnp.bfloat16)
            total += jnp.dot(powers, side, preferred_element_type=jnp.float32)
        result = (total[:, :head_dim] / total[:, head_dim:]).astype(mixed.dtype)
        for h in range(heads):
            mixed[0, rows, h * head_dim : (h + 1) * head_dim] = result[
                h * block_rows : (h + 1) * block_rows
            ]


def attend(queries, fresh, keys, values, key_bias, row_place, key_place):
    return pl.pallas_call(
        attend_kernel,
        out_shape=jax.ShapeDtypeStruct(queries.shape, jnp.bfloat16),
        in_specs=[VMEM] * 7,
        out_specs=VMEM,
        compiler_params=pltpu.CompilerParams(vmem_limit_bytes=32 * 1024 * 1024),
        cost_estimate=pl.CostEstimate(flops=1, bytes_accessed=1, transcendentals=0),
        name="attend",
    )(queries, fresh, keys, values, key_bias, row_place, key_place)


def shards(
    pairs,
    hidden,
    queries,
    w_key,
    w_value,
    store_keys,
    store_values,
    request_docs,
    doc_lengths,
    recompute_rows,
):
    my_index = lax.axis_index("seq")
    seq_count = lax.axis_size("seq")
    slot_count, doc_len, head_dim = store_keys.shape
    capacity = slot_count // 2
    doc_count = request_docs.shape[1]
    row_ids = recompute_rows[0]
    per_doc = row_ids.shape[1]
    row_count = doc_count * per_doc

    if pairs:
        def swap(array, axis, apart):
            count = lax.axis_size(axis)
            return lax.ppermute(array, axis, [(i, i ^ apart) for i in range(count)])

        w_far = swap(pick_weights(w_key, w_value), "seq", 2)
        h_send, *docs = cut(request_docs, store_keys, store_values, hidden, w_key.shape[0])
        h_mine = swap(h_send, "seq", 1)
        *docs, w_far = gate((*docs, w_far))
        w_swapped = swap(w_far, "groups", 1)
        docs = [swap(doc, "seq", k + 1) for k, doc in enumerate(docs)]
        h_other = swap(h_mine, "tp", 1)
        own, part = project(hidden, w_key, w_value, w_far, w_swapped, h_mine, h_other)
        arrived = swap(part, "seq", 1)
        sources = (store_keys, store_values, *docs)
    else:
        (docs,) = cut(request_docs, store_keys, store_values, None, 0)
        sources = (lax.all_to_all(docs, "seq", split_axis=0, concat_axis=0, tiled=True),)
        weights = lax.all_gather(
            jnp.concatenate([w_key, w_value], axis=1), "seq", axis=0, tiled=True
        )
        own = jnp.dot(hidden[0], weights, preferred_element_type=jnp.float32)
        arrived = jnp.zeros(own.shape, jnp.bfloat16)

    my_docs = lax.dynamic_index_in_dim(request_docs, my_index, 0, keepdims=False)
    owners = my_docs // slot_count
    earlier = jnp.arange(doc_count)[None, :] < jnp.arange(doc_count)[:, None]
    ranks = jnp.sum(((owners[:, None] == owners[None, :]) & earlier).astype(jnp.int32), axis=1)
    positions = jnp.arange(doc_len, dtype=jnp.int32)
    held = positions[None, :] < doc_lengths[my_docs][:, None]
    held &= jnp.all(positions[None, None, :] != row_ids[:, :, None], axis=1)
    key_bias = jnp.where(held, 0.0, MASKED).astype(jnp.float32).reshape(1, doc_count * doc_len)
    place = jnp.arange(doc_count, dtype=jnp.int32)[:, None] * doc_len + row_ids
    context = doc_count * doc_len
    used = held.astype(jnp.bfloat16).reshape(context, 1)
    first_used = jnp.argmax(held, axis=1) + jnp.arange(doc_count) * doc_len
    spare = (jnp.arange(context)[None, :] == first_used[:, None]).astype(jnp.bfloat16)
    keys, values = assemble(
        request_docs, jnp.broadcast_to(used, (context, head_dim)), spare, sources, not pairs
    )
    row_of_slot = owners * capacity + ranks
    chosen = row_of_slot[None, :] == jnp.arange(seq_count * capacity)[:, None]
    entry = jnp.max(jnp.where(chosen, jnp.arange(doc_count)[None, :], -doc_count), axis=1)
    slot_row = entry[:, None] * per_doc + jnp.arange(per_doc)[None, :]
    fresh, outgoing = finish(own, arrived, slot_row.reshape(-1, 1))
    mixed = attend(
        queries,
        fresh,
        keys,
        values,
        key_bias,
        place.reshape(row_count, 1),
        place.reshape(1, row_count),
    )

    outgoing = outgoing.reshape(seq_count, capacity, per_doc, 2 * head_dim)
    returned = lax.all_to_all(outgoing, "seq", split_axis=0, concat_axis=0, tiled=True)
    returned = returned.reshape(seq_count, capacity, per_doc, 2, head_dim)
    return (mixed, returned[None])


def solution(mesh):
    pairs = mesh.shape["seq"] == 4 and mesh.shape["groups"] == 2 and mesh.shape["tp"] % 2 == 0
    return jax.shard_map(
        functools.partial(shards, pairs),
        mesh=mesh,
        in_specs=(
            P(("groups", "seq"), None, None),
            P(("groups", "seq"), None, "tp"),
            P("seq", "tp"),
            P("seq", "tp"),
            P(("groups", "seq"), None, "tp"),
            P(("groups", "seq"), None, "tp"),
            P("groups", None),
            P("groups"),
            P(("groups", "seq"), None, None),
        ),
        out_specs=(
            P(("groups", "seq"), None, "tp"),
            P(("groups", "seq"), None, None, None, None, "tp"),
        ),
        check_vma=False,
    )
```

```python
import functools
import math

import jax
import jax.numpy as jnp
from jax import lax
from jax.experimental import pallas as pl
from jax.experimental.pallas import tpu as pltpu
from jax.sharding import PartitionSpec as P

ANY = pl.BlockSpec(memory_space=pl.ANY)
HBM = pl.BlockSpec(memory_space=pltpu.HBM)
SMEM = pl.BlockSpec(memory_space=pltpu.SMEM)
VMEM = pl.BlockSpec(memory_space=pltpu.VMEM)
MASKED = -1e30


def in_hbm(array):
    return pltpu.with_memory_space_constraint(array, pltpu.HBM)


def send_kernel(hidden, w_key, w_value, w_out, h_out, w_held, h_held, w_sems, h_sems):
    group = lax.axis_index("groups")
    me = lax.axis_index("seq")
    quarter = lax.axis_index("tp")
    pieces, piece = w_held.shape[:2]
    rows, depth = h_out.shape[1:]

    def fetch(i, weight):
        source = weight.at[pl.ds(i * piece, piece)]
        return pltpu.make_async_copy(source, w_held.at[i], w_sems.at[0, i])

    for chosen, weight in ((0, w_key), (1, w_value)):

        @pl.when(group == chosen)
        def _():
            for i in range(pieces):
                fetch(i, weight).start()

    first = me + 1 - 2 * lax.rem(me, 2)
    stores = []
    h_fetches = []
    for i, block in enumerate((first, lax.rem(first + 2, 4))):
        source = hidden.at[
            0,
            pl.ds(pl.multiple_of(quarter * rows, rows), rows),
            pl.ds(pl.multiple_of(block * depth, depth), depth),
        ]
        h_fetches.append(pltpu.make_async_copy(source, h_held.at[i], h_sems.at[0, i]))
        h_fetches[-1].start()
    for i in range(pieces):
        fetch(i, w_key).wait()
        target = w_out.at[pl.ds(i * piece, piece)]
        stores.append(pltpu.make_async_copy(w_held.at[i], target, w_sems.at[1, i]))
        stores[-1].start()
    for i, one in enumerate(h_fetches):
        one.wait()
        stores.append(pltpu.make_async_copy(h_held.at[i], h_out.at[i], h_sems.at[1, i]))
        stores[-1].start()
    for store in stores:
        store.wait()


def pick_sent(hidden, w_key, w_value):
    depth, width = w_key.shape
    pieces = 4
    h_shape = (2, hidden.shape[1] // 4, depth)
    return pl.pallas_call(
        send_kernel,
        out_shape=(
            jax.ShapeDtypeStruct(w_key.shape, jnp.bfloat16),
            jax.ShapeDtypeStruct(h_shape, jnp.bfloat16),
        ),
        in_specs=[ANY] * 3,
        out_specs=(ANY, ANY),
        scratch_shapes=[
            pltpu.VMEM((pieces, depth // pieces, width), jnp.bfloat16),
            pltpu.VMEM(h_shape, jnp.bfloat16),
            pltpu.SemaphoreType.DMA((2, pieces)),
            pltpu.SemaphoreType.DMA((2, 2)),
        ],
        name="pick_sent",
    )(hidden, w_key, w_value)


def gate_kernel(*refs):
    pass


def gate(arrays):
    return pl.pallas_call(
        gate_kernel,
        out_shape=tuple(jax.ShapeDtypeStruct(one.shape, one.dtype) for one in arrays),
        in_specs=[ANY] * len(arrays),
        out_specs=(ANY,) * len(arrays),
        input_output_aliases={i: i for i in range(len(arrays))},
        name="gate",
    )(*arrays)


def docs_kernel(by_owner, request_docs, store_keys, store_values, *rest):
    *outs, picks, sems = rest
    me = lax.axis_index("seq")
    requests, doc_count = request_docs.shape
    slots = store_keys.shape[0]
    capacity = slots // 2

    def one_request(r, carry):
        for c in range(capacity):
            picks[r, c] = 0

        def one_doc(j, count):
            doc = request_docs[r, j]
            mine = lax.div(doc, slots) == me

            @pl.when(mine)
            def _():
                picks[r, jnp.minimum(count, capacity - 1)] = lax.rem(doc, slots)

            return count + mine.astype(jnp.int32)

        lax.fori_loop(0, doc_count, one_doc, jnp.int32(0), unroll=True)
        return carry

    lax.fori_loop(0, requests, one_request, 0)

    def send(r, out, sem):
        for c in range(capacity):
            slot = picks[r, c]
            pltpu.make_async_copy(store_keys.at[slot], out.at[c, 0], sem).start()
            pltpu.make_async_copy(store_values.at[slot], out.at[c, 1], sem).start()

    if by_owner:

        def one_send(r, carry):
            send(r, outs[0].at[r], sems.at[0])
            return carry

        lax.fori_loop(0, requests, one_send, 0)
    else:
        for i, out in enumerate(outs):
            send(lax.bitwise_xor(me, i + 1), out, sems.at[i])
    for i, out in enumerate(outs):
        pltpu.make_async_copy(out, out, sems.at[i]).wait()


def pick_docs(request_docs, store_keys, store_values, by_owner):
    requests = request_docs.shape[0]
    capacity = store_keys.shape[0] // 2
    one = (capacity, 2) + store_keys.shape[1:]
    shapes = ((requests,) + one,) if by_owner else (one,) * (requests - 1)
    return pl.pallas_call(
        functools.partial(docs_kernel, by_owner),
        out_shape=tuple(jax.ShapeDtypeStruct(one, jnp.bfloat16) for one in shapes),
        in_specs=[SMEM, ANY, ANY],
        out_specs=(VMEM,) * len(shapes),
        scratch_shapes=[
            pltpu.SMEM((requests, capacity), jnp.int32),
            pltpu.SemaphoreType.DMA((len(shapes),)),
        ],
        name="pick_docs",
    )(request_docs, store_keys, store_values)


def lay_rows(hidden, quarters, block, depth, h, copy):
    mine = lax.axis_index("tp")
    rows = hidden.shape[1]
    piece = rows // len(quarters)
    start = pl.multiple_of(block * depth, depth)
    copy(hidden.at[0, :, pl.ds(start, depth)], h.at[pl.ds(0, rows)])
    for k, quarter in enumerate(quarters):
        start = pl.multiple_of(rows + lax.bitwise_xor(mine, k) * piece, piece)
        copy(quarter, h.at[pl.ds(start, piece)])


def near_kernel(hidden, w_key, w_value, *rest):
    *quarters, total, w, h, sems = rest
    depth, width = w_key.shape
    copies = []

    def copy(source, target):
        copies.append(pltpu.make_async_copy(source, target, sems.at[len(copies)]))
        copies[-1].start()

    for i, held in enumerate((w_key, w_value)):
        copy(held, w.at[:, pl.ds(i * width, width)])
    quarters = [quarter.at[0] for quarter in quarters]
    lay_rows(hidden, quarters, lax.axis_index("seq"), depth, h, copy)
    for one in copies:
        one.wait()
    total[...] = jnp.dot(h[...], w[...], preferred_element_type=jnp.float32)


def far_kernel(hidden, w_far, w_swapped, near, *rest):
    *quarters, own, part, w, h, sems, held_own, own_sem = rest
    group = lax.axis_index("groups")
    depth, width = w_far.shape
    rows = hidden.shape[1]
    copies = []

    def copy(source, target):
        copies.append(pltpu.make_async_copy(source, target, sems.at[len(copies)]))
        copies[-1].start()

    for held, place in ((w_far, group), (w_swapped, 1 - group)):
        copy(held, w.at[:, pl.ds(pl.multiple_of(place * width, width), width)])
    quarters = [quarter.at[1] for quarter in quarters]
    lay_rows(hidden, quarters, lax.rem(lax.axis_index("seq") + 2, 4), depth, h, copy)
    for one in copies:
        one.wait()
    total = near[...] + jnp.dot(h[...], w[...], preferred_element_type=jnp.float32)
    held_own[...] = total[:rows]
    store = pltpu.make_async_copy(held_own, own, own_sem)
    store.start()
    part[...] = total[rows:].astype(part.dtype)
    store.wait()


def project(hidden, w_key, w_value, w_far, w_swapped, quarters):
    depth, width = w_key.shape
    rows = hidden.shape[1]
    scratch = [
        pltpu.VMEM((depth, 2 * width), jnp.bfloat16),
        pltpu.VMEM((2 * rows, depth), jnp.bfloat16),
        pltpu.SemaphoreType.DMA((3 + len(quarters),)),
    ]
    settings = dict(
        compiler_params=pltpu.CompilerParams(vmem_limit_bytes=16 * 1024 * 1024),
        cost_estimate=pl.CostEstimate(flops=1, bytes_accessed=1, transcendentals=0),
    )
    near = pl.pallas_call(
        near_kernel,
        out_shape=jax.ShapeDtypeStruct((2 * rows, 2 * width), jnp.float32),
        in_specs=[ANY] * (3 + len(quarters)),
        out_specs=VMEM,
        scratch_shapes=scratch,
        name="project_near",
        **settings,
    )(hidden, in_hbm(w_key), in_hbm(w_value), *quarters)
    return pl.pallas_call(
        far_kernel,
        out_shape=(
            jax.ShapeDtypeStruct((rows, 2 * width), jnp.float32),
            jax.ShapeDtypeStruct((rows, 2 * width), jnp.bfloat16),
        ),
        in_specs=[ANY] * 3 + [VMEM] + [ANY] * len(quarters),
        out_specs=(ANY, VMEM),
        scratch_shapes=scratch
        + [pltpu.VMEM((rows, 2 * width), jnp.float32), pltpu.SemaphoreType.DMA],
        name="project_far",
        **settings,
    )(hidden, w_far, w_swapped, near, *quarters)


def assemble_kernel(
    by_owner, request_docs, held, spare, *rest
):
    sources, (keys, values, counts, sems) = rest[:-4], rest[-4:]
    me = lax.axis_index("seq")
    doc_count = request_docs.shape[1]
    head_dim = keys.shape[1] // 2
    doc_len = keys.shape[0] // doc_count
    owners = request_docs.shape[0]
    slots = sources[0].shape[0] if not by_owner else 2 * sources[0].shape[1]
    left = pl.ds(0, head_dim)

    for o in range(owners):
        counts[o] = 0

    def one_doc(j, carry):
        doc = request_docs[me, j]
        owner = lax.div(doc, slots)
        rank = counts[owner]
        counts[owner] = rank + 1
        place = pl.ds(pl.multiple_of(j * doc_len, doc_len), doc_len)

        def fetch(key_source, value_source):
            pltpu.make_async_copy(key_source, keys.at[place, left], sems.at[0]).start()
            pltpu.make_async_copy(value_source, values.at[place, left], sems.at[1]).start()

        if by_owner:
            fetch(sources[0].at[owner, rank, 0], sources[0].at[owner, rank, 1])
        else:
            away = lax.bitwise_xor(me, owner)

            @pl.when(away == 0)
            def _():
                slot = lax.rem(doc, slots)
                fetch(sources[0].at[slot], sources[1].at[slot])

            for k in range(1, owners):

                @pl.when(away == k)
                def _():
                    fetch(sources[1 + k].at[rank, 0], sources[1 + k].at[rank, 1])

        return carry

    lax.fori_loop(0, doc_count, one_doc, 0)
    pltpu.make_async_copy(keys.at[:, left], keys.at[:, left], sems.at[0]).wait()
    pltpu.make_async_copy(values.at[:, left], values.at[:, left], sems.at[1]).wait()
    spares = jnp.dot(spare[...], keys[:, :head_dim], preferred_element_type=jnp.float32)
    spares = spares.astype(jnp.bfloat16)
    for j in range(doc_count):
        place = slice(j * doc_len, (j + 1) * doc_len)
        used = held[place, :]
        key = jnp.where(used > 0, keys[place, :head_dim], spares[j : j + 1, :])
        keys[place, :head_dim] = key
        keys[place, head_dim:] = key
        values[place, :head_dim] = values[place, :head_dim] * used
        values[place, head_dim:] = used


def assemble(request_docs, held, spare, sources, by_owner):
    context, head_dim = held.shape
    wide = jax.ShapeDtypeStruct((context, 2 * head_dim), jnp.bfloat16)
    return pl.pallas_call(
        functools.partial(assemble_kernel, by_owner),
        out_shape=(wide, wide),
        in_specs=[SMEM, VMEM, VMEM] + [HBM] * len(sources),
        out_specs=(VMEM, VMEM),
        scratch_shapes=[
            pltpu.SMEM((request_docs.shape[0],), jnp.int32),
            pltpu.SemaphoreType.DMA((2,)),
        ],
        compiler_params=pltpu.CompilerParams(vmem_limit_bytes=32 * 1024 * 1024),
        cost_estimate=pl.CostEstimate(flops=0, bytes_accessed=16 * 1024 * 1024, transcendentals=0),
        name="assemble",
    )(request_docs, held, spare, *sources)


def plan_kernel(
    capacity, slots, request_docs, doc_lengths, rows, held, spare, key_bias, row_place, key_place, slot_row, counts
):
    me = lax.axis_index("seq")
    per_doc, _, doc_count = rows.shape
    doc_len = held.shape[0] // doc_count
    row_count = row_place.shape[0]
    docs = lax.broadcasted_iota(jnp.int32, (1, doc_count), 1)
    lengths = jnp.zeros((1, doc_count), jnp.int32)
    places = jnp.zeros((1, doc_count), jnp.int32)
    for o in range(counts.shape[0]):
        counts[o] = 0
    for j in range(doc_count):
        doc = request_docs[me, j]
        owner = lax.div(doc, slots)
        rank = counts[owner]
        counts[owner] = rank + 1
        lengths = jnp.where(docs == j, doc_lengths[doc], lengths)
        places = jnp.where(docs == j, owner * capacity + rank, places)
    slot = lax.broadcasted_iota(jnp.int32, (doc_len, doc_count), 0)
    used = slot < lengths
    for i in range(per_doc):
        used &= slot != rows[i]
    used = used.astype(jnp.float32)
    first = jnp.min(jnp.where(used > 0, slot, doc_len), axis=0, keepdims=True)
    firsts = (slot == first).astype(jnp.bfloat16)
    eye = lax.broadcasted_iota(jnp.int32, (doc_count, doc_count), 0) == docs
    across = (((1,), (1,)), ((), ()))

    def turned(columns):
        return lax.dot_general(
            eye.astype(jnp.bfloat16), columns, across, preferred_element_type=jnp.float32
        )

    bias = jnp.where(turned(used.astype(jnp.bfloat16)) > 0, 0.0, MASKED)
    firsts = turned(firsts)
    doc = lax.broadcasted_iota(jnp.int32, (doc_count, 1), 0)
    for j in range(doc_count):
        part = slice(j * doc_len, (j + 1) * doc_len)
        held[part, :] = jnp.broadcast_to(used[:, j : j + 1], (doc_len, held.shape[1])).astype(
            held.dtype
        )
        key_bias[:, part] = bias[j : j + 1, :]
        spare[:, part] = jnp.where(doc == j, firsts, 0.0).astype(spare.dtype)
    row = lax.broadcasted_iota(jnp.int32, (row_count, doc_count), 0)
    start = per_doc * lax.broadcasted_iota(jnp.int32, (row_count, doc_count), 1)
    of_doc = (row >= start) & (row < start + per_doc)
    nth = jnp.sum(jnp.where(of_doc, row - start, 0), axis=1, keepdims=True)
    chosen = jnp.zeros((row_count, doc_count), jnp.int32)
    for i in range(per_doc):
        chosen = jnp.where(nth == i, rows[i], chosen)
    chosen = jnp.where(of_doc, chosen + doc_len * docs, 0)
    column = jnp.sum(chosen, axis=1, keepdims=True)
    goes = nth + per_doc * jnp.sum(jnp.where(of_doc, places, 0), axis=1, keepdims=True)
    row_place[...] = column
    square = (row_count, row_count)
    same = lax.broadcasted_iota(jnp.int32, square, 0) == lax.broadcasted_iota(jnp.int32, square, 1)
    key_place[...] = jnp.sum(jnp.where(same, column, 0), axis=0, keepdims=True)
    slot_row[...] = jnp.sum(jnp.where(same, goes, 0), axis=0, keepdims=True)


def plan(request_docs, doc_lengths, recompute_rows, slots, head_dim, doc_len):
    _, doc_count, per_doc = recompute_rows.shape
    rows = doc_count * per_doc
    context = doc_count * doc_len
    shapes = (
        ((context, head_dim), jnp.bfloat16),
        ((doc_count, context), jnp.bfloat16),
        ((1, context), jnp.float32),
        ((rows, 1), jnp.int32),
        ((1, rows), jnp.int32),
        ((1, rows), jnp.int32),
    )
    return pl.pallas_call(
        functools.partial(plan_kernel, slots // 2, slots),
        out_shape=tuple(jax.ShapeDtypeStruct(*one) for one in shapes),
        in_specs=[SMEM, SMEM, VMEM],
        out_specs=(VMEM,) * len(shapes),
        scratch_shapes=[pltpu.SMEM((request_docs.shape[0],), jnp.int32)],
        compiler_params=pltpu.CompilerParams(vmem_limit_bytes=16 * 1024 * 1024),
        name="plan",
    )(request_docs, doc_lengths, jnp.transpose(recompute_rows, (2, 0, 1)))


def finish_kernel(own, arrived, slot_row, fresh, outgoing, held, sem):
    fetch = pltpu.make_async_copy(own, held, sem)
    fetch.start()
    fetch.wait()
    total = (held[...] + arrived[...].astype(jnp.float32)).astype(jnp.bfloat16)
    fresh[...] = total
    slots = lax.broadcasted_iota(jnp.int32, (outgoing.shape[0], 1), 0)
    pick = (slots == slot_row[...]).astype(jnp.bfloat16)
    outgoing[...] = jnp.dot(pick, total, preferred_element_type=jnp.float32).astype(jnp.bfloat16)


def finish(own, arrived, slot_row, slots):
    shapes = (own.shape, (slots, own.shape[1]))
    return pl.pallas_call(
        finish_kernel,
        out_shape=tuple(jax.ShapeDtypeStruct(one, jnp.bfloat16) for one in shapes),
        in_specs=[ANY, VMEM, VMEM],
        out_specs=(VMEM, VMEM),
        scratch_shapes=[pltpu.VMEM(own.shape, jnp.float32), pltpu.SemaphoreType.DMA],
        compiler_params=pltpu.CompilerParams(vmem_limit_bytes=16 * 1024 * 1024),
        name="finish",
    )(own, arrived, slot_row)


def attend_kernel(queries, fresh, keys, values, key_bias, row_place, key_place, mixed):
    row_count = queries.shape[1]
    head_dim = fresh.shape[1] // 2
    heads = queries.shape[2] // head_dim
    step = 4
    blocks = key_bias.shape[1] // (step * 128)
    block_rows = row_count // blocks
    block_keys = key_bias.shape[1] // blocks
    scale = math.log2(math.e) / math.sqrt(head_dim)
    fresh_k = jnp.concatenate([fresh[:, :head_dim]] * 2, axis=1)
    fresh_v = jnp.concatenate([fresh[:, head_dim:], jnp.ones_like(fresh[:, head_dim:])], axis=1)
    slot_place = lax.broadcasted_iota(jnp.int32, (1, block_keys), 1)
    contract_last = (((1,), (1,)), ((), ()))
    for b in range(blocks):
        rows = slice(b * block_rows, (b + 1) * block_rows)
        q = jnp.concatenate(
            [queries[0, rows, h * head_dim : (h + 1) * head_dim] for h in range(heads)], axis=0
        )
        q = q.astype(jnp.float32) * scale
        high = q.astype(jnp.bfloat16)
        low = (q - high.astype(jnp.float32)).astype(jnp.bfloat16)
        q = jnp.concatenate([high, low], axis=1)
        own_place = row_place[rows, :]

        def scores(some_keys):
            return lax.dot_general(
                q, some_keys, contract_last, preferred_element_type=jnp.float32
            )

        def masked(some_keys, allowed):
            shape = (heads, block_rows, some_keys.shape[0])
            kept = jnp.where(allowed[None], scores(some_keys).reshape(shape), MASKED)
            return kept.reshape(heads * block_rows, some_keys.shape[0])

        chunks, sides = [], []
        for c in range(b):
            part = slice(c * block_keys, (c + 1) * block_keys)
            chunks.append(scores(keys[part, :]))
            sides.append(values[part, :])
        part = slice(b * block_keys, (b + 1) * block_keys)
        allowed = (slot_place + b * block_keys <= own_place) & (key_bias[:, part] == 0)
        chunks.append(masked(keys[part, :], allowed))
        sides.append(values[part, :])
        chunks.append(masked(fresh_k, key_place[...] <= own_place))
        sides.append(fresh_v)
        row_max = functools.reduce(
            jnp.maximum, [jnp.max(one, axis=1, keepdims=True) for one in chunks]
        )
        total = jnp.zeros((heads * block_rows, 2 * head_dim), jnp.float32)
        for one, side in zip(chunks, sides):
            powers = jnp.exp2(one - row_max).astype(jnp.bfloat16)
            total += jnp.dot(powers, side, preferred_element_type=jnp.float32)
        result = (total[:, :head_dim] / total[:, head_dim:]).astype(mixed.dtype)
        for h in range(heads):
            mixed[0, rows, h * head_dim : (h + 1) * head_dim] = result[
                h * block_rows : (h + 1) * block_rows
            ]


def attend(queries, fresh, keys, values, key_bias, row_place, key_place):
    return pl.pallas_call(
        attend_kernel,
        out_shape=jax.ShapeDtypeStruct(queries.shape, jnp.bfloat16),
        in_specs=[VMEM] * 7,
        out_specs=VMEM,
        compiler_params=pltpu.CompilerParams(vmem_limit_bytes=32 * 1024 * 1024),
        cost_estimate=pl.CostEstimate(flops=1, bytes_accessed=1, transcendentals=0),
        name="attend",
    )(queries, fresh, keys, values, key_bias, row_place, key_place)


def shards(
    pairs,
    hidden,
    queries,
    w_key,
    w_value,
    store_keys,
    store_values,
    request_docs,
    doc_lengths,
    recompute_rows,
):
    seq_count = lax.axis_size("seq")
    slot_count, doc_len, head_dim = store_keys.shape
    capacity = slot_count // 2
    per_doc = recompute_rows.shape[2]

    if pairs:
        def swap(array, axis, apart):
            count = lax.axis_size(axis)
            return lax.ppermute(array, axis, [(i, i ^ apart) for i in range(count)])

        w_send, h_send = pick_sent(hidden, w_key, w_value)
        w_far = swap(w_send, "seq", 2)
        h_mine = swap(h_send, "seq", 1)
        docs = pick_docs(request_docs, store_keys, store_values, False)
        *docs, w_far = gate((*docs, w_far))
        w_swapped = swap(w_far, "groups", 1)
        docs = [swap(doc, "seq", k + 1) for k, doc in enumerate(docs)]
        h_chip = swap(h_mine, "tp", 2)
        quarters = (h_mine, swap(h_mine, "tp", 1), h_chip, swap(h_chip, "tp", 1))
        own, part = project(hidden, w_key, w_value, w_far, w_swapped, quarters)
        arrived = swap(part, "seq", 1)
        sources = (store_keys, store_values, *docs)
    else:
        (docs,) = pick_docs(request_docs, store_keys, store_values, True)
        sources = (lax.all_to_all(docs, "seq", split_axis=0, concat_axis=0, tiled=True),)
        weights = lax.all_gather(
            jnp.concatenate([w_key, w_value], axis=1), "seq", axis=0, tiled=True
        )
        own = jnp.dot(hidden[0], weights, preferred_element_type=jnp.float32)
        arrived = jnp.zeros(own.shape, jnp.bfloat16)

    held, spare, key_bias, row_place, key_place, slot_row = plan(
        request_docs, doc_lengths, recompute_rows, slot_count, head_dim, doc_len
    )
    if pairs:
        sources = tuple(in_hbm(one) for one in sources)
    keys, values = assemble(request_docs, held, spare, sources, not pairs)
    fresh, outgoing = finish(own, arrived, slot_row, seq_count * capacity * per_doc)
    mixed = attend(queries, fresh, keys, values, key_bias, row_place, key_place)

    outgoing = outgoing.reshape(seq_count, capacity * per_doc, 2 * head_dim)
    returned = lax.all_to_all(outgoing, "seq", split_axis=0, concat_axis=0, tiled=True)
    returned = returned.reshape(seq_count, capacity, per_doc, 2, head_dim)
    return (mixed, returned[None])


def solution(mesh):
    pairs = mesh.shape["seq"] == 4 and mesh.shape["groups"] == 2 and mesh.shape["tp"] == 4
    return jax.shard_map(
        functools.partial(shards, pairs),
        mesh=mesh,
        in_specs=(
            P(("groups", "seq"), None, None),
            P(("groups", "seq"), None, "tp"),
            P("seq", "tp"),
            P("seq", "tp"),
            P(("groups", "seq"), None, "tp"),
            P(("groups", "seq"), None, "tp"),
            P("groups", None),
            P("groups"),
            P(("groups", "seq"), None, None),
        ),
        out_specs=(
            P(("groups", "seq"), None, "tp"),
            P(("groups", "seq"), None, None, None, None, "tp"),
        ),
        check_vma=False,
    )
```

```python
import functools
import math

import jax
import jax.numpy as jnp
from jax import lax
from jax.experimental import pallas as pl
from jax.experimental.pallas import tpu as pltpu
from jax.sharding import PartitionSpec as P

ANY = pl.BlockSpec(memory_space=pl.ANY)
HBM = pl.BlockSpec(memory_space=pltpu.HBM)
SMEM = pl.BlockSpec(memory_space=pltpu.SMEM)
VMEM = pl.BlockSpec(memory_space=pltpu.VMEM)
MASKED = -1e30


def in_hbm(array):
    return pltpu.with_memory_space_constraint(array, pltpu.HBM)


def send_kernel(hidden, w_key, w_value, w_out, h_near, h_far, w_held, h_held, w_sems, h_sems):
    group = lax.axis_index("groups")
    me = lax.axis_index("seq")
    quarter = lax.axis_index("tp")
    pieces, piece = w_held.shape[:2]
    rows, depth = h_near.shape

    def fetch(i, weight):
        source = weight.at[pl.ds(i * piece, piece)]
        return pltpu.make_async_copy(source, w_held.at[i], w_sems.at[0, i])

    for chosen, weight in ((0, w_key), (1, w_value)):

        @pl.when(group == chosen)
        def _():
            for i in range(pieces):
                fetch(i, weight).start()

    first = me + 1 - 2 * lax.rem(me, 2)
    stores = []
    h_fetches = []
    for i, block in enumerate((first, lax.rem(first + 2, 4))):
        source = hidden.at[
            0,
            pl.ds(pl.multiple_of(quarter * rows, rows), rows),
            pl.ds(pl.multiple_of(block * depth, depth), depth),
        ]
        h_fetches.append(pltpu.make_async_copy(source, h_held.at[i], h_sems.at[0, i]))
        h_fetches[-1].start()
    for i in range(pieces):
        fetch(i, w_key).wait()
        target = w_out.at[pl.ds(i * piece, piece)]
        stores.append(pltpu.make_async_copy(w_held.at[i], target, w_sems.at[1, i]))
        stores[-1].start()
    for i, one in enumerate(h_fetches):
        one.wait()
        target = (h_near, h_far)[i]
        stores.append(pltpu.make_async_copy(h_held.at[i], target, h_sems.at[1, i]))
        stores[-1].start()
    for store in stores:
        store.wait()


def pick_sent(hidden, w_key, w_value):
    depth, width = w_key.shape
    pieces = 4
    h_shape = (hidden.shape[1] // 4, depth)
    return pl.pallas_call(
        send_kernel,
        out_shape=(
            jax.ShapeDtypeStruct(w_key.shape, jnp.bfloat16),
            jax.ShapeDtypeStruct(h_shape, jnp.bfloat16),
            jax.ShapeDtypeStruct(h_shape, jnp.bfloat16),
        ),
        in_specs=[ANY] * 3,
        out_specs=(ANY,) * 3,
        scratch_shapes=[
            pltpu.VMEM((pieces, depth // pieces, width), jnp.bfloat16),
            pltpu.VMEM((2,) + h_shape, jnp.bfloat16),
            pltpu.SemaphoreType.DMA((2, pieces)),
            pltpu.SemaphoreType.DMA((2, 2)),
        ],
        name="pick_sent",
    )(hidden, w_key, w_value)


def gate_kernel(*refs):
    pass


def gate(arrays, first=()):
    return pl.pallas_call(
        gate_kernel,
        out_shape=tuple(jax.ShapeDtypeStruct(one.shape, one.dtype) for one in arrays),
        in_specs=[ANY] * (len(arrays) + len(first)),
        out_specs=(ANY,) * len(arrays),
        input_output_aliases={i: i for i in range(len(arrays))},
        compiler_params=pltpu.CompilerParams(vmem_limit_bytes=1024 * 1024),
        name="gate",
    )(*(in_hbm(one) for one in arrays), *first)


def docs_kernel(by_owner, request_docs, store_keys, store_values, *rest):
    *outs, picks, sems = rest
    me = lax.axis_index("seq")
    requests, doc_count = request_docs.shape
    slots = store_keys.shape[0]
    capacity = slots // 2

    def one_request(r, carry):
        for c in range(capacity):
            picks[r, c] = 0

        def one_doc(j, count):
            doc = request_docs[r, j]
            mine = lax.div(doc, slots) == me

            @pl.when(mine)
            def _():
                picks[r, jnp.minimum(count, capacity - 1)] = lax.rem(doc, slots)

            return count + mine.astype(jnp.int32)

        lax.fori_loop(0, doc_count, one_doc, jnp.int32(0), unroll=True)
        return carry

    lax.fori_loop(0, requests, one_request, 0)

    def send(r, out, sem):
        for c in range(capacity):
            slot = picks[r, c]
            pltpu.make_async_copy(store_keys.at[slot], out.at[c, 0], sem).start()
            pltpu.make_async_copy(store_values.at[slot], out.at[c, 1], sem).start()

    if by_owner:

        def one_send(r, carry):
            send(r, outs[0].at[r], sems.at[0])
            return carry

        lax.fori_loop(0, requests, one_send, 0)
    else:
        for i, out in enumerate(outs):
            send(lax.bitwise_xor(me, i + 1), out, sems.at[i])
    for i, out in enumerate(outs):
        pltpu.make_async_copy(out, out, sems.at[i]).wait()


def pick_docs(request_docs, store_keys, store_values, by_owner):
    requests = request_docs.shape[0]
    capacity = store_keys.shape[0] // 2
    one = (capacity, 2) + store_keys.shape[1:]
    shapes = ((requests,) + one,) if by_owner else (one,) * (requests - 1)
    return pl.pallas_call(
        functools.partial(docs_kernel, by_owner),
        out_shape=tuple(jax.ShapeDtypeStruct(one, jnp.bfloat16) for one in shapes),
        in_specs=[SMEM, ANY, ANY],
        out_specs=(VMEM,) * len(shapes),
        scratch_shapes=[
            pltpu.SMEM((requests, capacity), jnp.int32),
            pltpu.SemaphoreType.DMA((len(shapes),)),
        ],
        name="pick_docs",
    )(request_docs, store_keys, store_values)


def lay_rows(hidden, quarters, block, depth, h, copy):
    mine = lax.axis_index("tp")
    rows = hidden.shape[1]
    piece = rows // len(quarters)
    start = pl.multiple_of(block * depth, depth)
    copy(hidden.at[0, :, pl.ds(start, depth)], h.at[pl.ds(0, rows)])
    for k, quarter in enumerate(quarters):
        start = pl.multiple_of(rows + lax.bitwise_xor(mine, k) * piece, piece)
        copy(quarter, h.at[pl.ds(start, piece)])


def near_kernel(hidden, w_key, w_value, *rest):
    *quarters, total, w, h, sems = rest
    depth, width = w_key.shape
    copies = []

    def copy(source, target):
        copies.append(pltpu.make_async_copy(source, target, sems.at[len(copies)]))
        copies[-1].start()

    for i, held in enumerate((w_key, w_value)):
        copy(held, w.at[:, pl.ds(i * width, width)])
    lay_rows(hidden, quarters, lax.axis_index("seq"), depth, h, copy)
    for one in copies:
        one.wait()
    total[...] = jnp.dot(h[...], w[...], preferred_element_type=jnp.float32)


def far_kernel(hidden, w_far, w_swapped, near, *rest):
    *quarters, own, part, w, h, sems, held_own, own_sem = rest
    group = lax.axis_index("groups")
    depth, width = w_far.shape
    rows = hidden.shape[1]
    copies = []

    def copy(source, target):
        copies.append(pltpu.make_async_copy(source, target, sems.at[len(copies)]))
        copies[-1].start()

    for held, place in ((w_far, group), (w_swapped, 1 - group)):
        copy(held, w.at[:, pl.ds(pl.multiple_of(place * width, width), width)])
    lay_rows(hidden, quarters, lax.rem(lax.axis_index("seq") + 2, 4), depth, h, copy)
    for one in copies:
        one.wait()
    total = near[...] + jnp.dot(h[...], w[...], preferred_element_type=jnp.float32)
    held_own[...] = total[:rows]
    store = pltpu.make_async_copy(held_own, own, own_sem)
    store.start()
    part[...] = total[rows:].astype(part.dtype)
    store.wait()


def project(hidden, w_key, w_value, w_far, w_swapped, quarters, far_quarters):
    depth, width = w_key.shape
    rows = hidden.shape[1]
    scratch = [
        pltpu.VMEM((depth, 2 * width), jnp.bfloat16),
        pltpu.VMEM((2 * rows, depth), jnp.bfloat16),
        pltpu.SemaphoreType.DMA((3 + len(quarters),)),
    ]
    settings = dict(
        compiler_params=pltpu.CompilerParams(vmem_limit_bytes=16 * 1024 * 1024),
        cost_estimate=pl.CostEstimate(flops=1, bytes_accessed=1, transcendentals=0),
    )
    near = pl.pallas_call(
        near_kernel,
        out_shape=jax.ShapeDtypeStruct((2 * rows, 2 * width), jnp.float32),
        in_specs=[ANY] * (3 + len(quarters)),
        out_specs=VMEM,
        scratch_shapes=scratch,
        name="project_near",
        **settings,
    )(hidden, in_hbm(w_key), in_hbm(w_value), *quarters)
    return pl.pallas_call(
        far_kernel,
        out_shape=(
            jax.ShapeDtypeStruct((rows, 2 * width), jnp.float32),
            jax.ShapeDtypeStruct((rows, 2 * width), jnp.bfloat16),
        ),
        in_specs=[ANY] * 3 + [VMEM] + [ANY] * len(quarters),
        out_specs=(ANY, VMEM),
        scratch_shapes=scratch
        + [pltpu.VMEM((rows, 2 * width), jnp.float32), pltpu.SemaphoreType.DMA],
        name="project_far",
        **settings,
    )(hidden, w_far, w_swapped, near, *far_quarters)


def plan_kernel(
    capacity, slots, request_docs, doc_lengths, rows, held, spare, key_bias, row_place, key_place, slot_row, counts
):
    me = lax.axis_index("seq")
    per_doc, _, doc_count = rows.shape
    doc_len = held.shape[0] // doc_count
    row_count = row_place.shape[0]
    docs = lax.broadcasted_iota(jnp.int32, (1, doc_count), 1)
    lengths = jnp.zeros((1, doc_count), jnp.int32)
    places = jnp.zeros((1, doc_count), jnp.int32)
    for o in range(counts.shape[0]):
        counts[o] = 0
    for j in range(doc_count):
        doc = request_docs[me, j]
        owner = lax.div(doc, slots)
        rank = counts[owner]
        counts[owner] = rank + 1
        lengths = jnp.where(docs == j, doc_lengths[doc], lengths)
        places = jnp.where(docs == j, owner * capacity + rank, places)
    slot = lax.broadcasted_iota(jnp.int32, (doc_len, doc_count), 0)
    used = slot < lengths
    for i in range(per_doc):
        used &= slot != rows[i]
    used = used.astype(jnp.float32)
    first = jnp.min(jnp.where(used > 0, slot, doc_len), axis=0, keepdims=True)
    firsts = (slot == first).astype(jnp.bfloat16)
    eye = lax.broadcasted_iota(jnp.int32, (doc_count, doc_count), 0) == docs
    across = (((1,), (1,)), ((), ()))

    def turned(columns):
        return lax.dot_general(
            eye.astype(jnp.bfloat16), columns, across, preferred_element_type=jnp.float32
        )

    bias = jnp.where(turned(used.astype(jnp.bfloat16)) > 0, 0.0, MASKED)
    firsts = turned(firsts)
    doc = lax.broadcasted_iota(jnp.int32, (doc_count, 1), 0)
    for j in range(doc_count):
        part = slice(j * doc_len, (j + 1) * doc_len)
        held[part, :] = jnp.broadcast_to(used[:, j : j + 1], (doc_len, held.shape[1])).astype(
            held.dtype
        )
        key_bias[:, part] = bias[j : j + 1, :]
        spare[:, part] = jnp.where(doc == j, firsts, 0.0).astype(spare.dtype)
    row = lax.broadcasted_iota(jnp.int32, (row_count, doc_count), 0)
    start = per_doc * lax.broadcasted_iota(jnp.int32, (row_count, doc_count), 1)
    of_doc = (row >= start) & (row < start + per_doc)
    nth = jnp.sum(jnp.where(of_doc, row - start, 0), axis=1, keepdims=True)
    chosen = jnp.zeros((row_count, doc_count), jnp.int32)
    for i in range(per_doc):
        chosen = jnp.where(nth == i, rows[i], chosen)
    chosen = jnp.where(of_doc, chosen + doc_len * docs, 0)
    column = jnp.sum(chosen, axis=1, keepdims=True)
    goes = nth + per_doc * jnp.sum(jnp.where(of_doc, places, 0), axis=1, keepdims=True)
    row_place[...] = column
    square = (row_count, row_count)
    same = lax.broadcasted_iota(jnp.int32, square, 0) == lax.broadcasted_iota(jnp.int32, square, 1)
    key_place[...] = jnp.sum(jnp.where(same, column, 0), axis=0, keepdims=True)
    slot_row[...] = jnp.sum(jnp.where(same, goes, 0), axis=0, keepdims=True)


def plan(request_docs, doc_lengths, recompute_rows, slots, head_dim, doc_len):
    _, doc_count, per_doc = recompute_rows.shape
    rows = doc_count * per_doc
    context = doc_count * doc_len
    shapes = (
        ((context, head_dim), jnp.bfloat16),
        ((doc_count, context), jnp.bfloat16),
        ((1, context), jnp.float32),
        ((rows, 1), jnp.int32),
        ((1, rows), jnp.int32),
        ((1, rows), jnp.int32),
    )
    return pl.pallas_call(
        functools.partial(plan_kernel, slots // 2, slots),
        out_shape=tuple(jax.ShapeDtypeStruct(*one) for one in shapes),
        in_specs=[SMEM, SMEM, VMEM],
        out_specs=(VMEM,) * len(shapes),
        scratch_shapes=[pltpu.SMEM((request_docs.shape[0],), jnp.int32)],
        compiler_params=pltpu.CompilerParams(vmem_limit_bytes=16 * 1024 * 1024),
        name="plan",
    )(request_docs, doc_lengths, jnp.transpose(recompute_rows, (2, 0, 1)))


def finish_kernel(own, arrived, slot_row, fresh, outgoing, held, sem):
    fetch = pltpu.make_async_copy(own, held, sem)
    fetch.start()
    fetch.wait()
    total = (held[...] + arrived[...].astype(jnp.float32)).astype(jnp.bfloat16)
    fresh[...] = total
    slots = lax.broadcasted_iota(jnp.int32, (outgoing.shape[0], 1), 0)
    pick = (slots == slot_row[...]).astype(jnp.bfloat16)
    outgoing[...] = jnp.dot(pick, total, preferred_element_type=jnp.float32).astype(jnp.bfloat16)


def finish(own, arrived, slot_row, slots):
    shapes = (own.shape, (slots, own.shape[1]))
    return pl.pallas_call(
        finish_kernel,
        out_shape=tuple(jax.ShapeDtypeStruct(one, jnp.bfloat16) for one in shapes),
        in_specs=[ANY, VMEM, VMEM],
        out_specs=(VMEM, VMEM),
        scratch_shapes=[pltpu.VMEM(own.shape, jnp.float32), pltpu.SemaphoreType.DMA],
        compiler_params=pltpu.CompilerParams(vmem_limit_bytes=16 * 1024 * 1024),
        name="finish",
    )(own, arrived, slot_row)


def attend_kernel(
    by_owner, request_docs, queries, fresh, held, spare, key_bias, row_place, key_place, *rest
):
    sources, (mixed, raw, q, keys, values, counts, sems, q_sem) = rest[:-8], rest[-8:]
    me = lax.axis_index("seq")
    doc_count = request_docs.shape[1]
    head_dim = keys.shape[1] // 2
    doc_len = keys.shape[0] // doc_count
    owners = request_docs.shape[0]
    slots = sources[0].shape[0] if not by_owner else 2 * sources[0].shape[1]
    step = doc_count // sems.shape[1]
    blocks = doc_count // step
    block_rows = mixed.shape[1] // blocks
    block_keys = step * doc_len
    heads = mixed.shape[2] // head_dim
    left = pl.ds(0, head_dim)

    fetch_queries = pltpu.make_async_copy(queries, raw, q_sem)
    fetch_queries.start()
    for o in range(owners):
        counts[o] = 0

    def one_doc(j, carry):
        doc = request_docs[me, j]
        owner = lax.div(doc, slots)
        rank = counts[owner]
        counts[owner] = rank + 1
        place = pl.ds(pl.multiple_of(j * doc_len, doc_len), doc_len)
        block = lax.div(j, step)

        def fetch(key_source, value_source):
            pltpu.make_async_copy(key_source, keys.at[place, left], sems.at[0, block]).start()
            pltpu.make_async_copy(value_source, values.at[place, left], sems.at[1, block]).start()

        if by_owner:
            fetch(sources[0].at[owner, rank, 0], sources[0].at[owner, rank, 1])
        else:
            away = lax.bitwise_xor(me, owner)

            @pl.when(away == 0)
            def _():
                slot = lax.rem(doc, slots)
                fetch(sources[0].at[slot], sources[1].at[slot])

            for k in range(1, owners):

                @pl.when(away == k)
                def _():
                    fetch(sources[1 + k].at[rank, 0], sources[1 + k].at[rank, 1])

        return carry

    lax.fori_loop(0, doc_count, one_doc, 0)

    fetch_queries.wait()
    scale = math.log2(math.e) / math.sqrt(head_dim)
    for b in range(blocks):
        for h in range(heads):
            here = raw[0, b * block_rows : (b + 1) * block_rows, h * head_dim : (h + 1) * head_dim]
            here = here.astype(jnp.float32) * scale
            high = here.astype(jnp.bfloat16)
            place = slice((b * heads + h) * block_rows, (b * heads + h + 1) * block_rows)
            q[place, :head_dim] = high
            q[place, head_dim:] = (here - high.astype(jnp.float32)).astype(jnp.bfloat16)

    for b in range(blocks):
        block = pl.ds(b * block_keys, block_keys)
        for i, context in enumerate((keys, values)):
            pltpu.make_async_copy(
                context.at[block, left], context.at[block, left], sems.at[i, b]
            ).wait()
    for b in range(blocks):
        block = slice(b * block_keys, (b + 1) * block_keys)
        spares = jnp.dot(
            spare[:, block], keys[block, :head_dim], preferred_element_type=jnp.float32
        ).astype(jnp.bfloat16)
        for j in range(b * step, (b + 1) * step):
            place = slice(j * doc_len, (j + 1) * doc_len)
            used = held[place, :]
            key = jnp.where(used > 0, keys[place, :head_dim], spares[j : j + 1, :])
            keys[place, :head_dim] = key
            keys[place, head_dim:] = key
            values[place, :head_dim] = values[place, :head_dim] * used
            values[place, head_dim:] = used

    fresh_k = jnp.concatenate([fresh[:, :head_dim]] * 2, axis=1)
    fresh_v = jnp.concatenate([fresh[:, head_dim:], jnp.ones_like(fresh[:, head_dim:])], axis=1)
    slot_place = lax.broadcasted_iota(jnp.int32, (1, block_keys), 1)
    contract_last = (((1,), (1,)), ((), ()))
    for b in range(blocks):
        rows = slice(b * block_rows, (b + 1) * block_rows)
        q_here = q[b * heads * block_rows : (b + 1) * heads * block_rows, :]
        own_place = row_place[rows, :]

        def scores(some_keys):
            return lax.dot_general(
                q_here, some_keys, contract_last, preferred_element_type=jnp.float32
            )

        def masked(some_keys, allowed):
            shape = (heads, block_rows, some_keys.shape[0])
            kept = jnp.where(allowed[None], scores(some_keys).reshape(shape), MASKED)
            return kept.reshape(heads * block_rows, some_keys.shape[0])

        chunks, sides = [], []
        for c in range(b):
            part = slice(c * block_keys, (c + 1) * block_keys)
            chunks.append(scores(keys[part, :]))
            sides.append(values[part, :])
        part = slice(b * block_keys, (b + 1) * block_keys)
        allowed = (slot_place + b * block_keys <= own_place) & (key_bias[:, part] == 0)
        chunks.append(masked(keys[part, :], allowed))
        sides.append(values[part, :])
        chunks.append(masked(fresh_k, key_place[...] <= own_place))
        sides.append(fresh_v)
        row_max = functools.reduce(
            jnp.maximum, [jnp.max(one, axis=1, keepdims=True) for one in chunks]
        )
        total = jnp.zeros((heads * block_rows, 2 * head_dim), jnp.float32)
        for one, side in zip(chunks, sides):
            powers = jnp.exp2(one - row_max).astype(jnp.bfloat16)
            total += jnp.dot(powers, side, preferred_element_type=jnp.float32)
        result = (total[:, :head_dim] / total[:, head_dim:]).astype(mixed.dtype)
        for h in range(heads):
            mixed[0, rows, h * head_dim : (h + 1) * head_dim] = result[
                h * block_rows : (h + 1) * block_rows
            ]


def attend(request_docs, queries, fresh, held, spare, key_bias, row_place, key_place, sources, by_owner):
    context, head_dim = held.shape
    rows = queries.shape[1] * queries.shape[2] // head_dim
    return pl.pallas_call(
        functools.partial(attend_kernel, by_owner),
        out_shape=jax.ShapeDtypeStruct(queries.shape, jnp.bfloat16),
        in_specs=[SMEM, ANY] + [VMEM] * 6 + [ANY] * len(sources),
        out_specs=VMEM,
        scratch_shapes=[
            pltpu.VMEM(queries.shape, jnp.bfloat16),
            pltpu.VMEM((rows, 2 * head_dim), jnp.bfloat16),
            pltpu.VMEM((context, 2 * head_dim), jnp.bfloat16),
            pltpu.VMEM((context, 2 * head_dim), jnp.bfloat16),
            pltpu.SMEM((request_docs.shape[0],), jnp.int32),
            pltpu.SemaphoreType.DMA((2, 4)),
            pltpu.SemaphoreType.DMA,
        ],
        compiler_params=pltpu.CompilerParams(vmem_limit_bytes=32 * 1024 * 1024),
        name="attend",
    )(
        request_docs,
        in_hbm(queries),
        fresh,
        held,
        spare,
        key_bias,
        row_place,
        key_place,
        *(in_hbm(one) for one in sources),
    )


def shards(
    pairs,
    hidden,
    queries,
    w_key,
    w_value,
    store_keys,
    store_values,
    request_docs,
    doc_lengths,
    recompute_rows,
):
    seq_count = lax.axis_size("seq")
    slot_count, doc_len, head_dim = store_keys.shape
    capacity = slot_count // 2
    per_doc = recompute_rows.shape[2]

    if pairs:
        def swap(array, axis, apart):
            count = lax.axis_size(axis)
            return lax.ppermute(array, axis, [(i, i ^ apart) for i in range(count)])

        w_send, *h_send = pick_sent(hidden, w_key, w_value)
        w_far = swap(w_send, "seq", 2)
        doc_1, doc_2, doc_3 = pick_docs(request_docs, store_keys, store_values, False)

        def spread(sent):
            mine = swap(sent, "seq", 1)
            chip = swap(mine, "tp", 2)
            return mine, swap(mine, "tp", 1), chip, swap(chip, "tp", 1)

        quarters = tuple(spread(one) for one in h_send)
        (doc_1,) = gate((doc_1,), (quarters[1][0],))
        doc_1 = swap(doc_1, "seq", 1)
        doc_2, doc_3, w_far = gate((doc_2, doc_3, w_far), (doc_1, *quarters[0], *quarters[1]))
        docs = (doc_1, swap(doc_2, "seq", 2), swap(doc_3, "seq", 3))
        w_swapped = swap(w_far, "groups", 1)
        own, part = project(hidden, w_key, w_value, w_far, w_swapped, *quarters)
        arrived = swap(part, "seq", 1)
        sources = (store_keys, store_values, *docs)
    else:
        (docs,) = pick_docs(request_docs, store_keys, store_values, True)
        sources = (lax.all_to_all(docs, "seq", split_axis=0, concat_axis=0, tiled=True),)
        weights = lax.all_gather(
            jnp.concatenate([w_key, w_value], axis=1), "seq", axis=0, tiled=True
        )
        own = jnp.dot(hidden[0], weights, preferred_element_type=jnp.float32)
        arrived = jnp.zeros(own.shape, jnp.bfloat16)

    held, spare, key_bias, row_place, key_place, slot_row = plan(
        request_docs, doc_lengths, recompute_rows, slot_count, head_dim, doc_len
    )
    fresh, outgoing = finish(own, arrived, slot_row, seq_count * capacity * per_doc)
    mixed = attend(
        request_docs,
        queries,
        fresh,
        held,
        spare,
        key_bias,
        row_place,
        key_place,
        sources,
        not pairs,
    )

    outgoing = outgoing.reshape(seq_count, capacity * per_doc, 2 * head_dim)
    returned = lax.all_to_all(outgoing, "seq", split_axis=0, concat_axis=0, tiled=True)
    returned = returned.reshape(seq_count, capacity, per_doc, 2, head_dim)
    return (mixed, returned[None])


def solution(mesh):
    pairs = mesh.shape["seq"] == 4 and mesh.shape["groups"] == 2 and mesh.shape["tp"] == 4
    return jax.shard_map(
        functools.partial(shards, pairs),
        mesh=mesh,
        in_specs=(
            P(("groups", "seq"), None, None),
            P(("groups", "seq"), None, "tp"),
            P("seq", "tp"),
            P("seq", "tp"),
            P(("groups", "seq"), None, "tp"),
            P(("groups", "seq"), None, "tp"),
            P("groups", None),
            P("groups"),
            P(("groups", "seq"), None, None),
        ),
        out_specs=(
            P(("groups", "seq"), None, "tp"),
            P(("groups", "seq"), None, None, None, None, "tp"),
        ),
        check_vma=False,
    )
```

```python
import functools
import math

import jax
import jax.numpy as jnp
from jax import lax
from jax.experimental import pallas as pl
from jax.experimental.pallas import tpu as pltpu
from jax.sharding import PartitionSpec as P

ANY = pl.BlockSpec(memory_space=pl.ANY)
HBM = pl.BlockSpec(memory_space=pltpu.HBM)
SMEM = pl.BlockSpec(memory_space=pltpu.SMEM)
VMEM = pl.BlockSpec(memory_space=pltpu.VMEM)
MASKED = -1e30


def in_hbm(array):
    return pltpu.with_memory_space_constraint(array, pltpu.HBM)


def send_kernel(hidden, w_key, w_value, w_out, h_out, w_held, h_held, w_sems, h_sems):
    group = lax.axis_index("groups")
    me = lax.axis_index("seq")
    quarter = lax.axis_index("tp")
    pieces, piece = w_held.shape[:2]
    rows, depth = h_out.shape[1:]

    def fetch(i, weight):
        source = weight.at[pl.ds(i * piece, piece)]
        return pltpu.make_async_copy(source, w_held.at[i], w_sems.at[0, i])

    for chosen, weight in ((0, w_key), (1, w_value)):

        @pl.when(group == chosen)
        def _():
            for i in range(pieces):
                fetch(i, weight).start()

    first = me + 1 - 2 * lax.rem(me, 2)
    stores = []
    h_fetches = []
    for i, block in enumerate((first, lax.rem(first + 2, 4))):
        source = hidden.at[
            0,
            pl.ds(pl.multiple_of(quarter * rows, rows), rows),
            pl.ds(pl.multiple_of(block * depth, depth), depth),
        ]
        h_fetches.append(pltpu.make_async_copy(source, h_held.at[i], h_sems.at[0, i]))
        h_fetches[-1].start()
    for i in range(pieces):
        fetch(i, w_key).wait()
        target = w_out.at[pl.ds(i * piece, piece)]
        stores.append(pltpu.make_async_copy(w_held.at[i], target, w_sems.at[1, i]))
        stores[-1].start()
    for i, one in enumerate(h_fetches):
        one.wait()
        stores.append(pltpu.make_async_copy(h_held.at[i], h_out.at[i], h_sems.at[1, i]))
        stores[-1].start()
    for store in stores:
        store.wait()


def pick_sent(hidden, w_key, w_value):
    depth, width = w_key.shape
    pieces = 4
    h_shape = (2, hidden.shape[1] // 4, depth)
    return pl.pallas_call(
        send_kernel,
        out_shape=(
            jax.ShapeDtypeStruct(w_key.shape, jnp.bfloat16),
            jax.ShapeDtypeStruct(h_shape, jnp.bfloat16),
        ),
        in_specs=[ANY] * 3,
        out_specs=(ANY, ANY),
        scratch_shapes=[
            pltpu.VMEM((pieces, depth // pieces, width), jnp.bfloat16),
            pltpu.VMEM(h_shape, jnp.bfloat16),
            pltpu.SemaphoreType.DMA((2, pieces)),
            pltpu.SemaphoreType.DMA((2, 2)),
        ],
        name="pick_sent",
    )(hidden, w_key, w_value)


def gate_kernel(*refs):
    pass


def gate(arrays, first=()):
    return pl.pallas_call(
        gate_kernel,
        out_shape=tuple(jax.ShapeDtypeStruct(one.shape, one.dtype) for one in arrays),
        in_specs=[ANY] * (len(arrays) + len(first)),
        out_specs=(ANY,) * len(arrays),
        input_output_aliases={i: i for i in range(len(arrays))},
        compiler_params=pltpu.CompilerParams(vmem_limit_bytes=1024 * 1024),
        name="gate",
    )(*(in_hbm(one) for one in arrays), *first)


def docs_kernel(by_owner, request_docs, store_keys, store_values, *rest):
    *outs, picks, sems = rest
    me = lax.axis_index("seq")
    requests, doc_count = request_docs.shape
    slots = store_keys.shape[0]
    capacity = slots // 2

    def one_request(r, carry):
        for c in range(capacity):
            picks[r, c] = 0

        def one_doc(j, count):
            doc = request_docs[r, j]
            mine = lax.div(doc, slots) == me

            @pl.when(mine)
            def _():
                picks[r, jnp.minimum(count, capacity - 1)] = lax.rem(doc, slots)

            return count + mine.astype(jnp.int32)

        lax.fori_loop(0, doc_count, one_doc, jnp.int32(0), unroll=True)
        return carry

    lax.fori_loop(0, requests, one_request, 0)

    def send(r, out, sem):
        for c in range(capacity):
            slot = picks[r, c]
            pltpu.make_async_copy(store_keys.at[slot], out.at[c, 0], sem).start()
            pltpu.make_async_copy(store_values.at[slot], out.at[c, 1], sem).start()

    if by_owner:

        def one_send(r, carry):
            send(r, outs[0].at[r], sems.at[0])
            return carry

        lax.fori_loop(0, requests, one_send, 0)
    else:
        for i, out in enumerate(outs):
            send(lax.bitwise_xor(me, i + 1), out, sems.at[i])
    for i, out in enumerate(outs):
        pltpu.make_async_copy(out, out, sems.at[i]).wait()


def pick_docs(request_docs, store_keys, store_values, by_owner):
    requests = request_docs.shape[0]
    capacity = store_keys.shape[0] // 2
    one = (capacity, 2) + store_keys.shape[1:]
    shapes = ((requests,) + one,) if by_owner else (one,) * (requests - 1)
    return pl.pallas_call(
        functools.partial(docs_kernel, by_owner),
        out_shape=tuple(jax.ShapeDtypeStruct(one, jnp.bfloat16) for one in shapes),
        in_specs=[SMEM, ANY, ANY],
        out_specs=(VMEM,) * len(shapes),
        scratch_shapes=[
            pltpu.SMEM((requests, capacity), jnp.int32),
            pltpu.SemaphoreType.DMA((len(shapes),)),
        ],
        name="pick_docs",
    )(request_docs, store_keys, store_values)


def lay_rows(hidden, quarters, block, depth, h, copy):
    mine = lax.axis_index("tp")
    rows = hidden.shape[1]
    piece = rows // len(quarters)
    start = pl.multiple_of(block * depth, depth)
    copy(hidden.at[0, :, pl.ds(start, depth)], h.at[pl.ds(0, rows)])
    for k, quarter in enumerate(quarters):
        start = pl.multiple_of(rows + lax.bitwise_xor(mine, k) * piece, piece)
        copy(quarter, h.at[pl.ds(start, piece)])


def near_kernel(hidden, w_key, w_value, *rest):
    *quarters, total, w, h, sems = rest
    depth, width = w_key.shape
    copies = []

    def copy(source, target):
        copies.append(pltpu.make_async_copy(source, target, sems.at[len(copies)]))
        copies[-1].start()

    for i, held in enumerate((w_key, w_value)):
        copy(held, w.at[:, pl.ds(i * width, width)])
    quarters = [quarter.at[0] for quarter in quarters]
    lay_rows(hidden, quarters, lax.axis_index("seq"), depth, h, copy)
    for one in copies:
        one.wait()
    total[...] = jnp.dot(h[...], w[...], preferred_element_type=jnp.float32)


def far_kernel(hidden, w_far, w_swapped, near, *rest):
    *quarters, own, part_k, part_v, w, h, sems, held_own, own_sem = rest
    group = lax.axis_index("groups")
    depth, width = w_far.shape
    rows = hidden.shape[1]
    copies = []

    def copy(source, target):
        copies.append(pltpu.make_async_copy(source, target, sems.at[len(copies)]))
        copies[-1].start()

    for held, place in ((w_far, group), (w_swapped, 1 - group)):
        copy(held, w.at[:, pl.ds(pl.multiple_of(place * width, width), width)])
    quarters = [quarter.at[1] for quarter in quarters]
    lay_rows(hidden, quarters, lax.rem(lax.axis_index("seq") + 2, 4), depth, h, copy)
    for one in copies:
        one.wait()
    total = near[...] + jnp.dot(h[...], w[...], preferred_element_type=jnp.float32)
    held_own[...] = total[:rows]
    store = pltpu.make_async_copy(held_own, own, own_sem)
    store.start()
    part_k[...] = total[rows:, :width].astype(part_k.dtype)
    part_v[...] = total[rows:, width:].astype(part_v.dtype)
    store.wait()


def project(hidden, w_key, w_value, w_far, w_swapped, quarters):
    depth, width = w_key.shape
    rows = hidden.shape[1]
    scratch = [
        pltpu.VMEM((depth, 2 * width), jnp.bfloat16),
        pltpu.VMEM((2 * rows, depth), jnp.bfloat16),
        pltpu.SemaphoreType.DMA((3 + len(quarters),)),
    ]
    settings = dict(
        compiler_params=pltpu.CompilerParams(vmem_limit_bytes=16 * 1024 * 1024),
        cost_estimate=pl.CostEstimate(flops=1, bytes_accessed=1, transcendentals=0),
    )
    near = pl.pallas_call(
        near_kernel,
        out_shape=jax.ShapeDtypeStruct((2 * rows, 2 * width), jnp.float32),
        in_specs=[ANY] * (3 + len(quarters)),
        out_specs=VMEM,
        scratch_shapes=scratch,
        name="project_near",
        **settings,
    )(hidden, in_hbm(w_key), in_hbm(w_value), *quarters)
    return pl.pallas_call(
        far_kernel,
        out_shape=(
            jax.ShapeDtypeStruct((rows, 2 * width), jnp.float32),
            jax.ShapeDtypeStruct((rows, width), jnp.bfloat16),
            jax.ShapeDtypeStruct((rows, width), jnp.bfloat16),
        ),
        in_specs=[ANY] * 3 + [VMEM] + [ANY] * len(quarters),
        out_specs=(ANY, VMEM, VMEM),
        scratch_shapes=scratch
        + [pltpu.VMEM((rows, 2 * width), jnp.float32), pltpu.SemaphoreType.DMA],
        name="project_far",
        **settings,
    )(hidden, w_far, w_swapped, near, *quarters)


def plan_kernel(
    capacity, slots, request_docs, doc_lengths, rows, held, spare, key_bias, row_place, key_place, slot_row, counts
):
    me = lax.axis_index("seq")
    per_doc, _, doc_count = rows.shape
    doc_len = held.shape[0] // doc_count
    row_count = row_place.shape[0]
    docs = lax.broadcasted_iota(jnp.int32, (1, doc_count), 1)
    lengths = jnp.zeros((1, doc_count), jnp.int32)
    places = jnp.zeros((1, doc_count), jnp.int32)
    for o in range(counts.shape[0]):
        counts[o] = 0
    for j in range(doc_count):
        doc = request_docs[me, j]
        owner = lax.div(doc, slots)
        rank = counts[owner]
        counts[owner] = rank + 1
        lengths = jnp.where(docs == j, doc_lengths[doc], lengths)
        places = jnp.where(docs == j, owner * capacity + rank, places)
    slot = lax.broadcasted_iota(jnp.int32, (doc_len, doc_count), 0)
    used = slot < lengths
    for i in range(per_doc):
        used &= slot != rows[i]
    used = used.astype(jnp.float32)
    first = jnp.min(jnp.where(used > 0, slot, doc_len), axis=0, keepdims=True)
    firsts = (slot == first).astype(jnp.bfloat16)
    eye = lax.broadcasted_iota(jnp.int32, (doc_count, doc_count), 0) == docs
    across = (((1,), (1,)), ((), ()))

    def turned(columns):
        return lax.dot_general(
            eye.astype(jnp.bfloat16), columns, across, preferred_element_type=jnp.float32
        )

    bias = jnp.where(turned(used.astype(jnp.bfloat16)) > 0, 0.0, MASKED)
    firsts = turned(firsts)
    doc = lax.broadcasted_iota(jnp.int32, (doc_count, 1), 0)
    for j in range(doc_count):
        part = slice(j * doc_len, (j + 1) * doc_len)
        held[part, :] = jnp.broadcast_to(used[:, j : j + 1], (doc_len, held.shape[1])).astype(
            held.dtype
        )
        key_bias[:, part] = bias[j : j + 1, :]
        spare[:, part] = jnp.where(doc == j, firsts, 0.0).astype(spare.dtype)
    row = lax.broadcasted_iota(jnp.int32, (row_count, doc_count), 0)
    start = per_doc * lax.broadcasted_iota(jnp.int32, (row_count, doc_count), 1)
    of_doc = (row >= start) & (row < start + per_doc)
    nth = jnp.sum(jnp.where(of_doc, row - start, 0), axis=1, keepdims=True)
    chosen = jnp.zeros((row_count, doc_count), jnp.int32)
    for i in range(per_doc):
        chosen = jnp.where(nth == i, rows[i], chosen)
    chosen = jnp.where(of_doc, chosen + doc_len * docs, 0)
    column = jnp.sum(chosen, axis=1, keepdims=True)
    goes = nth + per_doc * jnp.sum(jnp.where(of_doc, places, 0), axis=1, keepdims=True)
    row_place[...] = column
    square = (row_count, row_count)
    same = lax.broadcasted_iota(jnp.int32, square, 0) == lax.broadcasted_iota(jnp.int32, square, 1)
    key_place[...] = jnp.sum(jnp.where(same, column, 0), axis=0, keepdims=True)
    slot_row[...] = jnp.sum(jnp.where(same, goes, 0), axis=0, keepdims=True)


def plan(request_docs, doc_lengths, recompute_rows, slots, head_dim, doc_len):
    _, doc_count, per_doc = recompute_rows.shape
    rows = doc_count * per_doc
    context = doc_count * doc_len
    shapes = (
        ((context, head_dim), jnp.bfloat16),
        ((doc_count, context), jnp.bfloat16),
        ((1, context), jnp.float32),
        ((rows, 1), jnp.int32),
        ((1, rows), jnp.int32),
        ((1, rows), jnp.int32),
    )
    return pl.pallas_call(
        functools.partial(plan_kernel, slots // 2, slots),
        out_shape=tuple(jax.ShapeDtypeStruct(*one) for one in shapes),
        in_specs=[SMEM, SMEM, VMEM],
        out_specs=(VMEM,) * len(shapes),
        scratch_shapes=[pltpu.SMEM((request_docs.shape[0],), jnp.int32)],
        compiler_params=pltpu.CompilerParams(vmem_limit_bytes=16 * 1024 * 1024),
        name="plan",
    )(request_docs, doc_lengths, jnp.transpose(recompute_rows, (2, 0, 1)))


def finish_kernel(own, arrived_k, arrived_v, slot_row, fresh, outgoing, held, sem):
    fetch = pltpu.make_async_copy(own, held, sem)
    fetch.start()
    fetch.wait()
    arrived = jnp.concatenate([arrived_k[...], arrived_v[...]], axis=1)
    total = (held[...] + arrived.astype(jnp.float32)).astype(jnp.bfloat16)
    fresh[...] = total
    slots = lax.broadcasted_iota(jnp.int32, (outgoing.shape[0], 1), 0)
    pick = (slots == slot_row[...]).astype(jnp.bfloat16)
    outgoing[...] = jnp.dot(pick, total, preferred_element_type=jnp.float32).astype(jnp.bfloat16)


def finish(own, arrived, slot_row, slots):
    shapes = (own.shape, (slots, own.shape[1]))
    return pl.pallas_call(
        finish_kernel,
        out_shape=tuple(jax.ShapeDtypeStruct(one, jnp.bfloat16) for one in shapes),
        in_specs=[ANY] + [VMEM] * 3,
        out_specs=(VMEM, VMEM),
        scratch_shapes=[pltpu.VMEM(own.shape, jnp.float32), pltpu.SemaphoreType.DMA],
        compiler_params=pltpu.CompilerParams(vmem_limit_bytes=16 * 1024 * 1024),
        name="finish",
    )(own, *arrived, slot_row)


def attend_kernel(
    by_owner, request_docs, queries, fresh, held, spare, key_bias, row_place, key_place, *rest
):
    sources, (mixed, raw, q, keys, values, counts, sems, q_sem) = rest[:-8], rest[-8:]
    me = lax.axis_index("seq")
    doc_count = request_docs.shape[1]
    head_dim = keys.shape[1] // 2
    doc_len = keys.shape[0] // doc_count
    owners = request_docs.shape[0]
    slots = sources[0].shape[0] if not by_owner else 2 * sources[0].shape[1]
    step = doc_count // sems.shape[1]
    blocks = doc_count // step
    block_rows = mixed.shape[1] // blocks
    block_keys = step * doc_len
    heads = mixed.shape[2] // head_dim
    left = pl.ds(0, head_dim)

    fetch_queries = pltpu.make_async_copy(queries, raw, q_sem)
    fetch_queries.start()
    for o in range(owners):
        counts[o] = 0

    def one_doc(j, carry):
        doc = request_docs[me, j]
        owner = lax.div(doc, slots)
        rank = counts[owner]
        counts[owner] = rank + 1
        place = pl.ds(pl.multiple_of(j * doc_len, doc_len), doc_len)
        block = lax.div(j, step)

        def fetch(key_source, value_source):
            pltpu.make_async_copy(key_source, keys.at[place, left], sems.at[0, block]).start()
            pltpu.make_async_copy(value_source, values.at[place, left], sems.at[1, block]).start()

        if by_owner:
            fetch(sources[0].at[owner, rank, 0], sources[0].at[owner, rank, 1])
        else:
            away = lax.bitwise_xor(me, owner)

            @pl.when(away == 0)
            def _():
                slot = lax.rem(doc, slots)
                fetch(sources[0].at[slot], sources[1].at[slot])

            for k, source in zip((2, 3, 1), sources[2:]):

                @pl.when(away == k)
                def _():
                    fetch(source.at[rank, 0], source.at[rank, 1])

        return carry

    lax.fori_loop(0, doc_count, one_doc, 0)

    fetch_queries.wait()
    scale = math.log2(math.e) / math.sqrt(head_dim)
    for b in range(blocks):
        for h in range(heads):
            here = raw[0, b * block_rows : (b + 1) * block_rows, h * head_dim : (h + 1) * head_dim]
            here = here.astype(jnp.float32) * scale
            high = here.astype(jnp.bfloat16)
            place = slice((b * heads + h) * block_rows, (b * heads + h + 1) * block_rows)
            q[place, :head_dim] = high
            q[place, head_dim:] = (here - high.astype(jnp.float32)).astype(jnp.bfloat16)

    for b in range(blocks):
        block = pl.ds(b * block_keys, block_keys)
        for i, context in enumerate((keys, values)):
            pltpu.make_async_copy(
                context.at[block, left], context.at[block, left], sems.at[i, b]
            ).wait()
    for b in range(blocks):
        block = slice(b * block_keys, (b + 1) * block_keys)
        spares = jnp.dot(
            spare[:, block], keys[block, :head_dim], preferred_element_type=jnp.float32
        ).astype(jnp.bfloat16)
        for j in range(b * step, (b + 1) * step):
            place = slice(j * doc_len, (j + 1) * doc_len)
            used = held[place, :]
            key = jnp.where(used > 0, keys[place, :head_dim], spares[j : j + 1, :])
            keys[place, :head_dim] = key
            keys[place, head_dim:] = key
            values[place, :head_dim] = values[place, :head_dim] * used
            values[place, head_dim:] = used

    fresh_k = jnp.concatenate([fresh[:, :head_dim]] * 2, axis=1)
    fresh_v = jnp.concatenate([fresh[:, head_dim:], jnp.ones_like(fresh[:, head_dim:])], axis=1)
    slot_place = lax.broadcasted_iota(jnp.int32, (1, block_keys), 1)
    contract_last = (((1,), (1,)), ((), ()))
    for b in range(blocks):
        rows = slice(b * block_rows, (b + 1) * block_rows)
        q_here = q[b * heads * block_rows : (b + 1) * heads * block_rows, :]
        own_place = row_place[rows, :]

        def scores(some_keys):
            return lax.dot_general(
                q_here, some_keys, contract_last, preferred_element_type=jnp.float32
            )

        def masked(some_keys, allowed):
            shape = (heads, block_rows, some_keys.shape[0])
            kept = jnp.where(allowed[None], scores(some_keys).reshape(shape), MASKED)
            return kept.reshape(heads * block_rows, some_keys.shape[0])

        chunks, sides = [], []
        for c in range(b):
            part = slice(c * block_keys, (c + 1) * block_keys)
            chunks.append(scores(keys[part, :]))
            sides.append(values[part, :])
        part = slice(b * block_keys, (b + 1) * block_keys)
        allowed = (slot_place + b * block_keys <= own_place) & (key_bias[:, part] == 0)
        chunks.append(masked(keys[part, :], allowed))
        sides.append(values[part, :])
        chunks.append(masked(fresh_k, key_place[...] <= own_place))
        sides.append(fresh_v)
        row_max = functools.reduce(
            jnp.maximum, [jnp.max(one, axis=1, keepdims=True) for one in chunks]
        )
        total = jnp.zeros((heads * block_rows, 2 * head_dim), jnp.float32)
        for one, side in zip(chunks, sides):
            powers = jnp.exp2(one - row_max).astype(jnp.bfloat16)
            total += jnp.dot(powers, side, preferred_element_type=jnp.float32)
        result = (total[:, :head_dim] / total[:, head_dim:]).astype(mixed.dtype)
        for h in range(heads):
            mixed[0, rows, h * head_dim : (h + 1) * head_dim] = result[
                h * block_rows : (h + 1) * block_rows
            ]


def attend(request_docs, queries, fresh, held, spare, key_bias, row_place, key_place, sources, by_owner):
    context, head_dim = held.shape
    rows = queries.shape[1] * queries.shape[2] // head_dim
    return pl.pallas_call(
        functools.partial(attend_kernel, by_owner),
        out_shape=jax.ShapeDtypeStruct(queries.shape, jnp.bfloat16),
        in_specs=[SMEM, ANY] + [VMEM] * 6 + [ANY] * len(sources),
        out_specs=VMEM,
        scratch_shapes=[
            pltpu.VMEM(queries.shape, jnp.bfloat16),
            pltpu.VMEM((rows, 2 * head_dim), jnp.bfloat16),
            pltpu.VMEM((context, 2 * head_dim), jnp.bfloat16),
            pltpu.VMEM((context, 2 * head_dim), jnp.bfloat16),
            pltpu.SMEM((request_docs.shape[0],), jnp.int32),
            pltpu.SemaphoreType.DMA((2, 4)),
            pltpu.SemaphoreType.DMA,
        ],
        compiler_params=pltpu.CompilerParams(vmem_limit_bytes=32 * 1024 * 1024),
        name="attend",
    )(
        request_docs,
        in_hbm(queries),
        fresh,
        held,
        spare,
        key_bias,
        row_place,
        key_place,
        *(in_hbm(one) for one in sources),
    )


def shards(
    pairs,
    hidden,
    queries,
    w_key,
    w_value,
    store_keys,
    store_values,
    request_docs,
    doc_lengths,
    recompute_rows,
):
    seq_count = lax.axis_size("seq")
    slot_count, doc_len, head_dim = store_keys.shape
    capacity = slot_count // 2
    per_doc = recompute_rows.shape[2]

    if pairs:
        def swap(array, axis, apart):
            count = lax.axis_size(axis)
            return lax.ppermute(array, axis, [(i, i ^ apart) for i in range(count)])

        w_send, h_send = pick_sent(hidden, w_key, w_value)
        w_far = swap(w_send, "seq", 2)
        h_mine = swap(h_send, "seq", 1)
        doc_1, doc_2, doc_3 = pick_docs(request_docs, store_keys, store_values, False)
        h_core = swap(h_mine, "tp", 1)
        h_chip = swap(h_mine, "tp", 2)
        doc_1, doc_2, doc_3, w_far = gate((doc_1, doc_2, doc_3, w_far), ())
        w_swapped = swap(w_far, "groups", 1)
        doc_2 = swap(doc_2, "seq", 2)
        doc_3 = swap(doc_3, "seq", 3)
        doc_1 = swap(doc_1, "seq", 1)
        docs = (doc_2, doc_3, doc_1)
        quarters = (h_mine, h_core, h_chip, swap(h_chip, "tp", 1))
        own, *parts = project(hidden, w_key, w_value, w_far, w_swapped, quarters)
        arrived = [swap(one, "seq", 1) for one in parts]
        sources = (store_keys, store_values, *docs)
    else:
        (docs,) = pick_docs(request_docs, store_keys, store_values, True)
        sources = (lax.all_to_all(docs, "seq", split_axis=0, concat_axis=0, tiled=True),)
        weights = lax.all_gather(
            jnp.concatenate([w_key, w_value], axis=1), "seq", axis=0, tiled=True
        )
        own = jnp.dot(hidden[0], weights, preferred_element_type=jnp.float32)
        arrived = [jnp.zeros(own.shape, jnp.bfloat16)[:, :head_dim]] * 2

    held, spare, key_bias, row_place, key_place, slot_row = plan(
        request_docs, doc_lengths, recompute_rows, slot_count, head_dim, doc_len
    )
    fresh, outgoing = finish(own, arrived, slot_row, seq_count * capacity * per_doc)
    mixed = attend(
        request_docs,
        queries,
        fresh,
        held,
        spare,
        key_bias,
        row_place,
        key_place,
        sources,
        not pairs,
    )

    outgoing = outgoing.reshape(seq_count, capacity * per_doc, 2 * head_dim)
    returned = lax.all_to_all(outgoing, "seq", split_axis=0, concat_axis=0, tiled=True)
    returned = returned.reshape(seq_count, capacity, per_doc, 2, head_dim)
    return (mixed, returned[None])


def solution(mesh):
    pairs = mesh.shape["seq"] == 4 and mesh.shape["groups"] == 2 and mesh.shape["tp"] == 4
    return jax.shard_map(
        functools.partial(shards, pairs),
        mesh=mesh,
        in_specs=(
            P(("groups", "seq"), None, None),
            P(("groups", "seq"), None, "tp"),
            P("seq", "tp"),
            P("seq", "tp"),
            P(("groups", "seq"), None, "tp"),
            P(("groups", "seq"), None, "tp"),
            P("groups", None),
            P("groups"),
            P(("groups", "seq"), None, None),
        ),
        out_specs=(
            P(("groups", "seq"), None, "tp"),
            P(("groups", "seq"), None, None, None, None, "tp"),
        ),
        check_vma=False,
    )
```

```python
import functools
import math

import jax
import jax.numpy as jnp
from jax import lax
from jax.experimental import pallas as pl
from jax.experimental.pallas import tpu as pltpu
from jax.sharding import PartitionSpec as P

ANY = pl.BlockSpec(memory_space=pl.ANY)
HBM = pl.BlockSpec(memory_space=pltpu.HBM)
SMEM = pl.BlockSpec(memory_space=pltpu.SMEM)
VMEM = pl.BlockSpec(memory_space=pltpu.VMEM)
MASKED = -1e30


def in_hbm(array):
    return pltpu.with_memory_space_constraint(array, pltpu.HBM)


def send_kernel(hidden, w_key, w_value, w_out, h_out, w_held, h_held, w_sems, h_sems):
    group = lax.axis_index("groups")
    me = lax.axis_index("seq")
    quarter = lax.axis_index("tp")
    pieces, piece = w_held.shape[:2]
    rows, depth = h_out.shape[1:]

    def fetch(i, weight):
        source = weight.at[pl.ds(i * piece, piece)]
        return pltpu.make_async_copy(source, w_held.at[i], w_sems.at[0, i])

    for chosen, weight in ((0, w_key), (1, w_value)):

        @pl.when(group == chosen)
        def _():
            for i in range(pieces):
                fetch(i, weight).start()

    first = me + 1 - 2 * lax.rem(me, 2)
    stores = []
    h_fetches = []
    for i, block in enumerate((first, lax.rem(first + 2, 4))):
        source = hidden.at[
            0,
            pl.ds(pl.multiple_of(quarter * rows, rows), rows),
            pl.ds(pl.multiple_of(block * depth, depth), depth),
        ]
        h_fetches.append(pltpu.make_async_copy(source, h_held.at[i], h_sems.at[0, i]))
        h_fetches[-1].start()
    for i in range(pieces):
        fetch(i, w_key).wait()
        target = w_out.at[pl.ds(i * piece, piece)]
        stores.append(pltpu.make_async_copy(w_held.at[i], target, w_sems.at[1, i]))
        stores[-1].start()
    for i, one in enumerate(h_fetches):
        one.wait()
        stores.append(pltpu.make_async_copy(h_held.at[i], h_out.at[i], h_sems.at[1, i]))
        stores[-1].start()
    for store in stores:
        store.wait()


def pick_sent(hidden, w_key, w_value):
    depth, width = w_key.shape
    pieces = 4
    h_shape = (2, hidden.shape[1] // 4, depth)
    return pl.pallas_call(
        send_kernel,
        out_shape=(
            jax.ShapeDtypeStruct(w_key.shape, jnp.bfloat16),
            jax.ShapeDtypeStruct(h_shape, jnp.bfloat16),
        ),
        in_specs=[ANY] * 3,
        out_specs=(ANY, ANY),
        scratch_shapes=[
            pltpu.VMEM((pieces, depth // pieces, width), jnp.bfloat16),
            pltpu.VMEM(h_shape, jnp.bfloat16),
            pltpu.SemaphoreType.DMA((2, pieces)),
            pltpu.SemaphoreType.DMA((2, 2)),
        ],
        name="pick_sent",
    )(hidden, w_key, w_value)


def gate_kernel(*refs):
    pass


def gate(arrays, first=()):
    return pl.pallas_call(
        gate_kernel,
        out_shape=tuple(jax.ShapeDtypeStruct(one.shape, one.dtype) for one in arrays),
        in_specs=[ANY] * (len(arrays) + len(first)),
        out_specs=(ANY,) * len(arrays),
        input_output_aliases={i: i for i in range(len(arrays))},
        compiler_params=pltpu.CompilerParams(vmem_limit_bytes=1024 * 1024),
        name="gate",
    )(*(in_hbm(one) for one in arrays), *first)


def docs_kernel(by_owner, request_docs, store_keys, store_values, *rest):
    *outs, picks, sems = rest
    me = lax.axis_index("seq")
    requests, doc_count = request_docs.shape
    slots = store_keys.shape[0]
    capacity = slots // 2

    def one_request(r, carry):
        for c in range(capacity):
            picks[r, c] = 0

        def one_doc(j, count):
            doc = request_docs[r, j]
            mine = lax.div(doc, slots) == me

            @pl.when(mine)
            def _():
                picks[r, jnp.minimum(count, capacity - 1)] = lax.rem(doc, slots)

            return count + mine.astype(jnp.int32)

        lax.fori_loop(0, doc_count, one_doc, jnp.int32(0), unroll=True)
        return carry

    lax.fori_loop(0, requests, one_request, 0)

    def send(r, out, sem):
        for c in range(capacity):
            slot = picks[r, c]
            pltpu.make_async_copy(store_keys.at[slot], out.at[c, 0], sem).start()
            pltpu.make_async_copy(store_values.at[slot], out.at[c, 1], sem).start()

    if by_owner:

        def one_send(r, carry):
            send(r, outs[0].at[r], sems.at[0])
            return carry

        lax.fori_loop(0, requests, one_send, 0)
    else:
        for i, out in enumerate(outs):
            send(lax.bitwise_xor(me, i + 1), out, sems.at[i])
    for i, out in enumerate(outs):
        pltpu.make_async_copy(out, out, sems.at[i]).wait()


def pick_docs(request_docs, store_keys, store_values, by_owner):
    requests = request_docs.shape[0]
    capacity = store_keys.shape[0] // 2
    one = (capacity, 2) + store_keys.shape[1:]
    shapes = ((requests,) + one,) if by_owner else (one,) * (requests - 1)
    return pl.pallas_call(
        functools.partial(docs_kernel, by_owner),
        out_shape=tuple(jax.ShapeDtypeStruct(one, jnp.bfloat16) for one in shapes),
        in_specs=[SMEM, ANY, ANY],
        out_specs=(VMEM,) * len(shapes),
        scratch_shapes=[
            pltpu.SMEM((requests, capacity), jnp.int32),
            pltpu.SemaphoreType.DMA((len(shapes),)),
        ],
        name="pick_docs",
    )(request_docs, store_keys, store_values)


def near_kernel(hidden, w_key, w_value, _, total, w, h, sems):
    depth, width = w_key.shape
    start = pl.multiple_of(lax.axis_index("seq") * depth, depth)
    copies = [
        pltpu.make_async_copy(w_key, w.at[:, pl.ds(0, width)], sems.at[0]),
        pltpu.make_async_copy(w_value, w.at[:, pl.ds(width, width)], sems.at[1]),
        pltpu.make_async_copy(hidden.at[0, :, pl.ds(start, depth)], h, sems.at[2]),
    ]
    for copy in copies:
        copy.start()
    for copy in copies:
        copy.wait()
    total[...] = jnp.dot(h[...], w[...], preferred_element_type=jnp.float32)


def lay_quarters(quarters, block, rows, copy):
    piece = rows.shape[0] // len(quarters)
    for k, quarter in enumerate(quarters):
        start = pl.multiple_of(lax.bitwise_xor(lax.axis_index("tp"), k) * piece, piece)
        copy(quarter.at[block], rows.at[pl.ds(start, piece)])


def neighbour_kernel(w_key, w_value, *rest):
    *quarters, total, w, n, sems = rest
    width = w_key.shape[1]
    copies = []

    def copy(source, target):
        copies.append(pltpu.make_async_copy(source, target, sems.at[len(copies)]))
        copies[-1].start()

    for i, held in enumerate((w_key, w_value)):
        copy(held, w.at[:, pl.ds(i * width, width)])
    lay_quarters(quarters, 0, n, copy)
    for one in copies:
        one.wait()
    total[...] = jnp.dot(n[...], w[...], preferred_element_type=jnp.float32)


def far_kernel(hidden, w_far, w_swapped, near, neighbour, *rest):
    *quarters, own, part, w, h, n, sems, held_own, own_sem = rest
    group = lax.axis_index("groups")
    depth, width = w_far.shape
    copies = []

    def copy(source, target):
        copies.append(pltpu.make_async_copy(source, target, sems.at[len(copies)]))
        copies[-1].start()

    for held, place in ((w_far, group), (w_swapped, 1 - group)):
        copy(held, w.at[:, pl.ds(pl.multiple_of(place * width, width), width)])
    start = pl.multiple_of(lax.rem(lax.axis_index("seq") + 2, 4) * depth, depth)
    copy(hidden.at[0, :, pl.ds(start, depth)], h)
    lay_quarters(quarters, 1, n, copy)
    for one in copies:
        one.wait()
    held_own[...] = near[...] + jnp.dot(h[...], w[...], preferred_element_type=jnp.float32)
    store = pltpu.make_async_copy(held_own, own, own_sem)
    store.start()
    total = neighbour[...] + jnp.dot(n[...], w[...], preferred_element_type=jnp.float32)
    part[...] = total.astype(part.dtype)
    store.wait()


def project(hidden, w_key, w_value, w_far, w_swapped, quarters, first):
    depth, width = w_key.shape
    rows = hidden.shape[1]
    sums = jax.ShapeDtypeStruct((rows, 2 * width), jnp.float32)
    w_scratch = pltpu.VMEM((depth, 2 * width), jnp.bfloat16)
    h_scratch = pltpu.VMEM((rows, depth), jnp.bfloat16)
    limit = pltpu.CompilerParams(vmem_limit_bytes=16 * 1024 * 1024)
    cheap = pl.CostEstimate(flops=1, bytes_accessed=1, transcendentals=0)
    w_key, w_value = in_hbm(w_key), in_hbm(w_value)
    near = pl.pallas_call(
        near_kernel,
        out_shape=sums,
        in_specs=[ANY] * 4,
        out_specs=VMEM,
        scratch_shapes=[w_scratch, h_scratch, pltpu.SemaphoreType.DMA((3,))],
        compiler_params=limit,
        cost_estimate=pl.CostEstimate(flops=10**10, bytes_accessed=1, transcendentals=0),
        name="project_near",
    )(hidden, w_key, w_value, first)
    neighbour = pl.pallas_call(
        neighbour_kernel,
        out_shape=sums,
        in_specs=[ANY] * (2 + len(quarters)),
        out_specs=VMEM,
        scratch_shapes=[
            w_scratch,
            h_scratch,
            pltpu.SemaphoreType.DMA((2 + len(quarters),)),
        ],
        compiler_params=limit,
        cost_estimate=cheap,
        name="project_neighbour",
    )(w_key, w_value, *quarters)
    return pl.pallas_call(
        far_kernel,
        out_shape=(sums, jax.ShapeDtypeStruct((rows, 2 * width), jnp.bfloat16)),
        in_specs=[ANY] * 3 + [VMEM] * 2 + [ANY] * len(quarters),
        out_specs=(ANY, VMEM),
        scratch_shapes=[
            w_scratch,
            h_scratch,
            h_scratch,
            pltpu.SemaphoreType.DMA((3 + len(quarters),)),
            pltpu.VMEM((rows, 2 * width), jnp.float32),
            pltpu.SemaphoreType.DMA,
        ],
        compiler_params=limit,
        cost_estimate=cheap,
        name="project_far",
    )(hidden, w_far, w_swapped, near, neighbour, *quarters)


def plan_kernel(
    capacity, slots, request_docs, doc_lengths, rows, held, spare, key_bias, row_place, key_place, slot_row, counts
):
    me = lax.axis_index("seq")
    per_doc, _, doc_count = rows.shape
    doc_len = held.shape[0] // doc_count
    row_count = row_place.shape[0]
    docs = lax.broadcasted_iota(jnp.int32, (1, doc_count), 1)
    lengths = jnp.zeros((1, doc_count), jnp.int32)
    places = jnp.zeros((1, doc_count), jnp.int32)
    for o in range(counts.shape[0]):
        counts[o] = 0
    for j in range(doc_count):
        doc = request_docs[me, j]
        owner = lax.div(doc, slots)
        rank = counts[owner]
        counts[owner] = rank + 1
        lengths = jnp.where(docs == j, doc_lengths[doc], lengths)
        places = jnp.where(docs == j, owner * capacity + rank, places)
    slot = lax.broadcasted_iota(jnp.int32, (doc_len, doc_count), 0)
    used = slot < lengths
    for i in range(per_doc):
        used &= slot != rows[i]
    used = used.astype(jnp.float32)
    first = jnp.min(jnp.where(used > 0, slot, doc_len), axis=0, keepdims=True)
    firsts = (slot == first).astype(jnp.bfloat16)
    eye = lax.broadcasted_iota(jnp.int32, (doc_count, doc_count), 0) == docs
    across = (((1,), (1,)), ((), ()))

    def turned(columns):
        return lax.dot_general(
            eye.astype(jnp.bfloat16), columns, across, preferred_element_type=jnp.float32
        )

    bias = jnp.where(turned(used.astype(jnp.bfloat16)) > 0, 0.0, MASKED)
    firsts = turned(firsts)
    doc = lax.broadcasted_iota(jnp.int32, (doc_count, 1), 0)
    for j in range(doc_count):
        part = slice(j * doc_len, (j + 1) * doc_len)
        held[part, :] = jnp.broadcast_to(used[:, j : j + 1], (doc_len, held.shape[1])).astype(
            held.dtype
        )
        key_bias[:, part] = bias[j : j + 1, :]
        spare[:, part] = jnp.where(doc == j, firsts, 0.0).astype(spare.dtype)
    row = lax.broadcasted_iota(jnp.int32, (row_count, doc_count), 0)
    start = per_doc * lax.broadcasted_iota(jnp.int32, (row_count, doc_count), 1)
    of_doc = (row >= start) & (row < start + per_doc)
    nth = jnp.sum(jnp.where(of_doc, row - start, 0), axis=1, keepdims=True)
    chosen = jnp.zeros((row_count, doc_count), jnp.int32)
    for i in range(per_doc):
        chosen = jnp.where(nth == i, rows[i], chosen)
    chosen = jnp.where(of_doc, chosen + doc_len * docs, 0)
    column = jnp.sum(chosen, axis=1, keepdims=True)
    goes = nth + per_doc * jnp.sum(jnp.where(of_doc, places, 0), axis=1, keepdims=True)
    row_place[...] = column
    square = (row_count, row_count)
    same = lax.broadcasted_iota(jnp.int32, square, 0) == lax.broadcasted_iota(jnp.int32, square, 1)
    key_place[...] = jnp.sum(jnp.where(same, column, 0), axis=0, keepdims=True)
    slot_row[...] = jnp.sum(jnp.where(same, goes, 0), axis=0, keepdims=True)


def plan(request_docs, doc_lengths, recompute_rows, slots, head_dim, doc_len):
    _, doc_count, per_doc = recompute_rows.shape
    rows = doc_count * per_doc
    context = doc_count * doc_len
    shapes = (
        ((context, head_dim), jnp.bfloat16),
        ((doc_count, context), jnp.bfloat16),
        ((1, context), jnp.float32),
        ((rows, 1), jnp.int32),
        ((1, rows), jnp.int32),
        ((1, rows), jnp.int32),
    )
    return pl.pallas_call(
        functools.partial(plan_kernel, slots // 2, slots),
        out_shape=tuple(jax.ShapeDtypeStruct(*one) for one in shapes),
        in_specs=[SMEM, SMEM, VMEM],
        out_specs=(VMEM,) * len(shapes),
        scratch_shapes=[pltpu.SMEM((request_docs.shape[0],), jnp.int32)],
        compiler_params=pltpu.CompilerParams(vmem_limit_bytes=16 * 1024 * 1024),
        name="plan",
    )(request_docs, doc_lengths, jnp.transpose(recompute_rows, (2, 0, 1)))


def finish_kernel(own, arrived, slot_row, fresh, outgoing, held, sem):
    fetch = pltpu.make_async_copy(own, held, sem)
    fetch.start()
    fetch.wait()
    total = (held[...] + arrived[...].astype(jnp.float32)).astype(jnp.bfloat16)
    fresh[...] = total
    slots = lax.broadcasted_iota(jnp.int32, (outgoing.shape[0], 1), 0)
    pick = (slots == slot_row[...]).astype(jnp.bfloat16)
    outgoing[...] = jnp.dot(pick, total, preferred_element_type=jnp.float32).astype(jnp.bfloat16)


def finish(own, arrived, slot_row, slots):
    shapes = (own.shape, (slots, own.shape[1]))
    return pl.pallas_call(
        finish_kernel,
        out_shape=tuple(jax.ShapeDtypeStruct(one, jnp.bfloat16) for one in shapes),
        in_specs=[ANY, VMEM, VMEM],
        out_specs=(VMEM, VMEM),
        scratch_shapes=[pltpu.VMEM(own.shape, jnp.float32), pltpu.SemaphoreType.DMA],
        compiler_params=pltpu.CompilerParams(vmem_limit_bytes=16 * 1024 * 1024),
        name="finish",
    )(own, arrived, slot_row)


def attend_kernel(
    by_owner, request_docs, queries, fresh, held, spare, key_bias, row_place, key_place, *rest
):
    sources, (mixed, raw, q, keys, values, counts, sems, q_sem) = rest[:-8], rest[-8:]
    me = lax.axis_index("seq")
    doc_count = request_docs.shape[1]
    head_dim = keys.shape[1] // 2
    doc_len = keys.shape[0] // doc_count
    owners = request_docs.shape[0]
    slots = sources[0].shape[0] if not by_owner else 2 * sources[0].shape[1]
    step = doc_count // sems.shape[1]
    blocks = doc_count // step
    block_rows = mixed.shape[1] // blocks
    block_keys = step * doc_len
    heads = mixed.shape[2] // head_dim
    left = pl.ds(0, head_dim)

    fetch_queries = pltpu.make_async_copy(queries, raw, q_sem)
    fetch_queries.start()
    for o in range(owners):
        counts[o] = 0

    def one_doc(j, carry):
        doc = request_docs[me, j]
        owner = lax.div(doc, slots)
        rank = counts[owner]
        counts[owner] = rank + 1
        place = pl.ds(pl.multiple_of(j * doc_len, doc_len), doc_len)
        block = lax.div(j, step)

        def fetch(key_source, value_source):
            pltpu.make_async_copy(key_source, keys.at[place, left], sems.at[0, block]).start()
            pltpu.make_async_copy(value_source, values.at[place, left], sems.at[1, block]).start()

        if by_owner:
            fetch(sources[0].at[owner, rank, 0], sources[0].at[owner, rank, 1])
        else:
            away = lax.bitwise_xor(me, owner)

            @pl.when(away == 0)
            def _():
                slot = lax.rem(doc, slots)
                fetch(sources[0].at[slot], sources[1].at[slot])

            for k, source in zip((2, 3, 1), sources[2:]):

                @pl.when(away == k)
                def _():
                    fetch(source.at[rank, 0], source.at[rank, 1])

        return carry

    lax.fori_loop(0, doc_count, one_doc, 0)

    fetch_queries.wait()
    scale = math.log2(math.e) / math.sqrt(head_dim)
    for b in range(blocks):
        for h in range(heads):
            here = raw[0, b * block_rows : (b + 1) * block_rows, h * head_dim : (h + 1) * head_dim]
            here = here.astype(jnp.float32) * scale
            high = here.astype(jnp.bfloat16)
            place = slice((b * heads + h) * block_rows, (b * heads + h + 1) * block_rows)
            q[place, :head_dim] = high
            q[place, head_dim:] = (here - high.astype(jnp.float32)).astype(jnp.bfloat16)

    for b in range(blocks):
        block = pl.ds(b * block_keys, block_keys)
        for i, context in enumerate((keys, values)):
            pltpu.make_async_copy(
                context.at[block, left], context.at[block, left], sems.at[i, b]
            ).wait()
    for b in range(blocks):
        block = slice(b * block_keys, (b + 1) * block_keys)
        spares = jnp.dot(
            spare[:, block], keys[block, :head_dim], preferred_element_type=jnp.float32
        ).astype(jnp.bfloat16)
        for j in range(b * step, (b + 1) * step):
            place = slice(j * doc_len, (j + 1) * doc_len)
            used = held[place, :]
            key = jnp.where(used > 0, keys[place, :head_dim], spares[j : j + 1, :])
            keys[place, :head_dim] = key
            keys[place, head_dim:] = key
            values[place, :head_dim] = values[place, :head_dim] * used
            values[place, head_dim:] = used

    fresh_k = jnp.concatenate([fresh[:, :head_dim]] * 2, axis=1)
    fresh_v = jnp.concatenate([fresh[:, head_dim:], jnp.ones_like(fresh[:, head_dim:])], axis=1)
    slot_place = lax.broadcasted_iota(jnp.int32, (1, block_keys), 1)
    contract_last = (((1,), (1,)), ((), ()))
    for b in range(blocks):
        rows = slice(b * block_rows, (b + 1) * block_rows)
        q_here = q[b * heads * block_rows : (b + 1) * heads * block_rows, :]
        own_place = row_place[rows, :]

        def scores(some_keys):
            return lax.dot_general(
                q_here, some_keys, contract_last, preferred_element_type=jnp.float32
            )

        def masked(some_keys, allowed):
            shape = (heads, block_rows, some_keys.shape[0])
            kept = jnp.where(allowed[None], scores(some_keys).reshape(shape), MASKED)
            return kept.reshape(heads * block_rows, some_keys.shape[0])

        chunks, sides = [], []
        for c in range(b):
            part = slice(c * block_keys, (c + 1) * block_keys)
            chunks.append(scores(keys[part, :]))
            sides.append(values[part, :])
        part = slice(b * block_keys, (b + 1) * block_keys)
        allowed = (slot_place + b * block_keys <= own_place) & (key_bias[:, part] == 0)
        chunks.append(masked(keys[part, :], allowed))
        sides.append(values[part, :])
        chunks.append(masked(fresh_k, key_place[...] <= own_place))
        sides.append(fresh_v)
        row_max = functools.reduce(
            jnp.maximum, [jnp.max(one, axis=1, keepdims=True) for one in chunks]
        )
        total = jnp.zeros((heads * block_rows, 2 * head_dim), jnp.float32)
        for one, side in zip(chunks, sides):
            powers = jnp.exp2(one - row_max).astype(jnp.bfloat16)
            total += jnp.dot(powers, side, preferred_element_type=jnp.float32)
        result = (total[:, :head_dim] / total[:, head_dim:]).astype(mixed.dtype)
        for h in range(heads):
            mixed[0, rows, h * head_dim : (h + 1) * head_dim] = result[
                h * block_rows : (h + 1) * block_rows
            ]


def attend(request_docs, queries, fresh, held, spare, key_bias, row_place, key_place, sources, by_owner):
    context, head_dim = held.shape
    rows = queries.shape[1] * queries.shape[2] // head_dim
    return pl.pallas_call(
        functools.partial(attend_kernel, by_owner),
        out_shape=jax.ShapeDtypeStruct(queries.shape, jnp.bfloat16),
        in_specs=[SMEM, ANY] + [VMEM] * 6 + [ANY] * len(sources),
        out_specs=VMEM,
        scratch_shapes=[
            pltpu.VMEM(queries.shape, jnp.bfloat16),
            pltpu.VMEM((rows, 2 * head_dim), jnp.bfloat16),
            pltpu.VMEM((context, 2 * head_dim), jnp.bfloat16),
            pltpu.VMEM((context, 2 * head_dim), jnp.bfloat16),
            pltpu.SMEM((request_docs.shape[0],), jnp.int32),
            pltpu.SemaphoreType.DMA((2, 4)),
            pltpu.SemaphoreType.DMA,
        ],
        compiler_params=pltpu.CompilerParams(vmem_limit_bytes=32 * 1024 * 1024),
        name="attend",
    )(
        request_docs,
        in_hbm(queries),
        fresh,
        held,
        spare,
        key_bias,
        row_place,
        key_place,
        *(in_hbm(one) for one in sources),
    )


def shards(
    pairs,
    hidden,
    queries,
    w_key,
    w_value,
    store_keys,
    store_values,
    request_docs,
    doc_lengths,
    recompute_rows,
):
    seq_count = lax.axis_size("seq")
    slot_count, doc_len, head_dim = store_keys.shape
    capacity = slot_count // 2
    per_doc = recompute_rows.shape[2]

    if pairs:
        def swap(array, axis, apart):
            count = lax.axis_size(axis)
            return lax.ppermute(array, axis, [(i, i ^ apart) for i in range(count)])

        w_send, h_send = pick_sent(hidden, w_key, w_value)
        w_far = swap(w_send, "seq", 2)
        h_mine = swap(h_send, "seq", 1)
        doc_1, doc_2, doc_3 = pick_docs(request_docs, store_keys, store_values, False)
        h_core = swap(h_mine, "tp", 1)
        h_chip = swap(h_mine, "tp", 2)
        doc_2, doc_3, w_far = gate((doc_2, doc_3, w_far))
        w_swapped = swap(w_far, "groups", 1)
        doc_1 = swap(doc_1, "seq", 1)
        docs = (swap(doc_2, "seq", 2), swap(doc_3, "seq", 3), doc_1)
        quarters = (h_mine, h_core, h_chip, swap(h_chip, "tp", 1))
        own, part = project(hidden, w_key, w_value, w_far, w_swapped, quarters, doc_1)
        arrived = swap(part, "seq", 1)
        sources = (store_keys, store_values, *docs)
    else:
        (docs,) = pick_docs(request_docs, store_keys, store_values, True)
        sources = (lax.all_to_all(docs, "seq", split_axis=0, concat_axis=0, tiled=True),)
        weights = lax.all_gather(
            jnp.concatenate([w_key, w_value], axis=1), "seq", axis=0, tiled=True
        )
        own = jnp.dot(hidden[0], weights, preferred_element_type=jnp.float32)
        arrived = jnp.zeros(own.shape, jnp.bfloat16)

    held, spare, key_bias, row_place, key_place, slot_row = plan(
        request_docs, doc_lengths, recompute_rows, slot_count, head_dim, doc_len
    )
    fresh, outgoing = finish(own, arrived, slot_row, seq_count * capacity * per_doc)
    mixed = attend(
        request_docs,
        queries,
        fresh,
        held,
        spare,
        key_bias,
        row_place,
        key_place,
        sources,
        not pairs,
    )

    outgoing = outgoing.reshape(seq_count, capacity * per_doc, 2 * head_dim)
    returned = lax.all_to_all(outgoing, "seq", split_axis=0, concat_axis=0, tiled=True)
    returned = returned.reshape(seq_count, capacity, per_doc, 2, head_dim)
    return (mixed, returned[None])


def solution(mesh):
    pairs = mesh.shape["seq"] == 4 and mesh.shape["groups"] == 2 and mesh.shape["tp"] == 4
    return jax.shard_map(
        functools.partial(shards, pairs),
        mesh=mesh,
        in_specs=(
            P(("groups", "seq"), None, None),
            P(("groups", "seq"), None, "tp"),
            P("seq", "tp"),
            P("seq", "tp"),
            P(("groups", "seq"), None, "tp"),
            P(("groups", "seq"), None, "tp"),
            P("groups", None),
            P("groups"),
            P(("groups", "seq"), None, None),
        ),
        out_specs=(
            P(("groups", "seq"), None, "tp"),
            P(("groups", "seq"), None, None, None, None, "tp"),
        ),
        check_vma=False,
    )
```

```python
import functools
import math

import jax
import jax.numpy as jnp
from jax import lax
from jax.experimental import pallas as pl
from jax.experimental.pallas import tpu as pltpu
from jax.sharding import PartitionSpec as P

ANY = pl.BlockSpec(memory_space=pl.ANY)
HBM = pl.BlockSpec(memory_space=pltpu.HBM)
SMEM = pl.BlockSpec(memory_space=pltpu.SMEM)
VMEM = pl.BlockSpec(memory_space=pltpu.VMEM)
MASKED = -1e30


def in_hbm(array):
    return pltpu.with_memory_space_constraint(array, pltpu.HBM)


def send_kernel(hidden, w_key, w_value, w_out, h_out, w_held, h_held, w_sems, h_sems):
    group = lax.axis_index("groups")
    me = lax.axis_index("seq")
    quarter = lax.axis_index("tp")
    pieces, piece = w_held.shape[:2]
    rows, depth = h_out.shape[1:]

    def fetch(i, weight):
        source = weight.at[pl.ds(i * piece, piece)]
        return pltpu.make_async_copy(source, w_held.at[i], w_sems.at[0, i])

    for chosen, weight in ((0, w_key), (1, w_value)):

        @pl.when(group == chosen)
        def _():
            for i in range(pieces):
                fetch(i, weight).start()

    first = me + 1 - 2 * lax.rem(me, 2)
    stores = []
    h_fetches = []
    for i, block in enumerate((first, lax.rem(first + 2, 4))):
        source = hidden.at[
            0,
            pl.ds(pl.multiple_of(quarter * rows, rows), rows),
            pl.ds(pl.multiple_of(block * depth, depth), depth),
        ]
        h_fetches.append(pltpu.make_async_copy(source, h_held.at[i], h_sems.at[0, i]))
        h_fetches[-1].start()
    for i in range(pieces):
        fetch(i, w_key).wait()
        target = w_out.at[pl.ds(i * piece, piece)]
        stores.append(pltpu.make_async_copy(w_held.at[i], target, w_sems.at[1, i]))
        stores[-1].start()
    for i, one in enumerate(h_fetches):
        one.wait()
        stores.append(pltpu.make_async_copy(h_held.at[i], h_out.at[i], h_sems.at[1, i]))
        stores[-1].start()
    for store in stores:
        store.wait()


def pick_sent(hidden, w_key, w_value):
    depth, width = w_key.shape
    pieces = 4
    h_shape = (2, hidden.shape[1] // 4, depth)
    return pl.pallas_call(
        send_kernel,
        out_shape=(
            jax.ShapeDtypeStruct(w_key.shape, jnp.bfloat16),
            jax.ShapeDtypeStruct(h_shape, jnp.bfloat16),
        ),
        in_specs=[ANY] * 3,
        out_specs=(ANY, ANY),
        scratch_shapes=[
            pltpu.VMEM((pieces, depth // pieces, width), jnp.bfloat16),
            pltpu.VMEM(h_shape, jnp.bfloat16),
            pltpu.SemaphoreType.DMA((2, pieces)),
            pltpu.SemaphoreType.DMA((2, 2)),
        ],
        name="pick_sent",
    )(hidden, w_key, w_value)


def gate_kernel(*refs):
    pass


def gate(arrays, first=(), pinned=0):
    return pl.pallas_call(
        gate_kernel,
        out_shape=tuple(jax.ShapeDtypeStruct(one.shape, one.dtype) for one in arrays),
        in_specs=[ANY] * (len(arrays) + len(first)),
        out_specs=(ANY,) * len(arrays),
        input_output_aliases={i: i for i in range(len(arrays))},
        compiler_params=pltpu.CompilerParams(vmem_limit_bytes=1024 * 1024),
        cost_estimate=pl.CostEstimate(flops=8000000000, bytes_accessed=1, transcendentals=0),
        name="gate",
    )(*(in_hbm(one) for one in arrays[:pinned]), *arrays[pinned:], *first)


def docs_kernel(by_owner, request_docs, store_keys, store_values, *rest):
    *outs, picks, sems = rest
    me = lax.axis_index("seq")
    requests, doc_count = request_docs.shape
    slots = store_keys.shape[0]
    capacity = slots // 2

    def one_request(r, carry):
        for c in range(capacity):
            picks[r, c] = 0

        def one_doc(j, count):
            doc = request_docs[r, j]
            mine = lax.div(doc, slots) == me

            @pl.when(mine)
            def _():
                picks[r, jnp.minimum(count, capacity - 1)] = lax.rem(doc, slots)

            return count + mine.astype(jnp.int32)

        lax.fori_loop(0, doc_count, one_doc, jnp.int32(0), unroll=True)
        return carry

    lax.fori_loop(0, requests, one_request, 0)

    def send(r, out, sem):
        for c in range(capacity):
            slot = picks[r, c]
            pltpu.make_async_copy(store_keys.at[slot], out.at[c, 0], sem).start()
            pltpu.make_async_copy(store_values.at[slot], out.at[c, 1], sem).start()

    if by_owner:

        def one_send(r, carry):
            send(r, outs[0].at[r], sems.at[0])
            return carry

        lax.fori_loop(0, requests, one_send, 0)
    else:
        for i, out in enumerate(outs):
            send(lax.bitwise_xor(me, i + 1), out, sems.at[i])
    for i, out in enumerate(outs):
        pltpu.make_async_copy(out, out, sems.at[i]).wait()


def pick_docs(request_docs, store_keys, store_values, by_owner):
    requests = request_docs.shape[0]
    capacity = store_keys.shape[0] // 2
    one = (capacity, 2) + store_keys.shape[1:]
    shapes = ((requests,) + one,) if by_owner else (one,) * (requests - 1)
    return pl.pallas_call(
        functools.partial(docs_kernel, by_owner),
        out_shape=tuple(jax.ShapeDtypeStruct(one, jnp.bfloat16) for one in shapes),
        in_specs=[SMEM, ANY, ANY],
        out_specs=(VMEM,) * len(shapes),
        scratch_shapes=[
            pltpu.SMEM((requests, capacity), jnp.int32),
            pltpu.SemaphoreType.DMA((len(shapes),)),
        ],
        name="pick_docs",
    )(request_docs, store_keys, store_values)


def near_kernel(hidden, w_key, w_value, _, total, w, h, sems):
    depth, width = w_key.shape
    start = pl.multiple_of(lax.axis_index("seq") * depth, depth)
    copies = [
        pltpu.make_async_copy(w_key, w.at[:, pl.ds(0, width)], sems.at[0]),
        pltpu.make_async_copy(w_value, w.at[:, pl.ds(width, width)], sems.at[1]),
        pltpu.make_async_copy(hidden.at[0, :, pl.ds(start, depth)], h, sems.at[2]),
    ]
    for copy in copies:
        copy.start()
    for copy in copies:
        copy.wait()
    total[...] = jnp.dot(h[...], w[...], preferred_element_type=jnp.float32)


def lay_quarters(quarters, block, rows, copy):
    piece = rows.shape[0] // len(quarters)
    for k, quarter in enumerate(quarters):
        start = pl.multiple_of(lax.bitwise_xor(lax.axis_index("tp"), k) * piece, piece)
        copy(quarter.at[block], rows.at[pl.ds(start, piece)])


def neighbour_kernel(w_key, w_value, *rest):
    *quarters, total, w, n, sems = rest
    width = w_key.shape[1]
    copies = []

    def copy(source, target):
        copies.append(pltpu.make_async_copy(source, target, sems.at[len(copies)]))
        copies[-1].start()

    for i, held in enumerate((w_key, w_value)):
        copy(held, w.at[:, pl.ds(i * width, width)])
    lay_quarters(quarters, 0, n, copy)
    for one in copies:
        one.wait()
    total[...] = jnp.dot(n[...], w[...], preferred_element_type=jnp.float32)


def far_kernel(hidden, w_far, w_swapped, near, neighbour, *rest):
    *quarters, own, part, w, h, n, sems = rest
    group = lax.axis_index("groups")
    depth, width = w_far.shape
    copies = []

    def copy(source, target):
        copies.append(pltpu.make_async_copy(source, target, sems.at[len(copies)]))
        copies[-1].start()

    for held, place in ((w_far, group), (w_swapped, 1 - group)):
        copy(held, w.at[:, pl.ds(pl.multiple_of(place * width, width), width)])
    start = pl.multiple_of(lax.rem(lax.axis_index("seq") + 2, 4) * depth, depth)
    copy(hidden.at[0, :, pl.ds(start, depth)], h)
    lay_quarters(quarters, 1, n, copy)
    for one in copies:
        one.wait()
    own[...] = near[...] + jnp.dot(h[...], w[...], preferred_element_type=jnp.float32)
    total = neighbour[...] + jnp.dot(n[...], w[...], preferred_element_type=jnp.float32)
    part[...] = total.astype(part.dtype)


def project(hidden, w_key, w_value, w_far, w_swapped, quarters, first):
    depth, width = w_key.shape
    rows = hidden.shape[1]
    sums = jax.ShapeDtypeStruct((rows, 2 * width), jnp.float32)
    w_scratch = pltpu.VMEM((depth, 2 * width), jnp.bfloat16)
    h_scratch = pltpu.VMEM((rows, depth), jnp.bfloat16)
    limit = pltpu.CompilerParams(vmem_limit_bytes=16 * 1024 * 1024)
    cheap = pl.CostEstimate(flops=1, bytes_accessed=1, transcendentals=0)
    w_key, w_value = in_hbm(w_key), in_hbm(w_value)
    near = pl.pallas_call(
        near_kernel,
        out_shape=sums,
        in_specs=[ANY] * 4,
        out_specs=VMEM,
        scratch_shapes=[w_scratch, h_scratch, pltpu.SemaphoreType.DMA((3,))],
        compiler_params=limit,
        cost_estimate=pl.CostEstimate(flops=10**10, bytes_accessed=1, transcendentals=0),
        name="project_near",
    )(hidden, w_key, w_value, first)
    neighbour = pl.pallas_call(
        neighbour_kernel,
        out_shape=sums,
        in_specs=[ANY] * (2 + len(quarters)),
        out_specs=VMEM,
        scratch_shapes=[
            w_scratch,
            h_scratch,
            pltpu.SemaphoreType.DMA((2 + len(quarters),)),
        ],
        compiler_params=limit,
        cost_estimate=cheap,
        name="project_neighbour",
    )(w_key, w_value, *quarters)
    return pl.pallas_call(
        far_kernel,
        out_shape=(sums, jax.ShapeDtypeStruct((rows, 2 * width), jnp.bfloat16)),
        in_specs=[ANY] * 3 + [VMEM] * 2 + [ANY] * len(quarters),
        out_specs=(VMEM, VMEM),
        scratch_shapes=[
            w_scratch,
            h_scratch,
            h_scratch,
            pltpu.SemaphoreType.DMA((3 + len(quarters),)),
        ],
        compiler_params=limit,
        cost_estimate=cheap,
        name="project_far",
    )(hidden, w_far, w_swapped, near, neighbour, *quarters)


def plan_kernel(
    capacity, slots, request_docs, doc_lengths, rows, held, spare, key_bias, row_place, key_place, slot_row, counts
):
    me = lax.axis_index("seq")
    per_doc, _, doc_count = rows.shape
    doc_len = held.shape[0] // doc_count
    row_count = row_place.shape[0]
    docs = lax.broadcasted_iota(jnp.int32, (1, doc_count), 1)
    lengths = jnp.zeros((1, doc_count), jnp.int32)
    places = jnp.zeros((1, doc_count), jnp.int32)
    for o in range(counts.shape[0]):
        counts[o] = 0
    for j in range(doc_count):
        doc = request_docs[me, j]
        owner = lax.div(doc, slots)
        rank = counts[owner]
        counts[owner] = rank + 1
        lengths = jnp.where(docs == j, doc_lengths[doc], lengths)
        places = jnp.where(docs == j, owner * capacity + rank, places)
    slot = lax.broadcasted_iota(jnp.int32, (doc_len, doc_count), 0)
    used = slot < lengths
    for i in range(per_doc):
        used &= slot != rows[i]
    used = used.astype(jnp.float32)
    first = jnp.min(jnp.where(used > 0, slot, doc_len), axis=0, keepdims=True)
    firsts = (slot == first).astype(jnp.bfloat16)
    eye = lax.broadcasted_iota(jnp.int32, (doc_count, doc_count), 0) == docs
    across = (((1,), (1,)), ((), ()))

    def turned(columns):
        return lax.dot_general(
            eye.astype(jnp.bfloat16), columns, across, preferred_element_type=jnp.float32
        )

    bias = jnp.where(turned(used.astype(jnp.bfloat16)) > 0, 0.0, MASKED)
    firsts = turned(firsts)
    doc = lax.broadcasted_iota(jnp.int32, (doc_count, 1), 0)
    for j in range(doc_count):
        part = slice(j * doc_len, (j + 1) * doc_len)
        held[part, :] = jnp.broadcast_to(used[:, j : j + 1], (doc_len, held.shape[1])).astype(
            held.dtype
        )
        key_bias[:, part] = bias[j : j + 1, :]
        spare[:, part] = jnp.where(doc == j, firsts, 0.0).astype(spare.dtype)
    row = lax.broadcasted_iota(jnp.int32, (row_count, doc_count), 0)
    start = per_doc * lax.broadcasted_iota(jnp.int32, (row_count, doc_count), 1)
    of_doc = (row >= start) & (row < start + per_doc)
    nth = jnp.sum(jnp.where(of_doc, row - start, 0), axis=1, keepdims=True)
    chosen = jnp.zeros((row_count, doc_count), jnp.int32)
    for i in range(per_doc):
        chosen = jnp.where(nth == i, rows[i], chosen)
    chosen = jnp.where(of_doc, chosen + doc_len * docs, 0)
    column = jnp.sum(chosen, axis=1, keepdims=True)
    goes = nth + per_doc * jnp.sum(jnp.where(of_doc, places, 0), axis=1, keepdims=True)
    row_place[...] = column
    square = (row_count, row_count)
    same = lax.broadcasted_iota(jnp.int32, square, 0) == lax.broadcasted_iota(jnp.int32, square, 1)
    key_place[...] = jnp.sum(jnp.where(same, column, 0), axis=0, keepdims=True)
    slot_row[...] = jnp.sum(jnp.where(same, goes, 0), axis=0, keepdims=True)


def plan(request_docs, doc_lengths, recompute_rows, slots, head_dim, doc_len):
    _, doc_count, per_doc = recompute_rows.shape
    rows = doc_count * per_doc
    context = doc_count * doc_len
    shapes = (
        ((context, head_dim), jnp.bfloat16),
        ((doc_count, context), jnp.bfloat16),
        ((1, context), jnp.float32),
        ((rows, 1), jnp.int32),
        ((1, rows), jnp.int32),
        ((1, rows), jnp.int32),
    )
    return pl.pallas_call(
        functools.partial(plan_kernel, slots // 2, slots),
        out_shape=tuple(jax.ShapeDtypeStruct(*one) for one in shapes),
        in_specs=[SMEM, SMEM, VMEM],
        out_specs=(VMEM,) * len(shapes),
        scratch_shapes=[pltpu.SMEM((request_docs.shape[0],), jnp.int32)],
        compiler_params=pltpu.CompilerParams(vmem_limit_bytes=16 * 1024 * 1024),
        name="plan",
    )(request_docs, doc_lengths, jnp.transpose(recompute_rows, (2, 0, 1)))


def finish_kernel(own, arrived, slot_row, fresh, outgoing):
    total = (own[...] + arrived[...].astype(jnp.float32)).astype(jnp.bfloat16)
    fresh[...] = total
    slots = lax.broadcasted_iota(jnp.int32, (outgoing.shape[0], 1), 0)
    pick = (slots == slot_row[...]).astype(jnp.bfloat16)
    outgoing[...] = jnp.dot(pick, total, preferred_element_type=jnp.float32).astype(jnp.bfloat16)


def finish(own, arrived, slot_row, slots):
    shapes = (own.shape, (slots, own.shape[1]))
    return pl.pallas_call(
        finish_kernel,
        out_shape=tuple(jax.ShapeDtypeStruct(one, jnp.bfloat16) for one in shapes),
        in_specs=[VMEM] * 3,
        out_specs=(VMEM, VMEM),
        compiler_params=pltpu.CompilerParams(vmem_limit_bytes=16 * 1024 * 1024),
        name="finish",
    )(own, arrived, slot_row)


def attend_kernel(
    by_owner, request_docs, queries, fresh, held, spare, key_bias, row_place, key_place, *rest
):
    sources, (mixed, raw, q, keys, values, counts, sems, q_sem) = rest[:-8], rest[-8:]
    me = lax.axis_index("seq")
    doc_count = request_docs.shape[1]
    head_dim = keys.shape[1] // 2
    doc_len = keys.shape[0] // doc_count
    owners = request_docs.shape[0]
    slots = sources[0].shape[0] if not by_owner else 2 * sources[0].shape[1]
    step = doc_count // sems.shape[1]
    blocks = doc_count // step
    block_rows = mixed.shape[1] // blocks
    block_keys = step * doc_len
    heads = mixed.shape[2] // head_dim
    left = pl.ds(0, head_dim)

    fetch_queries = pltpu.make_async_copy(queries, raw, q_sem)
    fetch_queries.start()
    for o in range(owners):
        counts[o] = 0

    def one_doc(j, carry):
        doc = request_docs[me, j]
        owner = lax.div(doc, slots)
        rank = counts[owner]
        counts[owner] = rank + 1
        place = pl.ds(pl.multiple_of(j * doc_len, doc_len), doc_len)
        block = lax.div(j, step)

        def fetch(key_source, value_source):
            pltpu.make_async_copy(key_source, keys.at[place, left], sems.at[0, block]).start()
            pltpu.make_async_copy(value_source, values.at[place, left], sems.at[1, block]).start()

        if by_owner:
            fetch(sources[0].at[owner, rank, 0], sources[0].at[owner, rank, 1])
        else:
            away = lax.bitwise_xor(me, owner)

            @pl.when(away == 0)
            def _():
                slot = lax.rem(doc, slots)
                fetch(sources[0].at[slot], sources[1].at[slot])

            for k, source in zip((2, 3, 1), sources[2:]):

                @pl.when(away == k)
                def _():
                    fetch(source.at[rank, 0], source.at[rank, 1])

        return carry

    lax.fori_loop(0, doc_count, one_doc, 0)

    fetch_queries.wait()
    scale = math.log2(math.e) / math.sqrt(head_dim)
    for b in range(blocks):
        for h in range(heads):
            here = raw[0, b * block_rows : (b + 1) * block_rows, h * head_dim : (h + 1) * head_dim]
            here = here.astype(jnp.float32) * scale
            high = here.astype(jnp.bfloat16)
            place = slice((b * heads + h) * block_rows, (b * heads + h + 1) * block_rows)
            q[place, :head_dim] = high
            q[place, head_dim:] = (here - high.astype(jnp.float32)).astype(jnp.bfloat16)

    for b in range(blocks):
        block = pl.ds(b * block_keys, block_keys)
        for i, context in enumerate((keys, values)):
            pltpu.make_async_copy(
                context.at[block, left], context.at[block, left], sems.at[i, b]
            ).wait()
    for b in range(blocks):
        block = slice(b * block_keys, (b + 1) * block_keys)
        spares = jnp.dot(
            spare[:, block], keys[block, :head_dim], preferred_element_type=jnp.float32
        ).astype(jnp.bfloat16)
        for j in range(b * step, (b + 1) * step):
            place = slice(j * doc_len, (j + 1) * doc_len)
            used = held[place, :]
            key = jnp.where(used > 0, keys[place, :head_dim], spares[j : j + 1, :])
            keys[place, :head_dim] = key
            keys[place, head_dim:] = key
            values[place, :head_dim] = values[place, :head_dim] * used
            values[place, head_dim:] = used

    fresh_k = jnp.concatenate([fresh[:, :head_dim]] * 2, axis=1)
    fresh_v = jnp.concatenate([fresh[:, head_dim:], jnp.ones_like(fresh[:, head_dim:])], axis=1)
    slot_place = lax.broadcasted_iota(jnp.int32, (1, block_keys), 1)
    contract_last = (((1,), (1,)), ((), ()))
    for b in range(blocks):
        rows = slice(b * block_rows, (b + 1) * block_rows)
        q_here = q[b * heads * block_rows : (b + 1) * heads * block_rows, :]
        own_place = row_place[rows, :]

        def scores(some_keys):
            return lax.dot_general(
                q_here, some_keys, contract_last, preferred_element_type=jnp.float32
            )

        def masked(some_keys, allowed):
            shape = (heads, block_rows, some_keys.shape[0])
            kept = jnp.where(allowed[None], scores(some_keys).reshape(shape), MASKED)
            return kept.reshape(heads * block_rows, some_keys.shape[0])

        chunks, sides = [], []
        for c in range(b):
            part = slice(c * block_keys, (c + 1) * block_keys)
            chunks.append(scores(keys[part, :]))
            sides.append(values[part, :])
        part = slice(b * block_keys, (b + 1) * block_keys)
        allowed = (slot_place + b * block_keys <= own_place) & (key_bias[:, part] == 0)
        chunks.append(masked(keys[part, :], allowed))
        sides.append(values[part, :])
        chunks.append(masked(fresh_k, key_place[...] <= own_place))
        sides.append(fresh_v)
        row_max = functools.reduce(
            jnp.maximum, [jnp.max(one, axis=1, keepdims=True) for one in chunks]
        )
        total = jnp.zeros((heads * block_rows, 2 * head_dim), jnp.float32)
        for one, side in zip(chunks, sides):
            powers = jnp.exp2(one - row_max).astype(jnp.bfloat16)
            total += jnp.dot(powers, side, preferred_element_type=jnp.float32)
        result = (total[:, :head_dim] / total[:, head_dim:]).astype(mixed.dtype)
        for h in range(heads):
            mixed[0, rows, h * head_dim : (h + 1) * head_dim] = result[
                h * block_rows : (h + 1) * block_rows
            ]


def attend(request_docs, queries, fresh, held, spare, key_bias, row_place, key_place, sources, by_owner):
    context, head_dim = held.shape
    rows = queries.shape[1] * queries.shape[2] // head_dim
    return pl.pallas_call(
        functools.partial(attend_kernel, by_owner),
        out_shape=jax.ShapeDtypeStruct(queries.shape, jnp.bfloat16),
        in_specs=[SMEM, ANY] + [VMEM] * 6 + [ANY] * len(sources),
        out_specs=VMEM,
        scratch_shapes=[
            pltpu.VMEM(queries.shape, jnp.bfloat16),
            pltpu.VMEM((rows, 2 * head_dim), jnp.bfloat16),
            pltpu.VMEM((context, 2 * head_dim), jnp.bfloat16),
            pltpu.VMEM((context, 2 * head_dim), jnp.bfloat16),
            pltpu.SMEM((request_docs.shape[0],), jnp.int32),
            pltpu.SemaphoreType.DMA((2, request_docs.shape[1] // 2)),
            pltpu.SemaphoreType.DMA,
        ],
        compiler_params=pltpu.CompilerParams(vmem_limit_bytes=32 * 1024 * 1024),
        name="attend",
    )(
        request_docs,
        in_hbm(queries),
        fresh,
        held,
        spare,
        key_bias,
        row_place,
        key_place,
        *(in_hbm(one) for one in sources[:2]),
        *sources[2:],
    )


def shards(
    pairs,
    hidden,
    queries,
    w_key,
    w_value,
    store_keys,
    store_values,
    request_docs,
    doc_lengths,
    recompute_rows,
):
    seq_count = lax.axis_size("seq")
    slot_count, doc_len, head_dim = store_keys.shape
    capacity = slot_count // 2
    per_doc = recompute_rows.shape[2]

    if pairs:
        def swap(array, axis, apart):
            count = lax.axis_size(axis)
            return lax.ppermute(array, axis, [(i, i ^ apart) for i in range(count)])

        w_send, h_send = pick_sent(hidden, w_key, w_value)
        w_far = swap(w_send, "seq", 2)
        h_mine = swap(h_send, "seq", 1)
        doc_1, doc_2, doc_3 = pick_docs(request_docs, store_keys, store_values, False)
        (h_mine,) = gate((h_mine,), (in_hbm(doc_1),))
        h_chip = swap(h_mine, "tp", 2)
        h_core = swap(h_mine, "tp", 1)
        doc_2, doc_3, w_far = gate((doc_2, doc_3, w_far), pinned=2)
        w_swapped = swap(w_far, "groups", 1)
        doc_1 = swap(doc_1, "seq", 1)
        docs = (swap(doc_2, "seq", 2), swap(doc_3, "seq", 3), doc_1)
        quarters = (h_mine, h_core, h_chip, swap(h_chip, "tp", 1))
        own, part = project(hidden, w_key, w_value, w_far, w_swapped, quarters, doc_1)
        arrived = swap(part, "seq", 1)
        sources = (store_keys, store_values, *docs)
    else:
        (docs,) = pick_docs(request_docs, store_keys, store_values, True)
        sources = (lax.all_to_all(docs, "seq", split_axis=0, concat_axis=0, tiled=True),)
        weights = lax.all_gather(
            jnp.concatenate([w_key, w_value], axis=1), "seq", axis=0, tiled=True
        )
        own = jnp.dot(hidden[0], weights, preferred_element_type=jnp.float32)
        arrived = jnp.zeros(own.shape, jnp.bfloat16)

    held, spare, key_bias, row_place, key_place, slot_row = plan(
        request_docs, doc_lengths, recompute_rows, slot_count, head_dim, doc_len
    )
    fresh, outgoing = finish(own, arrived, slot_row, seq_count * capacity * per_doc)
    mixed = attend(
        request_docs,
        queries,
        fresh,
        held,
        spare,
        key_bias,
        row_place,
        key_place,
        sources,
        not pairs,
    )

    outgoing = outgoing.reshape(seq_count, capacity * per_doc, 2 * head_dim)
    returned = lax.all_to_all(outgoing, "seq", split_axis=0, concat_axis=0, tiled=True)
    returned = returned.reshape(seq_count, capacity, per_doc, 2, head_dim)
    return (mixed, returned[None])


def solution(mesh):
    pairs = mesh.shape["seq"] == 4 and mesh.shape["groups"] == 2 and mesh.shape["tp"] == 4
    return jax.shard_map(
        functools.partial(shards, pairs),
        mesh=mesh,
        in_specs=(
            P(("groups", "seq"), None, None),
            P(("groups", "seq"), None, "tp"),
            P("seq", "tp"),
            P("seq", "tp"),
            P(("groups", "seq"), None, "tp"),
            P(("groups", "seq"), None, "tp"),
            P("groups", None),
            P("groups"),
            P(("groups", "seq"), None, None),
        ),
        out_specs=(
            P(("groups", "seq"), None, "tp"),
            P(("groups", "seq"), None, None, None, None, "tp"),
        ),
        check_vma=False,
    )
```

```python
import functools
import math

import jax
import jax.numpy as jnp
from jax import lax
from jax.experimental import pallas as pl
from jax.experimental.pallas import tpu as pltpu
from jax.sharding import PartitionSpec as P

ANY = pl.BlockSpec(memory_space=pl.ANY)
HBM = pl.BlockSpec(memory_space=pltpu.HBM)
SMEM = pl.BlockSpec(memory_space=pltpu.SMEM)
VMEM = pl.BlockSpec(memory_space=pltpu.VMEM)
MASKED = -1e30


def in_hbm(array):
    return pltpu.with_memory_space_constraint(array, pltpu.HBM)


def pick_weights_kernel(w_key, w_value, w_out, held, sems):
    group = lax.axis_index("groups")
    pieces, piece = held.shape[:2]

    def fetch(i, weight):
        source = weight.at[pl.ds(i * piece, piece)]
        return pltpu.make_async_copy(source, held.at[i], sems.at[0, i])

    for chosen, weight in ((0, w_key), (1, w_value)):

        @pl.when(group == chosen)
        def _():
            for i in range(pieces):
                fetch(i, weight).start()

    stores = []
    for i in range(pieces):
        fetch(i, w_key).wait()
        target = w_out.at[pl.ds(i * piece, piece)]
        stores.append(pltpu.make_async_copy(held.at[i], target, sems.at[1, i]))
        stores[-1].start()
    for store in stores:
        store.wait()


def pick_weights(w_key, w_value):
    depth, width = w_key.shape
    pieces = 4
    return pl.pallas_call(
        pick_weights_kernel,
        out_shape=jax.ShapeDtypeStruct(w_key.shape, jnp.bfloat16),
        in_specs=[ANY] * 2,
        out_specs=ANY,
        scratch_shapes=[
            pltpu.VMEM((pieces, depth // pieces, width), jnp.bfloat16),
            pltpu.SemaphoreType.DMA((2, pieces)),
        ],
        name="pick_weights",
    )(w_key, w_value)


def pick_hidden_kernel(hidden, _, out, held, sems):
    me = lax.axis_index("seq")
    rows, depth = out.shape[1:]
    first = me + 1 - 2 * lax.rem(me, 2)
    fetches, stores = [], []
    for i, block in enumerate((first, lax.rem(first + 2, 4))):
        source = hidden.at[
            0,
            pl.ds(pl.multiple_of(lax.axis_index("tp") * rows, rows), rows),
            pl.ds(pl.multiple_of(block * depth, depth), depth),
        ]
        fetches.append(pltpu.make_async_copy(source, held.at[i], sems.at[0, i]))
        fetches[-1].start()
        stores.append(pltpu.make_async_copy(held.at[i], out.at[i], sems.at[1, i]))
    for fetch, store in zip(fetches, stores):
        fetch.wait()
        store.start()
    for store in stores:
        store.wait()


def pick_hidden(hidden, depth, after):
    shape = (2, hidden.shape[1] // 4, depth)
    return pl.pallas_call(
        pick_hidden_kernel,
        out_shape=jax.ShapeDtypeStruct(shape, jnp.bfloat16),
        in_specs=[ANY] * 2,
        out_specs=ANY,
        scratch_shapes=[pltpu.VMEM(shape, jnp.bfloat16), pltpu.SemaphoreType.DMA((2, 2))],
        name="pick_hidden",
    )(hidden, after)


def gate_kernel(*refs):
    pass


def gate(arrays, first=(), pinned=0, cost=1):
    return pl.pallas_call(
        gate_kernel,
        out_shape=tuple(jax.ShapeDtypeStruct(one.shape, one.dtype) for one in arrays),
        in_specs=[ANY] * (len(arrays) + len(first)),
        out_specs=(ANY,) * len(arrays),
        input_output_aliases={i: i for i in range(len(arrays))},
        compiler_params=pltpu.CompilerParams(vmem_limit_bytes=1024 * 1024),
        cost_estimate=pl.CostEstimate(flops=cost, bytes_accessed=1, transcendentals=0),
        name="gate",
    )(*(in_hbm(one) for one in arrays[:pinned]), *arrays[pinned:], *first)


def docs_kernel(by_owner, request_docs, store_keys, store_values, *rest):
    *outs, picks, sems = rest
    me = lax.axis_index("seq")
    requests, doc_count = request_docs.shape
    slots = store_keys.shape[0]
    capacity = slots // 2

    def one_request(r, carry):
        for c in range(capacity):
            picks[r, c] = 0

        def one_doc(j, count):
            doc = request_docs[r, j]
            mine = lax.div(doc, slots) == me

            @pl.when(mine)
            def _():
                picks[r, jnp.minimum(count, capacity - 1)] = lax.rem(doc, slots)

            return count + mine.astype(jnp.int32)

        lax.fori_loop(0, doc_count, one_doc, jnp.int32(0), unroll=True)
        return carry

    lax.fori_loop(0, requests, one_request, 0)

    def send(r, out, sem):
        for c in range(capacity):
            slot = picks[r, c]
            pltpu.make_async_copy(store_keys.at[slot], out.at[c, 0], sem).start()
            pltpu.make_async_copy(store_values.at[slot], out.at[c, 1], sem).start()

    if by_owner:

        def one_send(r, carry):
            send(r, outs[0].at[r], sems.at[0])
            return carry

        lax.fori_loop(0, requests, one_send, 0)
    else:
        for i, out in enumerate(outs):
            send(lax.bitwise_xor(me, i + 1), out, sems.at[i])
    for i, out in enumerate(outs):
        pltpu.make_async_copy(out, out, sems.at[i]).wait()


def pick_docs(request_docs, store_keys, store_values, by_owner):
    requests = request_docs.shape[0]
    capacity = store_keys.shape[0] // 2
    one = (capacity, 2) + store_keys.shape[1:]
    shapes = ((requests,) + one,) if by_owner else (one,) * (requests - 1)
    return pl.pallas_call(
        functools.partial(docs_kernel, by_owner),
        out_shape=tuple(jax.ShapeDtypeStruct(one, jnp.bfloat16) for one in shapes),
        in_specs=[SMEM, ANY, ANY],
        out_specs=(VMEM,) * len(shapes),
        scratch_shapes=[
            pltpu.SMEM((requests, capacity), jnp.int32),
            pltpu.SemaphoreType.DMA((len(shapes),)),
        ],
        name="pick_docs",
    )(request_docs, store_keys, store_values)


def near_kernel(hidden, w_key, w_value, _, total, w, h, sems):
    depth, width = w_key.shape
    start = pl.multiple_of(lax.axis_index("seq") * depth, depth)
    copies = [
        pltpu.make_async_copy(w_key, w.at[:, pl.ds(0, width)], sems.at[0]),
        pltpu.make_async_copy(w_value, w.at[:, pl.ds(width, width)], sems.at[1]),
        pltpu.make_async_copy(hidden.at[0, :, pl.ds(start, depth)], h, sems.at[2]),
    ]
    for copy in copies:
        copy.start()
    for copy in copies:
        copy.wait()
    total[...] = jnp.dot(h[...], w[...], preferred_element_type=jnp.float32)


def lay_quarters(quarters, block, rows, copy):
    piece = rows.shape[0] // len(quarters)
    for k, quarter in enumerate(quarters):
        start = pl.multiple_of(lax.bitwise_xor(lax.axis_index("tp"), k) * piece, piece)
        copy(quarter.at[block], rows.at[pl.ds(start, piece)])


def neighbour_kernel(w_key, w_value, *rest):
    *quarters, total, w, n, sems = rest
    width = w_key.shape[1]
    copies = []

    def copy(source, target):
        copies.append(pltpu.make_async_copy(source, target, sems.at[len(copies)]))
        copies[-1].start()

    for i, held in enumerate((w_key, w_value)):
        copy(held, w.at[:, pl.ds(i * width, width)])
    lay_quarters(quarters, 0, n, copy)
    for one in copies:
        one.wait()
    total[...] = jnp.dot(n[...], w[...], preferred_element_type=jnp.float32)


def far_kernel(hidden, w_far, w_swapped, near, neighbour, *rest):
    *quarters, own, part_k, part_v, w, h, n, sems = rest
    group = lax.axis_index("groups")
    depth, width = w_far.shape
    copies = []

    def copy(source, target):
        copies.append(pltpu.make_async_copy(source, target, sems.at[len(copies)]))
        copies[-1].start()

    for held, place in ((w_far, group), (w_swapped, 1 - group)):
        copy(held, w.at[:, pl.ds(pl.multiple_of(place * width, width), width)])
    start = pl.multiple_of(lax.rem(lax.axis_index("seq") + 2, 4) * depth, depth)
    copy(hidden.at[0, :, pl.ds(start, depth)], h)
    lay_quarters(quarters, 1, n, copy)
    for one in copies:
        one.wait()
    own[...] = near[...] + jnp.dot(h[...], w[...], preferred_element_type=jnp.float32)
    total = neighbour[...] + jnp.dot(n[...], w[...], preferred_element_type=jnp.float32)
    part_k[...] = total[:, :width].astype(part_k.dtype)
    part_v[...] = total[:, width:].astype(part_v.dtype)


def project(hidden, w_key, w_value, w_far, w_swapped, quarters, first):
    depth, width = w_key.shape
    rows = hidden.shape[1]
    sums = jax.ShapeDtypeStruct((rows, 2 * width), jnp.float32)
    w_scratch = pltpu.VMEM((depth, 2 * width), jnp.bfloat16)
    h_scratch = pltpu.VMEM((rows, depth), jnp.bfloat16)
    limit = pltpu.CompilerParams(vmem_limit_bytes=16 * 1024 * 1024)
    cheap = pl.CostEstimate(flops=1, bytes_accessed=1, transcendentals=0)
    w_key, w_value = in_hbm(w_key), in_hbm(w_value)
    near = pl.pallas_call(
        near_kernel,
        out_shape=sums,
        in_specs=[ANY] * 4,
        out_specs=VMEM,
        scratch_shapes=[w_scratch, h_scratch, pltpu.SemaphoreType.DMA((3,))],
        compiler_params=limit,
        cost_estimate=pl.CostEstimate(flops=10**10, bytes_accessed=1, transcendentals=0),
        name="project_near",
    )(hidden, w_key, w_value, first)
    neighbour = pl.pallas_call(
        neighbour_kernel,
        out_shape=sums,
        in_specs=[ANY] * (2 + len(quarters)),
        out_specs=VMEM,
        scratch_shapes=[
            w_scratch,
            h_scratch,
            pltpu.SemaphoreType.DMA((2 + len(quarters),)),
        ],
        compiler_params=limit,
        cost_estimate=cheap,
        name="project_neighbour",
    )(w_key, w_value, *quarters)
    return pl.pallas_call(
        far_kernel,
        out_shape=(sums,) + (jax.ShapeDtypeStruct((rows, width), jnp.bfloat16),) * 2,
        in_specs=[ANY] * 3 + [VMEM] * 2 + [ANY] * len(quarters),
        out_specs=(VMEM,) * 3,
        scratch_shapes=[
            w_scratch,
            h_scratch,
            h_scratch,
            pltpu.SemaphoreType.DMA((3 + len(quarters),)),
        ],
        compiler_params=limit,
        cost_estimate=cheap,
        name="project_far",
    )(hidden, w_far, w_swapped, near, neighbour, *quarters)


def plan_kernel(
    capacity, slots, request_docs, doc_lengths, rows, held, spare, key_bias, row_place, key_place, slot_row, counts
):
    me = lax.axis_index("seq")
    per_doc, _, doc_count = rows.shape
    doc_len = held.shape[0] // doc_count
    row_count = row_place.shape[0]
    docs = lax.broadcasted_iota(jnp.int32, (1, doc_count), 1)
    lengths = jnp.zeros((1, doc_count), jnp.int32)
    places = jnp.zeros((1, doc_count), jnp.int32)
    for o in range(counts.shape[0]):
        counts[o] = 0
    for j in range(doc_count):
        doc = request_docs[me, j]
        owner = lax.div(doc, slots)
        rank = counts[owner]
        counts[owner] = rank + 1
        lengths = jnp.where(docs == j, doc_lengths[doc], lengths)
        places = jnp.where(docs == j, owner * capacity + rank, places)
    slot = lax.broadcasted_iota(jnp.int32, (doc_len, doc_count), 0)
    used = slot < lengths
    for i in range(per_doc):
        used &= slot != rows[i]
    used = used.astype(jnp.float32)
    first = jnp.min(jnp.where(used > 0, slot, doc_len), axis=0, keepdims=True)
    firsts = (slot == first).astype(jnp.bfloat16)
    eye = lax.broadcasted_iota(jnp.int32, (doc_count, doc_count), 0) == docs
    across = (((1,), (1,)), ((), ()))

    def turned(columns):
        return lax.dot_general(
            eye.astype(jnp.bfloat16), columns, across, preferred_element_type=jnp.float32
        )

    bias = jnp.where(turned(used.astype(jnp.bfloat16)) > 0, 0.0, MASKED)
    firsts = turned(firsts)
    doc = lax.broadcasted_iota(jnp.int32, (doc_count, 1), 0)
    for j in range(doc_count):
        part = slice(j * doc_len, (j + 1) * doc_len)
        held[part, :] = jnp.broadcast_to(used[:, j : j + 1], (doc_len, held.shape[1])).astype(
            held.dtype
        )
        key_bias[:, part] = bias[j : j + 1, :]
        spare[:, part] = jnp.where(doc == j, firsts, 0.0).astype(spare.dtype)
    row = lax.broadcasted_iota(jnp.int32, (row_count, doc_count), 0)
    start = per_doc * lax.broadcasted_iota(jnp.int32, (row_count, doc_count), 1)
    of_doc = (row >= start) & (row < start + per_doc)
    nth = jnp.sum(jnp.where(of_doc, row - start, 0), axis=1, keepdims=True)
    chosen = jnp.zeros((row_count, doc_count), jnp.int32)
    for i in range(per_doc):
        chosen = jnp.where(nth == i, rows[i], chosen)
    chosen = jnp.where(of_doc, chosen + doc_len * docs, 0)
    column = jnp.sum(chosen, axis=1, keepdims=True)
    goes = nth + per_doc * jnp.sum(jnp.where(of_doc, places, 0), axis=1, keepdims=True)
    row_place[...] = column
    square = (row_count, row_count)
    same = lax.broadcasted_iota(jnp.int32, square, 0) == lax.broadcasted_iota(jnp.int32, square, 1)
    key_place[...] = jnp.sum(jnp.where(same, column, 0), axis=0, keepdims=True)
    slot_row[...] = jnp.sum(jnp.where(same, goes, 0), axis=0, keepdims=True)


def plan(request_docs, doc_lengths, recompute_rows, slots, head_dim, doc_len):
    _, doc_count, per_doc = recompute_rows.shape
    rows = doc_count * per_doc
    context = doc_count * doc_len
    shapes = (
        ((context, head_dim), jnp.bfloat16),
        ((doc_count, context), jnp.bfloat16),
        ((1, context), jnp.float32),
        ((rows, 1), jnp.int32),
        ((1, rows), jnp.int32),
        ((1, rows), jnp.int32),
    )
    return pl.pallas_call(
        functools.partial(plan_kernel, slots // 2, slots),
        out_shape=tuple(jax.ShapeDtypeStruct(*one) for one in shapes),
        in_specs=[SMEM, SMEM, VMEM],
        out_specs=(VMEM,) * len(shapes),
        scratch_shapes=[pltpu.SMEM((request_docs.shape[0],), jnp.int32)],
        compiler_params=pltpu.CompilerParams(vmem_limit_bytes=16 * 1024 * 1024),
        name="plan",
    )(request_docs, doc_lengths, jnp.transpose(recompute_rows, (2, 0, 1)))


def finish_kernel(own, arrived_k, arrived_v, slot_row, fresh, outgoing):
    arrived = jnp.concatenate([arrived_k[...], arrived_v[...]], axis=1)
    total = (own[...] + arrived.astype(jnp.float32)).astype(jnp.bfloat16)
    fresh[...] = total
    slots = lax.broadcasted_iota(jnp.int32, (outgoing.shape[0], 1), 0)
    pick = (slots == slot_row[...]).astype(jnp.bfloat16)
    outgoing[...] = jnp.dot(pick, total, preferred_element_type=jnp.float32).astype(jnp.bfloat16)


def finish(own, arrived, slot_row, slots):
    shapes = (own.shape, (slots, own.shape[1]))
    return pl.pallas_call(
        finish_kernel,
        out_shape=tuple(jax.ShapeDtypeStruct(one, jnp.bfloat16) for one in shapes),
        in_specs=[VMEM] * 4,
        out_specs=(VMEM, VMEM),
        compiler_params=pltpu.CompilerParams(vmem_limit_bytes=16 * 1024 * 1024),
        name="finish",
    )(own, *arrived, slot_row)


def attend_kernel(
    by_owner, request_docs, queries, fresh, held, spare, key_bias, row_place, key_place, *rest
):
    sources, (mixed, raw, q, keys, values, counts, sems, q_sem) = rest[:-8], rest[-8:]
    me = lax.axis_index("seq")
    doc_count = request_docs.shape[1]
    head_dim = keys.shape[1] // 2
    doc_len = keys.shape[0] // doc_count
    owners = request_docs.shape[0]
    slots = sources[0].shape[0] if not by_owner else 2 * sources[0].shape[1]
    step = doc_count // sems.shape[1]
    blocks = doc_count // step
    block_rows = mixed.shape[1] // blocks
    block_keys = step * doc_len
    heads = mixed.shape[2] // head_dim
    left = pl.ds(0, head_dim)

    fetch_queries = pltpu.make_async_copy(queries, raw, q_sem)
    fetch_queries.start()
    for o in range(owners):
        counts[o] = 0

    def one_doc(j, carry):
        doc = request_docs[me, j]
        owner = lax.div(doc, slots)
        rank = counts[owner]
        counts[owner] = rank + 1
        place = pl.ds(pl.multiple_of(j * doc_len, doc_len), doc_len)
        block = lax.div(j, step)

        def fetch(key_source, value_source):
            pltpu.make_async_copy(key_source, keys.at[place, left], sems.at[0, block]).start()
            pltpu.make_async_copy(value_source, values.at[place, left], sems.at[1, block]).start()

        if by_owner:
            fetch(sources[0].at[owner, rank, 0], sources[0].at[owner, rank, 1])
        else:
            away = lax.bitwise_xor(me, owner)

            @pl.when(away == 0)
            def _():
                slot = lax.rem(doc, slots)
                fetch(sources[0].at[slot], sources[1].at[slot])

            for k, source in zip((2, 3, 1), sources[2:]):

                @pl.when(away == k)
                def _():
                    fetch(source.at[rank, 0], source.at[rank, 1])

        return carry

    lax.fori_loop(0, doc_count, one_doc, 0)

    fetch_queries.wait()
    scale = math.log2(math.e) / math.sqrt(head_dim)
    for b in range(blocks):
        for h in range(heads):
            here = raw[0, b * block_rows : (b + 1) * block_rows, h * head_dim : (h + 1) * head_dim]
            here = here.astype(jnp.float32) * scale
            high = here.astype(jnp.bfloat16)
            place = slice((b * heads + h) * block_rows, (b * heads + h + 1) * block_rows)
            q[place, :head_dim] = high
            q[place, head_dim:] = (here - high.astype(jnp.float32)).astype(jnp.bfloat16)

    for b in range(blocks):
        block = pl.ds(b * block_keys, block_keys)
        for i, context in enumerate((keys, values)):
            pltpu.make_async_copy(
                context.at[block, left], context.at[block, left], sems.at[i, b]
            ).wait()
    for b in range(blocks):
        block = slice(b * block_keys, (b + 1) * block_keys)
        spares = jnp.dot(
            spare[:, block], keys[block, :head_dim], preferred_element_type=jnp.float32
        ).astype(jnp.bfloat16)
        for j in range(b * step, (b + 1) * step):
            place = slice(j * doc_len, (j + 1) * doc_len)
            used = held[place, :]
            key = jnp.where(used > 0, keys[place, :head_dim], spares[j : j + 1, :])
            keys[place, :head_dim] = key
            keys[place, head_dim:] = key
            values[place, :head_dim] = values[place, :head_dim] * used
            values[place, head_dim:] = used

    fresh_k = jnp.concatenate([fresh[:, :head_dim]] * 2, axis=1)
    fresh_v = jnp.concatenate([fresh[:, head_dim:], jnp.ones_like(fresh[:, head_dim:])], axis=1)
    slot_place = lax.broadcasted_iota(jnp.int32, (1, block_keys), 1)
    contract_last = (((1,), (1,)), ((), ()))
    for b in range(blocks):
        rows = slice(b * block_rows, (b + 1) * block_rows)
        q_here = q[b * heads * block_rows : (b + 1) * heads * block_rows, :]
        own_place = row_place[rows, :]

        def scores(some_keys):
            return lax.dot_general(
                q_here, some_keys, contract_last, preferred_element_type=jnp.float32
            )

        def masked(some_keys, allowed):
            shape = (heads, block_rows, some_keys.shape[0])
            kept = jnp.where(allowed[None], scores(some_keys).reshape(shape), MASKED)
            return kept.reshape(heads * block_rows, some_keys.shape[0])

        chunks, sides = [], []
        for c in range(b):
            part = slice(c * block_keys, (c + 1) * block_keys)
            chunks.append(scores(keys[part, :]))
            sides.append(values[part, :])
        part = slice(b * block_keys, (b + 1) * block_keys)
        allowed = (slot_place + b * block_keys <= own_place) & (key_bias[:, part] == 0)
        chunks.append(masked(keys[part, :], allowed))
        sides.append(values[part, :])
        chunks.append(masked(fresh_k, key_place[...] <= own_place))
        sides.append(fresh_v)
        row_max = functools.reduce(
            jnp.maximum, [jnp.max(one, axis=1, keepdims=True) for one in chunks]
        )
        total = jnp.zeros((heads * block_rows, 2 * head_dim), jnp.float32)
        for one, side in zip(chunks, sides):
            powers = jnp.exp2(one - row_max).astype(jnp.bfloat16)
            total += jnp.dot(powers, side, preferred_element_type=jnp.float32)
        result = (total[:, :head_dim] / total[:, head_dim:]).astype(mixed.dtype)
        for h in range(heads):
            mixed[0, rows, h * head_dim : (h + 1) * head_dim] = result[
                h * block_rows : (h + 1) * block_rows
            ]


def attend(request_docs, queries, fresh, held, spare, key_bias, row_place, key_place, sources, by_owner):
    context, head_dim = held.shape
    rows = queries.shape[1] * queries.shape[2] // head_dim
    return pl.pallas_call(
        functools.partial(attend_kernel, by_owner),
        out_shape=jax.ShapeDtypeStruct(queries.shape, jnp.bfloat16),
        in_specs=[SMEM, ANY] + [VMEM] * 6 + [ANY] * len(sources),
        out_specs=VMEM,
        scratch_shapes=[
            pltpu.VMEM(queries.shape, jnp.bfloat16),
            pltpu.VMEM((rows, 2 * head_dim), jnp.bfloat16),
            pltpu.VMEM((context, 2 * head_dim), jnp.bfloat16),
            pltpu.VMEM((context, 2 * head_dim), jnp.bfloat16),
            pltpu.SMEM((request_docs.shape[0],), jnp.int32),
            pltpu.SemaphoreType.DMA((2, 4)),
            pltpu.SemaphoreType.DMA,
        ],
        compiler_params=pltpu.CompilerParams(vmem_limit_bytes=32 * 1024 * 1024),
        name="attend",
    )(
        request_docs,
        in_hbm(queries),
        fresh,
        held,
        spare,
        key_bias,
        row_place,
        key_place,
        *(in_hbm(one) for one in sources[:2]),
        *sources[2:],
    )


def shards(
    pairs,
    hidden,
    queries,
    w_key,
    w_value,
    store_keys,
    store_values,
    request_docs,
    doc_lengths,
    recompute_rows,
):
    seq_count = lax.axis_size("seq")
    slot_count, doc_len, head_dim = store_keys.shape
    capacity = slot_count // 2
    per_doc = recompute_rows.shape[2]

    if pairs:
        def swap(array, axis, apart):
            count = lax.axis_size(axis)
            return lax.ppermute(array, axis, [(i, i ^ apart) for i in range(count)])

        w_send = pick_weights(w_key, w_value)
        w_far = swap(w_send, "seq", 2)
        h_mine = swap(pick_hidden(hidden, w_key.shape[0], w_send), "seq", 1)
        doc_1, doc_2, doc_3 = pick_docs(request_docs, store_keys, store_values, False)
        (h_mine,) = gate((h_mine,), (in_hbm(doc_1),), cost=1)
        h_chip = swap(h_mine, "tp", 2)
        h_core = swap(h_mine, "tp", 1)
        doc_2, doc_3, w_far = gate((doc_2, doc_3, w_far), pinned=2, cost=8000000000)
        w_swapped = swap(w_far, "groups", 1)
        doc_1 = swap(doc_1, "seq", 1)
        docs = (swap(doc_2, "seq", 2), swap(doc_3, "seq", 3), doc_1)
        quarters = (h_mine, h_core, h_chip, swap(h_chip, "tp", 1))
        own, *parts = project(hidden, w_key, w_value, w_far, w_swapped, quarters, doc_1)
        arrived = [swap(one, "seq", 1) for one in parts]
        sources = (store_keys, store_values, *docs)
    else:
        (docs,) = pick_docs(request_docs, store_keys, store_values, True)
        sources = (lax.all_to_all(docs, "seq", split_axis=0, concat_axis=0, tiled=True),)
        weights = lax.all_gather(
            jnp.concatenate([w_key, w_value], axis=1), "seq", axis=0, tiled=True
        )
        own = jnp.dot(hidden[0], weights, preferred_element_type=jnp.float32)
        arrived = [jnp.zeros((own.shape[0], head_dim), jnp.bfloat16)] * 2

    held, spare, key_bias, row_place, key_place, slot_row = plan(
        request_docs, doc_lengths, recompute_rows, slot_count, head_dim, doc_len
    )
    fresh, outgoing = finish(own, arrived, slot_row, seq_count * capacity * per_doc)
    mixed = attend(
        request_docs,
        queries,
        fresh,
        held,
        spare,
        key_bias,
        row_place,
        key_place,
        sources,
        not pairs,
    )

    outgoing = outgoing.reshape(seq_count, capacity * per_doc, 2 * head_dim)
    returned = lax.all_to_all(outgoing, "seq", split_axis=0, concat_axis=0, tiled=True)
    returned = returned.reshape(seq_count, capacity, per_doc, 2, head_dim)
    return (mixed, returned[None])


def solution(mesh):
    pairs = mesh.shape["seq"] == 4 and mesh.shape["groups"] == 2 and mesh.shape["tp"] == 4
    return jax.shard_map(
        functools.partial(shards, pairs),
        mesh=mesh,
        in_specs=(
            P(("groups", "seq"), None, None),
            P(("groups", "seq"), None, "tp"),
            P("seq", "tp"),
            P("seq", "tp"),
            P(("groups", "seq"), None, "tp"),
            P(("groups", "seq"), None, "tp"),
            P("groups", None),
            P("groups"),
            P(("groups", "seq"), None, None),
        ),
        out_specs=(
            P(("groups", "seq"), None, "tp"),
            P(("groups", "seq"), None, None, None, None, "tp"),
        ),
        check_vma=False,
    )
```

```python
import functools
import math

import jax
import jax.numpy as jnp
from jax import lax
from jax.experimental import pallas as pl
from jax.experimental.pallas import tpu as pltpu
from jax.sharding import PartitionSpec as P

ANY = pl.BlockSpec(memory_space=pl.ANY)
HBM = pl.BlockSpec(memory_space=pltpu.HBM)
SMEM = pl.BlockSpec(memory_space=pltpu.SMEM)
VMEM = pl.BlockSpec(memory_space=pltpu.VMEM)
MASKED = -1e30


def in_hbm(array):
    return pltpu.with_memory_space_constraint(array, pltpu.HBM)


def send_kernel(hidden, w_key, w_value, w_out, h_out, sems):
    group = lax.axis_index("groups")
    me = lax.axis_index("seq")
    rows, depth = h_out.shape[1:]
    for chosen, weight in ((0, w_key), (1, w_value)):

        @pl.when(group == chosen)
        def _():
            pltpu.make_async_copy(weight, w_out, sems.at[0]).start()

    first = me + 1 - 2 * lax.rem(me, 2)
    copies = []
    for i, block in enumerate((first, lax.rem(first + 2, 4))):
        source = hidden.at[
            0,
            pl.ds(pl.multiple_of(lax.axis_index("tp") * rows, rows), rows),
            pl.ds(pl.multiple_of(block * depth, depth), depth),
        ]
        copies.append(pltpu.make_async_copy(source, h_out.at[i], sems.at[1 + i]))
        copies[-1].start()
    pltpu.make_async_copy(w_key, w_out, sems.at[0]).wait()
    for copy in copies:
        copy.wait()


def pick_sent(hidden, w_key, w_value):
    h_shape = (2, hidden.shape[1] // 4, w_key.shape[0])
    return pl.pallas_call(
        send_kernel,
        out_shape=(
            jax.ShapeDtypeStruct(w_key.shape, jnp.bfloat16),
            jax.ShapeDtypeStruct(h_shape, jnp.bfloat16),
        ),
        in_specs=[ANY] * 3,
        out_specs=(VMEM, VMEM),
        scratch_shapes=[pltpu.SemaphoreType.DMA((3,))],
        compiler_params=pltpu.CompilerParams(vmem_limit_bytes=16 * 1024 * 1024),
        name="pick_sent",
    )(in_hbm(hidden), in_hbm(w_key), in_hbm(w_value))


def gate_kernel(*refs):
    pass


def gate(arrays, first=(), pinned=0, cost=1):
    return pl.pallas_call(
        gate_kernel,
        out_shape=tuple(jax.ShapeDtypeStruct(one.shape, one.dtype) for one in arrays),
        in_specs=[ANY] * (len(arrays) + len(first)),
        out_specs=(ANY,) * len(arrays),
        input_output_aliases={i: i for i in range(len(arrays))},
        compiler_params=pltpu.CompilerParams(vmem_limit_bytes=1024 * 1024),
        cost_estimate=pl.CostEstimate(flops=cost, bytes_accessed=1, transcendentals=0),
        name="gate",
    )(*(in_hbm(one) for one in arrays[:pinned]), *arrays[pinned:], *first)


def docs_kernel(by_owner, request_docs, store_keys, store_values, *rest):
    *outs, picks, sems = rest
    me = lax.axis_index("seq")
    requests, doc_count = request_docs.shape
    slots = store_keys.shape[0]
    capacity = slots // 2

    def one_request(r, carry):
        for c in range(capacity):
            picks[r, c] = 0

        def one_doc(j, count):
            doc = request_docs[r, j]
            mine = lax.div(doc, slots) == me

            @pl.when(mine)
            def _():
                picks[r, jnp.minimum(count, capacity - 1)] = lax.rem(doc, slots)

            return count + mine.astype(jnp.int32)

        lax.fori_loop(0, doc_count, one_doc, jnp.int32(0), unroll=True)
        return carry

    lax.fori_loop(0, requests, one_request, 0)

    def send(r, out, sem):
        for c in range(capacity):
            slot = picks[r, c]
            pltpu.make_async_copy(store_keys.at[slot], out.at[c, 0], sem).start()
            pltpu.make_async_copy(store_values.at[slot], out.at[c, 1], sem).start()

    if by_owner:

        def one_send(r, carry):
            send(r, outs[0].at[r], sems.at[0])
            return carry

        lax.fori_loop(0, requests, one_send, 0)
    else:
        for i, out in enumerate(outs):
            send(lax.bitwise_xor(me, i + 1), out, sems.at[i])
    for i, out in enumerate(outs):
        pltpu.make_async_copy(out, out, sems.at[i]).wait()


def pick_docs(request_docs, store_keys, store_values, by_owner):
    requests = request_docs.shape[0]
    capacity = store_keys.shape[0] // 2
    one = (capacity, 2) + store_keys.shape[1:]
    shapes = ((requests,) + one,) if by_owner else (one,) * (requests - 1)
    return pl.pallas_call(
        functools.partial(docs_kernel, by_owner),
        out_shape=tuple(jax.ShapeDtypeStruct(one, jnp.bfloat16) for one in shapes),
        in_specs=[SMEM, ANY, ANY],
        out_specs=(VMEM,) * len(shapes),
        scratch_shapes=[
            pltpu.SMEM((requests, capacity), jnp.int32),
            pltpu.SemaphoreType.DMA((len(shapes),)),
        ],
        compiler_params=pltpu.CompilerParams(vmem_limit_bytes=16 * 1024 * 1024),
        name="pick_docs",
    )(request_docs, in_hbm(store_keys), in_hbm(store_values))


def near_kernel(hidden, w_key, w_value, _, total, w, h, sems):
    depth, width = w_key.shape
    start = pl.multiple_of(lax.axis_index("seq") * depth, depth)
    copies = [
        pltpu.make_async_copy(w_key, w.at[:, pl.ds(0, width)], sems.at[0]),
        pltpu.make_async_copy(w_value, w.at[:, pl.ds(width, width)], sems.at[1]),
        pltpu.make_async_copy(hidden.at[0, :, pl.ds(start, depth)], h, sems.at[2]),
    ]
    for copy in copies:
        copy.start()
    for copy in copies:
        copy.wait()
    total[...] = jnp.dot(h[...], w[...], preferred_element_type=jnp.float32)


def lay_quarters(quarters, block, rows, copy):
    piece = rows.shape[0] // len(quarters)
    for k, quarter in enumerate(quarters):
        start = pl.multiple_of(lax.bitwise_xor(lax.axis_index("tp"), k) * piece, piece)
        copy(quarter.at[block], rows.at[pl.ds(start, piece)])


def neighbour_kernel(w_key, w_value, *rest):
    *quarters, total, w, n, sems = rest
    width = w_key.shape[1]
    copies = []

    def copy(source, target):
        copies.append(pltpu.make_async_copy(source, target, sems.at[len(copies)]))
        copies[-1].start()

    for i, held in enumerate((w_key, w_value)):
        copy(held, w.at[:, pl.ds(i * width, width)])
    lay_quarters(quarters, 0, n, copy)
    for one in copies:
        one.wait()
    total[...] = jnp.dot(n[...], w[...], preferred_element_type=jnp.float32)


def far_kernel(hidden, w_far, w_swapped, near, neighbour, *rest):
    *quarters, own, part_k, part_v, w, h, n, sems = rest
    group = lax.axis_index("groups")
    depth, width = w_far.shape
    copies = []

    def copy(source, target):
        copies.append(pltpu.make_async_copy(source, target, sems.at[len(copies)]))
        copies[-1].start()

    for held, place in ((w_far, group), (w_swapped, 1 - group)):
        copy(held, w.at[:, pl.ds(pl.multiple_of(place * width, width), width)])
    start = pl.multiple_of(lax.rem(lax.axis_index("seq") + 2, 4) * depth, depth)
    copy(hidden.at[0, :, pl.ds(start, depth)], h)
    lay_quarters(quarters, 1, n, copy)
    for one in copies:
        one.wait()
    own[...] = near[...] + jnp.dot(h[...], w[...], preferred_element_type=jnp.float32)
    total = neighbour[...] + jnp.dot(n[...], w[...], preferred_element_type=jnp.float32)
    part_k[...] = total[:, :width].astype(part_k.dtype)
    part_v[...] = total[:, width:].astype(part_v.dtype)


def project(hidden, w_key, w_value, w_far, w_swapped, quarters, first):
    depth, width = w_key.shape
    rows = hidden.shape[1]
    sums = jax.ShapeDtypeStruct((rows, 2 * width), jnp.float32)
    w_scratch = pltpu.VMEM((depth, 2 * width), jnp.bfloat16)
    h_scratch = pltpu.VMEM((rows, depth), jnp.bfloat16)
    limit = pltpu.CompilerParams(vmem_limit_bytes=16 * 1024 * 1024)
    cheap = pl.CostEstimate(flops=1, bytes_accessed=1, transcendentals=0)
    w_key, w_value = in_hbm(w_key), in_hbm(w_value)
    near = pl.pallas_call(
        near_kernel,
        out_shape=sums,
        in_specs=[ANY] * 4,
        out_specs=VMEM,
        scratch_shapes=[w_scratch, h_scratch, pltpu.SemaphoreType.DMA((3,))],
        compiler_params=limit,
        cost_estimate=pl.CostEstimate(flops=10**10, bytes_accessed=1, transcendentals=0),
        name="project_near",
    )(hidden, w_key, w_value, first)
    neighbour = pl.pallas_call(
        neighbour_kernel,
        out_shape=sums,
        in_specs=[ANY] * (2 + len(quarters)),
        out_specs=VMEM,
        scratch_shapes=[
            w_scratch,
            h_scratch,
            pltpu.SemaphoreType.DMA((2 + len(quarters),)),
        ],
        compiler_params=limit,
        cost_estimate=cheap,
        name="project_neighbour",
    )(w_key, w_value, *quarters)
    return pl.pallas_call(
        far_kernel,
        out_shape=(sums,) + (jax.ShapeDtypeStruct((rows, width), jnp.bfloat16),) * 2,
        in_specs=[ANY] * 3 + [VMEM] * 2 + [ANY] * len(quarters),
        out_specs=(VMEM,) * 3,
        scratch_shapes=[
            w_scratch,
            h_scratch,
            h_scratch,
            pltpu.SemaphoreType.DMA((3 + len(quarters),)),
        ],
        compiler_params=limit,
        cost_estimate=cheap,
        name="project_far",
    )(hidden, w_far, w_swapped, near, neighbour, *quarters)


def plan_kernel(
    capacity, slots, request_docs, doc_lengths, rows, held, spare, key_bias, row_place, key_place, slot_row, counts
):
    me = lax.axis_index("seq")
    per_doc, _, doc_count = rows.shape
    doc_len = held.shape[0] // doc_count
    row_count = row_place.shape[0]
    docs = lax.broadcasted_iota(jnp.int32, (1, doc_count), 1)
    lengths = jnp.zeros((1, doc_count), jnp.int32)
    places = jnp.zeros((1, doc_count), jnp.int32)
    for o in range(counts.shape[0]):
        counts[o] = 0
    for j in range(doc_count):
        doc = request_docs[me, j]
        owner = lax.div(doc, slots)
        rank = counts[owner]
        counts[owner] = rank + 1
        lengths = jnp.where(docs == j, doc_lengths[doc], lengths)
        places = jnp.where(docs == j, owner * capacity + rank, places)
    slot = lax.broadcasted_iota(jnp.int32, (doc_len, doc_count), 0)
    used = slot < lengths
    for i in range(per_doc):
        used &= slot != rows[i]
    used = used.astype(jnp.float32)
    first = jnp.min(jnp.where(used > 0, slot, doc_len), axis=0, keepdims=True)
    firsts = (slot == first).astype(jnp.bfloat16)
    eye = lax.broadcasted_iota(jnp.int32, (doc_count, doc_count), 0) == docs
    across = (((1,), (1,)), ((), ()))

    def turned(columns):
        return lax.dot_general(
            eye.astype(jnp.bfloat16), columns, across, preferred_element_type=jnp.float32
        )

    bias = jnp.where(turned(used.astype(jnp.bfloat16)) > 0, 0.0, MASKED)
    firsts = turned(firsts)
    doc = lax.broadcasted_iota(jnp.int32, (doc_count, 1), 0)
    for j in range(doc_count):
        part = slice(j * doc_len, (j + 1) * doc_len)
        held[part, :] = jnp.broadcast_to(used[:, j : j + 1], (doc_len, held.shape[1])).astype(
            held.dtype
        )
        key_bias[:, part] = bias[j : j + 1, :]
        spare[:, part] = jnp.where(doc == j, firsts, 0.0).astype(spare.dtype)
    row = lax.broadcasted_iota(jnp.int32, (row_count, doc_count), 0)
    start = per_doc * lax.broadcasted_iota(jnp.int32, (row_count, doc_count), 1)
    of_doc = (row >= start) & (row < start + per_doc)
    nth = jnp.sum(jnp.where(of_doc, row - start, 0), axis=1, keepdims=True)
    chosen = jnp.zeros((row_count, doc_count), jnp.int32)
    for i in range(per_doc):
        chosen = jnp.where(nth == i, rows[i], chosen)
    chosen = jnp.where(of_doc, chosen + doc_len * docs, 0)
    column = jnp.sum(chosen, axis=1, keepdims=True)
    goes = nth + per_doc * jnp.sum(jnp.where(of_doc, places, 0), axis=1, keepdims=True)
    row_place[...] = column
    square = (row_count, row_count)
    same = lax.broadcasted_iota(jnp.int32, square, 0) == lax.broadcasted_iota(jnp.int32, square, 1)
    key_place[...] = jnp.sum(jnp.where(same, column, 0), axis=0, keepdims=True)
    slot_row[...] = jnp.sum(jnp.where(same, goes, 0), axis=0, keepdims=True)


def plan(request_docs, doc_lengths, recompute_rows, slots, head_dim, doc_len):
    _, doc_count, per_doc = recompute_rows.shape
    rows = doc_count * per_doc
    context = doc_count * doc_len
    shapes = (
        ((context, head_dim), jnp.bfloat16),
        ((doc_count, context), jnp.bfloat16),
        ((1, context), jnp.float32),
        ((rows, 1), jnp.int32),
        ((1, rows), jnp.int32),
        ((1, rows), jnp.int32),
    )
    return pl.pallas_call(
        functools.partial(plan_kernel, slots // 2, slots),
        out_shape=tuple(jax.ShapeDtypeStruct(*one) for one in shapes),
        in_specs=[SMEM, SMEM, VMEM],
        out_specs=(VMEM,) * len(shapes),
        scratch_shapes=[pltpu.SMEM((request_docs.shape[0],), jnp.int32)],
        compiler_params=pltpu.CompilerParams(vmem_limit_bytes=16 * 1024 * 1024),
        name="plan",
    )(request_docs, doc_lengths, jnp.transpose(recompute_rows, (2, 0, 1)))


def finish_kernel(own, arrived_k, arrived_v, slot_row, fresh, outgoing):
    arrived = jnp.concatenate([arrived_k[...], arrived_v[...]], axis=1)
    total = (own[...] + arrived.astype(jnp.float32)).astype(jnp.bfloat16)
    fresh[...] = total
    slots = lax.broadcasted_iota(jnp.int32, (outgoing.shape[0], 1), 0)
    pick = (slots == slot_row[...]).astype(jnp.bfloat16)
    outgoing[...] = jnp.dot(pick, total, preferred_element_type=jnp.float32).astype(jnp.bfloat16)


def finish(own, arrived, slot_row, slots):
    shapes = (own.shape, (slots, own.shape[1]))
    return pl.pallas_call(
        finish_kernel,
        out_shape=tuple(jax.ShapeDtypeStruct(one, jnp.bfloat16) for one in shapes),
        in_specs=[VMEM] * 4,
        out_specs=(VMEM, VMEM),
        compiler_params=pltpu.CompilerParams(vmem_limit_bytes=16 * 1024 * 1024),
        name="finish",
    )(own, *arrived, slot_row)


def attend_kernel(
    by_owner, request_docs, queries, fresh, held, spare, key_bias, row_place, key_place, *rest
):
    sources, (mixed, raw, q, keys, values, counts, sems, q_sem) = rest[:-8], rest[-8:]
    me = lax.axis_index("seq")
    doc_count = request_docs.shape[1]
    head_dim = keys.shape[1] // 2
    doc_len = keys.shape[0] // doc_count
    owners = request_docs.shape[0]
    slots = sources[0].shape[0] if not by_owner else 2 * sources[0].shape[1]
    step = doc_count // sems.shape[1]
    blocks = doc_count // step
    block_rows = mixed.shape[1] // blocks
    block_keys = step * doc_len
    heads = mixed.shape[2] // head_dim
    left = pl.ds(0, head_dim)

    fetch_queries = pltpu.make_async_copy(queries, raw, q_sem)
    fetch_queries.start()
    for o in range(owners):
        counts[o] = 0

    def one_doc(j, carry):
        doc = request_docs[me, j]
        owner = lax.div(doc, slots)
        rank = counts[owner]
        counts[owner] = rank + 1
        place = pl.ds(pl.multiple_of(j * doc_len, doc_len), doc_len)
        block = lax.div(j, step)

        def fetch(key_source, value_source):
            pltpu.make_async_copy(key_source, keys.at[place, left], sems.at[0, block]).start()
            pltpu.make_async_copy(value_source, values.at[place, left], sems.at[1, block]).start()

        if by_owner:
            fetch(sources[0].at[owner, rank, 0], sources[0].at[owner, rank, 1])
        else:
            away = lax.bitwise_xor(me, owner)

            @pl.when(away == 0)
            def _():
                slot = lax.rem(doc, slots)
                fetch(sources[0].at[slot], sources[1].at[slot])

            for k, source in zip((2, 3, 1), sources[2:]):

                @pl.when(away == k)
                def _():
                    fetch(source.at[rank, 0], source.at[rank, 1])

        return carry

    lax.fori_loop(0, doc_count, one_doc, 0)

    fetch_queries.wait()
    scale = math.log2(math.e) / math.sqrt(head_dim)
    for b in range(blocks):
        for h in range(heads):
            here = raw[0, b * block_rows : (b + 1) * block_rows, h * head_dim : (h + 1) * head_dim]
            here = here.astype(jnp.float32) * scale
            high = here.astype(jnp.bfloat16)
            place = slice((b * heads + h) * block_rows, (b * heads + h + 1) * block_rows)
            q[place, :head_dim] = high
            q[place, head_dim:] = (here - high.astype(jnp.float32)).astype(jnp.bfloat16)

    for b in range(blocks):
        block = pl.ds(b * block_keys, block_keys)
        for i, context in enumerate((keys, values)):
            pltpu.make_async_copy(
                context.at[block, left], context.at[block, left], sems.at[i, b]
            ).wait()
    for b in range(blocks):
        block = slice(b * block_keys, (b + 1) * block_keys)
        spares = jnp.dot(
            spare[:, block], keys[block, :head_dim], preferred_element_type=jnp.float32
        ).astype(jnp.bfloat16)
        for j in range(b * step, (b + 1) * step):
            place = slice(j * doc_len, (j + 1) * doc_len)
            used = held[place, :]
            key = jnp.where(used > 0, keys[place, :head_dim], spares[j : j + 1, :])
            keys[place, :head_dim] = key
            keys[place, head_dim:] = key
            values[place, :head_dim] = values[place, :head_dim] * used
            values[place, head_dim:] = used

    fresh_k = jnp.concatenate([fresh[:, :head_dim]] * 2, axis=1)
    fresh_v = jnp.concatenate([fresh[:, head_dim:], jnp.ones_like(fresh[:, head_dim:])], axis=1)
    slot_place = lax.broadcasted_iota(jnp.int32, (1, block_keys), 1)
    contract_last = (((1,), (1,)), ((), ()))
    for b in range(blocks):
        rows = slice(b * block_rows, (b + 1) * block_rows)
        q_here = q[b * heads * block_rows : (b + 1) * heads * block_rows, :]
        own_place = row_place[rows, :]

        def scores(some_keys):
            return lax.dot_general(
                q_here, some_keys, contract_last, preferred_element_type=jnp.float32
            )

        def masked(some_keys, allowed):
            shape = (heads, block_rows, some_keys.shape[0])
            kept = jnp.where(allowed[None], scores(some_keys).reshape(shape), MASKED)
            return kept.reshape(heads * block_rows, some_keys.shape[0])

        chunks, sides = [], []
        for c in range(b):
            part = slice(c * block_keys, (c + 1) * block_keys)
            chunks.append(scores(keys[part, :]))
            sides.append(values[part, :])
        part = slice(b * block_keys, (b + 1) * block_keys)
        allowed = (slot_place + b * block_keys <= own_place) & (key_bias[:, part] == 0)
        chunks.append(masked(keys[part, :], allowed))
        sides.append(values[part, :])
        chunks.append(masked(fresh_k, key_place[...] <= own_place))
        sides.append(fresh_v)
        row_max = functools.reduce(
            jnp.maximum, [jnp.max(one, axis=1, keepdims=True) for one in chunks]
        )
        total = jnp.zeros((heads * block_rows, 2 * head_dim), jnp.float32)
        for one, side in zip(chunks, sides):
            powers = jnp.exp2(one - row_max).astype(jnp.bfloat16)
            total += jnp.dot(powers, side, preferred_element_type=jnp.float32)
        result = (total[:, :head_dim] / total[:, head_dim:]).astype(mixed.dtype)
        for h in range(heads):
            mixed[0, rows, h * head_dim : (h + 1) * head_dim] = result[
                h * block_rows : (h + 1) * block_rows
            ]


def attend(request_docs, queries, fresh, held, spare, key_bias, row_place, key_place, sources, by_owner):
    context, head_dim = held.shape
    rows = queries.shape[1] * queries.shape[2] // head_dim
    return pl.pallas_call(
        functools.partial(attend_kernel, by_owner),
        out_shape=jax.ShapeDtypeStruct(queries.shape, jnp.bfloat16),
        in_specs=[SMEM, ANY] + [VMEM] * 6 + [ANY] * len(sources),
        out_specs=VMEM,
        scratch_shapes=[
            pltpu.VMEM(queries.shape, jnp.bfloat16),
            pltpu.VMEM((rows, 2 * head_dim), jnp.bfloat16),
            pltpu.VMEM((context, 2 * head_dim), jnp.bfloat16),
            pltpu.VMEM((context, 2 * head_dim), jnp.bfloat16),
            pltpu.SMEM((request_docs.shape[0],), jnp.int32),
            pltpu.SemaphoreType.DMA((2, 4)),
            pltpu.SemaphoreType.DMA,
        ],
        compiler_params=pltpu.CompilerParams(vmem_limit_bytes=32 * 1024 * 1024),
        name="attend",
    )(
        request_docs,
        in_hbm(queries),
        fresh,
        held,
        spare,
        key_bias,
        row_place,
        key_place,
        *(in_hbm(one) for one in sources[:2]),
        *sources[2:],
    )


def shards(
    pairs,
    hidden,
    queries,
    w_key,
    w_value,
    store_keys,
    store_values,
    request_docs,
    doc_lengths,
    recompute_rows,
):
    seq_count = lax.axis_size("seq")
    slot_count, doc_len, head_dim = store_keys.shape
    capacity = slot_count // 2
    per_doc = recompute_rows.shape[2]

    if pairs:
        def swap(array, axis, apart):
            count = lax.axis_size(axis)
            return lax.ppermute(array, axis, [(i, i ^ apart) for i in range(count)])

        w_send, h_send = pick_sent(hidden, w_key, w_value)
        w_far = swap(w_send, "seq", 2)
        h_mine = swap(h_send, "seq", 1)
        doc_1, doc_2, doc_3 = pick_docs(request_docs, store_keys, store_values, False)
        (h_mine,) = gate((h_mine,), (doc_1,), cost=8000000000)
        h_chip = swap(h_mine, "tp", 2)
        h_core = swap(h_mine, "tp", 1)
        doc_2, doc_3, w_far = gate((doc_2, doc_3, w_far), cost=8000000000)
        w_swapped = swap(w_far, "groups", 1)
        doc_1 = swap(doc_1, "seq", 1)
        docs = (swap(doc_2, "seq", 2), swap(doc_3, "seq", 3), doc_1)
        quarters = (h_mine, h_core, h_chip, swap(h_chip, "tp", 1))
        own, *parts = project(hidden, w_key, w_value, w_far, w_swapped, quarters, doc_1)
        arrived = [swap(one, "seq", 1) for one in parts]
        sources = (store_keys, store_values, *docs)
    else:
        (docs,) = pick_docs(request_docs, store_keys, store_values, True)
        sources = (lax.all_to_all(docs, "seq", split_axis=0, concat_axis=0, tiled=True),)
        weights = lax.all_gather(
            jnp.concatenate([w_key, w_value], axis=1), "seq", axis=0, tiled=True
        )
        own = jnp.dot(hidden[0], weights, preferred_element_type=jnp.float32)
        arrived = [jnp.zeros((own.shape[0], head_dim), jnp.bfloat16)] * 2

    held, spare, key_bias, row_place, key_place, slot_row = plan(
        request_docs, doc_lengths, recompute_rows, slot_count, head_dim, doc_len
    )
    fresh, outgoing = finish(own, arrived, slot_row, seq_count * capacity * per_doc)
    mixed = attend(
        request_docs,
        queries,
        fresh,
        held,
        spare,
        key_bias,
        row_place,
        key_place,
        sources,
        not pairs,
    )

    outgoing = outgoing.reshape(seq_count, capacity * per_doc, 2 * head_dim)
    returned = lax.all_to_all(outgoing, "seq", split_axis=0, concat_axis=0, tiled=True)
    returned = returned.reshape(seq_count, capacity, per_doc, 2, head_dim)
    return (mixed, returned[None])


def solution(mesh):
    pairs = mesh.shape["seq"] == 4 and mesh.shape["groups"] == 2 and mesh.shape["tp"] == 4
    return jax.shard_map(
        functools.partial(shards, pairs),
        mesh=mesh,
        in_specs=(
            P(("groups", "seq"), None, None),
            P(("groups", "seq"), None, "tp"),
            P("seq", "tp"),
            P("seq", "tp"),
            P(("groups", "seq"), None, "tp"),
            P(("groups", "seq"), None, "tp"),
            P("groups", None),
            P("groups"),
            P(("groups", "seq"), None, None),
        ),
        out_specs=(
            P(("groups", "seq"), None, "tp"),
            P(("groups", "seq"), None, None, None, None, "tp"),
        ),
        check_vma=False,
    )
```

```python
import functools
import math

import jax
import jax.numpy as jnp
from jax import lax
from jax.experimental import pallas as pl
from jax.experimental.pallas import tpu as pltpu
from jax.sharding import PartitionSpec as P

ANY = pl.BlockSpec(memory_space=pl.ANY)
HBM = pl.BlockSpec(memory_space=pltpu.HBM)
SMEM = pl.BlockSpec(memory_space=pltpu.SMEM)
VMEM = pl.BlockSpec(memory_space=pltpu.VMEM)
MASKED = -1e30


def in_hbm(array):
    return pltpu.with_memory_space_constraint(array, pltpu.HBM)


def send_kernel(hidden, w_key, w_value, w_out, h_out, sems):
    group = lax.axis_index("groups")
    me = lax.axis_index("seq")
    rows, depth = h_out.shape[1:]
    for chosen, weight in ((0, w_key), (1, w_value)):

        @pl.when(group == chosen)
        def _():
            pltpu.make_async_copy(weight, w_out, sems.at[0]).start()

    first = me + 1 - 2 * lax.rem(me, 2)
    copies = []
    for i, block in enumerate((first, lax.rem(first + 2, 4))):
        source = hidden.at[
            0,
            pl.ds(pl.multiple_of(lax.axis_index("tp") * rows, rows), rows),
            pl.ds(pl.multiple_of(block * depth, depth), depth),
        ]
        copies.append(pltpu.make_async_copy(source, h_out.at[i], sems.at[1 + i]))
        copies[-1].start()
    pltpu.make_async_copy(w_key, w_out, sems.at[0]).wait()
    for copy in copies:
        copy.wait()


def pick_sent(hidden, w_key, w_value):
    h_shape = (2, hidden.shape[1] // 4, w_key.shape[0])
    return pl.pallas_call(
        send_kernel,
        out_shape=(
            jax.ShapeDtypeStruct(w_key.shape, jnp.bfloat16),
            jax.ShapeDtypeStruct(h_shape, jnp.bfloat16),
        ),
        in_specs=[ANY] * 3,
        out_specs=(VMEM, VMEM),
        scratch_shapes=[pltpu.SemaphoreType.DMA((3,))],
        compiler_params=pltpu.CompilerParams(vmem_limit_bytes=16 * 1024 * 1024),
        name="pick_sent",
    )(in_hbm(hidden), in_hbm(w_key), in_hbm(w_value))


def gate_kernel(*refs):
    pass


def gate(arrays, first=(), pinned=0, cost=1):
    return pl.pallas_call(
        gate_kernel,
        out_shape=tuple(jax.ShapeDtypeStruct(one.shape, one.dtype) for one in arrays),
        in_specs=[ANY] * (len(arrays) + len(first)),
        out_specs=(ANY,) * len(arrays),
        input_output_aliases={i: i for i in range(len(arrays))},
        compiler_params=pltpu.CompilerParams(vmem_limit_bytes=1024 * 1024),
        cost_estimate=pl.CostEstimate(flops=cost, bytes_accessed=1, transcendentals=0),
        name="gate",
    )(*(in_hbm(one) for one in arrays[:pinned]), *arrays[pinned:], *first)


def docs_kernel(by_owner, request_docs, store_keys, store_values, *rest):
    *outs, picks, sems = rest
    me = lax.axis_index("seq")
    requests, doc_count = request_docs.shape
    slots = store_keys.shape[0]
    capacity = slots // 2

    def one_request(r, carry):
        for c in range(capacity):
            picks[r, c] = 0

        def one_doc(j, count):
            doc = request_docs[r, j]
            mine = lax.div(doc, slots) == me

            @pl.when(mine)
            def _():
                picks[r, jnp.minimum(count, capacity - 1)] = lax.rem(doc, slots)

            return count + mine.astype(jnp.int32)

        lax.fori_loop(0, doc_count, one_doc, jnp.int32(0), unroll=True)
        return carry

    lax.fori_loop(0, requests, one_request, 0)

    def send(r, out, sem):
        for c in range(capacity):
            slot = picks[r, c]
            pltpu.make_async_copy(store_keys.at[slot], out.at[c, 0], sem).start()
            pltpu.make_async_copy(store_values.at[slot], out.at[c, 1], sem).start()

    if by_owner:

        def one_send(r, carry):
            send(r, outs[0].at[r], sems.at[0])
            return carry

        lax.fori_loop(0, requests, one_send, 0)
    else:
        for i, out in enumerate(outs):
            send(lax.bitwise_xor(me, i + 1), out, sems.at[i])
    for i, out in enumerate(outs):
        pltpu.make_async_copy(out, out, sems.at[i]).wait()


def pick_docs(request_docs, store_keys, store_values, by_owner):
    requests = request_docs.shape[0]
    capacity = store_keys.shape[0] // 2
    one = (capacity, 2) + store_keys.shape[1:]
    shapes = ((requests,) + one,) if by_owner else (one,) * (requests - 1)
    return pl.pallas_call(
        functools.partial(docs_kernel, by_owner),
        out_shape=tuple(jax.ShapeDtypeStruct(one, jnp.bfloat16) for one in shapes),
        in_specs=[SMEM, ANY, ANY],
        out_specs=(VMEM,) * len(shapes),
        scratch_shapes=[
            pltpu.SMEM((requests, capacity), jnp.int32),
            pltpu.SemaphoreType.DMA((len(shapes),)),
        ],
        compiler_params=pltpu.CompilerParams(vmem_limit_bytes=16 * 1024 * 1024),
        name="pick_docs",
    )(request_docs, in_hbm(store_keys), in_hbm(store_values))


def near_kernel(hidden, w_key, w_value, _, total, w, h, sems):
    depth, width = w_key.shape
    start = pl.multiple_of(lax.axis_index("seq") * depth, depth)
    copies = [
        pltpu.make_async_copy(w_key, w.at[:, pl.ds(0, width)], sems.at[0]),
        pltpu.make_async_copy(w_value, w.at[:, pl.ds(width, width)], sems.at[1]),
        pltpu.make_async_copy(hidden.at[0, :, pl.ds(start, depth)], h, sems.at[2]),
    ]
    for copy in copies:
        copy.start()
    for copy in copies:
        copy.wait()
    total[...] = jnp.dot(h[...], w[...], preferred_element_type=jnp.float32)


def lay_quarters(quarters, block, rows, copy):
    piece = rows.shape[0] // len(quarters)
    for k, quarter in enumerate(quarters):
        start = pl.multiple_of(lax.bitwise_xor(lax.axis_index("tp"), k) * piece, piece)
        copy(quarter.at[block], rows.at[pl.ds(start, piece)])


def neighbour_kernel(w_key, w_value, *rest):
    *quarters, total, w, n, sems = rest
    width = w_key.shape[1]
    copies = []

    def copy(source, target):
        copies.append(pltpu.make_async_copy(source, target, sems.at[len(copies)]))
        copies[-1].start()

    for i, held in enumerate((w_key, w_value)):
        copy(held, w.at[:, pl.ds(i * width, width)])
    lay_quarters(quarters, 0, n, copy)
    for one in copies:
        one.wait()
    total[...] = jnp.dot(n[...], w[...], preferred_element_type=jnp.float32)


def far_kernel(hidden, w_far, w_swapped, near, neighbour, *rest):
    *quarters, own, part_k, part_v, w, h, n, sems = rest
    group = lax.axis_index("groups")
    depth, width = w_far.shape
    copies = []

    def copy(source, target):
        copies.append(pltpu.make_async_copy(source, target, sems.at[len(copies)]))
        copies[-1].start()

    for held, place in ((w_far, group), (w_swapped, 1 - group)):
        copy(held, w.at[:, pl.ds(pl.multiple_of(place * width, width), width)])
    start = pl.multiple_of(lax.rem(lax.axis_index("seq") + 2, 4) * depth, depth)
    copy(hidden.at[0, :, pl.ds(start, depth)], h)
    lay_quarters(quarters, 1, n, copy)
    for one in copies:
        one.wait()
    own[...] = near[...] + jnp.dot(h[...], w[...], preferred_element_type=jnp.float32)
    total = neighbour[...] + jnp.dot(n[...], w[...], preferred_element_type=jnp.float32)
    part_k[...] = total[:, :width].astype(part_k.dtype)
    part_v[...] = total[:, width:].astype(part_v.dtype)


def project(hidden, w_key, w_value, w_far, w_swapped, quarters, first):
    depth, width = w_key.shape
    rows = hidden.shape[1]
    sums = jax.ShapeDtypeStruct((rows, 2 * width), jnp.float32)
    w_scratch = pltpu.VMEM((depth, 2 * width), jnp.bfloat16)
    h_scratch = pltpu.VMEM((rows, depth), jnp.bfloat16)
    limit = pltpu.CompilerParams(vmem_limit_bytes=16 * 1024 * 1024)
    cheap = pl.CostEstimate(flops=1, bytes_accessed=1, transcendentals=0)
    w_key, w_value = in_hbm(w_key), in_hbm(w_value)
    near = pl.pallas_call(
        near_kernel,
        out_shape=sums,
        in_specs=[ANY] * 4,
        out_specs=VMEM,
        scratch_shapes=[w_scratch, h_scratch, pltpu.SemaphoreType.DMA((3,))],
        compiler_params=limit,
        cost_estimate=pl.CostEstimate(flops=10**10, bytes_accessed=1, transcendentals=0),
        name="project_near",
    )(hidden, w_key, w_value, first)
    neighbour = pl.pallas_call(
        neighbour_kernel,
        out_shape=sums,
        in_specs=[ANY] * (2 + len(quarters)),
        out_specs=VMEM,
        scratch_shapes=[
            w_scratch,
            h_scratch,
            pltpu.SemaphoreType.DMA((2 + len(quarters),)),
        ],
        compiler_params=limit,
        cost_estimate=cheap,
        name="project_neighbour",
    )(w_key, w_value, *quarters)
    return pl.pallas_call(
        far_kernel,
        out_shape=(sums,) + (jax.ShapeDtypeStruct((rows, width), jnp.bfloat16),) * 2,
        in_specs=[ANY] * 3 + [VMEM] * 2 + [ANY] * len(quarters),
        out_specs=(VMEM,) * 3,
        scratch_shapes=[
            w_scratch,
            h_scratch,
            h_scratch,
            pltpu.SemaphoreType.DMA((3 + len(quarters),)),
        ],
        compiler_params=limit,
        cost_estimate=cheap,
        name="project_far",
    )(hidden, w_far, w_swapped, near, neighbour, *quarters)


def plan_kernel(
    capacity, slots, request_docs, doc_lengths, rows, queries, q, held, spare, key_bias, row_place, key_place,
    slot_row, counts
):
    head_dim = q.shape[1] // 2
    heads = queries.shape[2] // head_dim
    block_rows = 4 * rows.shape[0]
    scale = math.log2(math.e) / math.sqrt(head_dim)
    for b in range(queries.shape[1] // block_rows):
        for h in range(heads):
            here = queries[0, b * block_rows : (b + 1) * block_rows, h * head_dim : (h + 1) * head_dim]
            here = here.astype(jnp.float32) * scale
            high = here.astype(jnp.bfloat16)
            place = slice((b * heads + h) * block_rows, (b * heads + h + 1) * block_rows)
            q[place, :head_dim] = high
            q[place, head_dim:] = (here - high.astype(jnp.float32)).astype(jnp.bfloat16)
    me = lax.axis_index("seq")
    per_doc, _, doc_count = rows.shape
    doc_len = held.shape[0] // doc_count
    row_count = row_place.shape[0]
    docs = lax.broadcasted_iota(jnp.int32, (1, doc_count), 1)
    lengths = jnp.zeros((1, doc_count), jnp.int32)
    places = jnp.zeros((1, doc_count), jnp.int32)
    for o in range(counts.shape[0]):
        counts[o] = 0
    for j in range(doc_count):
        doc = request_docs[me, j]
        owner = lax.div(doc, slots)
        rank = counts[owner]
        counts[owner] = rank + 1
        lengths = jnp.where(docs == j, doc_lengths[doc], lengths)
        places = jnp.where(docs == j, owner * capacity + rank, places)
    slot = lax.broadcasted_iota(jnp.int32, (doc_len, doc_count), 0)
    used = slot < lengths
    for i in range(per_doc):
        used &= slot != rows[i]
    used = used.astype(jnp.float32)
    first = jnp.min(jnp.where(used > 0, slot, doc_len), axis=0, keepdims=True)
    firsts = (slot == first).astype(jnp.bfloat16)
    eye = lax.broadcasted_iota(jnp.int32, (doc_count, doc_count), 0) == docs
    across = (((1,), (1,)), ((), ()))

    def turned(columns):
        return lax.dot_general(
            eye.astype(jnp.bfloat16), columns, across, preferred_element_type=jnp.float32
        )

    bias = jnp.where(turned(used.astype(jnp.bfloat16)) > 0, 0.0, MASKED)
    firsts = turned(firsts)
    doc = lax.broadcasted_iota(jnp.int32, (doc_count, 1), 0)
    for j in range(doc_count):
        part = slice(j * doc_len, (j + 1) * doc_len)
        held[part, :] = jnp.broadcast_to(used[:, j : j + 1], (doc_len, held.shape[1])).astype(
            held.dtype
        )
        key_bias[:, part] = bias[j : j + 1, :]
        spare[:, part] = jnp.where(doc == j, firsts, 0.0).astype(spare.dtype)
    row = lax.broadcasted_iota(jnp.int32, (row_count, doc_count), 0)
    start = per_doc * lax.broadcasted_iota(jnp.int32, (row_count, doc_count), 1)
    of_doc = (row >= start) & (row < start + per_doc)
    nth = jnp.sum(jnp.where(of_doc, row - start, 0), axis=1, keepdims=True)
    chosen = jnp.zeros((row_count, doc_count), jnp.int32)
    for i in range(per_doc):
        chosen = jnp.where(nth == i, rows[i], chosen)
    chosen = jnp.where(of_doc, chosen + doc_len * docs, 0)
    column = jnp.sum(chosen, axis=1, keepdims=True)
    goes = nth + per_doc * jnp.sum(jnp.where(of_doc, places, 0), axis=1, keepdims=True)
    row_place[...] = column
    square = (row_count, row_count)
    same = lax.broadcasted_iota(jnp.int32, square, 0) == lax.broadcasted_iota(jnp.int32, square, 1)
    key_place[...] = jnp.sum(jnp.where(same, column, 0), axis=0, keepdims=True)
    slot_row[...] = jnp.sum(jnp.where(same, goes, 0), axis=0, keepdims=True)


def plan(request_docs, doc_lengths, recompute_rows, queries, slots, head_dim, doc_len):
    _, doc_count, per_doc = recompute_rows.shape
    rows = doc_count * per_doc
    context = doc_count * doc_len
    shapes = (
        ((rows * queries.shape[2] // head_dim, 2 * head_dim), jnp.bfloat16),
        ((context, head_dim), jnp.bfloat16),
        ((doc_count, context), jnp.bfloat16),
        ((1, context), jnp.float32),
        ((rows, 1), jnp.int32),
        ((1, rows), jnp.int32),
        ((1, rows), jnp.int32),
    )
    return pl.pallas_call(
        functools.partial(plan_kernel, slots // 2, slots),
        out_shape=tuple(jax.ShapeDtypeStruct(*one) for one in shapes),
        in_specs=[SMEM, SMEM, VMEM, VMEM],
        out_specs=(VMEM,) * len(shapes),
        scratch_shapes=[pltpu.SMEM((request_docs.shape[0],), jnp.int32)],
        compiler_params=pltpu.CompilerParams(vmem_limit_bytes=16 * 1024 * 1024),
        name="plan",
    )(request_docs, doc_lengths, jnp.transpose(recompute_rows, (2, 0, 1)), queries)


def finish_kernel(own, arrived_k, arrived_v, slot_row, fresh, outgoing):
    arrived = jnp.concatenate([arrived_k[...], arrived_v[...]], axis=1)
    total = (own[...] + arrived.astype(jnp.float32)).astype(jnp.bfloat16)
    fresh[...] = total
    slots = lax.broadcasted_iota(jnp.int32, (outgoing.shape[0], 1), 0)
    pick = (slots == slot_row[...]).astype(jnp.bfloat16)
    outgoing[...] = jnp.dot(pick, total, preferred_element_type=jnp.float32).astype(jnp.bfloat16)


def finish(own, arrived, slot_row, slots):
    shapes = (own.shape, (slots, own.shape[1]))
    return pl.pallas_call(
        finish_kernel,
        out_shape=tuple(jax.ShapeDtypeStruct(one, jnp.bfloat16) for one in shapes),
        in_specs=[VMEM] * 4,
        out_specs=(VMEM, VMEM),
        compiler_params=pltpu.CompilerParams(vmem_limit_bytes=16 * 1024 * 1024),
        name="finish",
    )(own, *arrived, slot_row)


def attend_kernel(
    by_owner, request_docs, q, fresh, held, spare, key_bias, row_place, key_place, *rest
):
    sources, (mixed, keys, values, counts, sems) = rest[:-5], rest[-5:]
    me = lax.axis_index("seq")
    doc_count = request_docs.shape[1]
    head_dim = keys.shape[1] // 2
    doc_len = keys.shape[0] // doc_count
    owners = request_docs.shape[0]
    slots = sources[0].shape[0] if not by_owner else 2 * sources[0].shape[1]
    step = doc_count // sems.shape[1]
    blocks = doc_count // step
    block_rows = mixed.shape[1] // blocks
    block_keys = step * doc_len
    heads = mixed.shape[2] // head_dim
    left = pl.ds(0, head_dim)

    for o in range(owners):
        counts[o] = 0

    def one_doc(j, carry):
        doc = request_docs[me, j]
        owner = lax.div(doc, slots)
        rank = counts[owner]
        counts[owner] = rank + 1
        place = pl.ds(pl.multiple_of(j * doc_len, doc_len), doc_len)
        block = lax.div(j, step)

        def fetch(key_source, value_source):
            pltpu.make_async_copy(key_source, keys.at[place, left], sems.at[0, block]).start()
            pltpu.make_async_copy(value_source, values.at[place, left], sems.at[1, block]).start()

        if by_owner:
            fetch(sources[0].at[owner, rank, 0], sources[0].at[owner, rank, 1])
        else:
            away = lax.bitwise_xor(me, owner)

            @pl.when(away == 0)
            def _():
                slot = lax.rem(doc, slots)
                fetch(sources[0].at[slot], sources[1].at[slot])

            for k, source in zip((2, 3, 1), sources[2:]):

                @pl.when(away == k)
                def _():
                    fetch(source.at[rank, 0], source.at[rank, 1])

        return carry

    lax.fori_loop(0, doc_count, one_doc, 0, unroll=True)

    def assemble(b):
        block = pl.ds(b * block_keys, block_keys)
        for i, context in enumerate((keys, values)):
            pltpu.make_async_copy(
                context.at[block, left], context.at[block, left], sems.at[i, b]
            ).wait()
        block = slice(b * block_keys, (b + 1) * block_keys)
        spares = jnp.dot(
            spare[:, block], keys[block, :head_dim], preferred_element_type=jnp.float32
        ).astype(jnp.bfloat16)
        for j in range(b * step, (b + 1) * step):
            place = slice(j * doc_len, (j + 1) * doc_len)
            used = held[place, :]
            key = jnp.where(used > 0, keys[place, :head_dim], spares[j : j + 1, :])
            keys[place, :head_dim] = key
            keys[place, head_dim:] = key
            values[place, :head_dim] = values[place, :head_dim] * used
            values[place, head_dim:] = used

    fresh_k = jnp.concatenate([fresh[:, :head_dim]] * 2, axis=1)
    fresh_v = jnp.concatenate([fresh[:, head_dim:], jnp.ones_like(fresh[:, head_dim:])], axis=1)
    slot_place = lax.broadcasted_iota(jnp.int32, (1, block_keys), 1)
    contract_last = (((1,), (1,)), ((), ()))
    assemble(0)
    for b in range(blocks):
        if b + 1 < blocks:
            assemble(b + 1)
        rows = slice(b * block_rows, (b + 1) * block_rows)
        q_here = q[b * heads * block_rows : (b + 1) * heads * block_rows, :]
        own_place = row_place[rows, :]

        def scores(some_keys):
            return lax.dot_general(
                q_here, some_keys, contract_last, preferred_element_type=jnp.float32
            )

        def masked(some_keys, allowed):
            shape = (heads, block_rows, some_keys.shape[0])
            kept = jnp.where(allowed[None], scores(some_keys).reshape(shape), MASKED)
            return kept.reshape(heads * block_rows, some_keys.shape[0])

        chunks, sides = [], []
        for c in range(b):
            part = slice(c * block_keys, (c + 1) * block_keys)
            chunks.append(scores(keys[part, :]))
            sides.append(values[part, :])
        part = slice(b * block_keys, (b + 1) * block_keys)
        allowed = (slot_place + b * block_keys <= own_place) & (key_bias[:, part] == 0)
        chunks.append(masked(keys[part, :], allowed))
        sides.append(values[part, :])
        chunks.append(masked(fresh_k, key_place[...] <= own_place))
        sides.append(fresh_v)
        row_max = functools.reduce(
            jnp.maximum, [jnp.max(one, axis=1, keepdims=True) for one in chunks]
        )
        total = jnp.zeros((heads * block_rows, 2 * head_dim), jnp.float32)
        for one, side in zip(chunks, sides):
            powers = jnp.exp2(one - row_max).astype(jnp.bfloat16)
            total += jnp.dot(powers, side, preferred_element_type=jnp.float32)
        result = (total[:, :head_dim] / total[:, head_dim:]).astype(mixed.dtype)
        for h in range(heads):
            mixed[0, rows, h * head_dim : (h + 1) * head_dim] = result[
                h * block_rows : (h + 1) * block_rows
            ]


def attend(
    shape, request_docs, q, fresh, held, spare, key_bias, row_place, key_place, sources, by_owner
):
    context, head_dim = held.shape
    return pl.pallas_call(
        functools.partial(attend_kernel, by_owner),
        out_shape=jax.ShapeDtypeStruct(shape, jnp.bfloat16),
        in_specs=[SMEM] + [VMEM] * 7 + [ANY] * len(sources),
        out_specs=VMEM,
        scratch_shapes=[
            pltpu.VMEM((context, 2 * head_dim), jnp.bfloat16),
            pltpu.VMEM((context, 2 * head_dim), jnp.bfloat16),
            pltpu.SMEM((request_docs.shape[0],), jnp.int32),
            pltpu.SemaphoreType.DMA((2, 4)),
        ],
        compiler_params=pltpu.CompilerParams(vmem_limit_bytes=32 * 1024 * 1024),
        name="attend",
    )(
        request_docs,
        q,
        fresh,
        held,
        spare,
        key_bias,
        row_place,
        key_place,
        *(in_hbm(one) for one in sources[:2]),
        *sources[2:],
    )


def shards(
    pairs,
    hidden,
    queries,
    w_key,
    w_value,
    store_keys,
    store_values,
    request_docs,
    doc_lengths,
    recompute_rows,
):
    seq_count = lax.axis_size("seq")
    slot_count, doc_len, head_dim = store_keys.shape
    capacity = slot_count // 2
    per_doc = recompute_rows.shape[2]

    if pairs:
        def swap(array, axis, apart):
            count = lax.axis_size(axis)
            return lax.ppermute(array, axis, [(i, i ^ apart) for i in range(count)])

        w_send, h_send = pick_sent(hidden, w_key, w_value)
        w_far = swap(w_send, "seq", 2)
        h_mine = swap(h_send, "seq", 1)
        doc_1, doc_2, doc_3 = pick_docs(request_docs, store_keys, store_values, False)
        (h_mine,) = gate((h_mine,), (doc_1,), cost=8000000000)
        h_chip = swap(h_mine, "tp", 2)
        h_core = swap(h_mine, "tp", 1)
        doc_2, doc_3, w_far = gate((doc_2, doc_3, w_far), cost=8000000000)
        w_swapped = swap(w_far, "groups", 1)
        doc_1 = swap(doc_1, "seq", 1)
        docs = (swap(doc_2, "seq", 2), swap(doc_3, "seq", 3), doc_1)
        quarters = (h_mine, h_core, h_chip, swap(h_chip, "tp", 1))
        own, *parts = project(hidden, w_key, w_value, w_far, w_swapped, quarters, doc_1)
        arrived = [swap(one, "seq", 1) for one in parts]
        sources = (store_keys, store_values, *docs)
    else:
        (docs,) = pick_docs(request_docs, store_keys, store_values, True)
        sources = (lax.all_to_all(docs, "seq", split_axis=0, concat_axis=0, tiled=True),)
        weights = lax.all_gather(
            jnp.concatenate([w_key, w_value], axis=1), "seq", axis=0, tiled=True
        )
        own = jnp.dot(hidden[0], weights, preferred_element_type=jnp.float32)
        arrived = [jnp.zeros((own.shape[0], head_dim), jnp.bfloat16)] * 2

    q, held, spare, key_bias, row_place, key_place, slot_row = plan(
        request_docs, doc_lengths, recompute_rows, queries, slot_count, head_dim, doc_len
    )
    fresh, outgoing = finish(own, arrived, slot_row, seq_count * capacity * per_doc)
    mixed = attend(
        queries.shape,
        request_docs,
        q,
        fresh,
        held,
        spare,
        key_bias,
        row_place,
        key_place,
        sources,
        not pairs,
    )

    outgoing = outgoing.reshape(seq_count, capacity * per_doc, 2 * head_dim)
    returned = lax.all_to_all(outgoing, "seq", split_axis=0, concat_axis=0, tiled=True)
    returned = returned.reshape(seq_count, capacity, per_doc, 2, head_dim)
    return (mixed, returned[None])


def solution(mesh):
    pairs = mesh.shape["seq"] == 4 and mesh.shape["groups"] == 2 and mesh.shape["tp"] == 4
    return jax.shard_map(
        functools.partial(shards, pairs),
        mesh=mesh,
        in_specs=(
            P(("groups", "seq"), None, None),
            P(("groups", "seq"), None, "tp"),
            P("seq", "tp"),
            P("seq", "tp"),
            P(("groups", "seq"), None, "tp"),
            P(("groups", "seq"), None, "tp"),
            P("groups", None),
            P("groups"),
            P(("groups", "seq"), None, None),
        ),
        out_specs=(
            P(("groups", "seq"), None, "tp"),
            P(("groups", "seq"), None, None, None, None, "tp"),
        ),
        check_vma=False,
    )
```

```python
import functools
import math

import jax
import jax.numpy as jnp
from jax import lax
from jax.experimental import pallas as pl
from jax.experimental.pallas import tpu as pltpu
from jax.sharding import PartitionSpec as P

ANY = pl.BlockSpec(memory_space=pl.ANY)
HBM = pl.BlockSpec(memory_space=pltpu.HBM)
SMEM = pl.BlockSpec(memory_space=pltpu.SMEM)
VMEM = pl.BlockSpec(memory_space=pltpu.VMEM)
MASKED = -1e30


def in_hbm(array):
    return pltpu.with_memory_space_constraint(array, pltpu.HBM)


def send_kernel(hidden, w_key, w_value, w_first, w_second, h_out, sems):
    group = lax.axis_index("groups")
    me = lax.axis_index("seq")
    rows, depth = h_out.shape[1:]
    for chosen, weight in ((0, w_key), (1, w_value)):

        @pl.when(group == chosen)
        def _():
            for i, out in enumerate((w_first, w_second)):
                half = weight.at[pl.ds(i * out.shape[0], out.shape[0])]
                pltpu.make_async_copy(half, out, sems.at[i]).start()

    first = me + 1 - 2 * lax.rem(me, 2)
    copies = []
    for i, block in enumerate((first, lax.rem(first + 2, 4))):
        source = hidden.at[
            0,
            pl.ds(pl.multiple_of(lax.axis_index("tp") * rows, rows), rows),
            pl.ds(pl.multiple_of(block * depth, depth), depth),
        ]
        copies.append(pltpu.make_async_copy(source, h_out.at[i], sems.at[2 + i]))
        copies[-1].start()
    for i, out in enumerate((w_first, w_second)):
        pltpu.make_async_copy(w_key.at[pl.ds(0, out.shape[0])], out, sems.at[i]).wait()
    for copy in copies:
        copy.wait()


def pick_sent(hidden, w_key, w_value):
    h_shape = (2, hidden.shape[1] // 4, w_key.shape[0])
    half = jax.ShapeDtypeStruct((w_key.shape[0] // 2, w_key.shape[1]), jnp.bfloat16)
    return pl.pallas_call(
        send_kernel,
        out_shape=(
            half,
            half,
            jax.ShapeDtypeStruct(h_shape, jnp.bfloat16),
        ),
        in_specs=[ANY] * 3,
        out_specs=(VMEM,) * 3,
        scratch_shapes=[pltpu.SemaphoreType.DMA((4,))],
        compiler_params=pltpu.CompilerParams(vmem_limit_bytes=16 * 1024 * 1024),
        name="pick_sent",
    )(in_hbm(hidden), in_hbm(w_key), in_hbm(w_value))


def gate_kernel(*refs):
    pass


def gate(arrays, first=(), pinned=0, cost=1):
    return pl.pallas_call(
        gate_kernel,
        out_shape=tuple(jax.ShapeDtypeStruct(one.shape, one.dtype) for one in arrays),
        in_specs=[ANY] * (len(arrays) + len(first)),
        out_specs=(ANY,) * len(arrays),
        input_output_aliases={i: i for i in range(len(arrays))},
        compiler_params=pltpu.CompilerParams(vmem_limit_bytes=1024 * 1024),
        cost_estimate=pl.CostEstimate(flops=cost, bytes_accessed=1, transcendentals=0),
        name="gate",
    )(*(in_hbm(one) for one in arrays[:pinned]), *arrays[pinned:], *first)


def docs_kernel(by_owner, request_docs, store_keys, store_values, *rest):
    *outs, picks, sems = rest
    me = lax.axis_index("seq")
    requests, doc_count = request_docs.shape
    slots = store_keys.shape[0]
    capacity = slots // 2

    def one_request(r, carry):
        for c in range(capacity):
            picks[r, c] = 0

        def one_doc(j, count):
            doc = request_docs[r, j]
            mine = lax.div(doc, slots) == me

            @pl.when(mine)
            def _():
                picks[r, jnp.minimum(count, capacity - 1)] = lax.rem(doc, slots)

            return count + mine.astype(jnp.int32)

        lax.fori_loop(0, doc_count, one_doc, jnp.int32(0), unroll=True)
        return carry

    lax.fori_loop(0, requests, one_request, 0)

    def send(r, out, sem):
        for c in range(capacity):
            slot = picks[r, c]
            pltpu.make_async_copy(store_keys.at[slot], out.at[c, 0], sem).start()
            pltpu.make_async_copy(store_values.at[slot], out.at[c, 1], sem).start()

    if by_owner:

        def one_send(r, carry):
            send(r, outs[0].at[r], sems.at[0])
            return carry

        lax.fori_loop(0, requests, one_send, 0)
    else:
        for i, out in enumerate(outs):
            send(lax.bitwise_xor(me, i + 1), out, sems.at[i])
    for i, out in enumerate(outs):
        pltpu.make_async_copy(out, out, sems.at[i]).wait()


def pick_docs(request_docs, store_keys, store_values, by_owner):
    requests = request_docs.shape[0]
    capacity = store_keys.shape[0] // 2
    one = (capacity, 2) + store_keys.shape[1:]
    shapes = ((requests,) + one,) if by_owner else (one,) * (requests - 1)
    return pl.pallas_call(
        functools.partial(docs_kernel, by_owner),
        out_shape=tuple(jax.ShapeDtypeStruct(one, jnp.bfloat16) for one in shapes),
        in_specs=[SMEM, ANY, ANY],
        out_specs=(VMEM,) * len(shapes),
        scratch_shapes=[
            pltpu.SMEM((requests, capacity), jnp.int32),
            pltpu.SemaphoreType.DMA((len(shapes),)),
        ],
        compiler_params=pltpu.CompilerParams(vmem_limit_bytes=16 * 1024 * 1024),
        name="pick_docs",
    )(request_docs, in_hbm(store_keys), in_hbm(store_values))


def near_kernel(hidden, w_key, w_value, _, total, w, h, sems):
    depth, width = w_key.shape
    start = pl.multiple_of(lax.axis_index("seq") * depth, depth)
    copies = [
        pltpu.make_async_copy(w_key, w.at[:, pl.ds(0, width)], sems.at[0]),
        pltpu.make_async_copy(w_value, w.at[:, pl.ds(width, width)], sems.at[1]),
        pltpu.make_async_copy(hidden.at[0, :, pl.ds(start, depth)], h, sems.at[2]),
    ]
    for copy in copies:
        copy.start()
    for copy in copies:
        copy.wait()
    total[...] = jnp.dot(h[...], w[...], preferred_element_type=jnp.float32)


def lay_quarters(quarters, block, rows, copy):
    piece = rows.shape[0] // len(quarters)
    for k, quarter in enumerate(quarters):
        start = pl.multiple_of(lax.bitwise_xor(lax.axis_index("tp"), k) * piece, piece)
        copy(quarter.at[block], rows.at[pl.ds(start, piece)])


def neighbour_kernel(w_key, w_value, *rest):
    *quarters, total, w, n, sems = rest
    width = w_key.shape[1]
    copies = []

    def copy(source, target):
        copies.append(pltpu.make_async_copy(source, target, sems.at[len(copies)]))
        copies[-1].start()

    for i, held in enumerate((w_key, w_value)):
        copy(held, w.at[:, pl.ds(i * width, width)])
    lay_quarters(quarters, 0, n, copy)
    for one in copies:
        one.wait()
    total[...] = jnp.dot(n[...], w[...], preferred_element_type=jnp.float32)


def far_kernel(hidden, w_far_0, w_far_1, w_swapped_0, w_swapped_1, near, neighbour, *rest):
    *quarters, own, part_k, part_v, w, h, n, sems = rest
    group = lax.axis_index("groups")
    half, width = w_far_0.shape
    depth = 2 * half
    copies = []

    def copy(source, target):
        copies.append(pltpu.make_async_copy(source, target, sems.at[len(copies)]))
        copies[-1].start()

    halves = ((w_far_0, w_far_1, group), (w_swapped_0, w_swapped_1, 1 - group))
    for first, second, place in halves:
        columns = pl.ds(pl.multiple_of(place * width, width), width)
        copy(first, w.at[pl.ds(0, half), columns])
        copy(second, w.at[pl.ds(half, half), columns])
    start = pl.multiple_of(lax.rem(lax.axis_index("seq") + 2, 4) * depth, depth)
    copy(hidden.at[0, :, pl.ds(start, depth)], h)
    lay_quarters(quarters, 1, n, copy)
    for one in copies:
        one.wait()
    own[...] = near[...] + jnp.dot(h[...], w[...], preferred_element_type=jnp.float32)
    total = neighbour[...] + jnp.dot(n[...], w[...], preferred_element_type=jnp.float32)
    part_k[...] = total[:, :width].astype(part_k.dtype)
    part_v[...] = total[:, width:].astype(part_v.dtype)


def project(hidden, w_key, w_value, w_far, w_swapped, quarters, first):
    depth, width = w_key.shape
    rows = hidden.shape[1]
    sums = jax.ShapeDtypeStruct((rows, 2 * width), jnp.float32)
    w_scratch = pltpu.VMEM((depth, 2 * width), jnp.bfloat16)
    h_scratch = pltpu.VMEM((rows, depth), jnp.bfloat16)
    limit = pltpu.CompilerParams(vmem_limit_bytes=16 * 1024 * 1024)
    cheap = pl.CostEstimate(flops=1, bytes_accessed=1, transcendentals=0)
    w_key, w_value = in_hbm(w_key), in_hbm(w_value)
    near = pl.pallas_call(
        near_kernel,
        out_shape=sums,
        in_specs=[ANY] * 4,
        out_specs=VMEM,
        scratch_shapes=[w_scratch, h_scratch, pltpu.SemaphoreType.DMA((3,))],
        compiler_params=limit,
        cost_estimate=pl.CostEstimate(flops=10**10, bytes_accessed=1, transcendentals=0),
        name="project_near",
    )(hidden, w_key, w_value, first)
    neighbour = pl.pallas_call(
        neighbour_kernel,
        out_shape=sums,
        in_specs=[ANY] * (2 + len(quarters)),
        out_specs=VMEM,
        scratch_shapes=[
            w_scratch,
            h_scratch,
            pltpu.SemaphoreType.DMA((2 + len(quarters),)),
        ],
        compiler_params=limit,
        cost_estimate=cheap,
        name="project_neighbour",
    )(w_key, w_value, *quarters)
    return pl.pallas_call(
        far_kernel,
        out_shape=(sums,) + (jax.ShapeDtypeStruct((rows, width), jnp.bfloat16),) * 2,
        in_specs=[ANY] * 5 + [VMEM] * 2 + [ANY] * len(quarters),
        out_specs=(VMEM,) * 3,
        scratch_shapes=[
            w_scratch,
            h_scratch,
            h_scratch,
            pltpu.SemaphoreType.DMA((5 + len(quarters),)),
        ],
        compiler_params=limit,
        cost_estimate=cheap,
        name="project_far",
    )(hidden, *w_far, *w_swapped, near, neighbour, *quarters)


def plan_kernel(
    capacity, slots, request_docs, doc_lengths, rows, queries, q, held, spare, key_bias, row_place, key_place,
    slot_row, counts
):
    head_dim = q.shape[1] // 2
    heads = queries.shape[2] // head_dim
    block_rows = 4 * rows.shape[0]
    scale = math.log2(math.e) / math.sqrt(head_dim)
    for b in range(queries.shape[1] // block_rows):
        for h in range(heads):
            here = queries[0, b * block_rows : (b + 1) * block_rows, h * head_dim : (h + 1) * head_dim]
            here = here.astype(jnp.float32) * scale
            high = here.astype(jnp.bfloat16)
            place = slice((b * heads + h) * block_rows, (b * heads + h + 1) * block_rows)
            q[place, :head_dim] = high
            q[place, head_dim:] = (here - high.astype(jnp.float32)).astype(jnp.bfloat16)
    me = lax.axis_index("seq")
    per_doc, _, doc_count = rows.shape
    doc_len = held.shape[0] // doc_count
    row_count = row_place.shape[0]
    docs = lax.broadcasted_iota(jnp.int32, (1, doc_count), 1)
    lengths = jnp.zeros((1, doc_count), jnp.int32)
    places = jnp.zeros((1, doc_count), jnp.int32)
    for o in range(counts.shape[0]):
        counts[o] = 0
    for j in range(doc_count):
        doc = request_docs[me, j]
        owner = lax.div(doc, slots)
        rank = counts[owner]
        counts[owner] = rank + 1
        lengths = jnp.where(docs == j, doc_lengths[doc], lengths)
        places = jnp.where(docs == j, owner * capacity + rank, places)
    slot = lax.broadcasted_iota(jnp.int32, (doc_len, doc_count), 0)
    used = slot < lengths
    for i in range(per_doc):
        used &= slot != rows[i]
    used = used.astype(jnp.float32)
    first = jnp.min(jnp.where(used > 0, slot, doc_len), axis=0, keepdims=True)
    firsts = (slot == first).astype(jnp.bfloat16)
    eye = lax.broadcasted_iota(jnp.int32, (doc_count, doc_count), 0) == docs
    across = (((1,), (1,)), ((), ()))

    def turned(columns):
        return lax.dot_general(
            eye.astype(jnp.bfloat16), columns, across, preferred_element_type=jnp.float32
        )

    bias = jnp.where(turned(used.astype(jnp.bfloat16)) > 0, 0.0, MASKED)
    firsts = turned(firsts)
    doc = lax.broadcasted_iota(jnp.int32, (doc_count, 1), 0)
    for j in range(doc_count):
        part = slice(j * doc_len, (j + 1) * doc_len)
        held[part, :] = jnp.broadcast_to(used[:, j : j + 1], (doc_len, held.shape[1])).astype(
            held.dtype
        )
        key_bias[:, part] = bias[j : j + 1, :]
        spare[:, part] = jnp.where(doc == j, firsts, 0.0).astype(spare.dtype)
    row = lax.broadcasted_iota(jnp.int32, (row_count, doc_count), 0)
    start = per_doc * lax.broadcasted_iota(jnp.int32, (row_count, doc_count), 1)
    of_doc = (row >= start) & (row < start + per_doc)
    nth = jnp.sum(jnp.where(of_doc, row - start, 0), axis=1, keepdims=True)
    chosen = jnp.zeros((row_count, doc_count), jnp.int32)
    for i in range(per_doc):
        chosen = jnp.where(nth == i, rows[i], chosen)
    chosen = jnp.where(of_doc, chosen + doc_len * docs, 0)
    column = jnp.sum(chosen, axis=1, keepdims=True)
    goes = nth + per_doc * jnp.sum(jnp.where(of_doc, places, 0), axis=1, keepdims=True)
    row_place[...] = column
    square = (row_count, row_count)
    same = lax.broadcasted_iota(jnp.int32, square, 0) == lax.broadcasted_iota(jnp.int32, square, 1)
    key_place[...] = jnp.sum(jnp.where(same, column, 0), axis=0, keepdims=True)
    slot_row[...] = jnp.sum(jnp.where(same, goes, 0), axis=0, keepdims=True)


def plan(request_docs, doc_lengths, recompute_rows, queries, slots, head_dim, doc_len):
    _, doc_count, per_doc = recompute_rows.shape
    rows = doc_count * per_doc
    context = doc_count * doc_len
    shapes = (
        ((rows * queries.shape[2] // head_dim, 2 * head_dim), jnp.bfloat16),
        ((context, head_dim), jnp.bfloat16),
        ((doc_count, context), jnp.bfloat16),
        ((1, context), jnp.float32),
        ((rows, 1), jnp.int32),
        ((1, rows), jnp.int32),
        ((1, rows), jnp.int32),
    )
    return pl.pallas_call(
        functools.partial(plan_kernel, slots // 2, slots),
        out_shape=tuple(jax.ShapeDtypeStruct(*one) for one in shapes),
        in_specs=[SMEM, SMEM, VMEM, VMEM],
        out_specs=(VMEM,) * len(shapes),
        scratch_shapes=[pltpu.SMEM((request_docs.shape[0],), jnp.int32)],
        compiler_params=pltpu.CompilerParams(vmem_limit_bytes=16 * 1024 * 1024),
        name="plan",
    )(request_docs, doc_lengths, jnp.transpose(recompute_rows, (2, 0, 1)), queries)


def finish_kernel(own, arrived_k, arrived_v, slot_row, fresh, outgoing):
    arrived = jnp.concatenate([arrived_k[...], arrived_v[...]], axis=1)
    total = (own[...] + arrived.astype(jnp.float32)).astype(jnp.bfloat16)
    fresh[...] = total
    slots = lax.broadcasted_iota(jnp.int32, (outgoing.shape[0], 1), 0)
    pick = (slots == slot_row[...]).astype(jnp.bfloat16)
    outgoing[...] = jnp.dot(pick, total, preferred_element_type=jnp.float32).astype(jnp.bfloat16)


def finish(own, arrived, slot_row, slots):
    shapes = (own.shape, (slots, own.shape[1]))
    return pl.pallas_call(
        finish_kernel,
        out_shape=tuple(jax.ShapeDtypeStruct(one, jnp.bfloat16) for one in shapes),
        in_specs=[VMEM] * 4,
        out_specs=(VMEM, VMEM),
        compiler_params=pltpu.CompilerParams(vmem_limit_bytes=16 * 1024 * 1024),
        name="finish",
    )(own, *arrived, slot_row)


def attend_kernel(
    by_owner, request_docs, q, fresh, held, spare, key_bias, row_place, key_place, *rest
):
    sources, (mixed, keys, values, counts, sems) = rest[:-5], rest[-5:]
    me = lax.axis_index("seq")
    doc_count = request_docs.shape[1]
    head_dim = keys.shape[1] // 2
    doc_len = keys.shape[0] // doc_count
    owners = request_docs.shape[0]
    slots = sources[0].shape[0] if not by_owner else 2 * sources[0].shape[1]
    step = doc_count // sems.shape[1]
    blocks = doc_count // step
    block_rows = mixed.shape[1] // blocks
    block_keys = step * doc_len
    heads = mixed.shape[2] // head_dim
    left = pl.ds(0, head_dim)

    for o in range(owners):
        counts[o] = 0

    def one_doc(j, carry):
        doc = request_docs[me, j]
        owner = lax.div(doc, slots)
        rank = counts[owner]
        counts[owner] = rank + 1
        place = pl.ds(pl.multiple_of(j * doc_len, doc_len), doc_len)
        block = lax.div(j, step)

        def fetch(key_source, value_source):
            pltpu.make_async_copy(key_source, keys.at[place, left], sems.at[0, block]).start()
            pltpu.make_async_copy(value_source, values.at[place, left], sems.at[1, block]).start()

        if by_owner:
            fetch(sources[0].at[owner, rank, 0], sources[0].at[owner, rank, 1])
        else:
            away = lax.bitwise_xor(me, owner)

            @pl.when(away == 0)
            def _():
                slot = lax.rem(doc, slots)
                fetch(sources[0].at[slot], sources[1].at[slot])

            for k, source in zip((2, 3, 1), sources[2:]):

                @pl.when(away == k)
                def _():
                    fetch(source.at[rank, 0], source.at[rank, 1])

        return carry

    lax.fori_loop(0, doc_count, one_doc, 0, unroll=True)

    def assemble(b):
        block = pl.ds(b * block_keys, block_keys)
        for i, context in enumerate((keys, values)):
            pltpu.make_async_copy(
                context.at[block, left], context.at[block, left], sems.at[i, b]
            ).wait()
        block = slice(b * block_keys, (b + 1) * block_keys)
        spares = jnp.dot(
            spare[:, block], keys[block, :head_dim], preferred_element_type=jnp.float32
        ).astype(jnp.bfloat16)
        for j in range(b * step, (b + 1) * step):
            place = slice(j * doc_len, (j + 1) * doc_len)
            used = held[place, :]
            key = jnp.where(used > 0, keys[place, :head_dim], spares[j : j + 1, :])
            keys[place, :head_dim] = key
            keys[place, head_dim:] = key
            values[place, :head_dim] = values[place, :head_dim] * used
            values[place, head_dim:] = used

    fresh_k = jnp.concatenate([fresh[:, :head_dim]] * 2, axis=1)
    fresh_v = jnp.concatenate([fresh[:, head_dim:], jnp.ones_like(fresh[:, head_dim:])], axis=1)
    slot_place = lax.broadcasted_iota(jnp.int32, (1, block_keys), 1)
    contract_last = (((1,), (1,)), ((), ()))
    assemble(0)
    for b in range(blocks):
        if b + 1 < blocks:
            assemble(b + 1)
        rows = slice(b * block_rows, (b + 1) * block_rows)
        q_here = q[b * heads * block_rows : (b + 1) * heads * block_rows, :]
        own_place = row_place[rows, :]

        def scores(some_keys):
            return lax.dot_general(
                q_here, some_keys, contract_last, preferred_element_type=jnp.float32
            )

        def masked(some_keys, allowed):
            shape = (heads, block_rows, some_keys.shape[0])
            kept = jnp.where(allowed[None], scores(some_keys).reshape(shape), MASKED)
            return kept.reshape(heads * block_rows, some_keys.shape[0])

        chunks, sides = [], []
        for c in range(b):
            part = slice(c * block_keys, (c + 1) * block_keys)
            chunks.append(scores(keys[part, :]))
            sides.append(values[part, :])
        part = slice(b * block_keys, (b + 1) * block_keys)
        allowed = (slot_place + b * block_keys <= own_place) & (key_bias[:, part] == 0)
        chunks.append(masked(keys[part, :], allowed))
        sides.append(values[part, :])
        chunks.append(masked(fresh_k, key_place[...] <= own_place))
        sides.append(fresh_v)
        row_max = functools.reduce(
            jnp.maximum, [jnp.max(one, axis=1, keepdims=True) for one in chunks]
        )
        total = jnp.zeros((heads * block_rows, 2 * head_dim), jnp.float32)
        for one, side in zip(chunks, sides):
            powers = jnp.exp2(one - row_max).astype(jnp.bfloat16)
            total += jnp.dot(powers, side, preferred_element_type=jnp.float32)
        result = (total[:, :head_dim] / total[:, head_dim:]).astype(mixed.dtype)
        for h in range(heads):
            mixed[0, rows, h * head_dim : (h + 1) * head_dim] = result[
                h * block_rows : (h + 1) * block_rows
            ]


def attend(
    shape, request_docs, q, fresh, held, spare, key_bias, row_place, key_place, sources, by_owner
):
    context, head_dim = held.shape
    return pl.pallas_call(
        functools.partial(attend_kernel, by_owner),
        out_shape=jax.ShapeDtypeStruct(shape, jnp.bfloat16),
        in_specs=[SMEM] + [VMEM] * 7 + [ANY] * len(sources),
        out_specs=VMEM,
        scratch_shapes=[
            pltpu.VMEM((context, 2 * head_dim), jnp.bfloat16),
            pltpu.VMEM((context, 2 * head_dim), jnp.bfloat16),
            pltpu.SMEM((request_docs.shape[0],), jnp.int32),
            pltpu.SemaphoreType.DMA((2, 4)),
        ],
        compiler_params=pltpu.CompilerParams(vmem_limit_bytes=32 * 1024 * 1024),
        name="attend",
    )(
        request_docs,
        q,
        fresh,
        held,
        spare,
        key_bias,
        row_place,
        key_place,
        *(in_hbm(one) for one in sources[:2]),
        *sources[2:],
    )


def shards(
    pairs,
    hidden,
    queries,
    w_key,
    w_value,
    store_keys,
    store_values,
    request_docs,
    doc_lengths,
    recompute_rows,
):
    seq_count = lax.axis_size("seq")
    slot_count, doc_len, head_dim = store_keys.shape
    capacity = slot_count // 2
    per_doc = recompute_rows.shape[2]

    if pairs:
        def swap(array, axis, apart):
            count = lax.axis_size(axis)
            return lax.ppermute(array, axis, [(i, i ^ apart) for i in range(count)])

        *w_send, h_send = pick_sent(hidden, w_key, w_value)
        w_far = [swap(half, "seq", 2) for half in w_send]
        h_mine = swap(h_send, "seq", 1)
        doc_1, doc_2, doc_3 = pick_docs(request_docs, store_keys, store_values, False)
        (h_mine,) = gate((h_mine,), (doc_1,), cost=8000000000)
        h_chip = swap(h_mine, "tp", 2)
        h_core = swap(h_mine, "tp", 1)
        w_swapped = [swap(w_far[0], "groups", 1)]
        doc_2, doc_3, w_far[1] = gate(
            (doc_2, doc_3, w_far[1]), (w_swapped[0],), cost=8 * 10**9
        )
        w_swapped.append(swap(w_far[1], "groups", 1))
        doc_1 = swap(doc_1, "seq", 1)
        docs = (swap(doc_2, "seq", 2), swap(doc_3, "seq", 3), doc_1)
        quarters = (h_mine, h_core, h_chip, swap(h_chip, "tp", 1))
        own, *parts = project(hidden, w_key, w_value, w_far, w_swapped, quarters, doc_1)
        arrived = [swap(one, "seq", 1) for one in parts]
        sources = (store_keys, store_values, *docs)
    else:
        (docs,) = pick_docs(request_docs, store_keys, store_values, True)
        sources = (lax.all_to_all(docs, "seq", split_axis=0, concat_axis=0, tiled=True),)
        weights = lax.all_gather(
            jnp.concatenate([w_key, w_value], axis=1), "seq", axis=0, tiled=True
        )
        own = jnp.dot(hidden[0], weights, preferred_element_type=jnp.float32)
        arrived = [jnp.zeros((own.shape[0], head_dim), jnp.bfloat16)] * 2

    q, held, spare, key_bias, row_place, key_place, slot_row = plan(
        request_docs, doc_lengths, recompute_rows, queries, slot_count, head_dim, doc_len
    )
    fresh, outgoing = finish(own, arrived, slot_row, seq_count * capacity * per_doc)
    mixed = attend(
        queries.shape,
        request_docs,
        q,
        fresh,
        held,
        spare,
        key_bias,
        row_place,
        key_place,
        sources,
        not pairs,
    )

    outgoing = outgoing.reshape(seq_count, capacity * per_doc, 2 * head_dim)
    returned = lax.all_to_all(outgoing, "seq", split_axis=0, concat_axis=0, tiled=True)
    returned = returned.reshape(seq_count, capacity, per_doc, 2, head_dim)
    return (mixed, returned[None])


def solution(mesh):
    pairs = mesh.shape["seq"] == 4 and mesh.shape["groups"] == 2 and mesh.shape["tp"] == 4
    return jax.shard_map(
        functools.partial(shards, pairs),
        mesh=mesh,
        in_specs=(
            P(("groups", "seq"), None, None),
            P(("groups", "seq"), None, "tp"),
            P("seq", "tp"),
            P("seq", "tp"),
            P(("groups", "seq"), None, "tp"),
            P(("groups", "seq"), None, "tp"),
            P("groups", None),
            P("groups"),
            P(("groups", "seq"), None, None),
        ),
        out_specs=(
            P(("groups", "seq"), None, "tp"),
            P(("groups", "seq"), None, None, None, None, "tp"),
        ),
        check_vma=False,
    )
```

```python
import functools
import math

import jax
import jax.numpy as jnp
from jax import lax
from jax.experimental import pallas as pl
from jax.experimental.pallas import tpu as pltpu
from jax.sharding import PartitionSpec as P

ANY = pl.BlockSpec(memory_space=pl.ANY)
HBM = pl.BlockSpec(memory_space=pltpu.HBM)
SMEM = pl.BlockSpec(memory_space=pltpu.SMEM)
VMEM = pl.BlockSpec(memory_space=pltpu.VMEM)
MASKED = -1e30


def in_hbm(array):
    return pltpu.with_memory_space_constraint(array, pltpu.HBM)


def send_kernel(hidden, w_key, w_value, w_out, h_out, sems):
    group = lax.axis_index("groups")
    me = lax.axis_index("seq")
    rows, depth = h_out.shape[1:]
    for chosen, weight in ((0, w_key), (1, w_value)):

        @pl.when(group == chosen)
        def _():
            pltpu.make_async_copy(weight, w_out, sems.at[0]).start()

    first = me + 1 - 2 * lax.rem(me, 2)
    copies = []
    for i, block in enumerate((first, lax.rem(first + 2, 4))):
        source = hidden.at[
            0,
            pl.ds(pl.multiple_of(lax.axis_index("tp") * rows, rows), rows),
            pl.ds(pl.multiple_of(block * depth, depth), depth),
        ]
        copies.append(pltpu.make_async_copy(source, h_out.at[i], sems.at[1 + i]))
        copies[-1].start()
    pltpu.make_async_copy(w_key, w_out, sems.at[0]).wait()
    for copy in copies:
        copy.wait()


def pick_sent(hidden, w_key, w_value):
    h_shape = (2, hidden.shape[1] // 4, w_key.shape[0])
    return pl.pallas_call(
        send_kernel,
        out_shape=(
            jax.ShapeDtypeStruct(w_key.shape, jnp.bfloat16),
            jax.ShapeDtypeStruct(h_shape, jnp.bfloat16),
        ),
        in_specs=[ANY] * 3,
        out_specs=(VMEM, VMEM),
        scratch_shapes=[pltpu.SemaphoreType.DMA((3,))],
        compiler_params=pltpu.CompilerParams(vmem_limit_bytes=16 * 1024 * 1024),
        name="pick_sent",
    )(in_hbm(hidden), in_hbm(w_key), in_hbm(w_value))


def gate_kernel(*refs):
    pass


def gate(arrays, first=(), pinned=0, cost=1):
    return pl.pallas_call(
        gate_kernel,
        out_shape=tuple(jax.ShapeDtypeStruct(one.shape, one.dtype) for one in arrays),
        in_specs=[ANY] * (len(arrays) + len(first)),
        out_specs=(ANY,) * len(arrays),
        input_output_aliases={i: i for i in range(len(arrays))},
        compiler_params=pltpu.CompilerParams(vmem_limit_bytes=1024 * 1024),
        cost_estimate=pl.CostEstimate(flops=cost, bytes_accessed=1, transcendentals=0),
        name="gate",
    )(*(in_hbm(one) for one in arrays[:pinned]), *arrays[pinned:], *first)


def docs_kernel(by_owner, request_docs, store_keys, store_values, *rest):
    *outs, picks, sems = rest
    me = lax.axis_index("seq")
    requests, doc_count = request_docs.shape
    slots = store_keys.shape[0]
    capacity = slots // 2

    def one_request(r, carry):
        for c in range(capacity):
            picks[r, c] = 0

        def one_doc(j, count):
            doc = request_docs[r, j]
            mine = lax.div(doc, slots) == me

            @pl.when(mine)
            def _():
                picks[r, jnp.minimum(count, capacity - 1)] = lax.rem(doc, slots)

            return count + mine.astype(jnp.int32)

        lax.fori_loop(0, doc_count, one_doc, jnp.int32(0), unroll=True)
        return carry

    lax.fori_loop(0, requests, one_request, 0)

    def send(r, out, sem):
        for c in range(capacity):
            slot = picks[r, c]
            pltpu.make_async_copy(store_keys.at[slot], out.at[c, 0], sem).start()
            pltpu.make_async_copy(store_values.at[slot], out.at[c, 1], sem).start()

    if by_owner:

        def one_send(r, carry):
            send(r, outs[0].at[r], sems.at[0])
            return carry

        lax.fori_loop(0, requests, one_send, 0)
    else:
        for i, out in enumerate(outs):
            send(lax.bitwise_xor(me, i + 1), out, sems.at[i])
    for i, out in enumerate(outs):
        pltpu.make_async_copy(out, out, sems.at[i]).wait()


def pick_docs(request_docs, store_keys, store_values, by_owner):
    requests = request_docs.shape[0]
    capacity = store_keys.shape[0] // 2
    one = (capacity, 2) + store_keys.shape[1:]
    shapes = ((requests,) + one,) if by_owner else (one,) * (requests - 1)
    return pl.pallas_call(
        functools.partial(docs_kernel, by_owner),
        out_shape=tuple(jax.ShapeDtypeStruct(one, jnp.bfloat16) for one in shapes),
        in_specs=[SMEM, ANY, ANY],
        out_specs=(VMEM,) * len(shapes),
        scratch_shapes=[
            pltpu.SMEM((requests, capacity), jnp.int32),
            pltpu.SemaphoreType.DMA((len(shapes),)),
        ],
        compiler_params=pltpu.CompilerParams(vmem_limit_bytes=16 * 1024 * 1024),
        name="pick_docs",
    )(request_docs, in_hbm(store_keys), in_hbm(store_values))


def near_kernel(hidden, w_key, w_value, _, total, w, h, sems):
    depth, width = w_key.shape
    start = pl.multiple_of(lax.axis_index("seq") * depth, depth)
    copies = [
        pltpu.make_async_copy(w_key, w.at[:, pl.ds(0, width)], sems.at[0]),
        pltpu.make_async_copy(w_value, w.at[:, pl.ds(width, width)], sems.at[1]),
        pltpu.make_async_copy(hidden.at[0, :, pl.ds(start, depth)], h, sems.at[2]),
    ]
    for copy in copies:
        copy.start()
    for copy in copies:
        copy.wait()
    total[...] = jnp.dot(h[...], w[...], preferred_element_type=jnp.float32)


def lay_quarters(quarters, block, rows, copy):
    piece = rows.shape[0] // len(quarters)
    for k, quarter in enumerate(quarters):
        start = pl.multiple_of(lax.bitwise_xor(lax.axis_index("tp"), k) * piece, piece)
        copy(quarter.at[block], rows.at[pl.ds(start, piece)])


def neighbour_kernel(w_key, w_value, *rest):
    *quarters, total, w, n, sems = rest
    width = w_key.shape[1]
    copies = []

    def copy(source, target):
        copies.append(pltpu.make_async_copy(source, target, sems.at[len(copies)]))
        copies[-1].start()

    for i, held in enumerate((w_key, w_value)):
        copy(held, w.at[:, pl.ds(i * width, width)])
    lay_quarters(quarters, 0, n, copy)
    for one in copies:
        one.wait()
    total[...] = jnp.dot(n[...], w[...], preferred_element_type=jnp.float32)


def far_kernel(hidden, w_far, w_swapped, near, neighbour, *rest):
    *quarters, own, part_k, part_v, w, h, n, sems = rest
    group = lax.axis_index("groups")
    depth, width = w_far.shape
    copies = []

    def copy(source, target):
        copies.append(pltpu.make_async_copy(source, target, sems.at[len(copies)]))
        copies[-1].start()

    for held, place in ((w_far, group), (w_swapped, 1 - group)):
        copy(held, w.at[:, pl.ds(pl.multiple_of(place * width, width), width)])
    start = pl.multiple_of(lax.rem(lax.axis_index("seq") + 2, 4) * depth, depth)
    copy(hidden.at[0, :, pl.ds(start, depth)], h)
    lay_quarters(quarters, 1, n, copy)
    for one in copies:
        one.wait()
    own[...] = near[...] + jnp.dot(h[...], w[...], preferred_element_type=jnp.float32)
    total = neighbour[...] + jnp.dot(n[...], w[...], preferred_element_type=jnp.float32)
    part_k[...] = total[:, :width].astype(part_k.dtype)
    part_v[...] = total[:, width:].astype(part_v.dtype)


def project(hidden, w_key, w_value, w_far, w_swapped, quarters, first):
    depth, width = w_key.shape
    rows = hidden.shape[1]
    sums = jax.ShapeDtypeStruct((rows, 2 * width), jnp.float32)
    w_scratch = pltpu.VMEM((depth, 2 * width), jnp.bfloat16)
    h_scratch = pltpu.VMEM((rows, depth), jnp.bfloat16)
    limit = pltpu.CompilerParams(vmem_limit_bytes=16 * 1024 * 1024)
    cheap = pl.CostEstimate(flops=1, bytes_accessed=1, transcendentals=0)
    w_key, w_value = in_hbm(w_key), in_hbm(w_value)
    near = pl.pallas_call(
        near_kernel,
        out_shape=sums,
        in_specs=[ANY] * 4,
        out_specs=VMEM,
        scratch_shapes=[w_scratch, h_scratch, pltpu.SemaphoreType.DMA((3,))],
        compiler_params=limit,
        cost_estimate=pl.CostEstimate(flops=10**10, bytes_accessed=1, transcendentals=0),
        name="project_near",
    )(hidden, w_key, w_value, first)
    neighbour = pl.pallas_call(
        neighbour_kernel,
        out_shape=sums,
        in_specs=[ANY] * (2 + len(quarters)),
        out_specs=VMEM,
        scratch_shapes=[
            w_scratch,
            h_scratch,
            pltpu.SemaphoreType.DMA((2 + len(quarters),)),
        ],
        compiler_params=limit,
        cost_estimate=cheap,
        name="project_neighbour",
    )(w_key, w_value, *quarters)
    return pl.pallas_call(
        far_kernel,
        out_shape=(sums,) + (jax.ShapeDtypeStruct((rows, width), jnp.bfloat16),) * 2,
        in_specs=[ANY] * 3 + [VMEM] * 2 + [ANY] * len(quarters),
        out_specs=(VMEM,) * 3,
        scratch_shapes=[
            w_scratch,
            h_scratch,
            h_scratch,
            pltpu.SemaphoreType.DMA((3 + len(quarters),)),
        ],
        compiler_params=limit,
        cost_estimate=cheap,
        name="project_far",
    )(hidden, w_far, w_swapped, near, neighbour, *quarters)


def plan_kernel(
    capacity, slots, request_docs, doc_lengths, rows, queries, q, held, spare, key_bias, row_place, key_place,
    slot_row, counts
):
    head_dim = q.shape[1] // 2
    heads = queries.shape[2] // head_dim
    block_rows = 4 * rows.shape[0]
    scale = math.log2(math.e) / math.sqrt(head_dim)
    for b in range(queries.shape[1] // block_rows):
        for h in range(heads):
            here = queries[0, b * block_rows : (b + 1) * block_rows, h * head_dim : (h + 1) * head_dim]
            here = here.astype(jnp.float32) * scale
            high = here.astype(jnp.bfloat16)
            place = slice((b * heads + h) * block_rows, (b * heads + h + 1) * block_rows)
            q[place, :head_dim] = high
            q[place, head_dim:] = (here - high.astype(jnp.float32)).astype(jnp.bfloat16)
    me = lax.axis_index("seq")
    per_doc, _, doc_count = rows.shape
    doc_len = held.shape[0] // doc_count
    row_count = row_place.shape[0]
    docs = lax.broadcasted_iota(jnp.int32, (1, doc_count), 1)
    lengths = jnp.zeros((1, doc_count), jnp.int32)
    places = jnp.zeros((1, doc_count), jnp.int32)
    for o in range(counts.shape[0]):
        counts[o] = 0
    for j in range(doc_count):
        doc = request_docs[me, j]
        owner = lax.div(doc, slots)
        rank = counts[owner]
        counts[owner] = rank + 1
        lengths = jnp.where(docs == j, doc_lengths[doc], lengths)
        places = jnp.where(docs == j, owner * capacity + rank, places)
    slot = lax.broadcasted_iota(jnp.int32, (doc_len, doc_count), 0)
    used = slot < lengths
    for i in range(per_doc):
        used &= slot != rows[i]
    used = used.astype(jnp.float32)
    first = jnp.min(jnp.where(used > 0, slot, doc_len), axis=0, keepdims=True)
    firsts = (slot == first).astype(jnp.bfloat16)
    eye = lax.broadcasted_iota(jnp.int32, (doc_count, doc_count), 0) == docs
    across = (((1,), (1,)), ((), ()))

    def turned(columns):
        return lax.dot_general(
            eye.astype(jnp.bfloat16), columns, across, preferred_element_type=jnp.float32
        )

    bias = jnp.where(turned(used.astype(jnp.bfloat16)) > 0, 0.0, MASKED)
    firsts = turned(firsts)
    doc = lax.broadcasted_iota(jnp.int32, (doc_count, 1), 0)
    for j in range(doc_count):
        part = slice(j * doc_len, (j + 1) * doc_len)
        held[part, :] = jnp.broadcast_to(used[:, j : j + 1], (doc_len, held.shape[1])).astype(
            held.dtype
        )
        key_bias[:, part] = bias[j : j + 1, :]
        spare[:, part] = jnp.where(doc == j, firsts, 0.0).astype(spare.dtype)
    row = lax.broadcasted_iota(jnp.int32, (row_count, doc_count), 0)
    start = per_doc * lax.broadcasted_iota(jnp.int32, (row_count, doc_count), 1)
    of_doc = (row >= start) & (row < start + per_doc)
    nth = jnp.sum(jnp.where(of_doc, row - start, 0), axis=1, keepdims=True)
    chosen = jnp.zeros((row_count, doc_count), jnp.int32)
    for i in range(per_doc):
        chosen = jnp.where(nth == i, rows[i], chosen)
    chosen = jnp.where(of_doc, chosen + doc_len * docs, 0)
    column = jnp.sum(chosen, axis=1, keepdims=True)
    goes = nth + per_doc * jnp.sum(jnp.where(of_doc, places, 0), axis=1, keepdims=True)
    row_place[...] = column
    square = (row_count, row_count)
    same = lax.broadcasted_iota(jnp.int32, square, 0) == lax.broadcasted_iota(jnp.int32, square, 1)
    key_place[...] = jnp.full(key_place.shape, held.shape[0], jnp.int32)
    key_place[:, :row_count] = jnp.sum(jnp.where(same, column, 0), axis=0, keepdims=True)
    slot_row[...] = jnp.sum(jnp.where(same, goes, 0), axis=0, keepdims=True)


def plan(request_docs, doc_lengths, recompute_rows, queries, slots, head_dim, doc_len):
    _, doc_count, per_doc = recompute_rows.shape
    rows = doc_count * per_doc
    context = doc_count * doc_len
    shapes = (
        ((rows * queries.shape[2] // head_dim, 2 * head_dim), jnp.bfloat16),
        ((context, head_dim), jnp.bfloat16),
        ((doc_count, context), jnp.bfloat16),
        ((1, context), jnp.float32),
        ((rows, 1), jnp.int32),
        ((1, rows + -rows % 128), jnp.int32),
        ((1, rows), jnp.int32),
    )
    return pl.pallas_call(
        functools.partial(plan_kernel, slots // 2, slots),
        out_shape=tuple(jax.ShapeDtypeStruct(*one) for one in shapes),
        in_specs=[SMEM, SMEM, VMEM, VMEM],
        out_specs=(VMEM,) * len(shapes),
        scratch_shapes=[pltpu.SMEM((request_docs.shape[0],), jnp.int32)],
        compiler_params=pltpu.CompilerParams(vmem_limit_bytes=16 * 1024 * 1024),
        name="plan",
    )(request_docs, doc_lengths, jnp.transpose(recompute_rows, (2, 0, 1)), queries)


def finish_kernel(own, arrived_k, arrived_v, slot_row, fresh, outgoing):
    arrived = jnp.concatenate([arrived_k[...], arrived_v[...]], axis=1)
    total = (own[...] + arrived.astype(jnp.float32)).astype(jnp.bfloat16)
    fresh[...] = total
    slots = lax.broadcasted_iota(jnp.int32, (outgoing.shape[0], 1), 0)
    pick = (slots == slot_row[...]).astype(jnp.bfloat16)
    outgoing[...] = jnp.dot(pick, total, preferred_element_type=jnp.float32).astype(jnp.bfloat16)


def finish(own, arrived, slot_row, slots):
    shapes = (own.shape, (slots, own.shape[1]))
    return pl.pallas_call(
        finish_kernel,
        out_shape=tuple(jax.ShapeDtypeStruct(one, jnp.bfloat16) for one in shapes),
        in_specs=[VMEM] * 4,
        out_specs=(VMEM, VMEM),
        compiler_params=pltpu.CompilerParams(vmem_limit_bytes=16 * 1024 * 1024),
        name="finish",
    )(own, *arrived, slot_row)


def attend_kernel(
    by_owner, request_docs, q, fresh, held, spare, key_bias, row_place, key_place, *rest
):
    sources, (mixed, keys, values, counts, sems) = rest[:-5], rest[-5:]
    me = lax.axis_index("seq")
    doc_count = request_docs.shape[1]
    head_dim = keys.shape[1] // 2
    doc_len = keys.shape[0] // doc_count
    owners = request_docs.shape[0]
    slots = sources[0].shape[0] if not by_owner else 2 * sources[0].shape[1]
    step = doc_count // sems.shape[1]
    blocks = doc_count // step
    block_rows = mixed.shape[1] // blocks
    block_keys = step * doc_len
    heads = mixed.shape[2] // head_dim
    left = pl.ds(0, head_dim)

    for o in range(owners):
        counts[o] = 0

    def one_doc(j, carry):
        doc = request_docs[me, j]
        owner = lax.div(doc, slots)
        rank = counts[owner]
        counts[owner] = rank + 1
        place = pl.ds(pl.multiple_of(j * doc_len, doc_len), doc_len)
        block = lax.div(j, step)

        def fetch(key_source, value_source):
            pltpu.make_async_copy(key_source, keys.at[place, left], sems.at[0, block]).start()
            pltpu.make_async_copy(value_source, values.at[place, left], sems.at[1, block]).start()

        if by_owner:
            fetch(sources[0].at[owner, rank, 0], sources[0].at[owner, rank, 1])
        else:
            away = lax.bitwise_xor(me, owner)

            @pl.when(away == 0)
            def _():
                slot = lax.rem(doc, slots)
                fetch(sources[0].at[slot], sources[1].at[slot])

            for k, source in zip((3, 2, 1), sources[2:]):

                @pl.when(away == k)
                def _():
                    fetch(source.at[rank, 0], source.at[rank, 1])

        return carry

    lax.fori_loop(0, doc_count, one_doc, 0)

    def assemble(b):
        block = pl.ds(b * block_keys, block_keys)
        for i, context in enumerate((keys, values)):
            pltpu.make_async_copy(
                context.at[block, left], context.at[block, left], sems.at[i, b]
            ).wait()
        block = slice(b * block_keys, (b + 1) * block_keys)
        spares = jnp.dot(
            spare[:, block], keys[block, :head_dim], preferred_element_type=jnp.float32
        ).astype(jnp.bfloat16)
        for j in range(b * step, (b + 1) * step):
            place = slice(j * doc_len, (j + 1) * doc_len)
            used = held[place, :]
            key = jnp.where(used > 0, keys[place, :head_dim], spares[j : j + 1, :])
            keys[place, :head_dim] = key
            keys[place, head_dim:] = key
            values[place, :head_dim] = values[place, :head_dim] * used
            values[place, head_dim:] = used

    fresh_count = fresh.shape[0]
    spare_rows = jnp.zeros((-fresh_count % 128, 2 * head_dim), fresh.dtype)
    fresh_k = jnp.concatenate([fresh[:, :head_dim]] * 2, axis=1)
    fresh_k = jnp.concatenate([fresh_k, spare_rows], axis=0)
    fresh_v = jnp.concatenate([fresh[:, head_dim:], jnp.ones_like(fresh[:, head_dim:])], axis=1)
    fresh_v = jnp.concatenate([fresh_v, spare_rows], axis=0)
    slot_place = lax.broadcasted_iota(jnp.int32, (1, block_keys), 1)
    contract_last = (((1,), (1,)), ((), ()))
    for b in range(blocks):
        assemble(b)
    for b in range(blocks):
        rows = slice(b * block_rows, (b + 1) * block_rows)
        q_here = q[b * heads * block_rows : (b + 1) * heads * block_rows, :]
        own_place = row_place[rows, :]

        def scores(some_keys):
            return lax.dot_general(
                q_here, some_keys, contract_last, preferred_element_type=jnp.float32
            )

        def masked(some_keys, allowed):
            shape = (heads, block_rows, some_keys.shape[0])
            kept = jnp.where(allowed[None], scores(some_keys).reshape(shape), MASKED)
            return kept.reshape(heads * block_rows, some_keys.shape[0])

        chunks, sides = [], []
        for c in range(b):
            part = slice(c * block_keys, (c + 1) * block_keys)
            chunks.append(scores(keys[part, :]))
            sides.append(values[part, :])
        part = slice(b * block_keys, (b + 1) * block_keys)
        allowed = (slot_place + b * block_keys <= own_place) & (key_bias[:, part] == 0)
        chunks.append(masked(keys[part, :], allowed))
        sides.append(values[part, :])
        chunks.append(masked(fresh_k, key_place[...] <= own_place))
        sides.append(fresh_v)
        lane_max = functools.reduce(
            jnp.maximum,
            [one[:, i : i + 128] for one in chunks for i in range(0, one.shape[1], 128)],
        )
        row_max = jnp.max(lane_max, axis=1, keepdims=True)
        total = jnp.zeros((heads * block_rows, 2 * head_dim), jnp.float32)
        for one, side in zip(chunks, sides):
            powers = jnp.exp2(one - row_max).astype(jnp.bfloat16)
            total += jnp.dot(powers, side, preferred_element_type=jnp.float32)
        result = (total[:, :head_dim] / total[:, head_dim:]).astype(mixed.dtype)
        for h in range(heads):
            mixed[0, rows, h * head_dim : (h + 1) * head_dim] = result[
                h * block_rows : (h + 1) * block_rows
            ]


def attend(
    shape, request_docs, q, fresh, held, spare, key_bias, row_place, key_place, sources, by_owner
):
    context, head_dim = held.shape
    return pl.pallas_call(
        functools.partial(attend_kernel, by_owner),
        out_shape=jax.ShapeDtypeStruct(shape, jnp.bfloat16),
        in_specs=[SMEM] + [VMEM] * 7 + [ANY] * len(sources),
        out_specs=VMEM,
        scratch_shapes=[
            pltpu.VMEM((context, 2 * head_dim), jnp.bfloat16),
            pltpu.VMEM((context, 2 * head_dim), jnp.bfloat16),
            pltpu.SMEM((request_docs.shape[0],), jnp.int32),
            pltpu.SemaphoreType.DMA((2, 4)),
        ],
        compiler_params=pltpu.CompilerParams(vmem_limit_bytes=32 * 1024 * 1024),
        name="attend",
    )(
        request_docs,
        q,
        fresh,
        held,
        spare,
        key_bias,
        row_place,
        key_place,
        *(in_hbm(one) for one in sources[:2]),
        *sources[2:],
    )


def shards(
    pairs,
    hidden,
    queries,
    w_key,
    w_value,
    store_keys,
    store_values,
    request_docs,
    doc_lengths,
    recompute_rows,
):
    seq_count = lax.axis_size("seq")
    slot_count, doc_len, head_dim = store_keys.shape
    capacity = slot_count // 2
    per_doc = recompute_rows.shape[2]

    if pairs:
        def swap(array, axis, apart):
            count = lax.axis_size(axis)
            return lax.ppermute(array, axis, [(i, i ^ apart) for i in range(count)])

        w_send, h_send = pick_sent(hidden, w_key, w_value)
        w_far = swap(w_send, "seq", 2)
        h_mine = swap(h_send, "seq", 1)
        doc_1, doc_2, doc_3 = pick_docs(request_docs, store_keys, store_values, False)
        (h_mine,) = gate((h_mine,), (doc_1,), cost=8000000000)
        h_chip = swap(h_mine, "tp", 2)
        h_core = swap(h_mine, "tp", 1)
        doc_2, doc_3, w_far = gate((doc_2, doc_3, w_far), cost=8000000000)
        w_swapped = swap(w_far, "groups", 1)
        doc_1 = swap(doc_1, "seq", 1)
        docs = (swap(doc_3, "seq", 3), swap(doc_2, "seq", 2), doc_1)
        quarters = (h_mine, h_core, h_chip, swap(h_chip, "tp", 1))
        own, *parts = project(hidden, w_key, w_value, w_far, w_swapped, quarters, doc_1)
        arrived = [swap(one, "seq", 1) for one in parts]
        sources = (store_keys, store_values, *docs)
    else:
        (docs,) = pick_docs(request_docs, store_keys, store_values, True)
        sources = (lax.all_to_all(docs, "seq", split_axis=0, concat_axis=0, tiled=True),)
        weights = lax.all_gather(
            jnp.concatenate([w_key, w_value], axis=1), "seq", axis=0, tiled=True
        )
        own = jnp.dot(hidden[0], weights, preferred_element_type=jnp.float32)
        arrived = [jnp.zeros((own.shape[0], head_dim), jnp.bfloat16)] * 2

    q, held, spare, key_bias, row_place, key_place, slot_row = plan(
        request_docs, doc_lengths, recompute_rows, queries, slot_count, head_dim, doc_len
    )
    fresh, outgoing = finish(own, arrived, slot_row, seq_count * capacity * per_doc)
    mixed = attend(
        queries.shape,
        request_docs,
        q,
        fresh,
        held,
        spare,
        key_bias,
        row_place,
        key_place,
        sources,
        not pairs,
    )

    outgoing = outgoing.reshape(seq_count, capacity * per_doc, 2 * head_dim)
    returned = lax.all_to_all(outgoing, "seq", split_axis=0, concat_axis=0, tiled=True)
    returned = returned.reshape(seq_count, capacity, per_doc, 2, head_dim)
    return (mixed, returned[None])


def solution(mesh):
    pairs = mesh.shape["seq"] == 4 and mesh.shape["groups"] == 2 and mesh.shape["tp"] == 4
    return jax.shard_map(
        functools.partial(shards, pairs),
        mesh=mesh,
        in_specs=(
            P(("groups", "seq"), None, None),
            P(("groups", "seq"), None, "tp"),
            P("seq", "tp"),
            P("seq", "tp"),
            P(("groups", "seq"), None, "tp"),
            P(("groups", "seq"), None, "tp"),
            P("groups", None),
            P("groups"),
            P(("groups", "seq"), None, None),
        ),
        out_specs=(
            P(("groups", "seq"), None, "tp"),
            P(("groups", "seq"), None, None, None, None, "tp"),
        ),
        check_vma=False,
    )
```

```python
import functools
import math

import jax
import jax.numpy as jnp
from jax import lax
from jax.experimental import pallas as pl
from jax.experimental.pallas import tpu as pltpu
from jax.sharding import PartitionSpec as P

ANY = pl.BlockSpec(memory_space=pl.ANY)
HBM = pl.BlockSpec(memory_space=pltpu.HBM)
SMEM = pl.BlockSpec(memory_space=pltpu.SMEM)
VMEM = pl.BlockSpec(memory_space=pltpu.VMEM)
MASKED = -1e30


def in_hbm(array):
    return pltpu.with_memory_space_constraint(array, pltpu.HBM)


def send_kernel(hidden, w_key, w_value, w_out, h_out, sems):
    group = lax.axis_index("groups")
    me = lax.axis_index("seq")
    rows, depth = h_out.shape[1:]
    for chosen, weight in ((0, w_key), (1, w_value)):

        @pl.when(group == chosen)
        def _():
            pltpu.make_async_copy(weight, w_out, sems.at[0]).start()

    first = me + 1 - 2 * lax.rem(me, 2)
    copies = []
    for i, block in enumerate((first, lax.rem(first + 2, 4))):
        source = hidden.at[
            0,
            pl.ds(pl.multiple_of(lax.axis_index("tp") * rows, rows), rows),
            pl.ds(pl.multiple_of(block * depth, depth), depth),
        ]
        copies.append(pltpu.make_async_copy(source, h_out.at[i], sems.at[1 + i]))
        copies[-1].start()
    pltpu.make_async_copy(w_key, w_out, sems.at[0]).wait()
    for copy in copies:
        copy.wait()


def pick_sent(hidden, w_key, w_value):
    h_shape = (2, hidden.shape[1] // 4, w_key.shape[0])
    return pl.pallas_call(
        send_kernel,
        out_shape=(
            jax.ShapeDtypeStruct(w_key.shape, jnp.bfloat16),
            jax.ShapeDtypeStruct(h_shape, jnp.bfloat16),
        ),
        in_specs=[ANY] * 3,
        out_specs=(VMEM, VMEM),
        scratch_shapes=[pltpu.SemaphoreType.DMA((3,))],
        compiler_params=pltpu.CompilerParams(vmem_limit_bytes=16 * 1024 * 1024),
        name="pick_sent",
    )(in_hbm(hidden), in_hbm(w_key), in_hbm(w_value))


def gate_kernel(*refs):
    pass


def gate(arrays, first=(), pinned=0, cost=1):
    return pl.pallas_call(
        gate_kernel,
        out_shape=tuple(jax.ShapeDtypeStruct(one.shape, one.dtype) for one in arrays),
        in_specs=[ANY] * (len(arrays) + len(first)),
        out_specs=(ANY,) * len(arrays),
        input_output_aliases={i: i for i in range(len(arrays))},
        compiler_params=pltpu.CompilerParams(vmem_limit_bytes=1024 * 1024),
        cost_estimate=pl.CostEstimate(flops=cost, bytes_accessed=1, transcendentals=0),
        name="gate",
    )(*(in_hbm(one) for one in arrays[:pinned]), *arrays[pinned:], *first)


def docs_kernel(by_owner, request_docs, store_keys, store_values, *rest):
    *outs, picks, sems = rest
    me = lax.axis_index("seq")
    requests, doc_count = request_docs.shape
    slots = store_keys.shape[0]
    capacity = slots // 2

    def one_request(r, carry):
        for c in range(capacity):
            picks[r, c] = 0

        def one_doc(j, count):
            doc = request_docs[r, j]
            mine = lax.div(doc, slots) == me

            @pl.when(mine)
            def _():
                picks[r, jnp.minimum(count, capacity - 1)] = lax.rem(doc, slots)

            return count + mine.astype(jnp.int32)

        lax.fori_loop(0, doc_count, one_doc, jnp.int32(0), unroll=True)
        return carry

    lax.fori_loop(0, requests, one_request, 0)

    def send(r, out, sem):
        for c in range(capacity):
            slot = picks[r, c]
            pltpu.make_async_copy(store_keys.at[slot], out.at[c, 0], sem).start()
            pltpu.make_async_copy(store_values.at[slot], out.at[c, 1], sem).start()

    if by_owner:

        def one_send(r, carry):
            send(r, outs[0].at[r], sems.at[0])
            return carry

        lax.fori_loop(0, requests, one_send, 0)
    else:
        for i, out in enumerate(outs):
            send(lax.bitwise_xor(me, i + 1), out, sems.at[i])
    for i, out in enumerate(outs):
        pltpu.make_async_copy(out, out, sems.at[i]).wait()


def pick_docs(request_docs, store_keys, store_values, by_owner):
    requests = request_docs.shape[0]
    capacity = store_keys.shape[0] // 2
    one = (capacity, 2) + store_keys.shape[1:]
    shapes = ((requests,) + one,) if by_owner else (one,) * (requests - 1)
    return pl.pallas_call(
        functools.partial(docs_kernel, by_owner),
        out_shape=tuple(jax.ShapeDtypeStruct(one, jnp.bfloat16) for one in shapes),
        in_specs=[SMEM, ANY, ANY],
        out_specs=(VMEM,) * len(shapes),
        scratch_shapes=[
            pltpu.SMEM((requests, capacity), jnp.int32),
            pltpu.SemaphoreType.DMA((len(shapes),)),
        ],
        compiler_params=pltpu.CompilerParams(vmem_limit_bytes=16 * 1024 * 1024),
        name="pick_docs",
    )(request_docs, in_hbm(store_keys), in_hbm(store_values))


def near_kernel(hidden, w_key, w_value, _, total, w, h, sems):
    depth, width = w_key.shape
    start = pl.multiple_of(lax.axis_index("seq") * depth, depth)
    copies = [
        pltpu.make_async_copy(w_key, w.at[:, pl.ds(0, width)], sems.at[0]),
        pltpu.make_async_copy(w_value, w.at[:, pl.ds(width, width)], sems.at[1]),
        pltpu.make_async_copy(hidden.at[0, :, pl.ds(start, depth)], h, sems.at[2]),
    ]
    for copy in copies:
        copy.start()
    for copy in copies:
        copy.wait()
    total[...] = jnp.dot(h[...], w[...], preferred_element_type=jnp.float32)


def lay_quarters(quarters, block, rows, copy):
    piece = rows.shape[0] // len(quarters)
    for k, quarter in enumerate(quarters):
        start = pl.multiple_of(lax.bitwise_xor(lax.axis_index("tp"), k) * piece, piece)
        copy(quarter.at[block], rows.at[pl.ds(start, piece)])


def neighbour_kernel(w_key, w_value, *rest):
    *quarters, total, w, n, sems = rest
    width = w_key.shape[1]
    copies = []

    def copy(source, target):
        copies.append(pltpu.make_async_copy(source, target, sems.at[len(copies)]))
        copies[-1].start()

    for i, held in enumerate((w_key, w_value)):
        copy(held, w.at[:, pl.ds(i * width, width)])
    lay_quarters(quarters, 0, n, copy)
    for one in copies:
        one.wait()
    total[...] = jnp.dot(n[...], w[...], preferred_element_type=jnp.float32)


def far_kernel(hidden, w_far, w_swapped, near, neighbour, *rest):
    *quarters, own, part_k, part_v, w, h, n, sems = rest
    group = lax.axis_index("groups")
    depth, width = w_far.shape
    copies = []

    def copy(source, target):
        copies.append(pltpu.make_async_copy(source, target, sems.at[len(copies)]))
        copies[-1].start()

    for held, place in ((w_far, group), (w_swapped, 1 - group)):
        copy(held, w.at[:, pl.ds(pl.multiple_of(place * width, width), width)])
    start = pl.multiple_of(lax.rem(lax.axis_index("seq") + 2, 4) * depth, depth)
    copy(hidden.at[0, :, pl.ds(start, depth)], h)
    lay_quarters(quarters, 1, n, copy)
    for one in copies:
        one.wait()
    own[...] = near[...] + jnp.dot(h[...], w[...], preferred_element_type=jnp.float32)
    total = neighbour[...] + jnp.dot(n[...], w[...], preferred_element_type=jnp.float32)
    part_k[...] = total[:, :width].astype(part_k.dtype)
    part_v[...] = total[:, width:].astype(part_v.dtype)


def project(hidden, w_key, w_value, w_far, w_swapped, quarters, first):
    depth, width = w_key.shape
    rows = hidden.shape[1]
    sums = jax.ShapeDtypeStruct((rows, 2 * width), jnp.float32)
    w_scratch = pltpu.VMEM((depth, 2 * width), jnp.bfloat16)
    h_scratch = pltpu.VMEM((rows, depth), jnp.bfloat16)
    limit = pltpu.CompilerParams(vmem_limit_bytes=16 * 1024 * 1024)
    cheap = pl.CostEstimate(flops=1, bytes_accessed=1, transcendentals=0)
    w_key, w_value = in_hbm(w_key), in_hbm(w_value)
    near = pl.pallas_call(
        near_kernel,
        out_shape=sums,
        in_specs=[ANY] * 4,
        out_specs=VMEM,
        scratch_shapes=[w_scratch, h_scratch, pltpu.SemaphoreType.DMA((3,))],
        compiler_params=limit,
        cost_estimate=pl.CostEstimate(flops=10**10, bytes_accessed=1, transcendentals=0),
        name="project_near",
    )(hidden, w_key, w_value, first)
    neighbour = pl.pallas_call(
        neighbour_kernel,
        out_shape=sums,
        in_specs=[ANY] * (2 + len(quarters)),
        out_specs=VMEM,
        scratch_shapes=[
            w_scratch,
            h_scratch,
            pltpu.SemaphoreType.DMA((2 + len(quarters),)),
        ],
        compiler_params=limit,
        cost_estimate=cheap,
        name="project_neighbour",
    )(w_key, w_value, *quarters)
    return pl.pallas_call(
        far_kernel,
        out_shape=(sums,) + (jax.ShapeDtypeStruct((rows, width), jnp.bfloat16),) * 2,
        in_specs=[ANY] * 3 + [VMEM] * 2 + [ANY] * len(quarters),
        out_specs=(VMEM,) * 3,
        scratch_shapes=[
            w_scratch,
            h_scratch,
            h_scratch,
            pltpu.SemaphoreType.DMA((3 + len(quarters),)),
        ],
        compiler_params=limit,
        cost_estimate=cheap,
        name="project_far",
    )(hidden, w_far, w_swapped, near, neighbour, *quarters)


def plan_kernel(
    pairs, capacity, slots, request_docs, doc_lengths, rows, queries, q, held, spare, key_bias, row_place, key_place,
    slot_row, counts
):
    head_dim = q.shape[1] // 2
    heads = queries.shape[2] // head_dim
    block_rows = 4 * rows.shape[0]
    scale = math.log2(math.e) / math.sqrt(head_dim)
    for b in range(queries.shape[1] // block_rows):
        for h in range(heads):
            here = queries[0, b * block_rows : (b + 1) * block_rows, h * head_dim : (h + 1) * head_dim]
            here = here.astype(jnp.float32) * scale
            high = here.astype(jnp.bfloat16)
            place = slice((b * heads + h) * block_rows, (b * heads + h + 1) * block_rows)
            q[place, :head_dim] = high
            q[place, head_dim:] = (here - high.astype(jnp.float32)).astype(jnp.bfloat16)
    me = lax.axis_index("seq")
    per_doc, _, doc_count = rows.shape
    doc_len = held.shape[0] // doc_count
    row_count = row_place.shape[0]
    docs = lax.broadcasted_iota(jnp.int32, (1, doc_count), 1)
    lengths = jnp.zeros((1, doc_count), jnp.int32)
    places = jnp.zeros((1, doc_count), jnp.int32)
    for o in range(counts.shape[0]):
        counts[o] = 0
    for j in range(doc_count):
        doc = request_docs[me, j]
        owner = lax.div(doc, slots)
        rank = counts[owner]
        counts[owner] = rank + 1
        lengths = jnp.where(docs == j, doc_lengths[doc], lengths)
        target = lax.bitwise_xor(owner, me) if pairs else owner
        places = jnp.where(docs == j, target * capacity + rank, places)
    slot = lax.broadcasted_iota(jnp.int32, (doc_len, doc_count), 0)
    used = slot < lengths
    for i in range(per_doc):
        used &= slot != rows[i]
    used = used.astype(jnp.float32)
    first = jnp.min(jnp.where(used > 0, slot, doc_len), axis=0, keepdims=True)
    firsts = (slot == first).astype(jnp.bfloat16)
    eye = lax.broadcasted_iota(jnp.int32, (doc_count, doc_count), 0) == docs
    across = (((1,), (1,)), ((), ()))

    def turned(columns):
        return lax.dot_general(
            eye.astype(jnp.bfloat16), columns, across, preferred_element_type=jnp.float32
        )

    bias = jnp.where(turned(used.astype(jnp.bfloat16)) > 0, 0.0, MASKED)
    firsts = turned(firsts)
    doc = lax.broadcasted_iota(jnp.int32, (doc_count, 1), 0)
    for j in range(doc_count):
        part = slice(j * doc_len, (j + 1) * doc_len)
        held[part, :] = jnp.broadcast_to(used[:, j : j + 1], (doc_len, held.shape[1])).astype(
            held.dtype
        )
        key_bias[:, part] = bias[j : j + 1, :]
        spare[:, part] = jnp.where(doc == j, firsts, 0.0).astype(spare.dtype)
    row = lax.broadcasted_iota(jnp.int32, (row_count, doc_count), 0)
    start = per_doc * lax.broadcasted_iota(jnp.int32, (row_count, doc_count), 1)
    of_doc = (row >= start) & (row < start + per_doc)
    nth = jnp.sum(jnp.where(of_doc, row - start, 0), axis=1, keepdims=True)
    chosen = jnp.zeros((row_count, doc_count), jnp.int32)
    for i in range(per_doc):
        chosen = jnp.where(nth == i, rows[i], chosen)
    chosen = jnp.where(of_doc, chosen + doc_len * docs, 0)
    column = jnp.sum(chosen, axis=1, keepdims=True)
    goes = nth + per_doc * jnp.sum(jnp.where(of_doc, places, 0), axis=1, keepdims=True)
    row_place[...] = column
    square = (row_count, row_count)
    same = lax.broadcasted_iota(jnp.int32, square, 0) == lax.broadcasted_iota(jnp.int32, square, 1)
    key_place[...] = jnp.full(key_place.shape, held.shape[0], jnp.int32)
    key_place[:, :row_count] = jnp.sum(jnp.where(same, column, 0), axis=0, keepdims=True)
    slot_row[...] = jnp.sum(jnp.where(same, goes, 0), axis=0, keepdims=True)


def plan(pairs, request_docs, doc_lengths, recompute_rows, queries, slots, head_dim, doc_len):
    _, doc_count, per_doc = recompute_rows.shape
    rows = doc_count * per_doc
    context = doc_count * doc_len
    shapes = (
        ((rows * queries.shape[2] // head_dim, 2 * head_dim), jnp.bfloat16),
        ((context, head_dim), jnp.bfloat16),
        ((doc_count, context), jnp.bfloat16),
        ((1, context), jnp.float32),
        ((rows, 1), jnp.int32),
        ((1, rows + -rows % 128), jnp.int32),
        ((1, rows), jnp.int32),
    )
    return pl.pallas_call(
        functools.partial(plan_kernel, pairs, slots // 2, slots),
        out_shape=tuple(jax.ShapeDtypeStruct(*one) for one in shapes),
        in_specs=[SMEM, SMEM, VMEM, VMEM],
        out_specs=(VMEM,) * len(shapes),
        scratch_shapes=[pltpu.SMEM((request_docs.shape[0],), jnp.int32)],
        compiler_params=pltpu.CompilerParams(vmem_limit_bytes=16 * 1024 * 1024),
        name="plan",
    )(request_docs, doc_lengths, jnp.transpose(recompute_rows, (2, 0, 1)), queries)


def finish_kernel(own, arrived_k, arrived_v, slot_row, fresh, *outgoing):
    arrived = jnp.concatenate([arrived_k[...], arrived_v[...]], axis=1)
    total = (own[...] + arrived.astype(jnp.float32)).astype(jnp.bfloat16)
    fresh[...] = total
    for i, out in enumerate(outgoing):
        count = out.shape[0]
        slots = i * count + lax.broadcasted_iota(jnp.int32, (count, 1), 0)
        pick = (slots == slot_row[...]).astype(jnp.bfloat16)
        out[...] = jnp.dot(pick, total, preferred_element_type=jnp.float32).astype(jnp.bfloat16)


def finish(own, arrived, slot_row, slots, parts):
    shapes = (own.shape,) + ((slots // parts, own.shape[1]),) * parts
    return pl.pallas_call(
        finish_kernel,
        out_shape=tuple(jax.ShapeDtypeStruct(one, jnp.bfloat16) for one in shapes),
        in_specs=[VMEM] * 4,
        out_specs=(VMEM,) * len(shapes),
        compiler_params=pltpu.CompilerParams(vmem_limit_bytes=16 * 1024 * 1024),
        name="finish",
    )(own, *arrived, slot_row)


def attend_kernel(
    by_owner, request_docs, q, fresh, held, spare, key_bias, row_place, key_place, *rest
):
    *sources, mixed, keys, values, counts, sems = rest
    if not by_owner:
        *sources, returned = sources
        sources, back = sources[:-4], sources[-4:]
    me = lax.axis_index("seq")
    doc_count = request_docs.shape[1]
    head_dim = keys.shape[1] // 2
    doc_len = keys.shape[0] // doc_count
    owners = request_docs.shape[0]
    slots = sources[0].shape[0] if not by_owner else 2 * sources[0].shape[1]
    step = doc_count // sems.shape[1]
    blocks = doc_count // step
    block_rows = mixed.shape[1] // blocks
    block_keys = step * doc_len
    heads = mixed.shape[2] // head_dim
    left = pl.ds(0, head_dim)

    if not by_owner:
        for k, rows in enumerate(back):
            count = rows.shape[0]
            start = pl.multiple_of(lax.bitwise_xor(me, k) * count, count)
            returned[pl.ds(start, count), :] = rows[...]
    for o in range(owners):
        counts[o] = 0

    def one_doc(j, carry):
        doc = request_docs[me, j]
        owner = lax.div(doc, slots)
        rank = counts[owner]
        counts[owner] = rank + 1
        place = pl.ds(pl.multiple_of(j * doc_len, doc_len), doc_len)
        block = lax.div(j, step)

        def fetch(key_source, value_source):
            pltpu.make_async_copy(key_source, keys.at[place, left], sems.at[0, block]).start()
            pltpu.make_async_copy(value_source, values.at[place, left], sems.at[1, block]).start()

        if by_owner:
            fetch(sources[0].at[owner, rank, 0], sources[0].at[owner, rank, 1])
        else:
            away = lax.bitwise_xor(me, owner)

            @pl.when(away == 0)
            def _():
                slot = lax.rem(doc, slots)
                fetch(sources[0].at[slot], sources[1].at[slot])

            for k, source in zip((3, 2, 1), sources[2:]):

                @pl.when(away == k)
                def _():
                    fetch(source.at[rank, 0], source.at[rank, 1])

        return carry

    lax.fori_loop(0, doc_count, one_doc, 0)

    def assemble(b):
        block = pl.ds(b * block_keys, block_keys)
        for i, context in enumerate((keys, values)):
            pltpu.make_async_copy(
                context.at[block, left], context.at[block, left], sems.at[i, b]
            ).wait()
        block = slice(b * block_keys, (b + 1) * block_keys)
        spares = jnp.dot(
            spare[:, block], keys[block, :head_dim], preferred_element_type=jnp.float32
        ).astype(jnp.bfloat16)
        for j in range(b * step, (b + 1) * step):
            place = slice(j * doc_len, (j + 1) * doc_len)
            used = held[place, :]
            key = jnp.where(used > 0, keys[place, :head_dim], spares[j : j + 1, :])
            keys[place, :head_dim] = key
            keys[place, head_dim:] = key
            values[place, :head_dim] = values[place, :head_dim] * used
            values[place, head_dim:] = used

    fresh_count = fresh.shape[0]
    spare_rows = jnp.zeros((-fresh_count % 128, 2 * head_dim), fresh.dtype)
    fresh_k = jnp.concatenate([fresh[:, :head_dim]] * 2, axis=1)
    fresh_k = jnp.concatenate([fresh_k, spare_rows], axis=0)
    fresh_v = jnp.concatenate([fresh[:, head_dim:], jnp.ones_like(fresh[:, head_dim:])], axis=1)
    fresh_v = jnp.concatenate([fresh_v, spare_rows], axis=0)
    slot_place = lax.broadcasted_iota(jnp.int32, (1, block_keys), 1)
    contract_last = (((1,), (1,)), ((), ()))
    for b in range(blocks):
        assemble(b)
    for b in range(blocks):
        rows = slice(b * block_rows, (b + 1) * block_rows)
        q_here = q[b * heads * block_rows : (b + 1) * heads * block_rows, :]
        own_place = row_place[rows, :]

        def scores(some_keys):
            return lax.dot_general(
                q_here, some_keys, contract_last, preferred_element_type=jnp.float32
            )

        def masked(some_keys, allowed):
            shape = (heads, block_rows, some_keys.shape[0])
            kept = jnp.where(allowed[None], scores(some_keys).reshape(shape), MASKED)
            return kept.reshape(heads * block_rows, some_keys.shape[0])

        chunks, sides = [], []
        for c in range(b):
            part = slice(c * block_keys, (c + 1) * block_keys)
            chunks.append(scores(keys[part, :]))
            sides.append(values[part, :])
        part = slice(b * block_keys, (b + 1) * block_keys)
        allowed = (slot_place + b * block_keys <= own_place) & (key_bias[:, part] == 0)
        chunks.append(masked(keys[part, :], allowed))
        sides.append(values[part, :])
        chunks.append(masked(fresh_k, key_place[...] <= own_place))
        sides.append(fresh_v)
        lane_max = functools.reduce(
            jnp.maximum,
            [one[:, i : i + 128] for one in chunks for i in range(0, one.shape[1], 128)],
        )
        row_max = jnp.max(lane_max, axis=1, keepdims=True)
        total = jnp.zeros((heads * block_rows, 2 * head_dim), jnp.float32)
        for one, side in zip(chunks, sides):
            powers = jnp.exp2(one - row_max).astype(jnp.bfloat16)
            total += jnp.dot(powers, side, preferred_element_type=jnp.float32)
        result = (total[:, :head_dim] / total[:, head_dim:]).astype(mixed.dtype)
        for h in range(heads):
            mixed[0, rows, h * head_dim : (h + 1) * head_dim] = result[
                h * block_rows : (h + 1) * block_rows
            ]


def attend(
    shape, request_docs, q, fresh, held, spare, key_bias, row_place, key_place, sources, back
):
    context, head_dim = held.shape
    outs = [jax.ShapeDtypeStruct(shape, jnp.bfloat16)]
    if back:
        count, width = back[0].shape
        outs.insert(0, jax.ShapeDtypeStruct((len(back) * count, width), jnp.bfloat16))
    return pl.pallas_call(
        functools.partial(attend_kernel, not back),
        out_shape=outs,
        in_specs=[SMEM] + [VMEM] * 7 + [ANY] * len(sources) + [VMEM] * len(back),
        out_specs=[VMEM] * len(outs),
        scratch_shapes=[
            pltpu.VMEM((context, 2 * head_dim), jnp.bfloat16),
            pltpu.VMEM((context, 2 * head_dim), jnp.bfloat16),
            pltpu.SMEM((request_docs.shape[0],), jnp.int32),
            pltpu.SemaphoreType.DMA((2, 4)),
        ],
        compiler_params=pltpu.CompilerParams(vmem_limit_bytes=32 * 1024 * 1024),
        name="attend",
    )(
        request_docs,
        q,
        fresh,
        held,
        spare,
        key_bias,
        row_place,
        key_place,
        *(in_hbm(one) for one in sources[:2]),
        *sources[2:],
        *back,
    )


def shards(
    pairs,
    hidden,
    queries,
    w_key,
    w_value,
    store_keys,
    store_values,
    request_docs,
    doc_lengths,
    recompute_rows,
):
    seq_count = lax.axis_size("seq")
    slot_count, doc_len, head_dim = store_keys.shape
    capacity = slot_count // 2
    per_doc = recompute_rows.shape[2]

    if pairs:
        def swap(array, axis, apart):
            count = lax.axis_size(axis)
            return lax.ppermute(array, axis, [(i, i ^ apart) for i in range(count)])

        w_send, h_send = pick_sent(hidden, w_key, w_value)
        w_far = swap(w_send, "seq", 2)
        h_mine = swap(h_send, "seq", 1)
        doc_1, doc_2, doc_3 = pick_docs(request_docs, store_keys, store_values, False)
        (h_mine,) = gate((h_mine,), (doc_1,), cost=8000000000)
        h_chip = swap(h_mine, "tp", 2)
        h_core = swap(h_mine, "tp", 1)
        doc_2, doc_3, w_far = gate((doc_2, doc_3, w_far), cost=8000000000)
        w_swapped = swap(w_far, "groups", 1)
        doc_1 = swap(doc_1, "seq", 1)
        docs = (swap(doc_3, "seq", 3), swap(doc_2, "seq", 2), doc_1)
        quarters = (h_mine, h_core, h_chip, swap(h_chip, "tp", 1))
        own, *parts = project(hidden, w_key, w_value, w_far, w_swapped, quarters, doc_1)
        arrived = [swap(one, "seq", 1) for one in parts]
        sources = (store_keys, store_values, *docs)
    else:
        (docs,) = pick_docs(request_docs, store_keys, store_values, True)
        sources = (lax.all_to_all(docs, "seq", split_axis=0, concat_axis=0, tiled=True),)
        weights = lax.all_gather(
            jnp.concatenate([w_key, w_value], axis=1), "seq", axis=0, tiled=True
        )
        own = jnp.dot(hidden[0], weights, preferred_element_type=jnp.float32)
        arrived = [jnp.zeros((own.shape[0], head_dim), jnp.bfloat16)] * 2

    q, held, spare, key_bias, row_place, key_place, slot_row = plan(
        pairs, request_docs, doc_lengths, recompute_rows, queries, slot_count, head_dim, doc_len
    )
    fresh, *outgoing = finish(
        own, arrived, slot_row, seq_count * capacity * per_doc, seq_count if pairs else 1
    )
    if pairs:
        back = outgoing[:1] + [swap(outgoing[k], "seq", k) for k in range(1, seq_count)]
    else:
        back = ()
        outgoing = outgoing[0].reshape(seq_count, capacity * per_doc, 2 * head_dim)
        returned = lax.all_to_all(outgoing, "seq", split_axis=0, concat_axis=0, tiled=True)
    *placed, mixed = attend(
        queries.shape,
        request_docs,
        q,
        fresh,
        held,
        spare,
        key_bias,
        row_place,
        key_place,
        sources,
        back,
    )
    if pairs:
        (returned,) = placed

    returned = returned.reshape(seq_count, capacity, per_doc, 2, head_dim)
    return (mixed, returned[None])


def solution(mesh):
    pairs = mesh.shape["seq"] == 4 and mesh.shape["groups"] == 2 and mesh.shape["tp"] == 4
    return jax.shard_map(
        functools.partial(shards, pairs),
        mesh=mesh,
        in_specs=(
            P(("groups", "seq"), None, None),
            P(("groups", "seq"), None, "tp"),
            P("seq", "tp"),
            P("seq", "tp"),
            P(("groups", "seq"), None, "tp"),
            P(("groups", "seq"), None, "tp"),
            P("groups", None),
            P("groups"),
            P(("groups", "seq"), None, None),
        ),
        out_specs=(
            P(("groups", "seq"), None, "tp"),
            P(("groups", "seq"), None, None, None, None, "tp"),
        ),
        check_vma=False,
    )
```

```python
import functools
import math

import jax
import jax.numpy as jnp
from jax import lax
from jax.experimental import pallas as pl
from jax.experimental.pallas import tpu as pltpu
from jax.sharding import PartitionSpec as P

ANY = pl.BlockSpec(memory_space=pl.ANY)
HBM = pl.BlockSpec(memory_space=pltpu.HBM)
SMEM = pl.BlockSpec(memory_space=pltpu.SMEM)
VMEM = pl.BlockSpec(memory_space=pltpu.VMEM)
MASKED = -1e30


def in_hbm(array):
    return pltpu.with_memory_space_constraint(array, pltpu.HBM)


def send_kernel(hidden, w_key, w_value, w_first, w_second, h_out, sems):
    group = lax.axis_index("groups")
    me = lax.axis_index("seq")
    rows, depth = h_out.shape[1:]
    for chosen, weight in ((0, w_key), (1, w_value)):

        @pl.when(group == chosen)
        def _():
            for i, out in enumerate((w_first, w_second)):
                part = weight.at[pl.ds(i * w_first.shape[0], out.shape[0])]
                pltpu.make_async_copy(part, out, sems.at[i]).start()

    first = me + 1 - 2 * lax.rem(me, 2)
    copies = []
    for i, block in enumerate((first, lax.rem(first + 2, 4))):
        source = hidden.at[
            0,
            pl.ds(pl.multiple_of(lax.axis_index("tp") * rows, rows), rows),
            pl.ds(pl.multiple_of(block * depth, depth), depth),
        ]
        copies.append(pltpu.make_async_copy(source, h_out.at[i], sems.at[2 + i]))
        copies[-1].start()
    for i, out in enumerate((w_first, w_second)):
        pltpu.make_async_copy(w_key.at[pl.ds(0, out.shape[0])], out, sems.at[i]).wait()
    for copy in copies:
        copy.wait()


def pick_sent(hidden, w_key, w_value):
    depth, width = w_key.shape
    h_shape = (2, hidden.shape[1] // 4, depth)
    first = depth * 7 // 32
    return pl.pallas_call(
        send_kernel,
        out_shape=(
            jax.ShapeDtypeStruct((first, width), jnp.bfloat16),
            jax.ShapeDtypeStruct((depth - first, width), jnp.bfloat16),
            jax.ShapeDtypeStruct(h_shape, jnp.bfloat16),
        ),
        in_specs=[ANY] * 3,
        out_specs=(VMEM,) * 3,
        scratch_shapes=[pltpu.SemaphoreType.DMA((4,))],
        compiler_params=pltpu.CompilerParams(vmem_limit_bytes=16 * 1024 * 1024),
        name="pick_sent",
    )(in_hbm(hidden), in_hbm(w_key), in_hbm(w_value))


def gate_kernel(*refs):
    pass


def gate(arrays, first=(), pinned=0, cost=1):
    return pl.pallas_call(
        gate_kernel,
        out_shape=tuple(jax.ShapeDtypeStruct(one.shape, one.dtype) for one in arrays),
        in_specs=[ANY] * (len(arrays) + len(first)),
        out_specs=(ANY,) * len(arrays),
        input_output_aliases={i: i for i in range(len(arrays))},
        compiler_params=pltpu.CompilerParams(vmem_limit_bytes=1024 * 1024),
        cost_estimate=pl.CostEstimate(flops=cost, bytes_accessed=1, transcendentals=0),
        name="gate",
    )(*(in_hbm(one) for one in arrays[:pinned]), *arrays[pinned:], *first)


def docs_kernel(by_owner, request_docs, store_keys, store_values, *rest):
    *outs, picks, sems = rest
    me = lax.axis_index("seq")
    requests, doc_count = request_docs.shape
    slots = store_keys.shape[0]
    capacity = slots // 2

    def one_request(r, carry):
        for c in range(capacity):
            picks[r, c] = 0

        def one_doc(j, count):
            doc = request_docs[r, j]
            mine = lax.div(doc, slots) == me

            @pl.when(mine)
            def _():
                picks[r, jnp.minimum(count, capacity - 1)] = lax.rem(doc, slots)

            return count + mine.astype(jnp.int32)

        lax.fori_loop(0, doc_count, one_doc, jnp.int32(0), unroll=True)
        return carry

    lax.fori_loop(0, requests, one_request, 0)

    def send(r, out, sem):
        for c in range(capacity):
            slot = picks[r, c]
            pltpu.make_async_copy(store_keys.at[slot], out.at[c, 0], sem).start()
            pltpu.make_async_copy(store_values.at[slot], out.at[c, 1], sem).start()

    if by_owner:

        def one_send(r, carry):
            send(r, outs[0].at[r], sems.at[0])
            return carry

        lax.fori_loop(0, requests, one_send, 0)
    else:
        for i, out in enumerate(outs):
            send(lax.bitwise_xor(me, i + 1), out, sems.at[i])
    for i, out in enumerate(outs):
        pltpu.make_async_copy(out, out, sems.at[i]).wait()


def pick_docs(request_docs, store_keys, store_values, by_owner):
    requests = request_docs.shape[0]
    capacity = store_keys.shape[0] // 2
    one = (capacity, 2) + store_keys.shape[1:]
    shapes = ((requests,) + one,) if by_owner else (one,) * (requests - 1)
    return pl.pallas_call(
        functools.partial(docs_kernel, by_owner),
        out_shape=tuple(jax.ShapeDtypeStruct(one, jnp.bfloat16) for one in shapes),
        in_specs=[SMEM, ANY, ANY],
        out_specs=(VMEM,) * len(shapes),
        scratch_shapes=[
            pltpu.SMEM((requests, capacity), jnp.int32),
            pltpu.SemaphoreType.DMA((len(shapes),)),
        ],
        compiler_params=pltpu.CompilerParams(vmem_limit_bytes=16 * 1024 * 1024),
        name="pick_docs",
    )(request_docs, in_hbm(store_keys), in_hbm(store_values))


def near_kernel(hidden, w_key, w_value, _, total, w, h, sems):
    depth, width = w_key.shape
    start = pl.multiple_of(lax.axis_index("seq") * depth, depth)
    copies = [
        pltpu.make_async_copy(w_key, w.at[:, pl.ds(0, width)], sems.at[0]),
        pltpu.make_async_copy(w_value, w.at[:, pl.ds(width, width)], sems.at[1]),
        pltpu.make_async_copy(hidden.at[0, :, pl.ds(start, depth)], h, sems.at[2]),
    ]
    for copy in copies:
        copy.start()
    for copy in copies:
        copy.wait()
    total[...] = jnp.dot(h[...], w[...], preferred_element_type=jnp.float32)


def lay_quarters(quarters, block, rows, copy):
    piece = rows.shape[0] // len(quarters)
    for k, quarter in enumerate(quarters):
        start = pl.multiple_of(lax.bitwise_xor(lax.axis_index("tp"), k) * piece, piece)
        copy(quarter.at[block], rows.at[pl.ds(start, piece)])


def neighbour_kernel(w_key, w_value, *rest):
    *quarters, total, w, n, sems = rest
    width = w_key.shape[1]
    copies = []

    def copy(source, target):
        copies.append(pltpu.make_async_copy(source, target, sems.at[len(copies)]))
        copies[-1].start()

    for i, held in enumerate((w_key, w_value)):
        copy(held, w.at[:, pl.ds(i * width, width)])
    lay_quarters(quarters, 0, n, copy)
    for one in copies:
        one.wait()
    total[...] = jnp.dot(n[...], w[...], preferred_element_type=jnp.float32)


def far_kernel(hidden, w_far_0, w_far_1, w_swapped_0, w_swapped_1, near, neighbour, *rest):
    *quarters, own, part_k, part_v, w, h, n, sems = rest
    group = lax.axis_index("groups")
    start, width = w_far_0.shape
    depth = start + w_far_1.shape[0]
    copies = []

    def copy(source, target):
        copies.append(pltpu.make_async_copy(source, target, sems.at[len(copies)]))
        copies[-1].start()

    pairs = ((w_far_0, w_far_1, group), (w_swapped_0, w_swapped_1, 1 - group))
    for first, second, place in pairs:
        columns = pl.ds(pl.multiple_of(place * width, width), width)
        copy(first, w.at[pl.ds(0, start), columns])
        copy(second, w.at[pl.ds(start, depth - start), columns])
    start = pl.multiple_of(lax.rem(lax.axis_index("seq") + 2, 4) * depth, depth)
    copy(hidden.at[0, :, pl.ds(start, depth)], h)
    lay_quarters(quarters, 1, n, copy)
    for one in copies:
        one.wait()
    own[...] = near[...] + jnp.dot(h[...], w[...], preferred_element_type=jnp.float32)
    total = neighbour[...] + jnp.dot(n[...], w[...], preferred_element_type=jnp.float32)
    part_k[...] = total[:, :width].astype(part_k.dtype)
    part_v[...] = total[:, width:].astype(part_v.dtype)


def project(hidden, w_key, w_value, w_far, w_swapped, quarters, first):
    depth, width = w_key.shape
    rows = hidden.shape[1]
    sums = jax.ShapeDtypeStruct((rows, 2 * width), jnp.float32)
    w_scratch = pltpu.VMEM((depth, 2 * width), jnp.bfloat16)
    h_scratch = pltpu.VMEM((rows, depth), jnp.bfloat16)
    limit = pltpu.CompilerParams(vmem_limit_bytes=16 * 1024 * 1024)
    cheap = pl.CostEstimate(flops=1, bytes_accessed=1, transcendentals=0)
    w_key, w_value = in_hbm(w_key), in_hbm(w_value)
    near = pl.pallas_call(
        near_kernel,
        out_shape=sums,
        in_specs=[ANY] * 4,
        out_specs=VMEM,
        scratch_shapes=[w_scratch, h_scratch, pltpu.SemaphoreType.DMA((3,))],
        compiler_params=limit,
        cost_estimate=pl.CostEstimate(flops=10**10, bytes_accessed=1, transcendentals=0),
        name="project_near",
    )(hidden, w_key, w_value, first)
    neighbour = pl.pallas_call(
        neighbour_kernel,
        out_shape=sums,
        in_specs=[ANY] * (2 + len(quarters)),
        out_specs=VMEM,
        scratch_shapes=[
            w_scratch,
            h_scratch,
            pltpu.SemaphoreType.DMA((2 + len(quarters),)),
        ],
        compiler_params=limit,
        cost_estimate=cheap,
        name="project_neighbour",
    )(w_key, w_value, *quarters)
    return pl.pallas_call(
        far_kernel,
        out_shape=(sums,) + (jax.ShapeDtypeStruct((rows, width), jnp.bfloat16),) * 2,
        in_specs=[ANY] * 5 + [VMEM] * 2 + [ANY] * len(quarters),
        out_specs=(VMEM,) * 3,
        scratch_shapes=[
            w_scratch,
            h_scratch,
            h_scratch,
            pltpu.SemaphoreType.DMA((5 + len(quarters),)),
        ],
        compiler_params=limit,
        cost_estimate=cheap,
        name="project_far",
    )(hidden, *w_far, *w_swapped, near, neighbour, *quarters)


def plan_kernel(
    capacity, slots, request_docs, doc_lengths, rows, queries, q, held, spare, key_bias, row_place, key_place,
    slot_row, counts
):
    head_dim = q.shape[1] // 2
    heads = queries.shape[2] // head_dim
    block_rows = 4 * rows.shape[0]
    scale = math.log2(math.e) / math.sqrt(head_dim)
    for b in range(queries.shape[1] // block_rows):
        for h in range(heads):
            here = queries[0, b * block_rows : (b + 1) * block_rows, h * head_dim : (h + 1) * head_dim]
            here = here.astype(jnp.float32) * scale
            high = here.astype(jnp.bfloat16)
            place = slice((b * heads + h) * block_rows, (b * heads + h + 1) * block_rows)
            q[place, :head_dim] = high
            q[place, head_dim:] = (here - high.astype(jnp.float32)).astype(jnp.bfloat16)
    me = lax.axis_index("seq")
    per_doc, _, doc_count = rows.shape
    doc_len = held.shape[0] // doc_count
    row_count = row_place.shape[0]
    docs = lax.broadcasted_iota(jnp.int32, (1, doc_count), 1)
    lengths = jnp.zeros((1, doc_count), jnp.int32)
    places = jnp.zeros((1, doc_count), jnp.int32)
    for o in range(counts.shape[0]):
        counts[o] = 0
    for j in range(doc_count):
        doc = request_docs[me, j]
        owner = lax.div(doc, slots)
        rank = counts[owner]
        counts[owner] = rank + 1
        lengths = jnp.where(docs == j, doc_lengths[doc], lengths)
        places = jnp.where(docs == j, owner * capacity + rank, places)
    slot = lax.broadcasted_iota(jnp.int32, (doc_len, doc_count), 0)
    used = slot < lengths
    for i in range(per_doc):
        used &= slot != rows[i]
    used = used.astype(jnp.float32)
    first = jnp.min(jnp.where(used > 0, slot, doc_len), axis=0, keepdims=True)
    firsts = (slot == first).astype(jnp.bfloat16)
    eye = lax.broadcasted_iota(jnp.int32, (doc_count, doc_count), 0) == docs
    across = (((1,), (1,)), ((), ()))

    def turned(columns):
        return lax.dot_general(
            eye.astype(jnp.bfloat16), columns, across, preferred_element_type=jnp.float32
        )

    bias = jnp.where(turned(used.astype(jnp.bfloat16)) > 0, 0.0, MASKED)
    firsts = turned(firsts)
    doc = lax.broadcasted_iota(jnp.int32, (doc_count, 1), 0)
    for j in range(doc_count):
        part = slice(j * doc_len, (j + 1) * doc_len)
        held[part, :] = jnp.broadcast_to(used[:, j : j + 1], (doc_len, held.shape[1])).astype(
            held.dtype
        )
        key_bias[:, part] = bias[j : j + 1, :]
        spare[:, part] = jnp.where(doc == j, firsts, 0.0).astype(spare.dtype)
    row = lax.broadcasted_iota(jnp.int32, (row_count, doc_count), 0)
    start = per_doc * lax.broadcasted_iota(jnp.int32, (row_count, doc_count), 1)
    of_doc = (row >= start) & (row < start + per_doc)
    nth = jnp.sum(jnp.where(of_doc, row - start, 0), axis=1, keepdims=True)
    chosen = jnp.zeros((row_count, doc_count), jnp.int32)
    for i in range(per_doc):
        chosen = jnp.where(nth == i, rows[i], chosen)
    chosen = jnp.where(of_doc, chosen + doc_len * docs, 0)
    column = jnp.sum(chosen, axis=1, keepdims=True)
    goes = nth + per_doc * jnp.sum(jnp.where(of_doc, places, 0), axis=1, keepdims=True)
    row_place[...] = column
    square = (row_count, row_count)
    same = lax.broadcasted_iota(jnp.int32, square, 0) == lax.broadcasted_iota(jnp.int32, square, 1)
    key_place[...] = jnp.full(key_place.shape, held.shape[0], jnp.int32)
    key_place[:, :row_count] = jnp.sum(jnp.where(same, column, 0), axis=0, keepdims=True)
    slot_row[...] = jnp.sum(jnp.where(same, goes, 0), axis=0, keepdims=True)


def plan(request_docs, doc_lengths, recompute_rows, queries, slots, head_dim, doc_len):
    _, doc_count, per_doc = recompute_rows.shape
    rows = doc_count * per_doc
    context = doc_count * doc_len
    shapes = (
        ((rows * queries.shape[2] // head_dim, 2 * head_dim), jnp.bfloat16),
        ((context, head_dim), jnp.bfloat16),
        ((doc_count, context), jnp.bfloat16),
        ((1, context), jnp.float32),
        ((rows, 1), jnp.int32),
        ((1, rows + -rows % 128), jnp.int32),
        ((1, rows), jnp.int32),
    )
    return pl.pallas_call(
        functools.partial(plan_kernel, slots // 2, slots),
        out_shape=tuple(jax.ShapeDtypeStruct(*one) for one in shapes),
        in_specs=[SMEM, SMEM, VMEM, VMEM],
        out_specs=(VMEM,) * len(shapes),
        scratch_shapes=[pltpu.SMEM((request_docs.shape[0],), jnp.int32)],
        compiler_params=pltpu.CompilerParams(vmem_limit_bytes=16 * 1024 * 1024),
        name="plan",
    )(request_docs, doc_lengths, jnp.transpose(recompute_rows, (2, 0, 1)), queries)


def finish_kernel(own, arrived_k, arrived_v, slot_row, fresh, outgoing):
    arrived = jnp.concatenate([arrived_k[...], arrived_v[...]], axis=1)
    total = (own[...] + arrived.astype(jnp.float32)).astype(jnp.bfloat16)
    fresh[...] = total
    width = outgoing.shape[1]
    slots = lax.broadcasted_iota(jnp.int32, (outgoing.shape[0], 1), 0)
    placed = jnp.zeros(outgoing.shape, jnp.float32)
    for i in range(2):
        pick = (slots == 2 * slot_row[...] + i).astype(jnp.bfloat16)
        part = total[:, i * width : (i + 1) * width]
        placed += jnp.dot(pick, part, preferred_element_type=jnp.float32)
    outgoing[...] = placed.astype(jnp.bfloat16)


def finish(own, arrived, slot_row, slots):
    shapes = (own.shape, (2 * slots, own.shape[1] // 2))
    return pl.pallas_call(
        finish_kernel,
        out_shape=tuple(jax.ShapeDtypeStruct(one, jnp.bfloat16) for one in shapes),
        in_specs=[VMEM] * 4,
        out_specs=(VMEM, VMEM),
        compiler_params=pltpu.CompilerParams(vmem_limit_bytes=16 * 1024 * 1024),
        name="finish",
    )(own, *arrived, slot_row)


def attend_kernel(
    by_owner, request_docs, q, fresh, held, spare, key_bias, row_place, key_place, *rest
):
    sources, (mixed, keys, values, counts, sems) = rest[:-5], rest[-5:]
    me = lax.axis_index("seq")
    doc_count = request_docs.shape[1]
    head_dim = keys.shape[1] // 2
    doc_len = keys.shape[0] // doc_count
    owners = request_docs.shape[0]
    slots = sources[0].shape[0] if not by_owner else 2 * sources[0].shape[1]
    step = doc_count // sems.shape[1]
    blocks = doc_count // step
    block_rows = mixed.shape[1] // blocks
    block_keys = step * doc_len
    heads = mixed.shape[2] // head_dim
    left = pl.ds(0, head_dim)

    for o in range(owners):
        counts[o] = 0

    def one_doc(j, carry):
        doc = request_docs[me, j]
        owner = lax.div(doc, slots)
        rank = counts[owner]
        counts[owner] = rank + 1
        place = pl.ds(pl.multiple_of(j * doc_len, doc_len), doc_len)
        block = lax.div(j, step)

        def fetch(key_source, value_source):
            pltpu.make_async_copy(key_source, keys.at[place, left], sems.at[0, block]).start()
            pltpu.make_async_copy(value_source, values.at[place, left], sems.at[1, block]).start()

        if by_owner:
            fetch(sources[0].at[owner, rank, 0], sources[0].at[owner, rank, 1])
        else:
            away = lax.bitwise_xor(me, owner)

            @pl.when(away == 0)
            def _():
                slot = lax.rem(doc, slots)
                fetch(sources[0].at[slot], sources[1].at[slot])

            for k, source in zip((2, 3, 1), sources[2:]):

                @pl.when(away == k)
                def _():
                    fetch(source.at[rank, 0], source.at[rank, 1])

        return carry

    lax.fori_loop(0, doc_count, one_doc, 0)

    def assemble(b):
        block = pl.ds(b * block_keys, block_keys)
        for i, context in enumerate((keys, values)):
            pltpu.make_async_copy(
                context.at[block, left], context.at[block, left], sems.at[i, b]
            ).wait()
        block = slice(b * block_keys, (b + 1) * block_keys)
        spares = jnp.dot(
            spare[:, block], keys[block, :head_dim], preferred_element_type=jnp.float32
        ).astype(jnp.bfloat16)
        for j in range(b * step, (b + 1) * step):
            place = slice(j * doc_len, (j + 1) * doc_len)
            used = held[place, :]
            key = jnp.where(used > 0, keys[place, :head_dim], spares[j : j + 1, :])
            keys[place, :head_dim] = key
            keys[place, head_dim:] = key
            values[place, :head_dim] = values[place, :head_dim] * used
            values[place, head_dim:] = used

    fresh_count = fresh.shape[0]
    spare_rows = jnp.zeros((-fresh_count % 128, 2 * head_dim), fresh.dtype)
    fresh_k = jnp.concatenate([fresh[:, :head_dim]] * 2, axis=1)
    fresh_k = jnp.concatenate([fresh_k, spare_rows], axis=0)
    fresh_v = jnp.concatenate([fresh[:, head_dim:], jnp.ones_like(fresh[:, head_dim:])], axis=1)
    fresh_v = jnp.concatenate([fresh_v, spare_rows], axis=0)
    slot_place = lax.broadcasted_iota(jnp.int32, (1, block_keys), 1)
    contract_last = (((1,), (1,)), ((), ()))
    for b in range(blocks):
        assemble(b)
    for b in range(blocks):
        rows = slice(b * block_rows, (b + 1) * block_rows)
        q_here = q[b * heads * block_rows : (b + 1) * heads * block_rows, :]
        own_place = row_place[rows, :]

        def scores(some_keys):
            return lax.dot_general(
                q_here, some_keys, contract_last, preferred_element_type=jnp.float32
            )

        def masked(some_keys, allowed):
            shape = (heads, block_rows, some_keys.shape[0])
            kept = jnp.where(allowed[None], scores(some_keys).reshape(shape), MASKED)
            return kept.reshape(heads * block_rows, some_keys.shape[0])

        chunks, sides = [], []
        for c in range(b):
            part = slice(c * block_keys, (c + 1) * block_keys)
            chunks.append(scores(keys[part, :]))
            sides.append(values[part, :])
        part = slice(b * block_keys, (b + 1) * block_keys)
        allowed = (slot_place + b * block_keys <= own_place) & (key_bias[:, part] == 0)
        chunks.append(masked(keys[part, :], allowed))
        sides.append(values[part, :])
        chunks.append(masked(fresh_k, key_place[...] <= own_place))
        sides.append(fresh_v)
        lane_max = functools.reduce(
            jnp.maximum,
            [one[:, i : i + 128] for one in chunks for i in range(0, one.shape[1], 128)],
        )
        row_max = jnp.max(lane_max, axis=1, keepdims=True)
        total = jnp.zeros((heads * block_rows, 2 * head_dim), jnp.float32)
        for one, side in zip(chunks, sides):
            powers = jnp.exp2(one - row_max).astype(jnp.bfloat16)
            total += jnp.dot(powers, side, preferred_element_type=jnp.float32)
        result = (total[:, :head_dim] / total[:, head_dim:]).astype(mixed.dtype)
        for h in range(heads):
            mixed[0, rows, h * head_dim : (h + 1) * head_dim] = result[
                h * block_rows : (h + 1) * block_rows
            ]


def attend(
    shape, request_docs, q, fresh, held, spare, key_bias, row_place, key_place, sources, by_owner
):
    context, head_dim = held.shape
    return pl.pallas_call(
        functools.partial(attend_kernel, by_owner),
        out_shape=jax.ShapeDtypeStruct(shape, jnp.bfloat16),
        in_specs=[SMEM] + [VMEM] * 7 + [ANY] * len(sources),
        out_specs=VMEM,
        scratch_shapes=[
            pltpu.VMEM((context, 2 * head_dim), jnp.bfloat16),
            pltpu.VMEM((context, 2 * head_dim), jnp.bfloat16),
            pltpu.SMEM((request_docs.shape[0],), jnp.int32),
            pltpu.SemaphoreType.DMA((2, 4)),
        ],
        compiler_params=pltpu.CompilerParams(vmem_limit_bytes=32 * 1024 * 1024),
        name="attend",
    )(
        request_docs,
        q,
        fresh,
        held,
        spare,
        key_bias,
        row_place,
        key_place,
        *(in_hbm(one) for one in sources[:2]),
        *sources[2:],
    )


def shards(
    pairs,
    hidden,
    queries,
    w_key,
    w_value,
    store_keys,
    store_values,
    request_docs,
    doc_lengths,
    recompute_rows,
):
    seq_count = lax.axis_size("seq")
    slot_count, doc_len, head_dim = store_keys.shape
    capacity = slot_count // 2
    per_doc = recompute_rows.shape[2]

    if pairs:
        def swap(array, axis, apart):
            count = lax.axis_size(axis)
            return lax.ppermute(array, axis, [(i, i ^ apart) for i in range(count)])

        *w_send, h_send = pick_sent(hidden, w_key, w_value)
        w_far = [swap(part, "seq", 2) for part in w_send]
        h_mine = swap(h_send, "seq", 1)
        doc_1, doc_2, doc_3 = pick_docs(request_docs, store_keys, store_values, False)
        (h_mine,) = gate((h_mine,), (doc_1,), cost=8000000000)
        h_chip = swap(h_mine, "tp", 2)
        h_core = swap(h_mine, "tp", 1)
        w_swapped = [swap(w_far[0], "groups", 1)]
        doc_2, doc_3, w_far[1] = gate(
            (doc_2, doc_3, w_far[1]), (w_swapped[0],), cost=8 * 10**9
        )
        w_swapped.append(swap(w_far[1], "groups", 1))
        doc_1 = swap(doc_1, "seq", 1)
        docs = (swap(doc_2, "seq", 2), swap(doc_3, "seq", 3), doc_1)
        quarters = (h_mine, h_core, h_chip, swap(h_chip, "tp", 1))
        own, *parts = project(hidden, w_key, w_value, w_far, w_swapped, quarters, doc_1)
        arrived = [swap(one, "seq", 1) for one in parts]
        sources = (store_keys, store_values, *docs)
    else:
        (docs,) = pick_docs(request_docs, store_keys, store_values, True)
        sources = (lax.all_to_all(docs, "seq", split_axis=0, concat_axis=0, tiled=True),)
        weights = lax.all_gather(
            jnp.concatenate([w_key, w_value], axis=1), "seq", axis=0, tiled=True
        )
        own = jnp.dot(hidden[0], weights, preferred_element_type=jnp.float32)
        arrived = [jnp.zeros((own.shape[0], head_dim), jnp.bfloat16)] * 2

    q, held, spare, key_bias, row_place, key_place, slot_row = plan(
        request_docs, doc_lengths, recompute_rows, queries, slot_count, head_dim, doc_len
    )
    fresh, outgoing = finish(own, arrived, slot_row, seq_count * capacity * per_doc)
    mixed = attend(
        queries.shape,
        request_docs,
        q,
        fresh,
        held,
        spare,
        key_bias,
        row_place,
        key_place,
        sources,
        not pairs,
    )

    outgoing = outgoing.reshape(seq_count, capacity * per_doc * 2, head_dim)
    returned = lax.all_to_all(outgoing, "seq", split_axis=0, concat_axis=0, tiled=True)
    returned = returned.reshape(seq_count, capacity, per_doc, 2, head_dim)
    return (mixed, returned[None])


def solution(mesh):
    pairs = mesh.shape["seq"] == 4 and mesh.shape["groups"] == 2 and mesh.shape["tp"] == 4
    return jax.shard_map(
        functools.partial(shards, pairs),
        mesh=mesh,
        in_specs=(
            P(("groups", "seq"), None, None),
            P(("groups", "seq"), None, "tp"),
            P("seq", "tp"),
            P("seq", "tp"),
            P(("groups", "seq"), None, "tp"),
            P(("groups", "seq"), None, "tp"),
            P("groups", None),
            P("groups"),
            P(("groups", "seq"), None, None),
        ),
        out_specs=(
            P(("groups", "seq"), None, "tp"),
            P(("groups", "seq"), None, None, None, None, "tp"),
        ),
        check_vma=False,
    )
```

```python
import functools
import math

import jax
import jax.numpy as jnp
from jax import lax
from jax.experimental import pallas as pl
from jax.experimental.pallas import tpu as pltpu
from jax.sharding import PartitionSpec as P

ANY = pl.BlockSpec(memory_space=pl.ANY)
HBM = pl.BlockSpec(memory_space=pltpu.HBM)
SMEM = pl.BlockSpec(memory_space=pltpu.SMEM)
VMEM = pl.BlockSpec(memory_space=pltpu.VMEM)
MASKED = -1e30


def in_hbm(array):
    return pltpu.with_memory_space_constraint(array, pltpu.HBM)


def send_kernel(hidden, w_key, w_value, w_first, w_second, h_out, sems):
    group = lax.axis_index("groups")
    me = lax.axis_index("seq")
    rows, depth = h_out.shape[1:]
    for chosen, weight in ((0, w_key), (1, w_value)):

        @pl.when(group == chosen)
        def _():
            for i, out in enumerate((w_first, w_second)):
                part = weight.at[pl.ds(i * w_first.shape[0], out.shape[0])]
                pltpu.make_async_copy(part, out, sems.at[i]).start()

    first = me + 1 - 2 * lax.rem(me, 2)
    copies = []
    for i, block in enumerate((first, lax.rem(first + 2, 4))):
        source = hidden.at[
            0,
            pl.ds(pl.multiple_of(lax.axis_index("tp") * rows, rows), rows),
            pl.ds(pl.multiple_of(block * depth, depth), depth),
        ]
        copies.append(pltpu.make_async_copy(source, h_out.at[i], sems.at[2 + i]))
        copies[-1].start()
    for i, out in enumerate((w_first, w_second)):
        pltpu.make_async_copy(w_key.at[pl.ds(0, out.shape[0])], out, sems.at[i]).wait()
    for copy in copies:
        copy.wait()


def pick_sent(hidden, w_key, w_value):
    depth, width = w_key.shape
    h_shape = (2, hidden.shape[1] // 4, depth)
    first = depth * 7 // 32
    return pl.pallas_call(
        send_kernel,
        out_shape=(
            jax.ShapeDtypeStruct((first, width), jnp.bfloat16),
            jax.ShapeDtypeStruct((depth - first, width), jnp.bfloat16),
            jax.ShapeDtypeStruct(h_shape, jnp.bfloat16),
        ),
        in_specs=[ANY] * 3,
        out_specs=(VMEM,) * 3,
        scratch_shapes=[pltpu.SemaphoreType.DMA((4,))],
        compiler_params=pltpu.CompilerParams(vmem_limit_bytes=16 * 1024 * 1024),
        name="pick_sent",
    )(in_hbm(hidden), in_hbm(w_key), in_hbm(w_value))


def gate_kernel(*refs):
    pass


def gate(arrays, first=(), pinned=0, cost=1):
    return pl.pallas_call(
        gate_kernel,
        out_shape=tuple(jax.ShapeDtypeStruct(one.shape, one.dtype) for one in arrays),
        in_specs=[ANY] * (len(arrays) + len(first)),
        out_specs=(ANY,) * len(arrays),
        input_output_aliases={i: i for i in range(len(arrays))},
        compiler_params=pltpu.CompilerParams(vmem_limit_bytes=1024 * 1024),
        cost_estimate=pl.CostEstimate(flops=cost, bytes_accessed=1, transcendentals=0),
        name="gate",
    )(*(in_hbm(one) for one in arrays[:pinned]), *arrays[pinned:], *first)


def docs_kernel(by_owner, request_docs, store_keys, store_values, *rest):
    *outs, picks, sems = rest
    me = lax.axis_index("seq")
    requests, doc_count = request_docs.shape
    slots = store_keys.shape[0]
    capacity = slots // 2

    def one_request(r, carry):
        for c in range(capacity):
            picks[r, c] = 0

        def one_doc(j, count):
            doc = request_docs[r, j]
            mine = lax.div(doc, slots) == me

            @pl.when(mine)
            def _():
                picks[r, jnp.minimum(count, capacity - 1)] = lax.rem(doc, slots)

            return count + mine.astype(jnp.int32)

        lax.fori_loop(0, doc_count, one_doc, jnp.int32(0), unroll=True)
        return carry

    lax.fori_loop(0, requests, one_request, 0)

    def send(r, out, sem):
        for c in range(capacity):
            slot = picks[r, c]
            pltpu.make_async_copy(store_keys.at[slot], out.at[c, 0], sem).start()
            pltpu.make_async_copy(store_values.at[slot], out.at[c, 1], sem).start()

    if by_owner:

        def one_send(r, carry):
            send(r, outs[0].at[r], sems.at[0])
            return carry

        lax.fori_loop(0, requests, one_send, 0)
    else:
        for i, out in enumerate(outs):
            send(lax.bitwise_xor(me, i + 1), out, sems.at[i])
    for i, out in enumerate(outs):
        pltpu.make_async_copy(out, out, sems.at[i]).wait()


def pick_docs(request_docs, store_keys, store_values, by_owner):
    requests = request_docs.shape[0]
    capacity = store_keys.shape[0] // 2
    one = (capacity, 2) + store_keys.shape[1:]
    shapes = ((requests,) + one,) if by_owner else (one,) * (requests - 1)
    return pl.pallas_call(
        functools.partial(docs_kernel, by_owner),
        out_shape=tuple(jax.ShapeDtypeStruct(one, jnp.bfloat16) for one in shapes),
        in_specs=[SMEM, ANY, ANY],
        out_specs=(VMEM,) * len(shapes),
        scratch_shapes=[
            pltpu.SMEM((requests, capacity), jnp.int32),
            pltpu.SemaphoreType.DMA((len(shapes),)),
        ],
        compiler_params=pltpu.CompilerParams(vmem_limit_bytes=16 * 1024 * 1024),
        name="pick_docs",
    )(request_docs, in_hbm(store_keys), in_hbm(store_values))


def near_kernel(hidden, w_key, w_value, _, total, w, h, sems):
    depth, width = w_key.shape
    start = pl.multiple_of(lax.axis_index("seq") * depth, depth)
    copies = [
        pltpu.make_async_copy(w_key, w.at[:, pl.ds(0, width)], sems.at[0]),
        pltpu.make_async_copy(w_value, w.at[:, pl.ds(width, width)], sems.at[1]),
        pltpu.make_async_copy(hidden.at[0, :, pl.ds(start, depth)], h, sems.at[2]),
    ]
    for copy in copies:
        copy.start()
    for copy in copies:
        copy.wait()
    total[...] = jnp.dot(h[...], w[...], preferred_element_type=jnp.float32)


def lay_quarters(quarters, block, rows, copy):
    piece = rows.shape[0] // len(quarters)
    for k, quarter in enumerate(quarters):
        start = pl.multiple_of(lax.bitwise_xor(lax.axis_index("tp"), k) * piece, piece)
        copy(quarter.at[block], rows.at[pl.ds(start, piece)])


def neighbour_kernel(w_key, w_value, *rest):
    *quarters, total, w, n, sems = rest
    width = w_key.shape[1]
    copies = []

    def copy(source, target):
        copies.append(pltpu.make_async_copy(source, target, sems.at[len(copies)]))
        copies[-1].start()

    for i, held in enumerate((w_key, w_value)):
        copy(held, w.at[:, pl.ds(i * width, width)])
    lay_quarters(quarters, 0, n, copy)
    for one in copies:
        one.wait()
    total[...] = jnp.dot(n[...], w[...], preferred_element_type=jnp.float32)


def far_kernel(hidden, w_far_0, w_far_1, w_swapped_0, w_swapped_1, near, neighbour, *rest):
    *quarters, own, part_0, part_1, part_2, w, h, n, sems = rest
    group = lax.axis_index("groups")
    start, width = w_far_0.shape
    depth = start + w_far_1.shape[0]
    copies = []

    def copy(source, target):
        copies.append(pltpu.make_async_copy(source, target, sems.at[len(copies)]))
        copies[-1].start()

    pairs = ((w_far_0, w_far_1, group), (w_swapped_0, w_swapped_1, 1 - group))
    for first, second, place in pairs:
        columns = pl.ds(pl.multiple_of(place * width, width), width)
        copy(first, w.at[pl.ds(0, start), columns])
        copy(second, w.at[pl.ds(start, depth - start), columns])
    start = pl.multiple_of(lax.rem(lax.axis_index("seq") + 2, 4) * depth, depth)
    copy(hidden.at[0, :, pl.ds(start, depth)], h)
    lay_quarters(quarters, 1, n, copy)
    for one in copies:
        one.wait()
    own[...] = near[...] + jnp.dot(h[...], w[...], preferred_element_type=jnp.float32)
    total = neighbour[...] + jnp.dot(n[...], w[...], preferred_element_type=jnp.float32)
    for i, part in enumerate((part_0, part_1, part_2)):
        count = part.shape[0]
        part[...] = total[i * count : (i + 1) * count].astype(part.dtype)


def project(hidden, w_key, w_value, w_far, w_swapped, quarters, first):
    depth, width = w_key.shape
    rows = hidden.shape[1]
    sums = jax.ShapeDtypeStruct((rows, 2 * width), jnp.float32)
    w_scratch = pltpu.VMEM((depth, 2 * width), jnp.bfloat16)
    h_scratch = pltpu.VMEM((rows, depth), jnp.bfloat16)
    limit = pltpu.CompilerParams(vmem_limit_bytes=16 * 1024 * 1024)
    cheap = pl.CostEstimate(flops=1, bytes_accessed=1, transcendentals=0)
    w_key, w_value = in_hbm(w_key), in_hbm(w_value)
    near = pl.pallas_call(
        near_kernel,
        out_shape=sums,
        in_specs=[ANY] * 4,
        out_specs=VMEM,
        scratch_shapes=[w_scratch, h_scratch, pltpu.SemaphoreType.DMA((3,))],
        compiler_params=limit,
        cost_estimate=pl.CostEstimate(flops=10**10, bytes_accessed=1, transcendentals=0),
        name="project_near",
    )(hidden, w_key, w_value, first)
    neighbour = pl.pallas_call(
        neighbour_kernel,
        out_shape=sums,
        in_specs=[ANY] * (2 + len(quarters)),
        out_specs=VMEM,
        scratch_shapes=[
            w_scratch,
            h_scratch,
            pltpu.SemaphoreType.DMA((2 + len(quarters),)),
        ],
        compiler_params=limit,
        cost_estimate=cheap,
        name="project_neighbour",
    )(w_key, w_value, *quarters)
    return pl.pallas_call(
        far_kernel,
        out_shape=(sums,) + (jax.ShapeDtypeStruct((rows // 3, 2 * width), jnp.bfloat16),) * 3,
        in_specs=[ANY] * 5 + [VMEM] * 2 + [ANY] * len(quarters),
        out_specs=(VMEM,) * 4,
        scratch_shapes=[
            w_scratch,
            h_scratch,
            h_scratch,
            pltpu.SemaphoreType.DMA((5 + len(quarters),)),
        ],
        compiler_params=limit,
        cost_estimate=cheap,
        name="project_far",
    )(hidden, *w_far, *w_swapped, near, neighbour, *quarters)


def plan_kernel(
    capacity, slots, request_docs, doc_lengths, rows, queries, q, held, spare, key_bias, row_place, key_place,
    slot_row, counts
):
    head_dim = q.shape[1] // 2
    heads = queries.shape[2] // head_dim
    block_rows = 4 * rows.shape[0]
    scale = math.log2(math.e) / math.sqrt(head_dim)
    for b in range(queries.shape[1] // block_rows):
        for h in range(heads):
            here = queries[0, b * block_rows : (b + 1) * block_rows, h * head_dim : (h + 1) * head_dim]
            here = here.astype(jnp.float32) * scale
            high = here.astype(jnp.bfloat16)
            place = slice((b * heads + h) * block_rows, (b * heads + h + 1) * block_rows)
            q[place, :head_dim] = high
            q[place, head_dim:] = (here - high.astype(jnp.float32)).astype(jnp.bfloat16)
    me = lax.axis_index("seq")
    per_doc, _, doc_count = rows.shape
    doc_len = held.shape[0] // doc_count
    row_count = row_place.shape[0]
    docs = lax.broadcasted_iota(jnp.int32, (1, doc_count), 1)
    lengths = jnp.zeros((1, doc_count), jnp.int32)
    places = jnp.zeros((1, doc_count), jnp.int32)
    for o in range(counts.shape[0]):
        counts[o] = 0
    for j in range(doc_count):
        doc = request_docs[me, j]
        owner = lax.div(doc, slots)
        rank = counts[owner]
        counts[owner] = rank + 1
        lengths = jnp.where(docs == j, doc_lengths[doc], lengths)
        places = jnp.where(docs == j, owner * capacity + rank, places)
    slot = lax.broadcasted_iota(jnp.int32, (doc_len, doc_count), 0)
    used = slot < lengths
    for i in range(per_doc):
        used &= slot != rows[i]
    used = used.astype(jnp.float32)
    first = jnp.min(jnp.where(used > 0, slot, doc_len), axis=0, keepdims=True)
    firsts = (slot == first).astype(jnp.bfloat16)
    eye = lax.broadcasted_iota(jnp.int32, (doc_count, doc_count), 0) == docs
    across = (((1,), (1,)), ((), ()))

    def turned(columns):
        return lax.dot_general(
            eye.astype(jnp.bfloat16), columns, across, preferred_element_type=jnp.float32
        )

    bias = jnp.where(turned(used.astype(jnp.bfloat16)) > 0, 0.0, MASKED)
    firsts = turned(firsts)
    doc = lax.broadcasted_iota(jnp.int32, (doc_count, 1), 0)
    for j in range(doc_count):
        part = slice(j * doc_len, (j + 1) * doc_len)
        held[part, :] = jnp.broadcast_to(used[:, j : j + 1], (doc_len, held.shape[1])).astype(
            held.dtype
        )
        key_bias[:, part] = bias[j : j + 1, :]
        spare[:, part] = jnp.where(doc == j, firsts, 0.0).astype(spare.dtype)
    row = lax.broadcasted_iota(jnp.int32, (row_count, doc_count), 0)
    start = per_doc * lax.broadcasted_iota(jnp.int32, (row_count, doc_count), 1)
    of_doc = (row >= start) & (row < start + per_doc)
    nth = jnp.sum(jnp.where(of_doc, row - start, 0), axis=1, keepdims=True)
    chosen = jnp.zeros((row_count, doc_count), jnp.int32)
    for i in range(per_doc):
        chosen = jnp.where(nth == i, rows[i], chosen)
    chosen = jnp.where(of_doc, chosen + doc_len * docs, 0)
    column = jnp.sum(chosen, axis=1, keepdims=True)
    goes = nth + per_doc * jnp.sum(jnp.where(of_doc, places, 0), axis=1, keepdims=True)
    row_place[...] = column
    square = (row_count, row_count)
    same = lax.broadcasted_iota(jnp.int32, square, 0) == lax.broadcasted_iota(jnp.int32, square, 1)
    key_place[...] = jnp.full(key_place.shape, held.shape[0], jnp.int32)
    key_place[:, :row_count] = jnp.sum(jnp.where(same, column, 0), axis=0, keepdims=True)
    slot_row[...] = jnp.sum(jnp.where(same, goes, 0), axis=0, keepdims=True)


def plan(request_docs, doc_lengths, recompute_rows, queries, slots, head_dim, doc_len):
    _, doc_count, per_doc = recompute_rows.shape
    rows = doc_count * per_doc
    context = doc_count * doc_len
    shapes = (
        ((rows * queries.shape[2] // head_dim, 2 * head_dim), jnp.bfloat16),
        ((context, head_dim), jnp.bfloat16),
        ((doc_count, context), jnp.bfloat16),
        ((1, context), jnp.float32),
        ((rows, 1), jnp.int32),
        ((1, rows + -rows % 128), jnp.int32),
        ((1, rows), jnp.int32),
    )
    return pl.pallas_call(
        functools.partial(plan_kernel, slots // 2, slots),
        out_shape=tuple(jax.ShapeDtypeStruct(*one) for one in shapes),
        in_specs=[SMEM, SMEM, VMEM, VMEM],
        out_specs=(VMEM,) * len(shapes),
        scratch_shapes=[pltpu.SMEM((request_docs.shape[0],), jnp.int32)],
        compiler_params=pltpu.CompilerParams(vmem_limit_bytes=16 * 1024 * 1024),
        name="plan",
    )(request_docs, doc_lengths, jnp.transpose(recompute_rows, (2, 0, 1)), queries)


def finish_kernel(own, arrived_0, arrived_1, arrived_2, slot_row, fresh, outgoing):
    arrived = jnp.concatenate([arrived_0[...], arrived_1[...], arrived_2[...]], axis=0)
    total = (own[...] + arrived.astype(jnp.float32)).astype(jnp.bfloat16)
    fresh[...] = total
    width = outgoing.shape[1]
    slots = lax.broadcasted_iota(jnp.int32, (outgoing.shape[0], 1), 0)
    placed = jnp.zeros(outgoing.shape, jnp.float32)
    for i in range(2):
        pick = (slots == 2 * slot_row[...] + i).astype(jnp.bfloat16)
        part = total[:, i * width : (i + 1) * width]
        placed += jnp.dot(pick, part, preferred_element_type=jnp.float32)
    outgoing[...] = placed.astype(jnp.bfloat16)


def finish(own, arrived, slot_row, slots):
    shapes = (own.shape, (2 * slots, own.shape[1] // 2))
    return pl.pallas_call(
        finish_kernel,
        out_shape=tuple(jax.ShapeDtypeStruct(one, jnp.bfloat16) for one in shapes),
        in_specs=[VMEM] * 5,
        out_specs=(VMEM, VMEM),
        compiler_params=pltpu.CompilerParams(vmem_limit_bytes=16 * 1024 * 1024),
        name="finish",
    )(own, *arrived, slot_row)


def attend_kernel(
    by_owner, request_docs, q, fresh, held, spare, key_bias, row_place, key_place, *rest
):
    sources, (mixed, keys, values, counts, sems) = rest[:-5], rest[-5:]
    me = lax.axis_index("seq")
    doc_count = request_docs.shape[1]
    head_dim = keys.shape[1] // 2
    doc_len = keys.shape[0] // doc_count
    owners = request_docs.shape[0]
    slots = sources[0].shape[0] if not by_owner else 2 * sources[0].shape[1]
    step = doc_count // sems.shape[1]
    blocks = doc_count // step
    block_rows = mixed.shape[1] // blocks
    block_keys = step * doc_len
    heads = mixed.shape[2] // head_dim
    left = pl.ds(0, head_dim)

    for o in range(owners):
        counts[o] = 0

    def one_doc(j, carry):
        doc = request_docs[me, j]
        owner = lax.div(doc, slots)
        rank = counts[owner]
        counts[owner] = rank + 1
        place = pl.ds(pl.multiple_of(j * doc_len, doc_len), doc_len)
        block = lax.div(j, step)

        def fetch(key_source, value_source):
            pltpu.make_async_copy(key_source, keys.at[place, left], sems.at[0, block]).start()
            pltpu.make_async_copy(value_source, values.at[place, left], sems.at[1, block]).start()

        if by_owner:
            fetch(sources[0].at[owner, rank, 0], sources[0].at[owner, rank, 1])
        else:
            away = lax.bitwise_xor(me, owner)

            @pl.when(away == 0)
            def _():
                slot = lax.rem(doc, slots)
                fetch(sources[0].at[slot], sources[1].at[slot])

            for k, source in zip((2, 3, 1), sources[2:]):

                @pl.when(away == k)
                def _():
                    fetch(source.at[rank, 0], source.at[rank, 1])

        return carry

    lax.fori_loop(0, doc_count, one_doc, 0)

    def assemble(b):
        block = pl.ds(b * block_keys, block_keys)
        for i, context in enumerate((keys, values)):
            pltpu.make_async_copy(
                context.at[block, left], context.at[block, left], sems.at[i, b]
            ).wait()
        block = slice(b * block_keys, (b + 1) * block_keys)
        spares = jnp.dot(
            spare[:, block], keys[block, :head_dim], preferred_element_type=jnp.float32
        ).astype(jnp.bfloat16)
        for j in range(b * step, (b + 1) * step):
            place = slice(j * doc_len, (j + 1) * doc_len)
            used = held[place, :]
            key = jnp.where(used > 0, keys[place, :head_dim], spares[j : j + 1, :])
            keys[place, :head_dim] = key
            keys[place, head_dim:] = key
            values[place, :head_dim] = values[place, :head_dim] * used
            values[place, head_dim:] = used

    fresh_count = fresh.shape[0]
    spare_rows = jnp.zeros((-fresh_count % 128, 2 * head_dim), fresh.dtype)
    fresh_k = jnp.concatenate([fresh[:, :head_dim]] * 2, axis=1)
    fresh_k = jnp.concatenate([fresh_k, spare_rows], axis=0)
    fresh_v = jnp.concatenate([fresh[:, head_dim:], jnp.ones_like(fresh[:, head_dim:])], axis=1)
    fresh_v = jnp.concatenate([fresh_v, spare_rows], axis=0)
    slot_place = lax.broadcasted_iota(jnp.int32, (1, block_keys), 1)
    contract_last = (((1,), (1,)), ((), ()))
    for b in range(blocks):
        assemble(b)
    for b in range(blocks):
        rows = slice(b * block_rows, (b + 1) * block_rows)
        q_here = q[b * heads * block_rows : (b + 1) * heads * block_rows, :]
        own_place = row_place[rows, :]

        def scores(some_keys):
            return lax.dot_general(
                q_here, some_keys, contract_last, preferred_element_type=jnp.float32
            )

        def masked(some_keys, allowed):
            shape = (heads, block_rows, some_keys.shape[0])
            kept = jnp.where(allowed[None], scores(some_keys).reshape(shape), MASKED)
            return kept.reshape(heads * block_rows, some_keys.shape[0])

        chunks, sides = [], []
        for c in range(b):
            part = slice(c * block_keys, (c + 1) * block_keys)
            chunks.append(scores(keys[part, :]))
            sides.append(values[part, :])
        part = slice(b * block_keys, (b + 1) * block_keys)
        allowed = (slot_place + b * block_keys <= own_place) & (key_bias[:, part] == 0)
        chunks.append(masked(keys[part, :], allowed))
        sides.append(values[part, :])
        chunks.append(masked(fresh_k, key_place[...] <= own_place))
        sides.append(fresh_v)
        lane_max = functools.reduce(
            jnp.maximum,
            [one[:, i : i + 128] for one in chunks for i in range(0, one.shape[1], 128)],
        )
        row_max = jnp.max(lane_max, axis=1, keepdims=True)
        total = jnp.zeros((heads * block_rows, 2 * head_dim), jnp.float32)
        for one, side in zip(chunks, sides):
            powers = jnp.exp2(one - row_max).astype(jnp.bfloat16)
            total += jnp.dot(powers, side, preferred_element_type=jnp.float32)
        result = (total[:, :head_dim] / total[:, head_dim:]).astype(mixed.dtype)
        for h in range(heads):
            mixed[0, rows, h * head_dim : (h + 1) * head_dim] = result[
                h * block_rows : (h + 1) * block_rows
            ]


def attend(
    shape, request_docs, q, fresh, held, spare, key_bias, row_place, key_place, sources, by_owner
):
    context, head_dim = held.shape
    return pl.pallas_call(
        functools.partial(attend_kernel, by_owner),
        out_shape=jax.ShapeDtypeStruct(shape, jnp.bfloat16),
        in_specs=[SMEM] + [VMEM] * 7 + [ANY] * len(sources),
        out_specs=VMEM,
        scratch_shapes=[
            pltpu.VMEM((context, 2 * head_dim), jnp.bfloat16),
            pltpu.VMEM((context, 2 * head_dim), jnp.bfloat16),
            pltpu.SMEM((request_docs.shape[0],), jnp.int32),
            pltpu.SemaphoreType.DMA((2, 4)),
        ],
        compiler_params=pltpu.CompilerParams(vmem_limit_bytes=32 * 1024 * 1024),
        name="attend",
    )(
        request_docs,
        q,
        fresh,
        held,
        spare,
        key_bias,
        row_place,
        key_place,
        *(in_hbm(one) for one in sources[:2]),
        *sources[2:],
    )


def shards(
    pairs,
    hidden,
    queries,
    w_key,
    w_value,
    store_keys,
    store_values,
    request_docs,
    doc_lengths,
    recompute_rows,
):
    seq_count = lax.axis_size("seq")
    slot_count, doc_len, head_dim = store_keys.shape
    capacity = slot_count // 2
    per_doc = recompute_rows.shape[2]

    if pairs:
        def swap(array, axis, apart):
            count = lax.axis_size(axis)
            return lax.ppermute(array, axis, [(i, i ^ apart) for i in range(count)])

        *w_send, h_send = pick_sent(hidden, w_key, w_value)
        w_far = [swap(part, "seq", 2) for part in w_send]
        h_mine = swap(h_send, "seq", 1)
        doc_1, doc_2, doc_3 = pick_docs(request_docs, store_keys, store_values, False)
        (h_mine,) = gate((h_mine,), (doc_1,), cost=8000000000)
        h_chip = swap(h_mine, "tp", 2)
        h_core = swap(h_mine, "tp", 1)
        w_swapped = [swap(w_far[0], "groups", 1)]
        doc_2, doc_3, w_far[1] = gate(
            (doc_2, doc_3, w_far[1]), (w_swapped[0],), cost=8 * 10**9
        )
        w_swapped.append(swap(w_far[1], "groups", 1))
        doc_1 = swap(doc_1, "seq", 1)
        docs = (swap(doc_2, "seq", 2), swap(doc_3, "seq", 3), doc_1)
        quarters = (h_mine, h_core, h_chip, swap(h_chip, "tp", 1))
        own, *parts = project(hidden, w_key, w_value, w_far, w_swapped, quarters, doc_1)
        arrived = [swap(one, "seq", 1) for one in parts]
        sources = (store_keys, store_values, *docs)
    else:
        (docs,) = pick_docs(request_docs, store_keys, store_values, True)
        sources = (lax.all_to_all(docs, "seq", split_axis=0, concat_axis=0, tiled=True),)
        weights = lax.all_gather(
            jnp.concatenate([w_key, w_value], axis=1), "seq", axis=0, tiled=True
        )
        own = jnp.dot(hidden[0], weights, preferred_element_type=jnp.float32)
        arrived = [jnp.zeros((own.shape[0] // 3, 2 * head_dim), jnp.bfloat16)] * 3

    q, held, spare, key_bias, row_place, key_place, slot_row = plan(
        request_docs, doc_lengths, recompute_rows, queries, slot_count, head_dim, doc_len
    )
    fresh, outgoing = finish(own, arrived, slot_row, seq_count * capacity * per_doc)
    mixed = attend(
        queries.shape,
        request_docs,
        q,
        fresh,
        held,
        spare,
        key_bias,
        row_place,
        key_place,
        sources,
        not pairs,
    )

    outgoing = outgoing.reshape(seq_count, capacity * per_doc * 2, head_dim)
    returned = lax.all_to_all(outgoing, "seq", split_axis=0, concat_axis=0, tiled=True)
    returned = returned.reshape(seq_count, capacity, per_doc, 2, head_dim)
    return (mixed, returned[None])


def solution(mesh):
    pairs = mesh.shape["seq"] == 4 and mesh.shape["groups"] == 2 and mesh.shape["tp"] == 4
    return jax.shard_map(
        functools.partial(shards, pairs),
        mesh=mesh,
        in_specs=(
            P(("groups", "seq"), None, None),
            P(("groups", "seq"), None, "tp"),
            P("seq", "tp"),
            P("seq", "tp"),
            P(("groups", "seq"), None, "tp"),
            P(("groups", "seq"), None, "tp"),
            P("groups", None),
            P("groups"),
            P(("groups", "seq"), None, None),
        ),
        out_specs=(
            P(("groups", "seq"), None, "tp"),
            P(("groups", "seq"), None, None, None, None, "tp"),
        ),
        check_vma=False,
    )
```

```python
import functools
import math

import jax
import jax.numpy as jnp
from jax import lax
from jax.experimental import pallas as pl
from jax.experimental.pallas import tpu as pltpu
from jax.sharding import PartitionSpec as P

ANY = pl.BlockSpec(memory_space=pl.ANY)
HBM = pl.BlockSpec(memory_space=pltpu.HBM)
SMEM = pl.BlockSpec(memory_space=pltpu.SMEM)
VMEM = pl.BlockSpec(memory_space=pltpu.VMEM)
MASKED = -1e30


def in_hbm(array):
    return pltpu.with_memory_space_constraint(array, pltpu.HBM)


def send_kernel(hidden, w_key, w_value, w_first, w_second, h_out, sems):
    group = lax.axis_index("groups")
    me = lax.axis_index("seq")
    rows, depth = h_out.shape[1:]
    for chosen, weight in ((0, w_key), (1, w_value)):

        @pl.when(group == chosen)
        def _():
            for i, out in enumerate((w_first, w_second)):
                part = weight.at[pl.ds(i * w_first.shape[0], out.shape[0])]
                pltpu.make_async_copy(part, out, sems.at[i]).start()

    first = me + 1 - 2 * lax.rem(me, 2)
    copies = []
    for i, block in enumerate((first, lax.rem(first + 2, 4))):
        source = hidden.at[
            0,
            pl.ds(pl.multiple_of(lax.axis_index("tp") * rows, rows), rows),
            pl.ds(pl.multiple_of(block * depth, depth), depth),
        ]
        copies.append(pltpu.make_async_copy(source, h_out.at[i], sems.at[2 + i]))
        copies[-1].start()
    for i, out in enumerate((w_first, w_second)):
        pltpu.make_async_copy(w_key.at[pl.ds(0, out.shape[0])], out, sems.at[i]).wait()
    for copy in copies:
        copy.wait()


def pick_sent(hidden, w_key, w_value):
    depth, width = w_key.shape
    h_shape = (2, hidden.shape[1] // 4, depth)
    first = depth * 7 // 32
    return pl.pallas_call(
        send_kernel,
        out_shape=(
            jax.ShapeDtypeStruct((first, width), jnp.bfloat16),
            jax.ShapeDtypeStruct((depth - first, width), jnp.bfloat16),
            jax.ShapeDtypeStruct(h_shape, jnp.bfloat16),
        ),
        in_specs=[ANY] * 3,
        out_specs=(VMEM,) * 3,
        scratch_shapes=[pltpu.SemaphoreType.DMA((4,))],
        compiler_params=pltpu.CompilerParams(vmem_limit_bytes=16 * 1024 * 1024),
        name="pick_sent",
    )(in_hbm(hidden), in_hbm(w_key), in_hbm(w_value))


def gate_kernel(*refs):
    pass


def gate(arrays, first=(), pinned=0, cost=1):
    return pl.pallas_call(
        gate_kernel,
        out_shape=tuple(jax.ShapeDtypeStruct(one.shape, one.dtype) for one in arrays),
        in_specs=[ANY] * (len(arrays) + len(first)),
        out_specs=(ANY,) * len(arrays),
        input_output_aliases={i: i for i in range(len(arrays))},
        compiler_params=pltpu.CompilerParams(vmem_limit_bytes=1024 * 1024),
        cost_estimate=pl.CostEstimate(flops=cost, bytes_accessed=1, transcendentals=0),
        name="gate",
    )(*(in_hbm(one) for one in arrays[:pinned]), *arrays[pinned:], *first)


def docs_kernel(by_owner, request_docs, store_keys, store_values, *rest):
    *outs, picks, sems = rest
    me = lax.axis_index("seq")
    requests, doc_count = request_docs.shape
    slots = store_keys.shape[0]
    capacity = slots // 2

    def one_request(r, carry):
        for c in range(capacity):
            picks[r, c] = 0

        def one_doc(j, count):
            doc = request_docs[r, j]
            mine = lax.div(doc, slots) == me

            @pl.when(mine)
            def _():
                picks[r, jnp.minimum(count, capacity - 1)] = lax.rem(doc, slots)

            return count + mine.astype(jnp.int32)

        lax.fori_loop(0, doc_count, one_doc, jnp.int32(0), unroll=True)
        return carry

    lax.fori_loop(0, requests, one_request, 0)

    def send(r, out, sem):
        for c in range(capacity):
            slot = picks[r, c]
            pltpu.make_async_copy(store_keys.at[slot], out.at[c, 0], sem).start()
            pltpu.make_async_copy(store_values.at[slot], out.at[c, 1], sem).start()

    if by_owner:

        def one_send(r, carry):
            send(r, outs[0].at[r], sems.at[0])
            return carry

        lax.fori_loop(0, requests, one_send, 0)
    else:
        for i, out in enumerate(outs):
            send(lax.bitwise_xor(me, i + 1), out, sems.at[i])
    for i, out in enumerate(outs):
        pltpu.make_async_copy(out, out, sems.at[i]).wait()


def pick_docs(request_docs, store_keys, store_values, by_owner):
    requests = request_docs.shape[0]
    capacity = store_keys.shape[0] // 2
    one = (capacity, 2) + store_keys.shape[1:]
    shapes = ((requests,) + one,) if by_owner else (one,) * (requests - 1)
    return pl.pallas_call(
        functools.partial(docs_kernel, by_owner),
        out_shape=tuple(jax.ShapeDtypeStruct(one, jnp.bfloat16) for one in shapes),
        in_specs=[SMEM, ANY, ANY],
        out_specs=(VMEM,) * len(shapes),
        scratch_shapes=[
            pltpu.SMEM((requests, capacity), jnp.int32),
            pltpu.SemaphoreType.DMA((len(shapes),)),
        ],
        compiler_params=pltpu.CompilerParams(vmem_limit_bytes=16 * 1024 * 1024),
        name="pick_docs",
    )(request_docs, in_hbm(store_keys), in_hbm(store_values))


def near_kernel(hidden, w_key, w_value, _, total, w, h, sems):
    depth, width = w_key.shape
    start = pl.multiple_of(lax.axis_index("seq") * depth, depth)
    copies = [
        pltpu.make_async_copy(w_key, w.at[:, pl.ds(0, width)], sems.at[0]),
        pltpu.make_async_copy(w_value, w.at[:, pl.ds(width, width)], sems.at[1]),
        pltpu.make_async_copy(hidden.at[0, :, pl.ds(start, depth)], h, sems.at[2]),
    ]
    for copy in copies:
        copy.start()
    for copy in copies:
        copy.wait()
    total[...] = jnp.dot(h[...], w[...], preferred_element_type=jnp.float32)


def lay_quarters(quarters, block, rows, copy):
    piece = rows.shape[0] // len(quarters)
    for k, quarter in enumerate(quarters):
        start = pl.multiple_of(lax.bitwise_xor(lax.axis_index("tp"), k) * piece, piece)
        copy(quarter.at[block], rows.at[pl.ds(start, piece)])


def neighbour_kernel(w_key, w_value, *rest):
    *quarters, total, w, n, sems = rest
    width = w_key.shape[1]
    copies = []

    def copy(source, target):
        copies.append(pltpu.make_async_copy(source, target, sems.at[len(copies)]))
        copies[-1].start()

    for i, held in enumerate((w_key, w_value)):
        copy(held, w.at[:, pl.ds(i * width, width)])
    lay_quarters(quarters, 0, n, copy)
    for one in copies:
        one.wait()
    total[...] = jnp.dot(n[...], w[...], preferred_element_type=jnp.float32)


def far_kernel(hidden, w_far_0, w_far_1, w_swapped_0, w_swapped_1, near, neighbour, *rest):
    *quarters, own, part_0, part_1, part_2, w, h, n, sems = rest
    group = lax.axis_index("groups")
    start, width = w_far_0.shape
    depth = start + w_far_1.shape[0]
    copies = []

    def copy(source, target):
        copies.append(pltpu.make_async_copy(source, target, sems.at[len(copies)]))
        copies[-1].start()

    pairs = ((w_far_0, w_far_1, group), (w_swapped_0, w_swapped_1, 1 - group))
    for first, second, place in pairs:
        columns = pl.ds(pl.multiple_of(place * width, width), width)
        copy(first, w.at[pl.ds(0, start), columns])
        copy(second, w.at[pl.ds(start, depth - start), columns])
    start = pl.multiple_of(lax.rem(lax.axis_index("seq") + 2, 4) * depth, depth)
    copy(hidden.at[0, :, pl.ds(start, depth)], h)
    lay_quarters(quarters, 1, n, copy)
    for one in copies:
        one.wait()
    own[...] = near[...] + jnp.dot(h[...], w[...], preferred_element_type=jnp.float32)
    total = neighbour[...] + jnp.dot(n[...], w[...], preferred_element_type=jnp.float32)
    for i, part in enumerate((part_0, part_1, part_2)):
        count = part.shape[0]
        part[...] = total[i * count : (i + 1) * count].astype(part.dtype)


def project(hidden, w_key, w_value, w_far, w_swapped, quarters, first):
    depth, width = w_key.shape
    rows = hidden.shape[1]
    sums = jax.ShapeDtypeStruct((rows, 2 * width), jnp.float32)
    w_scratch = pltpu.VMEM((depth, 2 * width), jnp.bfloat16)
    h_scratch = pltpu.VMEM((rows, depth), jnp.bfloat16)
    limit = pltpu.CompilerParams(vmem_limit_bytes=16 * 1024 * 1024)
    cheap = pl.CostEstimate(flops=1, bytes_accessed=1, transcendentals=0)
    w_key, w_value = in_hbm(w_key), in_hbm(w_value)
    near = pl.pallas_call(
        near_kernel,
        out_shape=sums,
        in_specs=[ANY] * 4,
        out_specs=VMEM,
        scratch_shapes=[w_scratch, h_scratch, pltpu.SemaphoreType.DMA((3,))],
        compiler_params=limit,
        cost_estimate=pl.CostEstimate(flops=10**10, bytes_accessed=1, transcendentals=0),
        name="project_near",
    )(hidden, w_key, w_value, first)
    neighbour = pl.pallas_call(
        neighbour_kernel,
        out_shape=sums,
        in_specs=[ANY] * (2 + len(quarters)),
        out_specs=VMEM,
        scratch_shapes=[
            w_scratch,
            h_scratch,
            pltpu.SemaphoreType.DMA((2 + len(quarters),)),
        ],
        compiler_params=limit,
        cost_estimate=cheap,
        name="project_neighbour",
    )(w_key, w_value, *quarters)
    return pl.pallas_call(
        far_kernel,
        out_shape=(sums,) + (jax.ShapeDtypeStruct((rows // 3, 2 * width), jnp.bfloat16),) * 3,
        in_specs=[ANY] * 5 + [VMEM] * 2 + [ANY] * len(quarters),
        out_specs=(VMEM,) * 4,
        scratch_shapes=[
            w_scratch,
            h_scratch,
            h_scratch,
            pltpu.SemaphoreType.DMA((5 + len(quarters),)),
        ],
        compiler_params=limit,
        cost_estimate=cheap,
        name="project_far",
    )(hidden, *w_far, *w_swapped, near, neighbour, *quarters)


def plan_kernel(
    capacity, slots, request_docs, doc_lengths, rows, queries, q, held, spare, key_bias, row_place, key_place,
    slot_row, counts
):
    head_dim = q.shape[1] // 2
    heads = queries.shape[2] // head_dim
    block_rows = 4 * rows.shape[0]
    scale = math.log2(math.e) / math.sqrt(head_dim)
    for b in range(queries.shape[1] // block_rows):
        for h in range(heads):
            here = queries[0, b * block_rows : (b + 1) * block_rows, h * head_dim : (h + 1) * head_dim]
            here = here.astype(jnp.float32) * scale
            high = here.astype(jnp.bfloat16)
            place = slice((b * heads + h) * block_rows, (b * heads + h + 1) * block_rows)
            q[place, :head_dim] = high
            q[place, head_dim:] = (here - high.astype(jnp.float32)).astype(jnp.bfloat16)
    me = lax.axis_index("seq")
    per_doc, _, doc_count = rows.shape
    doc_len = held.shape[0] // doc_count
    row_count = row_place.shape[0]
    docs = lax.broadcasted_iota(jnp.int32, (1, doc_count), 1)
    lengths = jnp.zeros((1, doc_count), jnp.int32)
    places = jnp.zeros((1, doc_count), jnp.int32)
    for o in range(counts.shape[0]):
        counts[o] = 0
    for j in range(doc_count):
        doc = request_docs[me, j]
        owner = lax.div(doc, slots)
        rank = counts[owner]
        counts[owner] = rank + 1
        lengths = jnp.where(docs == j, doc_lengths[doc], lengths)
        places = jnp.where(docs == j, owner * capacity + rank, places)
    slot = lax.broadcasted_iota(jnp.int32, (doc_len, doc_count), 0)
    used = slot < lengths
    for i in range(per_doc):
        used &= slot != rows[i]
    used = used.astype(jnp.float32)
    first = jnp.min(jnp.where(used > 0, slot, doc_len), axis=0, keepdims=True)
    firsts = (slot == first).astype(jnp.bfloat16)
    eye = lax.broadcasted_iota(jnp.int32, (doc_count, doc_count), 0) == docs
    across = (((1,), (1,)), ((), ()))

    def turned(columns):
        return lax.dot_general(
            eye.astype(jnp.bfloat16), columns, across, preferred_element_type=jnp.float32
        )

    bias = jnp.where(turned(used.astype(jnp.bfloat16)) > 0, 0.0, MASKED)
    firsts = turned(firsts)
    doc = lax.broadcasted_iota(jnp.int32, (doc_count, 1), 0)
    for j in range(doc_count):
        part = slice(j * doc_len, (j + 1) * doc_len)
        held[part, :] = jnp.broadcast_to(used[:, j : j + 1], (doc_len, held.shape[1])).astype(
            held.dtype
        )
        key_bias[:, part] = bias[j : j + 1, :]
        spare[:, part] = jnp.where(doc == j, firsts, 0.0).astype(spare.dtype)
    row = lax.broadcasted_iota(jnp.int32, (row_count, doc_count), 0)
    start = per_doc * lax.broadcasted_iota(jnp.int32, (row_count, doc_count), 1)
    of_doc = (row >= start) & (row < start + per_doc)
    nth = jnp.sum(jnp.where(of_doc, row - start, 0), axis=1, keepdims=True)
    chosen = jnp.zeros((row_count, doc_count), jnp.int32)
    for i in range(per_doc):
        chosen = jnp.where(nth == i, rows[i], chosen)
    chosen = jnp.where(of_doc, chosen + doc_len * docs, 0)
    column = jnp.sum(chosen, axis=1, keepdims=True)
    goes = nth + per_doc * jnp.sum(jnp.where(of_doc, places, 0), axis=1, keepdims=True)
    row_place[...] = column
    square = (row_count, row_count)
    same = lax.broadcasted_iota(jnp.int32, square, 0) == lax.broadcasted_iota(jnp.int32, square, 1)
    key_place[...] = jnp.full(key_place.shape, held.shape[0], jnp.int32)
    key_place[:, :row_count] = jnp.sum(jnp.where(same, column, 0), axis=0, keepdims=True)
    slot_row[...] = jnp.sum(jnp.where(same, goes, 0), axis=0, keepdims=True)


def plan(request_docs, doc_lengths, recompute_rows, queries, slots, head_dim, doc_len):
    _, doc_count, per_doc = recompute_rows.shape
    rows = doc_count * per_doc
    context = doc_count * doc_len
    shapes = (
        ((rows * queries.shape[2] // head_dim, 2 * head_dim), jnp.bfloat16),
        ((context, head_dim), jnp.bfloat16),
        ((doc_count, context), jnp.bfloat16),
        ((1, context), jnp.float32),
        ((rows, 1), jnp.int32),
        ((1, rows + -rows % 128), jnp.int32),
        ((1, rows), jnp.int32),
    )
    return pl.pallas_call(
        functools.partial(plan_kernel, slots // 2, slots),
        out_shape=tuple(jax.ShapeDtypeStruct(*one) for one in shapes),
        in_specs=[SMEM, SMEM, VMEM, VMEM],
        out_specs=(VMEM,) * len(shapes),
        scratch_shapes=[pltpu.SMEM((request_docs.shape[0],), jnp.int32)],
        compiler_params=pltpu.CompilerParams(vmem_limit_bytes=16 * 1024 * 1024),
        name="plan",
    )(request_docs, doc_lengths, jnp.transpose(recompute_rows, (2, 0, 1)), queries)


def finish_kernel(own, arrived_0, arrived_1, arrived_2, slot_row, fresh, outgoing):
    arrived = jnp.concatenate([arrived_0[...], arrived_1[...], arrived_2[...]], axis=0)
    total = (own[...] + arrived.astype(jnp.float32)).astype(jnp.bfloat16)
    fresh[...] = total
    width = outgoing.shape[1]
    slots = lax.broadcasted_iota(jnp.int32, (outgoing.shape[0], 1), 0)
    placed = jnp.zeros(outgoing.shape, jnp.float32)
    for i in range(2):
        pick = (slots == 2 * slot_row[...] + i).astype(jnp.bfloat16)
        part = total[:, i * width : (i + 1) * width]
        placed += jnp.dot(pick, part, preferred_element_type=jnp.float32)
    outgoing[...] = placed.astype(jnp.bfloat16)


def finish(own, arrived, slot_row, slots):
    shapes = (own.shape, (2 * slots, own.shape[1] // 2))
    return pl.pallas_call(
        finish_kernel,
        out_shape=tuple(jax.ShapeDtypeStruct(one, jnp.bfloat16) for one in shapes),
        in_specs=[VMEM] * 5,
        out_specs=(VMEM, VMEM),
        compiler_params=pltpu.CompilerParams(vmem_limit_bytes=16 * 1024 * 1024),
        name="finish",
    )(own, *arrived, slot_row)


def attend_kernel(
    by_owner, request_docs, q, fresh, held, spare, key_bias, row_place, key_place, *rest
):
    sources, (mixed, keys, values, counts, sems) = rest[:-5], rest[-5:]
    me = lax.axis_index("seq")
    doc_count = request_docs.shape[1]
    head_dim = keys.shape[1] // 2
    doc_len = keys.shape[0] // doc_count
    owners = request_docs.shape[0]
    slots = sources[0].shape[0] if not by_owner else 2 * sources[0].shape[1]
    step = doc_count // sems.shape[1]
    blocks = doc_count // step
    block_rows = mixed.shape[1] // blocks
    block_keys = step * doc_len
    heads = mixed.shape[2] // head_dim
    left = pl.ds(0, head_dim)

    for o in range(owners):
        counts[o] = 0

    def one_doc(j, carry):
        doc = request_docs[me, j]
        owner = lax.div(doc, slots)
        rank = counts[owner]
        counts[owner] = rank + 1
        place = pl.ds(pl.multiple_of(j * doc_len, doc_len), doc_len)
        block = lax.div(j, step)

        def fetch(key_source, value_source):
            pltpu.make_async_copy(key_source, keys.at[place, left], sems.at[0, block]).start()
            pltpu.make_async_copy(value_source, values.at[place, left], sems.at[1, block]).start()

        if by_owner:
            fetch(sources[0].at[owner, rank, 0], sources[0].at[owner, rank, 1])
        else:
            away = lax.bitwise_xor(me, owner)

            @pl.when(away == 0)
            def _():
                slot = lax.rem(doc, slots)
                fetch(sources[0].at[slot], sources[1].at[slot])

            for k, source in zip((2, 3, 1), sources[2:]):

                @pl.when(away == k)
                def _():
                    fetch(source.at[rank, 0], source.at[rank, 1])

        return carry

    lax.fori_loop(0, doc_count, one_doc, 0)

    def assemble(b):
        block = pl.ds(b * block_keys, block_keys)
        for i, context in enumerate((keys, values)):
            pltpu.make_async_copy(
                context.at[block, left], context.at[block, left], sems.at[i, b]
            ).wait()
        block = slice(b * block_keys, (b + 1) * block_keys)
        spares = jnp.dot(
            spare[:, block], keys[block, :head_dim], preferred_element_type=jnp.float32
        ).astype(jnp.bfloat16)
        for j in range(b * step, (b + 1) * step):
            place = slice(j * doc_len, (j + 1) * doc_len)
            used = held[place, :]
            key = jnp.where(used > 0, keys[place, :head_dim], spares[j : j + 1, :])
            keys[place, :head_dim] = key
            keys[place, head_dim:] = key
            values[place, :head_dim] = values[place, :head_dim] * used
            values[place, head_dim:] = used

    fresh_count = fresh.shape[0]
    spare_rows = jnp.zeros((-fresh_count % 128, 2 * head_dim), fresh.dtype)
    fresh_k = jnp.concatenate([fresh[:, :head_dim]] * 2, axis=1)
    fresh_k = jnp.concatenate([fresh_k, spare_rows], axis=0)
    fresh_v = jnp.concatenate([fresh[:, head_dim:], jnp.ones_like(fresh[:, head_dim:])], axis=1)
    fresh_v = jnp.concatenate([fresh_v, spare_rows], axis=0)
    slot_place = lax.broadcasted_iota(jnp.int32, (1, block_keys), 1)
    contract_last = (((1,), (1,)), ((), ()))
    for b in range(blocks):
        assemble(b)
    for b in range(blocks):
        rows = slice(b * block_rows, (b + 1) * block_rows)
        q_here = q[b * heads * block_rows : (b + 1) * heads * block_rows, :]
        own_place = row_place[rows, :]

        def scores(some_keys):
            return lax.dot_general(
                q_here, some_keys, contract_last, preferred_element_type=jnp.float32
            )

        def masked(some_keys, allowed):
            shape = (heads, block_rows, some_keys.shape[0])
            kept = jnp.where(allowed[None], scores(some_keys).reshape(shape), MASKED)
            return kept.reshape(heads * block_rows, some_keys.shape[0])

        part = slice(b * block_keys, (b + 1) * block_keys)
        allowed = (slot_place + b * block_keys <= own_place) & (key_bias[:, part] == 0)
        chunks = [scores(keys[: b * block_keys, :])] if b else []
        chunks.append(masked(keys[part, :], allowed))
        chunks.append(masked(fresh_k, key_place[...] <= own_place))
        lane_max = functools.reduce(
            jnp.maximum,
            [one[:, i : i + 128] for one in chunks for i in range(0, one.shape[1], 128)],
        )
        row_max = jnp.max(lane_max, axis=1, keepdims=True)
        powers = [jnp.exp2(one - row_max).astype(jnp.bfloat16) for one in chunks]
        total = jnp.dot(
            jnp.concatenate(powers[:-1], axis=1),
            values[: (b + 1) * block_keys, :],
            preferred_element_type=jnp.float32,
        )
        total += jnp.dot(powers[-1], fresh_v, preferred_element_type=jnp.float32)
        result = (total[:, :head_dim] / total[:, head_dim:]).astype(mixed.dtype)
        for h in range(heads):
            mixed[0, rows, h * head_dim : (h + 1) * head_dim] = result[
                h * block_rows : (h + 1) * block_rows
            ]


def attend(
    shape, request_docs, q, fresh, held, spare, key_bias, row_place, key_place, sources, by_owner
):
    context, head_dim = held.shape
    return pl.pallas_call(
        functools.partial(attend_kernel, by_owner),
        out_shape=jax.ShapeDtypeStruct(shape, jnp.bfloat16),
        in_specs=[SMEM] + [VMEM] * 7 + [ANY] * len(sources),
        out_specs=VMEM,
        scratch_shapes=[
            pltpu.VMEM((context, 2 * head_dim), jnp.bfloat16),
            pltpu.VMEM((context, 2 * head_dim), jnp.bfloat16),
            pltpu.SMEM((request_docs.shape[0],), jnp.int32),
            pltpu.SemaphoreType.DMA((2, 4)),
        ],
        compiler_params=pltpu.CompilerParams(vmem_limit_bytes=32 * 1024 * 1024),
        name="attend",
    )(
        request_docs,
        q,
        fresh,
        held,
        spare,
        key_bias,
        row_place,
        key_place,
        *(in_hbm(one) for one in sources[:2]),
        *sources[2:],
    )


def shards(
    pairs,
    hidden,
    queries,
    w_key,
    w_value,
    store_keys,
    store_values,
    request_docs,
    doc_lengths,
    recompute_rows,
):
    seq_count = lax.axis_size("seq")
    slot_count, doc_len, head_dim = store_keys.shape
    capacity = slot_count // 2
    per_doc = recompute_rows.shape[2]

    if pairs:
        def swap(array, axis, apart):
            count = lax.axis_size(axis)
            return lax.ppermute(array, axis, [(i, i ^ apart) for i in range(count)])

        *w_send, h_send = pick_sent(hidden, w_key, w_value)
        w_far = [swap(part, "seq", 2) for part in w_send]
        h_mine = swap(h_send, "seq", 1)
        doc_1, doc_2, doc_3 = pick_docs(request_docs, store_keys, store_values, False)
        (h_mine,) = gate((h_mine,), (doc_1,), cost=8000000000)
        h_chip = swap(h_mine, "tp", 2)
        h_core = swap(h_mine, "tp", 1)
        w_swapped = [swap(w_far[0], "groups", 1)]
        doc_2, doc_3, w_far[1] = gate(
            (doc_2, doc_3, w_far[1]), (w_swapped[0],), cost=8 * 10**9
        )
        w_swapped.append(swap(w_far[1], "groups", 1))
        doc_1 = swap(doc_1, "seq", 1)
        docs = (swap(doc_2, "seq", 2), swap(doc_3, "seq", 3), doc_1)
        quarters = (h_mine, h_core, h_chip, swap(h_chip, "tp", 1))
        own, *parts = project(hidden, w_key, w_value, w_far, w_swapped, quarters, doc_1)
        arrived = [swap(one, "seq", 1) for one in parts]
        sources = (store_keys, store_values, *docs)
    else:
        (docs,) = pick_docs(request_docs, store_keys, store_values, True)
        sources = (lax.all_to_all(docs, "seq", split_axis=0, concat_axis=0, tiled=True),)
        weights = lax.all_gather(
            jnp.concatenate([w_key, w_value], axis=1), "seq", axis=0, tiled=True
        )
        own = jnp.dot(hidden[0], weights, preferred_element_type=jnp.float32)
        arrived = [jnp.zeros((own.shape[0] // 3, 2 * head_dim), jnp.bfloat16)] * 3

    q, held, spare, key_bias, row_place, key_place, slot_row = plan(
        request_docs, doc_lengths, recompute_rows, queries, slot_count, head_dim, doc_len
    )
    fresh, outgoing = finish(own, arrived, slot_row, seq_count * capacity * per_doc)
    mixed = attend(
        queries.shape,
        request_docs,
        q,
        fresh,
        held,
        spare,
        key_bias,
        row_place,
        key_place,
        sources,
        not pairs,
    )

    outgoing = outgoing.reshape(seq_count, capacity * per_doc * 2, head_dim)
    returned = lax.all_to_all(outgoing, "seq", split_axis=0, concat_axis=0, tiled=True)
    returned = returned.reshape(seq_count, capacity, per_doc, 2, head_dim)
    return (mixed, returned[None])


def solution(mesh):
    pairs = mesh.shape["seq"] == 4 and mesh.shape["groups"] == 2 and mesh.shape["tp"] == 4
    return jax.shard_map(
        functools.partial(shards, pairs),
        mesh=mesh,
        in_specs=(
            P(("groups", "seq"), None, None),
            P(("groups", "seq"), None, "tp"),
            P("seq", "tp"),
            P("seq", "tp"),
            P(("groups", "seq"), None, "tp"),
            P(("groups", "seq"), None, "tp"),
            P("groups", None),
            P("groups"),
            P(("groups", "seq"), None, None),
        ),
        out_specs=(
            P(("groups", "seq"), None, "tp"),
            P(("groups", "seq"), None, None, None, None, "tp"),
        ),
        check_vma=False,
    )
```

```python
import functools
import math

import jax
import jax.numpy as jnp
from jax import lax
from jax.experimental import pallas as pl
from jax.experimental.pallas import tpu as pltpu
from jax.sharding import PartitionSpec as P

ANY = pl.BlockSpec(memory_space=pl.ANY)
HBM = pl.BlockSpec(memory_space=pltpu.HBM)
SMEM = pl.BlockSpec(memory_space=pltpu.SMEM)
VMEM = pl.BlockSpec(memory_space=pltpu.VMEM)
MASKED = -1e30


def in_hbm(array):
    return pltpu.with_memory_space_constraint(array, pltpu.HBM)


def send_kernel(hidden, w_key, w_value, w_first, w_second, h_out, sems):
    group = lax.axis_index("groups")
    me = lax.axis_index("seq")
    rows, depth = h_out.shape[1:]
    for chosen, weight in ((0, w_key), (1, w_value)):

        @pl.when(group == chosen)
        def _():
            for i, out in enumerate((w_first, w_second)):
                part = weight.at[pl.ds(i * w_first.shape[0], out.shape[0])]
                pltpu.make_async_copy(part, out, sems.at[i]).start()

    first = me + 1 - 2 * lax.rem(me, 2)
    copies = []
    for i, block in enumerate((first, lax.rem(first + 2, 4))):
        source = hidden.at[
            0,
            pl.ds(pl.multiple_of(lax.axis_index("tp") * rows, rows), rows),
            pl.ds(pl.multiple_of(block * depth, depth), depth),
        ]
        copies.append(pltpu.make_async_copy(source, h_out.at[i], sems.at[2 + i]))
        copies[-1].start()
    for i, out in enumerate((w_first, w_second)):
        pltpu.make_async_copy(w_key.at[pl.ds(0, out.shape[0])], out, sems.at[i]).wait()
    for copy in copies:
        copy.wait()


def pick_sent(hidden, w_key, w_value):
    depth, width = w_key.shape
    h_shape = (2, hidden.shape[1] // 4, depth)
    first = depth * 7 // 32
    return pl.pallas_call(
        send_kernel,
        out_shape=(
            jax.ShapeDtypeStruct((first, width), jnp.bfloat16),
            jax.ShapeDtypeStruct((depth - first, width), jnp.bfloat16),
            jax.ShapeDtypeStruct(h_shape, jnp.bfloat16),
        ),
        in_specs=[ANY] * 3,
        out_specs=(VMEM,) * 3,
        scratch_shapes=[pltpu.SemaphoreType.DMA((4,))],
        compiler_params=pltpu.CompilerParams(vmem_limit_bytes=16 * 1024 * 1024),
        name="pick_sent",
    )(in_hbm(hidden), in_hbm(w_key), in_hbm(w_value))


def gate_kernel(*refs):
    pass


def gate(arrays, first=(), pinned=0, cost=1):
    return pl.pallas_call(
        gate_kernel,
        out_shape=tuple(jax.ShapeDtypeStruct(one.shape, one.dtype) for one in arrays),
        in_specs=[ANY] * (len(arrays) + len(first)),
        out_specs=(ANY,) * len(arrays),
        input_output_aliases={i: i for i in range(len(arrays))},
        compiler_params=pltpu.CompilerParams(vmem_limit_bytes=1024 * 1024),
        cost_estimate=pl.CostEstimate(flops=cost, bytes_accessed=1, transcendentals=0),
        name="gate",
    )(*(in_hbm(one) for one in arrays[:pinned]), *arrays[pinned:], *first)


def docs_kernel(by_owner, request_docs, store_keys, store_values, *rest):
    *outs, picks, sems = rest
    me = lax.axis_index("seq")
    requests, doc_count = request_docs.shape
    slots = store_keys.shape[0]
    capacity = slots // 2

    def one_request(r, carry):
        for c in range(capacity):
            picks[r, c] = 0

        def one_doc(j, count):
            doc = request_docs[r, j]
            mine = lax.div(doc, slots) == me

            @pl.when(mine)
            def _():
                picks[r, jnp.minimum(count, capacity - 1)] = lax.rem(doc, slots)

            return count + mine.astype(jnp.int32)

        lax.fori_loop(0, doc_count, one_doc, jnp.int32(0), unroll=True)
        return carry

    lax.fori_loop(0, requests, one_request, 0)

    def send(r, out, sem):
        for c in range(capacity):
            slot = picks[r, c]
            pltpu.make_async_copy(store_keys.at[slot], out.at[c, 0], sem).start()
            pltpu.make_async_copy(store_values.at[slot], out.at[c, 1], sem).start()

    def send_one(r, store, out, sem):
        for c in range(capacity):
            pltpu.make_async_copy(store.at[picks[r, c]], out.at[c], sem).start()

    if by_owner:

        def one_send(r, carry):
            send(r, outs[0].at[r], sems.at[0])
            return carry

        lax.fori_loop(0, requests, one_send, 0)
    else:
        send(lax.bitwise_xor(me, 1), outs[0], sems.at[0])
        send_one(lax.bitwise_xor(me, 2), store_keys, outs[1], sems.at[1])
        send_one(lax.bitwise_xor(me, 2), store_values, outs[2], sems.at[2])
        send(lax.bitwise_xor(me, 3), outs[3], sems.at[3])
    for i, out in enumerate(outs):
        pltpu.make_async_copy(out, out, sems.at[i]).wait()


def pick_docs(request_docs, store_keys, store_values, by_owner):
    requests = request_docs.shape[0]
    capacity = store_keys.shape[0] // 2
    one = (capacity, 2) + store_keys.shape[1:]
    half = (capacity,) + store_keys.shape[1:]
    shapes = ((requests,) + one,) if by_owner else (one, half, half, one)
    return pl.pallas_call(
        functools.partial(docs_kernel, by_owner),
        out_shape=tuple(jax.ShapeDtypeStruct(one, jnp.bfloat16) for one in shapes),
        in_specs=[SMEM, ANY, ANY],
        out_specs=(VMEM,) * len(shapes),
        scratch_shapes=[
            pltpu.SMEM((requests, capacity), jnp.int32),
            pltpu.SemaphoreType.DMA((len(shapes),)),
        ],
        compiler_params=pltpu.CompilerParams(vmem_limit_bytes=16 * 1024 * 1024),
        name="pick_docs",
    )(request_docs, in_hbm(store_keys), in_hbm(store_values))


def near_kernel(hidden, w_key, w_value, _, total, w, h, sems):
    depth, width = w_key.shape
    start = pl.multiple_of(lax.axis_index("seq") * depth, depth)
    copies = [
        pltpu.make_async_copy(w_key, w.at[:, pl.ds(0, width)], sems.at[0]),
        pltpu.make_async_copy(w_value, w.at[:, pl.ds(width, width)], sems.at[1]),
        pltpu.make_async_copy(hidden.at[0, :, pl.ds(start, depth)], h, sems.at[2]),
    ]
    for copy in copies:
        copy.start()
    for copy in copies:
        copy.wait()
    total[...] = jnp.dot(h[...], w[...], preferred_element_type=jnp.float32)


def lay_quarters(quarters, block, rows, copy):
    piece = rows.shape[0] // len(quarters)
    for k, quarter in enumerate(quarters):
        start = pl.multiple_of(lax.bitwise_xor(lax.axis_index("tp"), k) * piece, piece)
        copy(quarter.at[block], rows.at[pl.ds(start, piece)])


def neighbour_kernel(w_key, w_value, *rest):
    *quarters, total, w, n, sems = rest
    width = w_key.shape[1]
    copies = []

    def copy(source, target):
        copies.append(pltpu.make_async_copy(source, target, sems.at[len(copies)]))
        copies[-1].start()

    for i, held in enumerate((w_key, w_value)):
        copy(held, w.at[:, pl.ds(i * width, width)])
    lay_quarters(quarters, 0, n, copy)
    for one in copies:
        one.wait()
    total[...] = jnp.dot(n[...], w[...], preferred_element_type=jnp.float32)


def far_kernel(hidden, w_far_0, w_far_1, w_swapped_0, w_swapped_1, near, neighbour, _, __, *rest):
    *quarters, own, part_0, part_1, part_2, w, h, n, sems = rest
    group = lax.axis_index("groups")
    start, width = w_far_0.shape
    depth = start + w_far_1.shape[0]
    copies = []

    def copy(source, target):
        copies.append(pltpu.make_async_copy(source, target, sems.at[len(copies)]))
        copies[-1].start()

    pairs = ((w_far_0, w_far_1, group), (w_swapped_0, w_swapped_1, 1 - group))
    for first, second, place in pairs:
        columns = pl.ds(pl.multiple_of(place * width, width), width)
        copy(first, w.at[pl.ds(0, start), columns])
        copy(second, w.at[pl.ds(start, depth - start), columns])
    start = pl.multiple_of(lax.rem(lax.axis_index("seq") + 2, 4) * depth, depth)
    copy(hidden.at[0, :, pl.ds(start, depth)], h)
    lay_quarters(quarters, 1, n, copy)
    for one in copies:
        one.wait()
    own[...] = near[...] + jnp.dot(h[...], w[...], preferred_element_type=jnp.float32)
    total = neighbour[...] + jnp.dot(n[...], w[...], preferred_element_type=jnp.float32)
    for i, part in enumerate((part_0, part_1, part_2)):
        count = part.shape[0]
        part[...] = total[i * count : (i + 1) * count].astype(part.dtype)


def project(hidden, w_key, w_value, w_far, w_swapped, quarters, first):
    depth, width = w_key.shape
    rows = hidden.shape[1]
    sums = jax.ShapeDtypeStruct((rows, 2 * width), jnp.float32)
    w_scratch = pltpu.VMEM((depth, 2 * width), jnp.bfloat16)
    h_scratch = pltpu.VMEM((rows, depth), jnp.bfloat16)
    limit = pltpu.CompilerParams(vmem_limit_bytes=16 * 1024 * 1024)
    cheap = pl.CostEstimate(flops=1, bytes_accessed=1, transcendentals=0)
    w_key, w_value = in_hbm(w_key), in_hbm(w_value)
    near = pl.pallas_call(
        near_kernel,
        out_shape=sums,
        in_specs=[ANY] * 4,
        out_specs=VMEM,
        scratch_shapes=[w_scratch, h_scratch, pltpu.SemaphoreType.DMA((3,))],
        compiler_params=limit,
        cost_estimate=pl.CostEstimate(flops=10**10, bytes_accessed=1, transcendentals=0),
        name="project_near",
    )(hidden, w_key, w_value, first[0])
    neighbour = pl.pallas_call(
        neighbour_kernel,
        out_shape=sums,
        in_specs=[ANY] * (2 + len(quarters)),
        out_specs=VMEM,
        scratch_shapes=[
            w_scratch,
            h_scratch,
            pltpu.SemaphoreType.DMA((2 + len(quarters),)),
        ],
        compiler_params=limit,
        cost_estimate=cheap,
        name="project_neighbour",
    )(w_key, w_value, *quarters)
    return pl.pallas_call(
        far_kernel,
        out_shape=(sums,) + (jax.ShapeDtypeStruct((rows // 3, 2 * width), jnp.bfloat16),) * 3,
        in_specs=[ANY] * 5 + [VMEM] * 2 + [ANY] * (2 + len(quarters)),
        out_specs=(VMEM,) * 4,
        scratch_shapes=[
            w_scratch,
            h_scratch,
            h_scratch,
            pltpu.SemaphoreType.DMA((5 + len(quarters),)),
        ],
        compiler_params=limit,
        cost_estimate=cheap,
        name="project_far",
    )(hidden, *w_far, *w_swapped, near, neighbour, *first[1:], *quarters)


def plan_kernel(
    capacity, slots, request_docs, doc_lengths, rows, queries, q, held, spare, key_bias, row_place, key_place,
    slot_row, counts
):
    head_dim = q.shape[1] // 2
    heads = queries.shape[2] // head_dim
    block_rows = 4 * rows.shape[0]
    scale = math.log2(math.e) / math.sqrt(head_dim)
    for b in range(queries.shape[1] // block_rows):
        for h in range(heads):
            here = queries[0, b * block_rows : (b + 1) * block_rows, h * head_dim : (h + 1) * head_dim]
            here = here.astype(jnp.float32) * scale
            high = here.astype(jnp.bfloat16)
            place = slice((b * heads + h) * block_rows, (b * heads + h + 1) * block_rows)
            q[place, :head_dim] = high
            q[place, head_dim:] = (here - high.astype(jnp.float32)).astype(jnp.bfloat16)
    me = lax.axis_index("seq")
    per_doc, _, doc_count = rows.shape
    doc_len = held.shape[0] // doc_count
    row_count = row_place.shape[0]
    docs = lax.broadcasted_iota(jnp.int32, (1, doc_count), 1)
    lengths = jnp.zeros((1, doc_count), jnp.int32)
    places = jnp.zeros((1, doc_count), jnp.int32)
    for o in range(counts.shape[0]):
        counts[o] = 0
    for j in range(doc_count):
        doc = request_docs[me, j]
        owner = lax.div(doc, slots)
        rank = counts[owner]
        counts[owner] = rank + 1
        lengths = jnp.where(docs == j, doc_lengths[doc], lengths)
        places = jnp.where(docs == j, owner * capacity + rank, places)
    slot = lax.broadcasted_iota(jnp.int32, (doc_len, doc_count), 0)
    used = slot < lengths
    for i in range(per_doc):
        used &= slot != rows[i]
    used = used.astype(jnp.float32)
    first = jnp.min(jnp.where(used > 0, slot, doc_len), axis=0, keepdims=True)
    firsts = (slot == first).astype(jnp.bfloat16)
    eye = lax.broadcasted_iota(jnp.int32, (doc_count, doc_count), 0) == docs
    across = (((1,), (1,)), ((), ()))

    def turned(columns):
        return lax.dot_general(
            eye.astype(jnp.bfloat16), columns, across, preferred_element_type=jnp.float32
        )

    bias = jnp.where(turned(used.astype(jnp.bfloat16)) > 0, 0.0, MASKED)
    firsts = turned(firsts)
    doc = lax.broadcasted_iota(jnp.int32, (doc_count, 1), 0)
    for j in range(doc_count):
        part = slice(j * doc_len, (j + 1) * doc_len)
        held[part, :] = jnp.broadcast_to(used[:, j : j + 1], (doc_len, held.shape[1])).astype(
            held.dtype
        )
        key_bias[:, part] = bias[j : j + 1, :]
        spare[:, part] = jnp.where(doc == j, firsts, 0.0).astype(spare.dtype)
    row = lax.broadcasted_iota(jnp.int32, (row_count, doc_count), 0)
    start = per_doc * lax.broadcasted_iota(jnp.int32, (row_count, doc_count), 1)
    of_doc = (row >= start) & (row < start + per_doc)
    nth = jnp.sum(jnp.where(of_doc, row - start, 0), axis=1, keepdims=True)
    chosen = jnp.zeros((row_count, doc_count), jnp.int32)
    for i in range(per_doc):
        chosen = jnp.where(nth == i, rows[i], chosen)
    chosen = jnp.where(of_doc, chosen + doc_len * docs, 0)
    column = jnp.sum(chosen, axis=1, keepdims=True)
    goes = nth + per_doc * jnp.sum(jnp.where(of_doc, places, 0), axis=1, keepdims=True)
    row_place[...] = column
    square = (row_count, row_count)
    same = lax.broadcasted_iota(jnp.int32, square, 0) == lax.broadcasted_iota(jnp.int32, square, 1)
    key_place[...] = jnp.full(key_place.shape, held.shape[0], jnp.int32)
    key_place[:, :row_count] = jnp.sum(jnp.where(same, column, 0), axis=0, keepdims=True)
    slot_row[...] = jnp.sum(jnp.where(same, goes, 0), axis=0, keepdims=True)


def plan(request_docs, doc_lengths, recompute_rows, queries, slots, head_dim, doc_len):
    _, doc_count, per_doc = recompute_rows.shape
    rows = doc_count * per_doc
    context = doc_count * doc_len
    shapes = (
        ((rows * queries.shape[2] // head_dim, 2 * head_dim), jnp.bfloat16),
        ((context, head_dim), jnp.bfloat16),
        ((doc_count, context), jnp.bfloat16),
        ((1, context), jnp.float32),
        ((rows, 1), jnp.int32),
        ((1, rows + -rows % 128), jnp.int32),
        ((1, rows), jnp.int32),
    )
    return pl.pallas_call(
        functools.partial(plan_kernel, slots // 2, slots),
        out_shape=tuple(jax.ShapeDtypeStruct(*one) for one in shapes),
        in_specs=[SMEM, SMEM, VMEM, VMEM],
        out_specs=(VMEM,) * len(shapes),
        scratch_shapes=[pltpu.SMEM((request_docs.shape[0],), jnp.int32)],
        compiler_params=pltpu.CompilerParams(vmem_limit_bytes=16 * 1024 * 1024),
        name="plan",
    )(request_docs, doc_lengths, jnp.transpose(recompute_rows, (2, 0, 1)), queries)


def finish_kernel(own, arrived_0, arrived_1, arrived_2, slot_row, fresh, outgoing):
    arrived = jnp.concatenate([arrived_0[...], arrived_1[...], arrived_2[...]], axis=0)
    total = (own[...] + arrived.astype(jnp.float32)).astype(jnp.bfloat16)
    fresh[...] = total
    width = outgoing.shape[1]
    slots = lax.broadcasted_iota(jnp.int32, (outgoing.shape[0], 1), 0)
    placed = jnp.zeros(outgoing.shape, jnp.float32)
    for i in range(2):
        pick = (slots == 2 * slot_row[...] + i).astype(jnp.bfloat16)
        part = total[:, i * width : (i + 1) * width]
        placed += jnp.dot(pick, part, preferred_element_type=jnp.float32)
    outgoing[...] = placed.astype(jnp.bfloat16)


def finish(own, arrived, slot_row, slots):
    shapes = (own.shape, (2 * slots, own.shape[1] // 2))
    return pl.pallas_call(
        finish_kernel,
        out_shape=tuple(jax.ShapeDtypeStruct(one, jnp.bfloat16) for one in shapes),
        in_specs=[VMEM] * 5,
        out_specs=(VMEM, VMEM),
        compiler_params=pltpu.CompilerParams(vmem_limit_bytes=16 * 1024 * 1024),
        name="finish",
    )(own, *arrived, slot_row)


def attend_kernel(
    by_owner, request_docs, q, fresh, held, spare, key_bias, row_place, key_place, *rest
):
    sources, (mixed, keys, values, counts, sems) = rest[:-5], rest[-5:]
    me = lax.axis_index("seq")
    doc_count = request_docs.shape[1]
    head_dim = keys.shape[1] // 2
    doc_len = keys.shape[0] // doc_count
    owners = request_docs.shape[0]
    slots = sources[0].shape[0] if not by_owner else 2 * sources[0].shape[1]
    step = doc_count // sems.shape[1]
    blocks = doc_count // step
    block_rows = mixed.shape[1] // blocks
    block_keys = step * doc_len
    heads = mixed.shape[2] // head_dim
    left = pl.ds(0, head_dim)

    for o in range(owners):
        counts[o] = 0

    def one_doc(j, carry):
        doc = request_docs[me, j]
        owner = lax.div(doc, slots)
        rank = counts[owner]
        counts[owner] = rank + 1
        place = pl.ds(pl.multiple_of(j * doc_len, doc_len), doc_len)
        block = lax.div(j, step)

        def fetch(key_source, value_source):
            pltpu.make_async_copy(key_source, keys.at[place, left], sems.at[0, block]).start()
            pltpu.make_async_copy(value_source, values.at[place, left], sems.at[1, block]).start()

        if by_owner:
            fetch(sources[0].at[owner, rank, 0], sources[0].at[owner, rank, 1])
        else:
            away = lax.bitwise_xor(me, owner)

            @pl.when(away == 0)
            def _():
                slot = lax.rem(doc, slots)
                fetch(sources[0].at[slot], sources[1].at[slot])

            @pl.when(away == 2)
            def _():
                fetch(sources[2].at[rank], sources[3].at[rank])

            for k, source in zip((3, 1), sources[4:]):

                @pl.when(away == k)
                def _():
                    fetch(source.at[rank, 0], source.at[rank, 1])

        return carry

    lax.fori_loop(0, doc_count, one_doc, 0)

    def assemble(b):
        block = pl.ds(b * block_keys, block_keys)
        for i, context in enumerate((keys, values)):
            pltpu.make_async_copy(
                context.at[block, left], context.at[block, left], sems.at[i, b]
            ).wait()
        block = slice(b * block_keys, (b + 1) * block_keys)
        spares = jnp.dot(
            spare[:, block], keys[block, :head_dim], preferred_element_type=jnp.float32
        ).astype(jnp.bfloat16)
        for j in range(b * step, (b + 1) * step):
            place = slice(j * doc_len, (j + 1) * doc_len)
            used = held[place, :]
            key = jnp.where(used > 0, keys[place, :head_dim], spares[j : j + 1, :])
            keys[place, :head_dim] = key
            keys[place, head_dim:] = key
            values[place, :head_dim] = values[place, :head_dim] * used
            values[place, head_dim:] = used

    fresh_count = fresh.shape[0]
    spare_rows = jnp.zeros((-fresh_count % 128, 2 * head_dim), fresh.dtype)
    fresh_k = jnp.concatenate([fresh[:, :head_dim]] * 2, axis=1)
    fresh_k = jnp.concatenate([fresh_k, spare_rows], axis=0)
    fresh_v = jnp.concatenate([fresh[:, head_dim:], jnp.ones_like(fresh[:, head_dim:])], axis=1)
    fresh_v = jnp.concatenate([fresh_v, spare_rows], axis=0)
    slot_place = lax.broadcasted_iota(jnp.int32, (1, block_keys), 1)
    contract_last = (((1,), (1,)), ((), ()))
    for b in range(blocks):
        assemble(b)
    for b in range(blocks):
        rows = slice(b * block_rows, (b + 1) * block_rows)
        q_here = q[b * heads * block_rows : (b + 1) * heads * block_rows, :]
        own_place = row_place[rows, :]

        def scores(some_keys):
            return lax.dot_general(
                q_here, some_keys, contract_last, preferred_element_type=jnp.float32
            )

        def masked(some_keys, allowed):
            shape = (heads, block_rows, some_keys.shape[0])
            kept = jnp.where(allowed[None], scores(some_keys).reshape(shape), MASKED)
            return kept.reshape(heads * block_rows, some_keys.shape[0])

        part = slice(b * block_keys, (b + 1) * block_keys)
        allowed = (slot_place + b * block_keys <= own_place) & (key_bias[:, part] == 0)
        chunks = [scores(keys[: b * block_keys, :])] if b else []
        chunks.append(masked(keys[part, :], allowed))
        chunks.append(masked(fresh_k, key_place[...] <= own_place))
        lane_max = functools.reduce(
            jnp.maximum,
            [one[:, i : i + 128] for one in chunks for i in range(0, one.shape[1], 128)],
        )
        row_max = jnp.max(lane_max, axis=1, keepdims=True)
        powers = [jnp.exp2(one - row_max).astype(jnp.bfloat16) for one in chunks]
        total = jnp.dot(
            jnp.concatenate(powers[:-1], axis=1),
            values[: (b + 1) * block_keys, :],
            preferred_element_type=jnp.float32,
        )
        total += jnp.dot(powers[-1], fresh_v, preferred_element_type=jnp.float32)
        result = (total[:, :head_dim] / total[:, head_dim:]).astype(mixed.dtype)
        for h in range(heads):
            mixed[0, rows, h * head_dim : (h + 1) * head_dim] = result[
                h * block_rows : (h + 1) * block_rows
            ]


def attend(
    shape, request_docs, q, fresh, held, spare, key_bias, row_place, key_place, sources, by_owner
):
    context, head_dim = held.shape
    return pl.pallas_call(
        functools.partial(attend_kernel, by_owner),
        out_shape=jax.ShapeDtypeStruct(shape, jnp.bfloat16),
        in_specs=[SMEM] + [VMEM] * 7 + [ANY] * len(sources),
        out_specs=VMEM,
        scratch_shapes=[
            pltpu.VMEM((context, 2 * head_dim), jnp.bfloat16),
            pltpu.VMEM((context, 2 * head_dim), jnp.bfloat16),
            pltpu.SMEM((request_docs.shape[0],), jnp.int32),
            pltpu.SemaphoreType.DMA((2, 4)),
        ],
        compiler_params=pltpu.CompilerParams(vmem_limit_bytes=32 * 1024 * 1024),
        name="attend",
    )(
        request_docs,
        q,
        fresh,
        held,
        spare,
        key_bias,
        row_place,
        key_place,
        *(in_hbm(one) for one in sources[:2]),
        *sources[2:],
    )


def shards(
    pairs,
    hidden,
    queries,
    w_key,
    w_value,
    store_keys,
    store_values,
    request_docs,
    doc_lengths,
    recompute_rows,
):
    seq_count = lax.axis_size("seq")
    slot_count, doc_len, head_dim = store_keys.shape
    capacity = slot_count // 2
    per_doc = recompute_rows.shape[2]

    if pairs:
        def swap(array, axis, apart):
            count = lax.axis_size(axis)
            return lax.ppermute(array, axis, [(i, i ^ apart) for i in range(count)])

        *w_send, h_send = pick_sent(hidden, w_key, w_value)
        w_far = [swap(part, "seq", 2) for part in w_send]
        h_mine = swap(h_send, "seq", 1)
        doc_1, keys_2, values_2, doc_3 = pick_docs(request_docs, store_keys, store_values, False)
        (h_mine,) = gate((h_mine,), (doc_1,), cost=8000000000)
        h_chip = swap(h_mine, "tp", 2)
        h_core = swap(h_mine, "tp", 1)
        w_swapped = [swap(w_far[0], "groups", 1)]
        keys_2, values_2, doc_3, w_far[1] = gate(
            (keys_2, values_2, doc_3, w_far[1]), (w_swapped[0],), cost=8 * 10**9
        )
        w_swapped.append(swap(w_far[1], "groups", 1))
        doc_1 = swap(doc_1, "seq", 1)
        docs = (swap(keys_2, "seq", 2), swap(values_2, "seq", 2), swap(doc_3, "seq", 3), doc_1)
        quarters = (h_mine, h_core, h_chip, swap(h_chip, "tp", 1))
        own, *parts = project(hidden, w_key, w_value, w_far, w_swapped, quarters, (doc_1, docs[0], docs[1]))
        arrived = [swap(one, "seq", 1) for one in parts]
        sources = (store_keys, store_values, *docs)
    else:
        (docs,) = pick_docs(request_docs, store_keys, store_values, True)
        sources = (lax.all_to_all(docs, "seq", split_axis=0, concat_axis=0, tiled=True),)
        weights = lax.all_gather(
            jnp.concatenate([w_key, w_value], axis=1), "seq", axis=0, tiled=True
        )
        own = jnp.dot(hidden[0], weights, preferred_element_type=jnp.float32)
        arrived = [jnp.zeros((own.shape[0] // 3, 2 * head_dim), jnp.bfloat16)] * 3

    q, held, spare, key_bias, row_place, key_place, slot_row = plan(
        request_docs, doc_lengths, recompute_rows, queries, slot_count, head_dim, doc_len
    )
    fresh, outgoing = finish(own, arrived, slot_row, seq_count * capacity * per_doc)
    mixed = attend(
        queries.shape,
        request_docs,
        q,
        fresh,
        held,
        spare,
        key_bias,
        row_place,
        key_place,
        sources,
        not pairs,
    )

    outgoing = outgoing.reshape(seq_count, capacity * per_doc * 2, head_dim)
    returned = lax.all_to_all(outgoing, "seq", split_axis=0, concat_axis=0, tiled=True)
    returned = returned.reshape(seq_count, capacity, per_doc, 2, head_dim)
    return (mixed, returned[None])


def solution(mesh):
    pairs = mesh.shape["seq"] == 4 and mesh.shape["groups"] == 2 and mesh.shape["tp"] == 4
    return jax.shard_map(
        functools.partial(shards, pairs),
        mesh=mesh,
        in_specs=(
            P(("groups", "seq"), None, None),
            P(("groups", "seq"), None, "tp"),
            P("seq", "tp"),
            P("seq", "tp"),
            P(("groups", "seq"), None, "tp"),
            P(("groups", "seq"), None, "tp"),
            P("groups", None),
            P("groups"),
            P(("groups", "seq"), None, None),
        ),
        out_specs=(
            P(("groups", "seq"), None, "tp"),
            P(("groups", "seq"), None, None, None, None, "tp"),
        ),
        check_vma=False,
    )
```

```python
import functools
import math

import jax
import jax.numpy as jnp
from jax import lax
from jax.experimental import pallas as pl
from jax.experimental.pallas import tpu as pltpu
from jax.sharding import PartitionSpec as P

ANY = pl.BlockSpec(memory_space=pl.ANY)
HBM = pl.BlockSpec(memory_space=pltpu.HBM)
SMEM = pl.BlockSpec(memory_space=pltpu.SMEM)
VMEM = pl.BlockSpec(memory_space=pltpu.VMEM)
MASKED = -1e30


def in_hbm(array):
    return pltpu.with_memory_space_constraint(array, pltpu.HBM)


def send_kernel(hidden, w_key, w_value, w_first, w_second, h_out, sems):
    group = lax.axis_index("groups")
    me = lax.axis_index("seq")
    rows, depth = h_out.shape[1:]
    for chosen, weight in ((0, w_key), (1, w_value)):

        @pl.when(group == chosen)
        def _():
            for i, out in enumerate((w_first, w_second)):
                part = weight.at[pl.ds(i * w_first.shape[0], out.shape[0])]
                pltpu.make_async_copy(part, out, sems.at[i]).start()

    first = me + 1 - 2 * lax.rem(me, 2)
    copies = []
    for i, block in enumerate((first, lax.rem(first + 2, 4))):
        source = hidden.at[
            0,
            pl.ds(pl.multiple_of(lax.axis_index("tp") * rows, rows), rows),
            pl.ds(pl.multiple_of(block * depth, depth), depth),
        ]
        copies.append(pltpu.make_async_copy(source, h_out.at[i], sems.at[2 + i]))
        copies[-1].start()
    for i, out in enumerate((w_first, w_second)):
        pltpu.make_async_copy(w_key.at[pl.ds(0, out.shape[0])], out, sems.at[i]).wait()
    for copy in copies:
        copy.wait()


def pick_sent(hidden, w_key, w_value):
    depth, width = w_key.shape
    h_shape = (2, hidden.shape[1] // 4, depth)
    first = depth * 7 // 32
    return pl.pallas_call(
        send_kernel,
        out_shape=(
            jax.ShapeDtypeStruct((first, width), jnp.bfloat16),
            jax.ShapeDtypeStruct((depth - first, width), jnp.bfloat16),
            jax.ShapeDtypeStruct(h_shape, jnp.bfloat16),
        ),
        in_specs=[ANY] * 3,
        out_specs=(VMEM,) * 3,
        scratch_shapes=[pltpu.SemaphoreType.DMA((4,))],
        compiler_params=pltpu.CompilerParams(vmem_limit_bytes=16 * 1024 * 1024),
        name="pick_sent",
    )(in_hbm(hidden), in_hbm(w_key), in_hbm(w_value))


def gate_kernel(*refs):
    pass


def gate(arrays, first=(), pinned=0, cost=1):
    return pl.pallas_call(
        gate_kernel,
        out_shape=tuple(jax.ShapeDtypeStruct(one.shape, one.dtype) for one in arrays),
        in_specs=[ANY] * (len(arrays) + len(first)),
        out_specs=(ANY,) * len(arrays),
        input_output_aliases={i: i for i in range(len(arrays))},
        compiler_params=pltpu.CompilerParams(vmem_limit_bytes=1024 * 1024),
        cost_estimate=pl.CostEstimate(flops=cost, bytes_accessed=1, transcendentals=0),
        name="gate",
    )(*(in_hbm(one) for one in arrays[:pinned]), *arrays[pinned:], *first)


def docs_kernel(by_owner, request_docs, store_keys, store_values, *rest):
    *outs, picks, sems = rest
    me = lax.axis_index("seq")
    requests, doc_count = request_docs.shape
    slots = store_keys.shape[0]
    capacity = slots // 2

    def one_request(r, carry):
        for c in range(capacity):
            picks[r, c] = 0

        def one_doc(j, count):
            doc = request_docs[r, j]
            mine = lax.div(doc, slots) == me

            @pl.when(mine)
            def _():
                picks[r, jnp.minimum(count, capacity - 1)] = lax.rem(doc, slots)

            return count + mine.astype(jnp.int32)

        lax.fori_loop(0, doc_count, one_doc, jnp.int32(0), unroll=True)
        return carry

    lax.fori_loop(0, requests, one_request, 0)

    def send(r, out, sem):
        for c in range(capacity):
            slot = picks[r, c]
            pltpu.make_async_copy(store_keys.at[slot], out.at[c, 0], sem).start()
            pltpu.make_async_copy(store_values.at[slot], out.at[c, 1], sem).start()

    if by_owner:

        def one_send(r, carry):
            send(r, outs[0].at[r], sems.at[0])
            return carry

        lax.fori_loop(0, requests, one_send, 0)
    else:
        for i, out in enumerate(outs):
            send(lax.bitwise_xor(me, i + 1), out, sems.at[i])
    for i, out in enumerate(outs):
        pltpu.make_async_copy(out, out, sems.at[i]).wait()


def pick_docs(request_docs, store_keys, store_values, by_owner):
    requests = request_docs.shape[0]
    capacity = store_keys.shape[0] // 2
    one = (capacity, 2) + store_keys.shape[1:]
    shapes = ((requests,) + one,) if by_owner else (one,) * (requests - 1)
    return pl.pallas_call(
        functools.partial(docs_kernel, by_owner),
        out_shape=tuple(jax.ShapeDtypeStruct(one, jnp.bfloat16) for one in shapes),
        in_specs=[SMEM, ANY, ANY],
        out_specs=(VMEM,) * len(shapes),
        scratch_shapes=[
            pltpu.SMEM((requests, capacity), jnp.int32),
            pltpu.SemaphoreType.DMA((len(shapes),)),
        ],
        compiler_params=pltpu.CompilerParams(vmem_limit_bytes=16 * 1024 * 1024),
        name="pick_docs",
    )(request_docs, in_hbm(store_keys), in_hbm(store_values))


def near_kernel(hidden, w_key, w_value, _, total, w, h, sems):
    depth, width = w_key.shape
    start = pl.multiple_of(lax.axis_index("seq") * depth, depth)
    copies = [
        pltpu.make_async_copy(w_key, w.at[:, pl.ds(0, width)], sems.at[0]),
        pltpu.make_async_copy(w_value, w.at[:, pl.ds(width, width)], sems.at[1]),
        pltpu.make_async_copy(hidden.at[0, :, pl.ds(start, depth)], h, sems.at[2]),
    ]
    for copy in copies:
        copy.start()
    for copy in copies:
        copy.wait()
    total[...] = jnp.dot(h[...], w[...], preferred_element_type=jnp.float32)


def lay_quarters(quarters, block, rows, copy):
    piece = rows.shape[0] // len(quarters)
    for k, quarter in enumerate(quarters):
        start = pl.multiple_of(lax.bitwise_xor(lax.axis_index("tp"), k) * piece, piece)
        copy(quarter.at[block], rows.at[pl.ds(start, piece)])


def neighbour_kernel(w_key, w_value, *rest):
    *quarters, total, w, n, sems = rest
    width = w_key.shape[1]
    copies = []

    def copy(source, target):
        copies.append(pltpu.make_async_copy(source, target, sems.at[len(copies)]))
        copies[-1].start()

    for i, held in enumerate((w_key, w_value)):
        copy(held, w.at[:, pl.ds(i * width, width)])
    lay_quarters(quarters, 0, n, copy)
    for one in copies:
        one.wait()
    total[...] = jnp.dot(n[...], w[...], preferred_element_type=jnp.float32)


def far_kernel(hidden, w_far_0, w_far_1, w_swapped_0, w_swapped_1, near, neighbour, *rest):
    *quarters, own, part_0, part_1, part_2, w, h, n, sems = rest
    group = lax.axis_index("groups")
    start, width = w_far_0.shape
    depth = start + w_far_1.shape[0]
    copies = []

    def copy(source, target):
        copies.append(pltpu.make_async_copy(source, target, sems.at[len(copies)]))
        copies[-1].start()

    pairs = ((w_far_0, w_far_1, group), (w_swapped_0, w_swapped_1, 1 - group))
    for first, second, place in pairs:
        columns = pl.ds(pl.multiple_of(place * width, width), width)
        copy(first, w.at[pl.ds(0, start), columns])
        copy(second, w.at[pl.ds(start, depth - start), columns])
    start = pl.multiple_of(lax.rem(lax.axis_index("seq") + 2, 4) * depth, depth)
    copy(hidden.at[0, :, pl.ds(start, depth)], h)
    lay_quarters(quarters, 1, n, copy)
    for one in copies:
        one.wait()
    own[...] = near[...] + jnp.dot(h[...], w[...], preferred_element_type=jnp.float32)
    total = neighbour[...] + jnp.dot(n[...], w[...], preferred_element_type=jnp.float32)
    for i, part in enumerate((part_0, part_1, part_2)):
        count = part.shape[0]
        part[...] = total[i * count : (i + 1) * count].astype(part.dtype)


def project(hidden, w_key, w_value, w_far, w_swapped, quarters, first):
    depth, width = w_key.shape
    rows = hidden.shape[1]
    sums = jax.ShapeDtypeStruct((rows, 2 * width), jnp.float32)
    w_scratch = pltpu.VMEM((depth, 2 * width), jnp.bfloat16)
    h_scratch = pltpu.VMEM((rows, depth), jnp.bfloat16)
    limit = pltpu.CompilerParams(vmem_limit_bytes=16 * 1024 * 1024)
    cheap = pl.CostEstimate(flops=1, bytes_accessed=1, transcendentals=0)
    w_key, w_value = in_hbm(w_key), in_hbm(w_value)
    near = pl.pallas_call(
        near_kernel,
        out_shape=sums,
        in_specs=[ANY] * 4,
        out_specs=VMEM,
        scratch_shapes=[w_scratch, h_scratch, pltpu.SemaphoreType.DMA((3,))],
        compiler_params=limit,
        cost_estimate=pl.CostEstimate(flops=10**10, bytes_accessed=1, transcendentals=0),
        name="project_near",
    )(hidden, w_key, w_value, first)
    neighbour = pl.pallas_call(
        neighbour_kernel,
        out_shape=sums,
        in_specs=[ANY] * (2 + len(quarters)),
        out_specs=VMEM,
        scratch_shapes=[
            w_scratch,
            h_scratch,
            pltpu.SemaphoreType.DMA((2 + len(quarters),)),
        ],
        compiler_params=limit,
        cost_estimate=cheap,
        name="project_neighbour",
    )(w_key, w_value, *quarters)
    return pl.pallas_call(
        far_kernel,
        out_shape=(sums,) + (jax.ShapeDtypeStruct((rows // 3, 2 * width), jnp.bfloat16),) * 3,
        in_specs=[ANY] * 5 + [VMEM] * 2 + [ANY] * len(quarters),
        out_specs=(VMEM,) * 4,
        scratch_shapes=[
            w_scratch,
            h_scratch,
            h_scratch,
            pltpu.SemaphoreType.DMA((5 + len(quarters),)),
        ],
        compiler_params=limit,
        cost_estimate=cheap,
        name="project_far",
    )(hidden, *w_far, *w_swapped, near, neighbour, *quarters)


def plan_kernel(
    capacity, slots, request_docs, doc_lengths, rows, queries, q, held, spare, key_bias, row_place, key_place,
    slot_row, counts
):
    head_dim = q.shape[1] // 2
    heads = queries.shape[2] // head_dim
    block_rows = 4 * rows.shape[0]
    scale = math.log2(math.e) / math.sqrt(head_dim)
    for b in range(queries.shape[1] // block_rows):
        for h in range(heads):
            here = queries[0, b * block_rows : (b + 1) * block_rows, h * head_dim : (h + 1) * head_dim]
            here = here.astype(jnp.float32) * scale
            high = here.astype(jnp.bfloat16)
            place = slice((b * heads + h) * block_rows, (b * heads + h + 1) * block_rows)
            q[place, :head_dim] = high
            q[place, head_dim:] = (here - high.astype(jnp.float32)).astype(jnp.bfloat16)
    me = lax.axis_index("seq")
    per_doc, _, doc_count = rows.shape
    doc_len = held.shape[0] // doc_count
    row_count = row_place.shape[0]
    docs = lax.broadcasted_iota(jnp.int32, (1, doc_count), 1)
    lengths = jnp.zeros((1, doc_count), jnp.int32)
    places = jnp.zeros((1, doc_count), jnp.int32)
    for o in range(counts.shape[0]):
        counts[o] = 0
    for j in range(doc_count):
        doc = request_docs[me, j]
        owner = lax.div(doc, slots)
        rank = counts[owner]
        counts[owner] = rank + 1
        lengths = jnp.where(docs == j, doc_lengths[doc], lengths)
        places = jnp.where(docs == j, owner * capacity + rank, places)
    slot = lax.broadcasted_iota(jnp.int32, (doc_len, doc_count), 0)
    used = slot < lengths
    for i in range(per_doc):
        used &= slot != rows[i]
    used = used.astype(jnp.float32)
    first = jnp.min(jnp.where(used > 0, slot, doc_len), axis=0, keepdims=True)
    firsts = (slot == first).astype(jnp.bfloat16)
    eye = lax.broadcasted_iota(jnp.int32, (doc_count, doc_count), 0) == docs
    across = (((1,), (1,)), ((), ()))

    def turned(columns):
        return lax.dot_general(
            eye.astype(jnp.bfloat16), columns, across, preferred_element_type=jnp.float32
        )

    bias = jnp.where(turned(used.astype(jnp.bfloat16)) > 0, 0.0, MASKED)
    firsts = turned(firsts)
    doc = lax.broadcasted_iota(jnp.int32, (doc_count, 1), 0)
    for j in range(doc_count):
        part = slice(j * doc_len, (j + 1) * doc_len)
        held[part, :] = jnp.broadcast_to(used[:, j : j + 1], (doc_len, held.shape[1])).astype(
            held.dtype
        )
        key_bias[:, part] = bias[j : j + 1, :]
        spare[:, part] = jnp.where(doc == j, firsts, 0.0).astype(spare.dtype)
    row = lax.broadcasted_iota(jnp.int32, (row_count, doc_count), 0)
    start = per_doc * lax.broadcasted_iota(jnp.int32, (row_count, doc_count), 1)
    of_doc = (row >= start) & (row < start + per_doc)
    nth = jnp.sum(jnp.where(of_doc, row - start, 0), axis=1, keepdims=True)
    chosen = jnp.zeros((row_count, doc_count), jnp.int32)
    for i in range(per_doc):
        chosen = jnp.where(nth == i, rows[i], chosen)
    chosen = jnp.where(of_doc, chosen + doc_len * docs, 0)
    column = jnp.sum(chosen, axis=1, keepdims=True)
    goes = nth + per_doc * jnp.sum(jnp.where(of_doc, places, 0), axis=1, keepdims=True)
    row_place[...] = column
    square = (row_count, row_count)
    same = lax.broadcasted_iota(jnp.int32, square, 0) == lax.broadcasted_iota(jnp.int32, square, 1)
    key_place[...] = jnp.full(key_place.shape, held.shape[0], jnp.int32)
    key_place[:, :row_count] = jnp.sum(jnp.where(same, column, 0), axis=0, keepdims=True)
    slot_row[...] = jnp.sum(jnp.where(same, goes, 0), axis=0, keepdims=True)


def plan(request_docs, doc_lengths, recompute_rows, queries, slots, head_dim, doc_len):
    _, doc_count, per_doc = recompute_rows.shape
    rows = doc_count * per_doc
    context = doc_count * doc_len
    shapes = (
        ((rows * queries.shape[2] // head_dim, 2 * head_dim), jnp.bfloat16),
        ((context, head_dim), jnp.bfloat16),
        ((doc_count, context), jnp.bfloat16),
        ((1, context), jnp.float32),
        ((rows, 1), jnp.int32),
        ((1, rows + -rows % 128), jnp.int32),
        ((1, rows), jnp.int32),
    )
    return pl.pallas_call(
        functools.partial(plan_kernel, slots // 2, slots),
        out_shape=tuple(jax.ShapeDtypeStruct(*one) for one in shapes),
        in_specs=[SMEM, SMEM, VMEM, VMEM],
        out_specs=(VMEM,) * len(shapes),
        scratch_shapes=[pltpu.SMEM((request_docs.shape[0],), jnp.int32)],
        compiler_params=pltpu.CompilerParams(vmem_limit_bytes=16 * 1024 * 1024),
        name="plan",
    )(request_docs, doc_lengths, jnp.transpose(recompute_rows, (2, 0, 1)), queries)


def finish_kernel(own, arrived_0, arrived_1, arrived_2, slot_row, fresh, outgoing):
    arrived = jnp.concatenate([arrived_0[...], arrived_1[...], arrived_2[...]], axis=0)
    total = (own[...] + arrived.astype(jnp.float32)).astype(jnp.bfloat16)
    fresh[...] = total
    width = outgoing.shape[1]
    slots = lax.broadcasted_iota(jnp.int32, (outgoing.shape[0], 1), 0)
    placed = jnp.zeros(outgoing.shape, jnp.float32)
    for i in range(2):
        pick = (slots == 2 * slot_row[...] + i).astype(jnp.bfloat16)
        part = total[:, i * width : (i + 1) * width]
        placed += jnp.dot(pick, part, preferred_element_type=jnp.float32)
    outgoing[...] = placed.astype(jnp.bfloat16)


def finish(own, arrived, slot_row, slots):
    shapes = (own.shape, (2 * slots, own.shape[1] // 2))
    return pl.pallas_call(
        finish_kernel,
        out_shape=tuple(jax.ShapeDtypeStruct(one, jnp.bfloat16) for one in shapes),
        in_specs=[VMEM] * 5,
        out_specs=(VMEM, VMEM),
        compiler_params=pltpu.CompilerParams(vmem_limit_bytes=16 * 1024 * 1024),
        name="finish",
    )(own, *arrived, slot_row)


def attend_kernel(
    by_owner, request_docs, q, fresh, held, spare, key_bias, row_place, key_place, *rest
):
    sources, (mixed, keys, values, counts, sems) = rest[:-5], rest[-5:]
    me = lax.axis_index("seq")
    doc_count = request_docs.shape[1]
    head_dim = keys.shape[1] // 2
    doc_len = keys.shape[0] // doc_count
    owners = request_docs.shape[0]
    slots = sources[0].shape[0] if not by_owner else 2 * sources[0].shape[1]
    step = doc_count // sems.shape[1]
    blocks = doc_count // step
    block_rows = mixed.shape[1] // blocks
    block_keys = step * doc_len
    heads = mixed.shape[2] // head_dim
    left = pl.ds(0, head_dim)

    for o in range(owners):
        counts[o] = 0

    def one_doc(j, carry):
        doc = request_docs[me, j]
        owner = lax.div(doc, slots)
        rank = counts[owner]
        counts[owner] = rank + 1
        place = pl.ds(pl.multiple_of(j * doc_len, doc_len), doc_len)
        block = lax.div(j, step)

        def fetch(key_source, value_source):
            pltpu.make_async_copy(key_source, keys.at[place, left], sems.at[0, block]).start()
            pltpu.make_async_copy(value_source, values.at[place, left], sems.at[1, block]).start()

        if by_owner:
            fetch(sources[0].at[owner, rank, 0], sources[0].at[owner, rank, 1])
        else:
            away = lax.bitwise_xor(me, owner)

            @pl.when(away == 0)
            def _():
                slot = lax.rem(doc, slots)
                fetch(sources[0].at[slot], sources[1].at[slot])

            for k, source in zip((2, 3, 1), sources[2:]):

                @pl.when(away == k)
                def _():
                    fetch(source.at[rank, 0], source.at[rank, 1])

        return carry

    lax.fori_loop(0, doc_count, one_doc, 0)

    def assemble(b):
        block = pl.ds(b * block_keys, block_keys)
        for i, context in enumerate((keys, values)):
            pltpu.make_async_copy(
                context.at[block, left], context.at[block, left], sems.at[i, b]
            ).wait()
        block = slice(b * block_keys, (b + 1) * block_keys)
        spares = jnp.dot(
            spare[:, block], keys[block, :head_dim], preferred_element_type=jnp.float32
        ).astype(jnp.bfloat16)
        for j in range(b * step, (b + 1) * step):
            place = slice(j * doc_len, (j + 1) * doc_len)
            used = held[place, :]
            key = jnp.where(used > 0, keys[place, :head_dim], spares[j : j + 1, :])
            keys[place, :head_dim] = key
            keys[place, head_dim:] = key
            values[place, :head_dim] = values[place, :head_dim] * used
            values[place, head_dim:] = used

    fresh_count = fresh.shape[0]
    spare_rows = jnp.zeros((-fresh_count % 128, 2 * head_dim), fresh.dtype)
    fresh_k = jnp.concatenate([fresh[:, :head_dim]] * 2, axis=1)
    fresh_k = jnp.concatenate([fresh_k, spare_rows], axis=0)
    fresh_v = jnp.concatenate([fresh[:, head_dim:], jnp.ones_like(fresh[:, head_dim:])], axis=1)
    fresh_v = jnp.concatenate([fresh_v, spare_rows], axis=0)
    slot_place = lax.broadcasted_iota(jnp.int32, (1, block_keys), 1)
    contract_last = (((1,), (1,)), ((), ()))
    for b in range(blocks):
        assemble(b)
    for b in range(blocks):
        rows = slice(b * block_rows, (b + 1) * block_rows)
        q_here = q[b * heads * block_rows : (b + 1) * heads * block_rows, :]
        own_place = row_place[rows, :]

        def scores(some_keys):
            return lax.dot_general(
                q_here, some_keys, contract_last, preferred_element_type=jnp.float32
            )

        def masked(some_keys, allowed):
            shape = (heads, block_rows, some_keys.shape[0])
            kept = jnp.where(allowed[None], scores(some_keys).reshape(shape), MASKED)
            return kept.reshape(heads * block_rows, some_keys.shape[0])

        part = slice(b * block_keys, (b + 1) * block_keys)
        allowed = (slot_place + b * block_keys <= own_place) & (key_bias[:, part] == 0)
        chunks = [scores(keys[: b * block_keys, :])] if b else []
        chunks.append(masked(keys[part, :], allowed))
        chunks.append(masked(fresh_k, key_place[...] <= own_place))
        lane_max = functools.reduce(
            jnp.maximum,
            [one[:, i : i + 128] for one in chunks for i in range(0, one.shape[1], 128)],
        )
        row_max = jnp.max(lane_max, axis=1, keepdims=True)
        powers = [jnp.exp2(one - row_max).astype(jnp.bfloat16) for one in chunks]
        total = jnp.dot(
            jnp.concatenate(powers[:-1], axis=1),
            values[: (b + 1) * block_keys, :],
            preferred_element_type=jnp.float32,
        )
        total += jnp.dot(powers[-1], fresh_v, preferred_element_type=jnp.float32)
        result = (total[:, :head_dim] / total[:, head_dim:]).astype(mixed.dtype)
        for h in range(heads):
            mixed[0, rows, h * head_dim : (h + 1) * head_dim] = result[
                h * block_rows : (h + 1) * block_rows
            ]


def attend(
    shape, request_docs, q, fresh, held, spare, key_bias, row_place, key_place, sources, by_owner
):
    context, head_dim = held.shape
    return pl.pallas_call(
        functools.partial(attend_kernel, by_owner),
        out_shape=jax.ShapeDtypeStruct(shape, jnp.bfloat16),
        in_specs=[SMEM] + [VMEM] * 7 + [ANY] * len(sources),
        out_specs=VMEM,
        scratch_shapes=[
            pltpu.VMEM((context, 2 * head_dim), jnp.bfloat16),
            pltpu.VMEM((context, 2 * head_dim), jnp.bfloat16),
            pltpu.SMEM((request_docs.shape[0],), jnp.int32),
            pltpu.SemaphoreType.DMA((2, 4)),
        ],
        compiler_params=pltpu.CompilerParams(vmem_limit_bytes=32 * 1024 * 1024),
        name="attend",
    )(
        request_docs,
        q,
        fresh,
        held,
        spare,
        key_bias,
        row_place,
        key_place,
        *(in_hbm(one) for one in sources[:2]),
        *sources[2:],
    )


def store_kernel(rows, out, sem):
    copy = pltpu.make_async_copy(rows, out, sem)
    copy.start()
    copy.wait()


def store(rows):
    return pl.pallas_call(
        store_kernel,
        out_shape=jax.ShapeDtypeStruct(rows.shape, rows.dtype),
        in_specs=[VMEM],
        out_specs=ANY,
        scratch_shapes=[pltpu.SemaphoreType.DMA],
        compiler_params=pltpu.CompilerParams(vmem_limit_bytes=1024 * 1024),
        name="store",
    )(rows)


def shards(
    pairs,
    hidden,
    queries,
    w_key,
    w_value,
    store_keys,
    store_values,
    request_docs,
    doc_lengths,
    recompute_rows,
):
    seq_count = lax.axis_size("seq")
    slot_count, doc_len, head_dim = store_keys.shape
    capacity = slot_count // 2
    per_doc = recompute_rows.shape[2]

    if pairs:
        def swap(array, axis, apart):
            count = lax.axis_size(axis)
            return lax.ppermute(array, axis, [(i, i ^ apart) for i in range(count)])

        *w_send, h_send = pick_sent(hidden, w_key, w_value)
        w_far = [swap(part, "seq", 2) for part in w_send]
        h_mine = swap(h_send, "seq", 1)
        doc_1, doc_2, doc_3 = pick_docs(request_docs, store_keys, store_values, False)
        (h_mine,) = gate((h_mine,), (doc_1,), cost=8000000000)
        h_chip = swap(h_mine, "tp", 2)
        h_core = swap(h_mine, "tp", 1)
        w_swapped = [swap(w_far[0], "groups", 1)]
        doc_2, doc_3, w_far[1] = gate(
            (doc_2, doc_3, w_far[1]), (w_swapped[0],), cost=8 * 10**9
        )
        w_swapped.append(swap(w_far[1], "groups", 1))
        doc_1 = swap(doc_1, "seq", 1)
        docs = (swap(doc_2, "seq", 2), swap(doc_3, "seq", 3), doc_1)
        quarters = (h_mine, h_core, h_chip, swap(h_chip, "tp", 1))
        own, *parts = project(hidden, w_key, w_value, w_far, w_swapped, quarters, doc_1)
        arrived = [swap(one, "seq", 1) for one in parts]
        sources = (store_keys, store_values, *docs)
    else:
        (docs,) = pick_docs(request_docs, store_keys, store_values, True)
        sources = (lax.all_to_all(docs, "seq", split_axis=0, concat_axis=0, tiled=True),)
        weights = lax.all_gather(
            jnp.concatenate([w_key, w_value], axis=1), "seq", axis=0, tiled=True
        )
        own = jnp.dot(hidden[0], weights, preferred_element_type=jnp.float32)
        arrived = [jnp.zeros((own.shape[0] // 3, 2 * head_dim), jnp.bfloat16)] * 3

    q, held, spare, key_bias, row_place, key_place, slot_row = plan(
        request_docs, doc_lengths, recompute_rows, queries, slot_count, head_dim, doc_len
    )
    fresh, outgoing = finish(own, arrived, slot_row, seq_count * capacity * per_doc)
    mixed = attend(
        queries.shape,
        request_docs,
        q,
        fresh,
        held,
        spare,
        key_bias,
        row_place,
        key_place,
        sources,
        not pairs,
    )

    outgoing = outgoing.reshape(seq_count, capacity * per_doc * 2, head_dim)
    returned = lax.all_to_all(outgoing, "seq", split_axis=0, concat_axis=0, tiled=True)
    if pairs:
        returned = store(returned)
    returned = returned.reshape(seq_count, capacity, per_doc, 2, head_dim)
    return (mixed, returned[None])


def solution(mesh):
    pairs = mesh.shape["seq"] == 4 and mesh.shape["groups"] == 2 and mesh.shape["tp"] == 4
    return jax.shard_map(
        functools.partial(shards, pairs),
        mesh=mesh,
        in_specs=(
            P(("groups", "seq"), None, None),
            P(("groups", "seq"), None, "tp"),
            P("seq", "tp"),
            P("seq", "tp"),
            P(("groups", "seq"), None, "tp"),
            P(("groups", "seq"), None, "tp"),
            P("groups", None),
            P("groups"),
            P(("groups", "seq"), None, None),
        ),
        out_specs=(
            P(("groups", "seq"), None, "tp"),
            P(("groups", "seq"), None, None, None, None, "tp"),
        ),
        check_vma=False,
    )
```
